32 devices in a mesh: fsdp: 16 (over z, x, core), tp: 2 (over y).
Axes of the slice: x: 2, y: 2, z: 4, core: 2. Of those that a mesh axis runs over, the one named last changes fastest.
Arguments:
- inputs: bfloat16 [10240, 2048], P(('fsdp', 'tp')), may hold values from -12 to 12
- cotangent: bfloat16 [10240, 2048], P(('fsdp', 'tp')), may hold values from -12 to 12
- lengths: int32 [16], replicated, may hold values from 384 to 640, as said below
- owners: int32 [16], replicated, may hold values from 0 to 15, each once
- qkv_weight: float32 [2048, 4096], P('fsdp', 'tp'), may hold values from -0.125 to 0.125
- out_weight: float32 [2048, 2048], P('tp', 'fsdp'), may hold values from -0.5 to 0.5
- gate_up_weight: float32 [2048, 12288], P('fsdp', 'tp'), may hold values from -0.125 to 0.125
- down_weight: float32 [6144, 2048], P('tp', 'fsdp'), may hold values from -0.12757759 to 0.12757759
- norm_gains: float32 [4352], replicated, may hold values from 0.3 to 3
- qkv_moment: float32 [2048, 4096], P('fsdp', 'tp'), may hold values from -9.1552734e-05 to 9.1552734e-05
- out_moment: float32 [2048, 2048], P('tp', 'fsdp'), may hold values from -9.1552734e-05 to 9.1552734e-05
- gate_up_moment: float32 [2048, 12288], P('fsdp', 'tp'), may hold values from -9.1552734e-05 to 9.1552734e-05
- down_moment: float32 [6144, 2048], P('tp', 'fsdp'), may hold values from -9.1552734e-05 to 9.1552734e-05
- gains_moment: float32 [4352], replicated, may hold values from -0.00036621094 to 0.00036621094
- qkv_square: float32 [2048, 4096], P('fsdp', 'tp'), may hold values from 1.9866497e-11 to 7.946599e-11
- out_square: float32 [2048, 2048], P('tp', 'fsdp'), may hold values from 1.9866497e-11 to 7.946599e-11
- gate_up_square: float32 [2048, 12288], P('fsdp', 'tp'), may hold values from 1.9866497e-11 to 7.946599e-11
- down_square: float32 [6144, 2048], P('tp', 'fsdp'), may hold values from 1.9866497e-11 to 7.946599e-11
- gains_square: float32 [4352], replicated, may hold values from 3.1786396e-10 to 1.2714558e-09
Outputs:
- output: bfloat16 [10240, 2048], P(('fsdp', 'tp'))
- input_grad: bfloat16 [10240, 2048], P(('fsdp', 'tp'))
- grad_norm: float32 [], replicated
- new_qkv: float32 [2048, 4096], P('fsdp', 'tp')
- new_qkv_moment: float32 [2048, 4096], P('fsdp', 'tp')
- new_qkv_square: float32 [2048, 4096], P('fsdp', 'tp')
- qkv_copy: bfloat16 [2048, 4096], P('fsdp', 'tp')
- new_out: float32 [2048, 2048], P('tp', 'fsdp')
- new_out_moment: float32 [2048, 2048], P('tp', 'fsdp')
- new_out_square: float32 [2048, 2048], P('tp', 'fsdp')
- out_copy: bfloat16 [2048, 2048], P('tp', 'fsdp')
- new_gate_up: float32 [2048, 12288], P('fsdp', 'tp')
- new_gate_up_moment: float32 [2048, 12288], P('fsdp', 'tp')
- new_gate_up_square: float32 [2048, 12288], P('fsdp', 'tp')
- gate_up_copy: bfloat16 [2048, 12288], P('fsdp', 'tp')
- new_down: float32 [6144, 2048], P('tp', 'fsdp')
- new_down_moment: float32 [6144, 2048], P('tp', 'fsdp')
- new_down_square: float32 [6144, 2048], P('tp', 'fsdp')
- down_copy: bfloat16 [6144, 2048], P('tp', 'fsdp')
- new_gains: float32 [4352], replicated
- new_gains_moment: float32 [4352], replicated
- new_gains_square: float32 [4352], replicated
The draws below stay inside these ranges and needn't reach their ends.
Inputs may be any that keep to these rules, and one draw needn't show every extreme that they name: `lengths`: every length is a multiple of 128; one sequence has exactly 640 tokens and one exactly 384.
All inputs are finite; a program needn't handle non-finite values.
Results may differ from the reference program's by a relative error of at most 0.019.
Values may be sent and summed in bfloat16 or wider, within the bound.
A program may use at most 384 MiB of HBM per device.

```python
import math
from functools import partial
import jax
import jax.numpy as jnp
from jax import lax

D = 2048
H = 16
KV = 8
HD = 128
FF = 6144
TOK_G = 640
QUANT = 128
STEP = 10
GROUPS = 2
TOKENS = 10240
NPARAMS = 50336000
N_FSDP = 16


def draw_lengths(key, part):
    key = jax.random.fold_in(key, 11)
    pick_key, level_key = jax.random.split(key)
    offsets = jax.random.randint(level_key, (N_FSDP,), 0, 3)
    chosen = jax.random.randint(pick_key, (), 0, N_FSDP)
    indices = jnp.arange(N_FSDP)
    offsets = jnp.where(indices == chosen, 0, offsets)
    offsets = jnp.where(indices == (chosen + 1) % N_FSDP, 2, offsets)
    return (TOK_G - offsets * QUANT).astype(jnp.int32)


def draw_down_weight(key, part):
    key = jax.random.fold_in(key, 13)
    entries = jnp.clip(jax.random.normal(key, (FF, D)), -6.0, 6.0)
    ramp = jnp.exp(jnp.linspace(jnp.log(0.75), jnp.log(1.3), FF))
    return (entries * ramp[:, None] * FF ** (-0.5)).astype(jnp.float32)


def draw_norm_gains(key, part):
    key = jax.random.fold_in(key, 12)
    first_key, second_key = jax.random.split(key)
    ramp = jnp.exp(jnp.linspace(jnp.log(0.75), jnp.log(1.3), D))
    rough = jax.random.uniform(first_key, (2, D), minval=0.7, maxval=1.4)
    wide_part = (ramp[None, :] * rough).reshape(2 * D)
    head_part = jax.random.uniform(second_key, (2 * HD,), minval=0.6, maxval=1.6)
    return jnp.concatenate([wide_part, head_part]).astype(jnp.float32)


def raised(array, stream_key, source, target, parts, factor):
    owner, partner = [(jnp.arange(array.shape[axis_at]) // (array.shape[axis_at] // parts)).reshape([-1 if axis == axis_at else 1 for axis in range(array.ndim)]) for axis_at in (source, target)]
    chosen = jax.random.permutation(stream_key, parts)[partner]
    strong = (owner == chosen) | (owner == (partner + parts // 2) % parts)
    return jnp.where(strong, factor * array, array)


def level_of(stream_key, shape, shards, least, high):
    level, own = 1.0, jax.random.fold_in(stream_key, 6)
    for dim, parts in shards:
        draws = jnp.exp(jax.random.uniform(jax.random.fold_in(own, dim), (parts,), jnp.float32, least / len(shards), high / len(shards)))
        level = level * jnp.repeat(draws, shape[dim] // parts).reshape([-1 if axis == dim else 1 for axis in range(len(shape))])
    return level


def scatter_about(own_key, dims, scale, limit, pieces=(), kind=jnp.bfloat16):
    values = scale * jax.random.normal(own_key, dims, jnp.float32)
    if pieces:
        values = values * level_of(own_key, dims, pieces, -0.22, 0.18)
    return jnp.clip(values, -limit, limit).astype(kind)


def noise_with(own_key, extent, scale, bound, cuts, heavy, held_as=jnp.bfloat16):
    values = scale * jax.random.normal(own_key, extent, jnp.float32)
    if cuts:
        values = values * level_of(own_key, extent, cuts, -0.22, 0.18)
    return jnp.clip(raised(values, jax.random.fold_in(own_key, 3), *heavy), -bound, bound).astype(held_as)


def setup_inputs(seed: int = 0) -> dict:
    streams_of = jax.random.split(jax.random.key(seed), 20)
    return {
        "inputs": noise_with(streams_of[0], (TOKENS, D), 1.0, 12.0, ((0, 32),), (0, 1, 32, 2.75)),
        "cotangent": noise_with(streams_of[1], (TOKENS, D), 1.0, 12.0, ((0, 32),), (0, 1, 32, 2.75)),
        "lengths": draw_lengths(jax.random.fold_in(streams_of[19], 71), 0),
        "owners": jax.random.permutation(streams_of[3], N_FSDP).astype(jnp.int32),
        "qkv_weight": scatter_about(streams_of[4], (D, (H + 2 * KV) * HD), D ** -0.5, 0.125, ((0, 16), (1, 2)), jnp.float32),
        "out_weight": scatter_about(streams_of[5], (H * HD, D), (max(1, H * HD // 16)) ** -0.5, 0.5, ((0, 2), (1, 16)), jnp.float32),
        "gate_up_weight": scatter_about(streams_of[6], (D, 2 * FF), D ** -0.5, 0.125, ((0, 16), (1, 2)), jnp.float32),
        "down_weight": draw_down_weight(jax.random.fold_in(streams_of[19], 71), 0),
        "norm_gains": draw_norm_gains(jax.random.fold_in(streams_of[19], 71), 0),
        "qkv_moment": scatter_about(streams_of[9], (D, (H + 2 * KV) * HD), (0.11 * NPARAMS ** -0.5), 9.1552734375e-05, ((0, 16), (1, 2)), jnp.float32),
        "out_moment": scatter_about(streams_of[10], (H * HD, D), (0.11 * NPARAMS ** -0.5), 9.1552734375e-05, ((0, 2), (1, 16)), jnp.float32),
        "gate_up_moment": scatter_about(streams_of[11], (D, 2 * FF), (0.11 * NPARAMS ** -0.5), 9.1552734375e-05, ((0, 16), (1, 2)), jnp.float32),
        "down_moment": scatter_about(streams_of[12], (FF, D), (0.11 * NPARAMS ** -0.5), 9.1552734375e-05, ((0, 2), (1, 16)), jnp.float32),
        "gains_moment": scatter_about(streams_of[13], (2 * D + 2 * HD,), (0.44 * NPARAMS ** -0.5), 0.00036621094, (), jnp.float32),
        "qkv_square": jnp.clip(jnp.exp(math.log(7.946598934438498e-11) - 1.3862944 * jax.random.uniform(streams_of[14], (D, (H + 2 * KV) * HD), jnp.float32) ** level_of(streams_of[14], (D, (H + 2 * KV) * HD), ((0, 16), (1, 2)), -0.2, 0.2)), 1.9866497336096245e-11, 7.946598934438498e-11),
        "out_square": jnp.clip(jnp.exp(math.log(7.946598934438498e-11) - 1.3862944 * jax.random.uniform(streams_of[15], (H * HD, D), jnp.float32) ** level_of(streams_of[15], (H * HD, D), ((0, 2), (1, 16)), -0.2, 0.2)), 1.9866497336096245e-11, 7.946598934438498e-11),
        "gate_up_square": jnp.clip(jnp.exp(math.log(7.946598934438498e-11) - 1.3862944 * jax.random.uniform(streams_of[16], (D, 2 * FF), jnp.float32) ** level_of(streams_of[16], (D, 2 * FF), ((0, 16), (1, 2)), -0.2, 0.2)), 1.9866497336096245e-11, 7.946598934438498e-11),
        "down_square": jnp.clip(jnp.exp(math.log(7.946598934438498e-11) - 1.3862944 * jax.random.uniform(streams_of[17], (FF, D), jnp.float32) ** level_of(streams_of[17], (FF, D), ((0, 2), (1, 16)), -0.2, 0.2)), 1.9866497336096245e-11, 7.946598934438498e-11),
        "gains_square": jnp.clip(jnp.exp(jax.random.uniform(streams_of[18], (2 * D + 2 * HD,), jnp.float32, math.log(3.178639573775399e-10), math.log(1.2714558295101597e-09))), 3.178639573775399e-10, 1.2714558295101597e-09),
    }


norm_epsilon = 1e-06
rope_base = 1000000.0
clip_norm = 1.0
learn_rate = 0.04
gain_rate = 0.8
beta_first = 0.9
beta_second = 0.999
adam_epsilon = 1e-08
weight_decay = 0.1
masked_score = -1e+30

@jax.custom_vjp
def low(v):
    return lax.optimization_barrier(v.astype(jnp.bfloat16)).astype(jnp.float32)

@jax.custom_vjp
def low_back(v):
    return v

def low_keep(v):
    return (low(v), None)

def low_pass(kept, grad):
    return (grad,)

def back_keep(v):
    return (v, None)

def back_low(kept, grad):
    return (low(grad),)
low.defvjp(low_keep, low_pass)
low_back.defvjp(back_keep, back_low)

def rms_scale(values):
    return lax.rsqrt(lax.optimization_barrier(jnp.mean(values * values, axis=-1, keepdims=True)) + norm_epsilon)

def norm_apply(values, gain):
    return values * rms_scale(values) * gain

def rotary(positions, width):
    half_width = width // 2
    frequency = rope_base ** (-(jnp.arange(half_width, dtype=jnp.float32) * 2.0 / width))
    angles = positions.astype(jnp.float32)[:, None] * frequency[None, :]
    return (jnp.cos(angles), jnp.sin(angles))

def rotate(values, cos_table, sin_table):
    half_width = values.shape[-1] // 2
    first_half = values[..., :half_width]
    second_half = values[..., half_width:]
    cosine = cos_table[:, None, :]
    sine_part = sin_table[:, None, :]
    return jnp.concatenate([first_half * cosine - second_half * sine_part, second_half * cosine + first_half * sine_part], axis=-1)

def head_prepare(raw, gain, cos_table, sin_table):
    return rotate(norm_apply(raw, gain), cos_table, sin_table)

def swish_product(gate_part, up_part):
    return jax.nn.silu(gate_part) * up_part

def layer_group(block, qkv_weight, out_weight, gate_up_weight, down_weight, norm_gains, length):
    highest = lax.Precision.HIGHEST
    row_count = block.shape[0]
    positions = jnp.arange(row_count)
    attn_gain = norm_gains[:D]
    mlp_gain = norm_gains[D:2 * D]
    query_gain = norm_gains[2 * D:2 * D + HD]
    key_gain = norm_gains[2 * D + HD:]
    local_heads = H // GROUPS
    local_groups = KV // GROUPS
    local_hidden = FF // GROUPS
    repeat = H // KV
    normed_attn = low(norm_apply(block, attn_gain))
    projected = low_back(jnp.dot(normed_attn, low(qkv_weight), precision=highest))
    projected = projected.reshape(row_count, GROUPS, (local_heads + 2 * local_groups) * HD)
    query_raw = projected[:, :, :local_heads * HD].reshape(row_count, H, HD)
    key_raw = projected[:, :, local_heads * HD:(local_heads + local_groups) * HD].reshape(row_count, KV, HD)
    value_raw = projected[:, :, (local_heads + local_groups) * HD:].reshape(row_count, KV, HD)
    cos_table, sin_table = rotary(positions, HD)
    queries = low(head_prepare(query_raw, query_gain, cos_table, sin_table))
    key_heads = jnp.repeat(low(head_prepare(key_raw, key_gain, cos_table, sin_table)), repeat, axis=1)
    value_heads = jnp.repeat(low(value_raw), repeat, axis=1)
    key_mask = (positions[None, :] <= positions[:, None]) & (positions[None, :] < length)
    scores = low_back(jnp.einsum('qhd,khd->hqk', queries, key_heads, precision=highest) * HD ** (-0.5))
    scores = jnp.where(key_mask[None], scores, masked_score)
    attention = jax.nn.softmax(scores, axis=-1)
    mixed_heads = jnp.einsum('hqk,khd->qhd', low(attention), value_heads, precision=highest)
    attended = low(low_back(mixed_heads.reshape(row_count, H * HD)))
    attn_branch = low_back(jnp.dot(attended, low(out_weight), precision=highest))
    hidden = block + attn_branch
    normed_mlp = low(norm_apply(hidden, mlp_gain))
    gate_up = low_back(jnp.dot(normed_mlp, low(gate_up_weight), precision=highest))
    gate_up = gate_up.reshape(row_count, GROUPS, 2, local_hidden)
    gate_part = gate_up[:, :, 0].reshape(row_count, FF)
    up_part = gate_up[:, :, 1].reshape(row_count, FF)
    activated = low(swish_product(gate_part, up_part))
    mlp_branch = low_back(jnp.dot(activated, low(down_weight), precision=highest))
    return hidden + mlp_branch

def adam_update(weight, gradient, moment_one, moment_two, factor, decay_rate, rate_value):
    clipped = gradient * factor
    moment_one = beta_first * moment_one + (1.0 - beta_first) * clipped
    moment_two = beta_second * moment_two + (1.0 - beta_second) * clipped * clipped
    first_fixed = moment_one / (1.0 - beta_first ** STEP)
    second_fixed = moment_two / (1.0 - beta_second ** STEP)
    weight = weight - rate_value * (first_fixed / (jnp.sqrt(second_fixed) + adam_epsilon) + decay_rate * weight)
    return (weight, moment_one, moment_two)

def reference(inputs, cotangent, lengths, owners, qkv_weight, out_weight, gate_up_weight, down_weight, norm_gains, qkv_moment, out_moment, gate_up_moment, down_moment, gains_moment, qkv_square, out_square, gate_up_square, down_square, gains_square):
    group_ids = jnp.arange(N_FSDP)
    group_length = lax.optimization_barrier(jnp.sum(jnp.where(owners[None, :] == group_ids[:, None], lengths[None, :], 0), axis=1)).astype(jnp.int32)
    parameters = (qkv_weight, out_weight, gate_up_weight, down_weight, norm_gains)
    blocks = inputs.astype(jnp.float32).reshape(N_FSDP, TOK_G, D)
    grad_blocks = cotangent.astype(jnp.float32).reshape(N_FSDP, TOK_G, D)

    def group_forward(block, weights, length):
        return layer_group(block, weights[0], weights[1], weights[2], weights[3], weights[4], length)

    def group_step(totals, scan_item):
        block, grad_block, length = scan_item
        valid_rows = (jnp.arange(TOK_G) < length).astype(jnp.float32)[:, None]
        result, pullback = jax.vjp(partial(group_forward, length=length), block, parameters)
        grad_block_in, grad_params = pullback(grad_block * valid_rows)
        totals = jax.tree.map(jnp.add, totals, grad_params)
        return (totals, (result, grad_block_in))
    zero_grads = jax.tree.map(jnp.zeros_like, parameters)
    gradients, (outputs, input_grads) = lax.scan(group_step, zero_grads, (blocks, grad_blocks, group_length))
    square_total = sum((jnp.sum(member * member) for member in gradients))
    grad_norm = jnp.sqrt(square_total)
    factor = jnp.minimum(1.0, clip_norm / (grad_norm + 1e-06))
    moments = (qkv_moment, out_moment, gate_up_moment, down_moment, gains_moment)
    squares = (qkv_square, out_square, gate_up_square, down_square, gains_square)
    results = []
    for number in range(5):
        decay_rate = weight_decay if number < 4 else 0.0
        rate_value = learn_rate if number < 4 else gain_rate
        new_weight, new_one, new_two = adam_update(parameters[number], gradients[number], moments[number], squares[number], factor, decay_rate, rate_value)
        results.append((new_weight, new_one, new_two))
    output = outputs.reshape(TOKENS, D).astype(jnp.bfloat16)
    input_grad = input_grads.reshape(TOKENS, D).astype(jnp.bfloat16)
    return (output, input_grad, grad_norm, results[0][0], results[0][1], results[0][2], results[0][0].astype(jnp.bfloat16), results[1][0], results[1][1], results[1][2], results[1][0].astype(jnp.bfloat16), results[2][0], results[2][1], results[2][2], results[2][0].astype(jnp.bfloat16), results[3][0], results[3][1], results[3][2], results[3][0].astype(jnp.bfloat16), results[4][0], results[4][1], results[4][2])
```

```python
from functools import partial

import jax
import jax.numpy as jnp
from jax import lax
from jax.sharding import PartitionSpec as P

D = 2048
H = 16
KV = 8
HD = 128
FF = 6144
STEP = 10


norm_epsilon = 1e-06
rope_base = 1000000.0
clip_norm = 1.0
learn_rate = 0.04
gain_rate = 0.8
beta_first = 0.9
beta_second = 0.999
adam_epsilon = 1e-08
weight_decay = 0.1
masked_score = -1e30


def rms_scale(values):
    return lax.rsqrt(jnp.mean(values * values, axis=-1, keepdims=True) + norm_epsilon)


def norm_apply(values, gain):
    return values * rms_scale(values) * gain


def rotary(positions, width):
    half_width = width // 2
    frequency = rope_base ** (-(jnp.arange(half_width, dtype=jnp.float32) * 2.0 / width))
    angles = positions.astype(jnp.float32)[:, None] * frequency[None, :]
    return (jnp.cos(angles), jnp.sin(angles))


def rotate(values, cos_table, sin_table):
    half_width = values.shape[-1] // 2
    first_half = values[..., :half_width]
    second_half = values[..., half_width:]
    cosine = cos_table[:, None, :]
    sine_part = sin_table[:, None, :]
    return jnp.concatenate(
        [
            first_half * cosine - second_half * sine_part,
            second_half * cosine + first_half * sine_part,
        ],
        axis=-1,
    )


def head_prepare(raw, gain, cos_table, sin_table):
    return rotate(norm_apply(raw, gain), cos_table, sin_table)


def swish_product(gate_part, up_part):
    return jax.nn.silu(gate_part) * up_part


def score_block(queries, key_heads, key_mask, score_scale):
    scores = (
        jnp.einsum("qgrd,kgd->grqk", queries, key_heads, preferred_element_type=jnp.float32)
        * score_scale
    )
    return jnp.where(key_mask[None, None], scores, masked_score)


def gather_rows(values):
    return lax.all_gather(values, "tp", axis=0, tiled=True)


def sum_rows(values):
    return lax.psum_scatter(
        values.astype(jnp.bfloat16), "tp", scatter_dimension=0, tiled=True
    ).astype(jnp.float32)


def gather_grads(values):
    return lax.all_gather(values, "tp", axis=0, tiled=True)


def sum_grads(values):
    return lax.psum_scatter(
        values.astype(jnp.bfloat16), "tp", scatter_dimension=0, tiled=True
    ).astype(jnp.float32)


def sum_weight(values, axis):
    return lax.psum_scatter(
        values.astype(jnp.bfloat16), "fsdp", scatter_dimension=axis, tiled=True
    ).astype(jnp.float32)


def adam_update(weight, gradient, moment_one, moment_two, factor, decay_rate, rate_value):
    clipped = gradient * factor
    moment_one = beta_first * moment_one + (1.0 - beta_first) * clipped
    moment_two = beta_second * moment_two + (1.0 - beta_second) * clipped * clipped
    first_fixed = moment_one / (1.0 - beta_first**STEP)
    second_fixed = moment_two / (1.0 - beta_second**STEP)
    weight = weight - rate_value * (
        first_fixed / (jnp.sqrt(second_fixed) + adam_epsilon) + decay_rate * weight
    )
    return (weight, moment_one, moment_two)


def local(
    inputs,
    cotangent,
    lengths,
    owners,
    qkv_weight,
    out_weight,
    gate_up_weight,
    down_weight,
    norm_gains,
    qkv_moment,
    out_moment,
    gate_up_moment,
    down_moment,
    gains_moment,
    qkv_square,
    out_square,
    gate_up_square,
    down_square,
    gains_square,
):
    tp_count = lax.axis_size("tp")
    local_heads = H // tp_count
    local_groups = KV // tp_count
    local_hidden = FF // tp_count
    repeat = H // KV
    half_rows = inputs.shape[0]
    row_count = half_rows * tp_count
    group_rank = lax.axis_index("fsdp")
    length = jnp.sum(jnp.where(owners == group_rank, lengths, 0))
    positions = jnp.arange(row_count)
    key_mask = (positions[None, :] <= positions[:, None]) & (positions[None, :] < length)
    own_rows = lax.axis_index("tp") * half_rows + jnp.arange(half_rows)
    valid_rows = (own_rows < length).astype(jnp.float32)[:, None]
    cos_table, sin_table = rotary(positions, HD)
    score_scale = HD ** (-0.5)
    attn_gain = norm_gains[:D]
    mlp_gain = norm_gains[D : 2 * D]
    query_gain = norm_gains[2 * D : 2 * D + HD]
    key_gain = norm_gains[2 * D + HD :]
    head_apply = partial(head_prepare, cos_table=cos_table, sin_table=sin_table)
    qkv_shard = qkv_weight.astype(jnp.bfloat16)
    out_shard = out_weight.astype(jnp.bfloat16)
    gate_up_shard = gate_up_weight.astype(jnp.bfloat16)
    down_shard = down_weight.astype(jnp.bfloat16)
    qkv_full, out_full, gate_up_full, down_full = (
        lax.all_gather(qkv_shard, "fsdp", axis=0, tiled=True),
        lax.all_gather(out_shard, "fsdp", axis=1, tiled=True),
        lax.all_gather(gate_up_shard, "fsdp", axis=0, tiled=True),
        lax.all_gather(down_shard, "fsdp", axis=1, tiled=True),
    )
    residual_in = inputs.astype(jnp.float32)
    normed_attn = gather_rows(norm_apply(residual_in, attn_gain).astype(jnp.bfloat16))
    projected = jnp.dot(normed_attn, qkv_full, preferred_element_type=jnp.float32)
    query_raw = projected[:, : local_heads * HD].reshape(row_count, local_heads, HD)
    key_raw = projected[:, local_heads * HD : (local_heads + local_groups) * HD].reshape(
        row_count, local_groups, HD
    )
    value_raw = projected[:, (local_heads + local_groups) * HD :].reshape(
        row_count, local_groups, HD
    )
    queries = (
        head_apply(query_raw, query_gain)
        .astype(jnp.bfloat16)
        .reshape(row_count, local_groups, repeat, HD)
    )
    key_heads = head_apply(key_raw, key_gain).astype(jnp.bfloat16)
    value_heads = value_raw.astype(jnp.bfloat16)
    scores = score_block(queries, key_heads, key_mask, score_scale)
    row_max = jnp.max(scores, axis=-1, keepdims=True)
    exponent = jnp.exp(scores - row_max)
    row_total = jnp.sum(exponent, axis=-1, keepdims=True)
    log_total = row_max + jnp.log(row_total)
    attention = exponent / row_total
    attended = (
        jnp.einsum(
            "grqk,kgd->qgrd",
            attention.astype(jnp.bfloat16),
            value_heads,
            preferred_element_type=jnp.float32,
        )
        .reshape(row_count, local_heads * HD)
        .astype(jnp.bfloat16)
    )
    attn_branch = sum_rows(jnp.dot(attended, out_full, preferred_element_type=jnp.float32))
    hidden = residual_in + attn_branch
    normed_mlp = gather_rows(norm_apply(hidden, mlp_gain).astype(jnp.bfloat16))
    gate_up = jnp.dot(normed_mlp, gate_up_full, preferred_element_type=jnp.float32)
    gate_part = gate_up[:, :local_hidden]
    up_part = gate_up[:, local_hidden:]
    activated = swish_product(gate_part, up_part).astype(jnp.bfloat16)
    mlp_branch = sum_rows(jnp.dot(activated, down_full, preferred_element_type=jnp.float32))
    output = (hidden + mlp_branch).astype(jnp.bfloat16)
    grad_output = cotangent.astype(jnp.float32) * valid_rows
    grad_low = gather_grads(grad_output.astype(jnp.bfloat16))
    grad_activated = jnp.einsum(
        "td,fd->tf", grad_low, down_full, preferred_element_type=jnp.float32
    )
    swish_pull = jax.vjp(swish_product, gate_part, up_part)[1]
    grad_gate, grad_up = swish_pull(grad_activated)
    grad_gate_up = jnp.concatenate([grad_gate, grad_up], axis=1).astype(jnp.bfloat16)
    grad_normed_mlp = sum_grads(
        jnp.einsum("tf,df->td", grad_gate_up, gate_up_full, preferred_element_type=jnp.float32)
    )
    mlp_pull = jax.vjp(norm_apply, hidden, mlp_gain)[1]
    grad_hidden_norm, grad_mlp_gain = mlp_pull(grad_normed_mlp)
    grad_hidden = grad_output + grad_hidden_norm
    grad_attn = gather_grads(grad_hidden.astype(jnp.bfloat16))
    grad_attended = jnp.einsum("td,cd->tc", grad_attn, out_full, preferred_element_type=jnp.float32)
    grad_attended = grad_attended.astype(jnp.bfloat16).reshape(row_count, local_groups, repeat, HD)
    attention = jnp.exp(score_block(queries, key_heads, key_mask, score_scale) - log_total)
    grad_probs = jnp.einsum(
        "qgrd,kgd->grqk", grad_attended, value_heads, preferred_element_type=jnp.float32
    )
    grad_values = jnp.einsum(
        "grqk,qgrd->kgd",
        attention.astype(jnp.bfloat16),
        grad_attended,
        preferred_element_type=jnp.float32,
    )
    inner_sum = jnp.sum(attention * grad_probs, axis=-1, keepdims=True)
    grad_scores = (attention * (grad_probs - inner_sum)).astype(jnp.bfloat16)
    grad_queries = (
        jnp.einsum("grqk,kgd->qgrd", grad_scores, key_heads, preferred_element_type=jnp.float32)
        * score_scale
    )
    grad_keys = (
        jnp.einsum("grqk,qgrd->kgd", grad_scores, queries, preferred_element_type=jnp.float32)
        * score_scale
    )
    query_pull = jax.vjp(head_apply, query_raw, query_gain)[1]
    grad_query_raw, grad_query_gain = query_pull(grad_queries.reshape(row_count, local_heads, HD))
    key_pull = jax.vjp(head_apply, key_raw, key_gain)[1]
    grad_key_raw, grad_key_gain = key_pull(grad_keys)
    grad_projected = jnp.concatenate(
        [
            grad_query_raw.reshape(row_count, local_heads * HD),
            grad_key_raw.reshape(row_count, local_groups * HD),
            grad_values.reshape(row_count, local_groups * HD),
        ],
        axis=1,
    ).astype(jnp.bfloat16)
    grad_down = jnp.einsum("tf,td->fd", activated, grad_low, preferred_element_type=jnp.float32)
    grad_gate_up_weight = jnp.einsum(
        "td,tf->df", normed_mlp, grad_gate_up, preferred_element_type=jnp.float32
    )
    grad_out_weight = jnp.einsum(
        "tc,td->cd", attended, grad_attn, preferred_element_type=jnp.float32
    )
    grad_qkv_weight = jnp.einsum(
        "td,tc->dc", normed_attn, grad_projected, preferred_element_type=jnp.float32
    )
    qkv_sum, out_sum, gate_up_sum, down_sum = (
        sum_weight(grad_qkv_weight, 0),
        sum_weight(grad_out_weight, 1),
        sum_weight(grad_gate_up_weight, 0),
        sum_weight(grad_down, 1),
    )
    grad_normed_attn = sum_grads(
        jnp.einsum("tc,dc->td", grad_projected, qkv_full, preferred_element_type=jnp.float32)
    )
    attn_pull = jax.vjp(norm_apply, residual_in, attn_gain)[1]
    grad_input_norm, grad_attn_gain = attn_pull(grad_normed_attn)
    input_grad = (grad_hidden + grad_input_norm).astype(jnp.bfloat16)
    gain_part = jnp.concatenate([grad_attn_gain, grad_mlp_gain, grad_query_gain, grad_key_gain])
    square_part = sum(
        (jnp.sum(member * member) for member in (qkv_sum, out_sum, gate_up_sum, down_sum))
    )
    gain_grad, square_total = lax.psum((gain_part, square_part), ("fsdp", "tp"))
    grad_norm = jnp.sqrt(square_total + jnp.sum(gain_grad * gain_grad))
    factor = jnp.minimum(1.0, clip_norm / (grad_norm + 1e-06))
    new_qkv, new_qkv_one, new_qkv_two = adam_update(
        qkv_weight, qkv_sum, qkv_moment, qkv_square, factor, weight_decay, learn_rate
    )
    new_out, new_out_one, new_out_two = adam_update(
        out_weight, out_sum, out_moment, out_square, factor, weight_decay, learn_rate
    )
    new_gate_up, new_gate_up_one, new_gate_up_two = adam_update(
        gate_up_weight,
        gate_up_sum,
        gate_up_moment,
        gate_up_square,
        factor,
        weight_decay,
        learn_rate,
    )
    new_down, new_down_one, new_down_two = adam_update(
        down_weight, down_sum, down_moment, down_square, factor, weight_decay, learn_rate
    )
    new_gains, new_gains_one, new_gains_two = adam_update(
        norm_gains, gain_grad, gains_moment, gains_square, factor, 0.0, gain_rate
    )
    return (
        output,
        input_grad,
        grad_norm,
        new_qkv,
        new_qkv_one,
        new_qkv_two,
        new_qkv.astype(jnp.bfloat16),
        new_out,
        new_out_one,
        new_out_two,
        new_out.astype(jnp.bfloat16),
        new_gate_up,
        new_gate_up_one,
        new_gate_up_two,
        new_gate_up.astype(jnp.bfloat16),
        new_down,
        new_down_one,
        new_down_two,
        new_down.astype(jnp.bfloat16),
        new_gains,
        new_gains_one,
        new_gains_two,
    )


def solution(mesh):
    return jax.shard_map(
        local,
        mesh=mesh,
        in_specs=(
            P(("fsdp", "tp"), None),
            P(("fsdp", "tp"), None),
            P(),
            P(),
            P("fsdp", "tp"),
            P("tp", "fsdp"),
            P("fsdp", "tp"),
            P("tp", "fsdp"),
            P(),
            P("fsdp", "tp"),
            P("tp", "fsdp"),
            P("fsdp", "tp"),
            P("tp", "fsdp"),
            P(),
            P("fsdp", "tp"),
            P("tp", "fsdp"),
            P("fsdp", "tp"),
            P("tp", "fsdp"),
            P(),
        ),
        out_specs=(
            P(("fsdp", "tp"), None),
            P(("fsdp", "tp"), None),
            P(),
            P("fsdp", "tp"),
            P("fsdp", "tp"),
            P("fsdp", "tp"),
            P("fsdp", "tp"),
            P("tp", "fsdp"),
            P("tp", "fsdp"),
            P("tp", "fsdp"),
            P("tp", "fsdp"),
            P("fsdp", "tp"),
            P("fsdp", "tp"),
            P("fsdp", "tp"),
            P("fsdp", "tp"),
            P("tp", "fsdp"),
            P("tp", "fsdp"),
            P("tp", "fsdp"),
            P("tp", "fsdp"),
            P(),
            P(),
            P(),
        ),
        check_vma=False,
    )
```

```python
from functools import partial

import jax
import jax.numpy as jnp
from jax import lax
from jax.sharding import Mesh, PartitionSpec as P

D = 2048
H = 16
KV = 8
HD = 128
FF = 6144
STEP = 10


norm_epsilon = 1e-06
rope_base = 1000000.0
clip_norm = 1.0
learn_rate = 0.04
gain_rate = 0.8
beta_first = 0.9
beta_second = 0.999
adam_epsilon = 1e-08
weight_decay = 0.1
masked_score = -1e30

NEAR = 2
CORE = 2
TEAM = NEAR * CORE
LAYER = ("near", "core", "tp")


def rms_scale(values):
    return lax.rsqrt(jnp.mean(values * values, axis=-1, keepdims=True) + norm_epsilon)


def norm_apply(values, gain):
    return values * rms_scale(values) * gain


def rotary(positions, width):
    half_width = width // 2
    frequency = rope_base ** (-(jnp.arange(half_width, dtype=jnp.float32) * 2.0 / width))
    angles = positions.astype(jnp.float32)[:, None] * frequency[None, :]
    return (jnp.cos(angles), jnp.sin(angles))


def rotate(values, cos_table, sin_table):
    half_width = values.shape[-1] // 2
    first_half = values[..., :half_width]
    second_half = values[..., half_width:]
    cosine = cos_table[:, None, :]
    sine_part = sin_table[:, None, :]
    return jnp.concatenate(
        [
            first_half * cosine - second_half * sine_part,
            second_half * cosine + first_half * sine_part,
        ],
        axis=-1,
    )


def head_prepare(raw, gain, cos_table, sin_table):
    return rotate(norm_apply(raw, gain), cos_table, sin_table)


def swish_product(gate_part, up_part):
    return jax.nn.silu(gate_part) * up_part


def score_block(queries, key_heads, key_mask, score_scale):
    scores = (
        jnp.einsum("sqrd,skd->srqk", queries, key_heads, preferred_element_type=jnp.float32)
        * score_scale
    )
    return jnp.where(key_mask[:, None], scores, masked_score)


def swap(values, axis):
    return lax.ppermute(values, axis, [(0, 1), (1, 0)])


def pick(values, index):
    return lax.dynamic_index_in_dim(values, index, 0, keepdims=False)


def put(buffer, values, *index):
    zero = jnp.zeros((), jnp.int32)
    start = tuple(index) + (zero,) * (buffer.ndim - len(index))
    return lax.dynamic_update_slice(buffer, values[(None,) * len(index)], start)


def gather_rows(values):
    near, core, tp = (lax.axis_index(name) for name in LAYER)
    half = values.shape[0] // 2
    buffer = jnp.zeros((NEAR, CORE, 2) + values.shape, values.dtype)
    by_near = swap(values, "near")
    by_tp = swap(values, "tp")
    far_top = swap(by_tp[:half], "near")
    far_low = swap(by_near[half:], "tp")
    by_both = jnp.concatenate([far_top, far_low], axis=0)
    for where_near, where_tp, block in (
        (near, tp, values),
        (1 - near, tp, by_near),
        (near, 1 - tp, by_tp),
        (1 - near, 1 - tp, by_both),
    ):
        buffer = put(buffer, block, where_near, core, where_tp)
        buffer = put(buffer, swap(block, "core"), where_near, 1 - core, where_tp)
    return buffer.reshape(-1, values.shape[1])


def sum_rows(values, multiply):
    near, core, tp = (lax.axis_index(name) for name in LAYER)
    blocks = values.reshape(NEAR, CORE, 2, -1, values.shape[1])

    def part(which):
        chosen = lax.dynamic_index_in_dim(blocks, which, 1, keepdims=False)
        flat = chosen.reshape(-1, values.shape[1])
        return multiply(flat).reshape(NEAR, 2, -1, D)

    theirs = swap(part(1 - core).astype(jnp.bfloat16), "core")
    ours = part(core) + theirs.astype(jnp.float32)

    def block(where_near, where_tp):
        return pick(pick(ours, where_near), where_tp)

    far = block(1 - near, 1 - tp).astype(jnp.bfloat16)
    half = far.shape[0] // 2
    top = swap(far[:half], "near").astype(jnp.float32)
    low = swap(far[half:], "tp").astype(jnp.float32)
    to_tp = block(near, 1 - tp)
    to_tp = jnp.concatenate([to_tp[:half] + top, to_tp[half:]], axis=0)
    to_near = block(1 - near, tp)
    to_near = jnp.concatenate([to_near[:half], to_near[half:] + low], axis=0)
    from_tp = swap(to_tp.astype(jnp.bfloat16), "tp").astype(jnp.float32)
    from_near = swap(to_near.astype(jnp.bfloat16), "near").astype(jnp.float32)
    return block(near, tp) + from_tp + from_near


def team_swap(values, offset):
    pairs = [(member, member ^ offset) for member in range(TEAM)]
    return lax.ppermute(values, ("near", "core"), pairs)


def team_exchange(pieces):
    own = lax.axis_index("near") * CORE + lax.axis_index("core")
    buffer = jnp.zeros_like(pieces)
    buffer = put(buffer, pick(pieces, own), own)
    for offset in range(1, TEAM):
        there = own ^ offset
        buffer = put(buffer, team_swap(pick(pieces, there), offset), there)
    return buffer


def split_columns(values, widths):
    members = []
    for member in range(TEAM):
        start, parts = 0, []
        for width in widths:
            share = width // TEAM
            first = start + member * share
            parts.append(values[:, first : first + share])
            start += width
        members.append(jnp.concatenate(parts, axis=1))
    return jnp.stack(members)


def join_columns(pieces, widths):
    parts, start = [], 0
    for width in widths:
        share = width // TEAM
        parts += [pieces[member, :, start : start + share] for member in range(TEAM)]
        start += share
    return jnp.concatenate(parts, axis=1)


def gather_weight(shard, widths):
    mixed = team_exchange(split_columns(shard, widths))
    mixed = mixed.reshape(-1, mixed.shape[-1])
    return lax.all_gather(mixed, "outer", axis=0, tiled=True)


def sum_weight(gradient):
    return lax.psum_scatter(
        gradient.astype(jnp.bfloat16), "outer", scatter_dimension=0, tiled=True
    )


def return_weight(summed, widths):
    pieces = summed.reshape(TEAM, -1, summed.shape[-1])
    return join_columns(team_exchange(pieces), widths).astype(jnp.float32)


def adam_update(weight, gradient, moment_one, moment_two, factor, decay_rate, rate_value):
    clipped = gradient * factor
    moment_one = beta_first * moment_one + (1.0 - beta_first) * clipped
    moment_two = beta_second * moment_two + (1.0 - beta_second) * clipped * clipped
    first_fixed = moment_one / (1.0 - beta_first**STEP)
    second_fixed = moment_two / (1.0 - beta_second**STEP)
    weight = weight - rate_value * (
        first_fixed / (jnp.sqrt(second_fixed) + adam_epsilon) + decay_rate * weight
    )
    return (weight, moment_one, moment_two)


def dot(left, right, contract):
    return lax.dot_general(
        left, right, ((contract[0], contract[1]), ((), ())), preferred_element_type=jnp.float32
    )


def times(left, right):
    return dot(left, right, ((1,), (0,)))


def times_across(left, right):
    return dot(left, right, ((1,), (1,)))


def over_rows(left, right):
    return dot(left, right, ((0,), (0,)))


def local(
    inputs,
    cotangent,
    lengths,
    owners,
    qkv_weight,
    out_weight,
    gate_up_weight,
    down_weight,
    norm_gains,
    qkv_moment,
    out_moment,
    gate_up_moment,
    down_moment,
    gains_moment,
    qkv_square,
    out_square,
    gate_up_square,
    down_square,
    gains_square,
):
    tp_count = lax.axis_size("tp")
    half_rows = inputs.shape[0]
    row_count = half_rows * tp_count
    heads = H // tp_count // TEAM
    hidden_units = FF // tp_count // TEAM
    qkv_widths = (H * HD // tp_count, KV * HD // tp_count, KV * HD // tp_count)
    out_widths = (H * HD // tp_count,)
    gate_up_widths = (FF // tp_count, FF // tp_count)
    down_widths = (FF // tp_count,)

    first_group = lax.axis_index("outer") * TEAM
    group_ids = first_group + jnp.arange(TEAM)
    group_length = jnp.sum(
        jnp.where(owners[None, :] == group_ids[:, None], lengths[None, :], 0), axis=1
    )
    own_group = lax.axis_index("near") * CORE + lax.axis_index("core")
    positions = jnp.arange(row_count)
    key_mask = (positions[None, None, :] <= positions[None, :, None]) & (
        positions[None, None, :] < group_length[:, None, None]
    )
    own_rows = lax.axis_index("tp") * half_rows + jnp.arange(half_rows)
    valid_rows = (own_rows < pick(group_length, own_group)).astype(jnp.float32)[:, None]
    cos_table, sin_table = rotary(jnp.tile(positions, TEAM), HD)
    score_scale = HD ** (-0.5)
    attn_gain = norm_gains[:D]
    mlp_gain = norm_gains[D : 2 * D]
    query_gain = norm_gains[2 * D : 2 * D + HD]
    key_gain = norm_gains[2 * D + HD :]
    head_apply = partial(head_prepare, cos_table=cos_table, sin_table=sin_table)

    qkv_full = gather_weight(qkv_weight.astype(jnp.bfloat16), qkv_widths)
    out_full = gather_weight(out_weight.astype(jnp.bfloat16).T, out_widths)
    gate_up_full = gather_weight(gate_up_weight.astype(jnp.bfloat16), gate_up_widths)
    down_full = gather_weight(down_weight.astype(jnp.bfloat16).T, down_widths)

    residual_in = inputs.astype(jnp.float32)
    normed_attn = gather_rows(norm_apply(residual_in, attn_gain).astype(jnp.bfloat16))
    projected = times(normed_attn, qkv_full)
    all_rows = projected.shape[0]
    query_raw = projected[:, : heads * HD].reshape(all_rows, heads, HD)
    key_raw = projected[:, heads * HD : (heads + 1) * HD].reshape(all_rows, 1, HD)
    value_heads = projected[:, (heads + 1) * HD :].astype(jnp.bfloat16)
    value_heads = value_heads.reshape(TEAM, row_count, HD)
    queries = head_apply(query_raw, query_gain).astype(jnp.bfloat16)
    queries = queries.reshape(TEAM, row_count, heads, HD)
    key_heads = head_apply(key_raw, key_gain).astype(jnp.bfloat16)
    key_heads = key_heads.reshape(TEAM, row_count, HD)
    scores = score_block(queries, key_heads, key_mask, score_scale)
    row_max = jnp.max(scores, axis=-1, keepdims=True)
    exponent = jnp.exp(scores - row_max)
    row_total = jnp.sum(exponent, axis=-1, keepdims=True)
    log_total = row_max + jnp.log(row_total)
    attention = exponent / row_total
    attended = (
        jnp.einsum(
            "srqk,skd->sqrd",
            attention.astype(jnp.bfloat16),
            value_heads,
            preferred_element_type=jnp.float32,
        )
        .reshape(all_rows, heads * HD)
        .astype(jnp.bfloat16)
    )
    attn_branch = sum_rows(attended, lambda rows: times_across(rows, out_full))
    hidden = residual_in + attn_branch
    normed_mlp = gather_rows(norm_apply(hidden, mlp_gain).astype(jnp.bfloat16))
    gate_up = times(normed_mlp, gate_up_full)
    gate_part = gate_up[:, :hidden_units]
    up_part = gate_up[:, hidden_units:]
    activated = swish_product(gate_part, up_part).astype(jnp.bfloat16)
    mlp_branch = sum_rows(activated, lambda rows: times_across(rows, down_full))
    output = (hidden + mlp_branch).astype(jnp.bfloat16)

    grad_output = cotangent.astype(jnp.float32) * valid_rows
    grad_low = gather_rows(grad_output.astype(jnp.bfloat16))
    grad_activated = times(grad_low, down_full)
    swish_pull = jax.vjp(swish_product, gate_part, up_part)[1]
    grad_gate, grad_up = swish_pull(grad_activated)
    grad_gate_up = jnp.concatenate([grad_gate, grad_up], axis=1).astype(jnp.bfloat16)
    grad_normed_mlp = sum_rows(grad_gate_up, lambda rows: times_across(rows, gate_up_full))
    down_sum = sum_weight(over_rows(grad_low, activated))
    gate_up_sum = sum_weight(over_rows(normed_mlp, grad_gate_up))
    mlp_pull = jax.vjp(norm_apply, hidden, mlp_gain)[1]
    grad_hidden_norm, grad_mlp_gain = mlp_pull(grad_normed_mlp)
    grad_hidden = grad_output + grad_hidden_norm
    grad_attn = gather_rows(grad_hidden.astype(jnp.bfloat16))
    grad_attended = times(grad_attn, out_full).astype(jnp.bfloat16)
    grad_attended = grad_attended.reshape(TEAM, row_count, heads, HD)
    out_sum = sum_weight(over_rows(grad_attn, attended))
    attention = jnp.exp(score_block(queries, key_heads, key_mask, score_scale) - log_total)
    grad_probs = jnp.einsum(
        "sqrd,skd->srqk", grad_attended, value_heads, preferred_element_type=jnp.float32
    )
    grad_values = jnp.einsum(
        "srqk,sqrd->skd",
        attention.astype(jnp.bfloat16),
        grad_attended,
        preferred_element_type=jnp.float32,
    )
    inner_sum = jnp.sum(attention * grad_probs, axis=-1, keepdims=True)
    grad_scores = (attention * (grad_probs - inner_sum)).astype(jnp.bfloat16)
    grad_queries = (
        jnp.einsum("srqk,skd->sqrd", grad_scores, key_heads, preferred_element_type=jnp.float32)
        * score_scale
    )
    grad_keys = (
        jnp.einsum("srqk,sqrd->skd", grad_scores, queries, preferred_element_type=jnp.float32)
        * score_scale
    )
    query_pull = jax.vjp(head_apply, query_raw, query_gain)[1]
    grad_query_raw, grad_query_gain = query_pull(grad_queries.reshape(all_rows, heads, HD))
    key_pull = jax.vjp(head_apply, key_raw, key_gain)[1]
    grad_key_raw, grad_key_gain = key_pull(grad_keys.reshape(all_rows, 1, HD))
    grad_projected = jnp.concatenate(
        [
            grad_query_raw.reshape(all_rows, heads * HD),
            grad_key_raw.reshape(all_rows, HD),
            grad_values.reshape(all_rows, HD),
        ],
        axis=1,
    ).astype(jnp.bfloat16)
    qkv_sum = sum_weight(over_rows(normed_attn, grad_projected))
    grad_normed_attn = sum_rows(grad_projected, lambda rows: times_across(rows, qkv_full))
    attn_pull = jax.vjp(norm_apply, residual_in, attn_gain)[1]
    grad_input_norm, grad_attn_gain = attn_pull(grad_normed_attn)
    input_grad = (grad_hidden + grad_input_norm).astype(jnp.bfloat16)
    gain_part = jnp.concatenate([grad_attn_gain, grad_mlp_gain, grad_query_gain, grad_key_gain])
    square_part = sum(
        jnp.sum(jnp.square(member.astype(jnp.float32)))
        for member in (qkv_sum, out_sum, gate_up_sum, down_sum)
    )
    gain_grad, square_total = lax.psum((gain_part, square_part), ("outer",) + LAYER)
    down_grad = return_weight(down_sum, down_widths).T
    gate_up_grad = return_weight(gate_up_sum, gate_up_widths)
    out_grad = return_weight(out_sum, out_widths).T
    qkv_grad = return_weight(qkv_sum, qkv_widths)
    grad_norm = jnp.sqrt(square_total + jnp.sum(gain_grad * gain_grad))
    factor = jnp.minimum(1.0, clip_norm / (grad_norm + 1e-06))
    new_qkv, new_qkv_one, new_qkv_two = adam_update(
        qkv_weight, qkv_grad, qkv_moment, qkv_square, factor, weight_decay, learn_rate
    )
    new_out, new_out_one, new_out_two = adam_update(
        out_weight, out_grad, out_moment, out_square, factor, weight_decay, learn_rate
    )
    new_gate_up, new_gate_up_one, new_gate_up_two = adam_update(
        gate_up_weight,
        gate_up_grad,
        gate_up_moment,
        gate_up_square,
        factor,
        weight_decay,
        learn_rate,
    )
    new_down, new_down_one, new_down_two = adam_update(
        down_weight, down_grad, down_moment, down_square, factor, weight_decay, learn_rate
    )
    new_gains, new_gains_one, new_gains_two = adam_update(
        norm_gains, gain_grad, gains_moment, gains_square, factor, 0.0, gain_rate
    )
    return (
        output,
        input_grad,
        grad_norm,
        new_qkv,
        new_qkv_one,
        new_qkv_two,
        new_qkv.astype(jnp.bfloat16),
        new_out,
        new_out_one,
        new_out_two,
        new_out.astype(jnp.bfloat16),
        new_gate_up,
        new_gate_up_one,
        new_gate_up_two,
        new_gate_up.astype(jnp.bfloat16),
        new_down,
        new_down_one,
        new_down_two,
        new_down.astype(jnp.bfloat16),
        new_gains,
        new_gains_one,
        new_gains_two,
    )


def solution(mesh):
    fsdp_count, tp_count = mesh.shape["fsdp"], mesh.shape["tp"]
    cut = mesh.devices.reshape(fsdp_count // TEAM, NEAR, CORE, tp_count)
    cut_mesh = Mesh(cut, ("outer",) + LAYER)
    fsdp = ("outer", "near", "core")
    rows = P(fsdp + ("tp",), None)
    wide = P(fsdp, "tp")
    tall = P("tp", fsdp)
    weights = (wide, tall, wide, tall, P())
    return jax.shard_map(
        local,
        mesh=cut_mesh,
        in_specs=(rows, rows, P(), P()) + weights * 3,
        out_specs=(rows, rows, P()) + (wide,) * 4 + (tall,) * 4 + (wide,) * 4 + (tall,) * 4 + (P(),) * 3,
        check_vma=False,
    )
```

```python
import jax
import jax.numpy as jnp
from jax import lax
from jax.experimental import pallas as pl
from jax.experimental.pallas import tpu as pltpu
from jax.sharding import Mesh, PartitionSpec as P

D = 2048
H = 16
KV = 8
HD = 128
FF = 6144
STEP = 10


norm_epsilon = 1e-06
rope_base = 1000000.0
clip_norm = 1.0
learn_rate = 0.04
gain_rate = 0.8
beta_first = 0.9
beta_second = 0.999
adam_epsilon = 1e-08
weight_decay = 0.1
masked_score = -1e30

NEAR = 2
CORE = 2
TEAM = NEAR * CORE
LAYER = ("near", "core", "tp")
BLOCK = 128
PAD = 128


def rms_scale(values):
    return lax.rsqrt(jnp.mean(values * values, axis=-1, keepdims=True) + norm_epsilon)


def swish_product(gate_part, up_part):
    return jax.nn.silu(gate_part) * up_part


def swap(values, axis):
    return lax.ppermute(values, axis, [(0, 1), (1, 0)])


def pick(values, index):
    return lax.dynamic_index_in_dim(values, index, 0, keepdims=False)


def put(buffer, values, *index):
    zero = jnp.zeros((), jnp.int32)
    start = tuple(index) + (zero,) * (buffer.ndim - len(index))
    return lax.dynamic_update_slice(buffer, values[(None,) * len(index)], start)


def by_twin(values, multiply):
    core = lax.axis_index("core")
    blocks = values.reshape(NEAR, CORE, 2, -1, values.shape[1])

    def part(which):
        chosen = lax.dynamic_index_in_dim(blocks, which, 1, keepdims=False)
        return multiply(chosen.reshape(-1, values.shape[1])).reshape(NEAR, 2, -1, D)

    return part(1 - core), part(core)


def sum_rows(values, multiply):
    near, _, tp = (lax.axis_index(name) for name in LAYER)
    theirs, ours = by_twin(values, multiply)
    ours = ours + swap(theirs.astype(jnp.bfloat16), "core").astype(jnp.float32)

    def block(where_near, where_tp):
        return pick(pick(ours, where_near), where_tp)

    far = block(1 - near, 1 - tp).astype(jnp.bfloat16)
    half = far.shape[0] // 2
    top = swap(far[:half], "near").astype(jnp.float32)
    low = swap(far[half:], "tp").astype(jnp.float32)
    to_tp = block(near, 1 - tp)
    to_tp = jnp.concatenate([to_tp[:half] + top, to_tp[half:]], axis=0)
    to_near = block(1 - near, tp)
    to_near = jnp.concatenate([to_near[:half], to_near[half:] + low], axis=0)
    from_tp = swap(to_tp.astype(jnp.bfloat16), "tp").astype(jnp.float32)
    from_near = swap(to_near.astype(jnp.bfloat16), "near").astype(jnp.float32)
    return block(near, tp) + from_tp + from_near


MESH_ID = pl.DeviceIdType.MESH
VMEM_LIMIT = 48 * 1024 * 1024
CHUNK = 16
GATHER_COPIES = 13
SUM_COPIES = 10


def spots():
    return tuple(lax.axis_index(name) for name in LAYER)


def greet():
    barrier = pltpu.get_barrier_semaphore()
    for name, spot in zip(LAYER, spots()):
        pl.semaphore_signal(
            barrier, inc=1, device_id={name: 1 - spot}, device_id_type=MESH_ID
        )
    pl.semaphore_wait(barrier, len(LAYER))


def link(source, target, send_sem, recv_sem, name):
    spot = lax.axis_index(name)
    return pltpu.make_async_remote_copy(
        src_ref=source,
        dst_ref=target,
        send_sem=send_sem,
        recv_sem=recv_sem,
        device_id={name: 1 - spot},
        device_id_type=MESH_ID,
    )


def run_gather(own, out, send, recv, own_sem):
    near, core, tp = spots()
    rows = own.shape[0]
    low, high = pl.ds(0, rows // 2), pl.ds(rows // 2, rows // 2)

    def go(number, source, target, name):
        copy = link(source, target, send.at[number], recv.at[number], name)
        copy.start()
        return copy

    def pass_on(number, block, part, name):
        ref = out.at[block[0], block[1], block[2], part]
        return go(number, ref, ref, name)

    here = (near, core, tp)
    beside = (1 - near, core, tp)
    across = (near, core, 1 - tp)
    far = (1 - near, core, 1 - tp)
    tp_low = go(0, own.at[low], out.at[near, core, tp, low], "tp")
    near_high = go(1, own.at[high], out.at[near, core, tp, high], "near")
    tp_high = go(2, own.at[high], out.at[near, core, tp, high], "tp")
    near_low = go(3, own.at[low], out.at[near, core, tp, low], "near")
    twin = [go(4, own, out.at[near, core, tp], "core")]
    keep = pltpu.make_async_copy(own, out.at[near, core, tp], own_sem)
    keep.start()
    tp_low.wait_recv()
    far_low = pass_on(5, across, low, "near")
    twin.append(pass_on(6, across, low, "core"))
    near_high.wait_recv()
    far_high = pass_on(7, beside, high, "tp")
    twin.append(pass_on(8, beside, high, "core"))
    tp_high.wait_recv()
    twin.append(pass_on(9, across, high, "core"))
    near_low.wait_recv()
    twin.append(pass_on(10, beside, low, "core"))
    far_low.wait_recv()
    twin.append(pass_on(11, far, low, "core"))
    far_high.wait_recv()
    twin.append(pass_on(12, far, high, "core"))
    for copy in twin:
        copy.wait_recv()
    for copy in [tp_low, near_high, tp_high, near_low, far_low, far_high] + twin:
        copy.wait_send()
    keep.wait()


def add_rows(target, start, count, *sources):
    @pl.loop(0, count // CHUNK)
    def _(step):
        at = pl.ds(pl.multiple_of(start + step * CHUNK, CHUNK), CHUNK)
        total = None
        for source, shift in sources:
            where = pl.ds(pl.multiple_of(start - shift + step * CHUNK, CHUNK), CHUNK)
            value = source[where].astype(jnp.float32)
            total = value if total is None else total + value
        target[at] = total.astype(target.dtype)


def run_sum(part, total, held, send, recv, local_sem):
    mine, theirs, far, to_tp, to_near, way_near, way_tp, from_tp, from_near = held
    near, core, tp = spots()
    rows = total.shape[0]
    half = rows // 2
    low, high = pl.ds(0, half), pl.ds(half, half)
    order = [(1 - near, 1 - tp), (near, 1 - tp), (1 - near, tp), (near, tp)]
    twin, keep = [], []
    for number, (a, b) in enumerate(order):
        copy = link(
            part.at[a, 1 - core, b], theirs.at[number], send.at[number], recv.at[number], "core"
        )
        copy.start()
        twin.append(copy)
        copy = pltpu.make_async_copy(part.at[a, core, b], mine.at[number], local_sem.at[number])
        copy.start()
        keep.append(copy)

    def ready(number):
        keep[number].wait()
        twin[number].wait_recv()
        return (mine.at[number], 0), (theirs.at[number], 0)

    def go(number, source, target, name):
        copy = link(source, target, send.at[number], recv.at[number], name)
        copy.start()
        return copy

    pair = ready(0)
    add_rows(far, 0, half, *pair)
    far_low = go(4, far.at[low], way_near, "near")
    add_rows(far, half, half, *pair)
    far_high = go(5, far.at[high], way_tp, "tp")
    pair = ready(1)
    add_rows(to_tp, half, half, *pair)
    tp_high = go(6, to_tp.at[high], from_tp.at[high], "tp")
    other = ready(2)
    add_rows(to_near, 0, half, *other)
    near_low = go(7, to_near.at[low], from_near.at[low], "near")
    far_low.wait_recv()
    add_rows(to_tp, 0, half, *pair, (way_near, 0))
    tp_low = go(8, to_tp.at[low], from_tp.at[low], "tp")
    far_high.wait_recv()
    add_rows(to_near, half, half, *other, (way_tp, half))
    near_high = go(9, to_near.at[high], from_near.at[high], "near")
    pair = ready(3)
    add_rows(total, 0, rows, *pair)
    tp_high.wait_recv()
    near_low.wait_recv()
    tp_low.wait_recv()
    near_high.wait_recv()
    for copy in twin + [far_low, far_high, tp_high, near_low, tp_low, near_high]:
        copy.wait_send()
    return from_tp, from_near


def sum_scratch(rows, width):
    low = jnp.bfloat16
    return [
        pltpu.VMEM((4, rows, width), low),
        pltpu.VMEM((4, rows, width), low),
        pltpu.VMEM((rows, width), low),
        pltpu.VMEM((rows, width), low),
        pltpu.VMEM((rows, width), low),
        pltpu.VMEM((rows // 2, width), low),
        pltpu.VMEM((rows // 2, width), low),
        pltpu.VMEM((rows, width), low),
        pltpu.VMEM((rows, width), low),
        pltpu.SemaphoreType.DMA((SUM_COPIES,)),
        pltpu.SemaphoreType.DMA((SUM_COPIES,)),
        pltpu.SemaphoreType.DMA((4,)),
    ]


def gather_scratch():
    return [
        pltpu.SemaphoreType.DMA((GATHER_COPIES,)),
        pltpu.SemaphoreType.DMA((GATHER_COPIES,)),
        pltpu.SemaphoreType.DMA,
    ]


def params(number):
    return pltpu.CompilerParams(
        collective_id=number, has_side_effects=True, vmem_limit_bytes=VMEM_LIMIT
    )


def link_cost(rows, width, exchanges):
    return pl.CostEstimate(
        flops=0, bytes_accessed=exchanges * rows * width * 240, transcendentals=0
    )


def in_vmem():
    return pl.BlockSpec(memory_space=pltpu.VMEM)


def anywhere():
    return pl.BlockSpec(memory_space=pl.ANY)


def gather_rows(values, number, name):
    rows, width = values.shape

    def kernel(own, out, send, recv, own_sem):
        greet()
        run_gather(own, out, send, recv, own_sem)

    full = pl.pallas_call(
        kernel,
        name=name,
        out_shape=jax.ShapeDtypeStruct((NEAR, CORE, 2, rows, width), values.dtype),
        in_specs=[anywhere()],
        out_specs=anywhere(),
        scratch_shapes=gather_scratch(),
        compiler_params=params(number),
        cost_estimate=link_cost(rows, width, 1),
    )(values)
    return full.reshape(-1, width)


def row_loop(rows, body):
    @pl.loop(0, rows // CHUNK)
    def _(step):
        body(pl.ds(pl.multiple_of(step * CHUNK, CHUNK), CHUNK))


def spread(part, rows):
    return part.reshape(NEAR, CORE, 2, rows, part.shape[-1])


def branch_and_norm(part, residual, gain, number, name):
    rows, width = residual.shape

    def kernel(part, residual, gain, hidden, out, *scratch):
        held, (send, recv, local_sem, normed, g_send, g_recv, own_sem) = scratch[:9], scratch[9:]
        greet()
        from_tp, from_near = run_sum(part, hidden, held, send, recv, local_sem)

        def finish(at):
            value = hidden[at] + from_tp[at].astype(jnp.float32)
            value = value + from_near[at].astype(jnp.float32)
            value = residual[at].astype(jnp.float32) + value
            hidden[at] = value
            normed[at] = (value * rms_scale(value) * gain[...]).astype(jnp.bfloat16)

        row_loop(rows, finish)
        run_gather(normed, out, g_send, g_recv, own_sem)

    hidden, full = pl.pallas_call(
        kernel,
        name=name,
        out_shape=(
            jax.ShapeDtypeStruct((rows, width), jnp.float32),
            jax.ShapeDtypeStruct((NEAR, CORE, 2, rows, width), jnp.bfloat16),
        ),
        in_specs=[anywhere(), in_vmem(), in_vmem()],
        out_specs=(in_vmem(), anywhere()),
        scratch_shapes=sum_scratch(rows, width)
        + [pltpu.VMEM((rows, width), jnp.bfloat16)]
        + gather_scratch(),
        compiler_params=params(number),
        cost_estimate=link_cost(rows, width, 2),
    )(spread(part, rows), residual, gain.reshape(1, width))
    return hidden, full.reshape(-1, width)


def norm_back(value, gain, grad):
    scale = rms_scale(value)
    scaled = grad * gain
    inner = jnp.mean(scaled * value, axis=-1, keepdims=True)
    return scale * scaled - value * (scale * scale * scale * inner), grad * value * scale


def norm_back_rows(part, values, upstream, gain, number, name, gather):
    rows, width = values.shape

    def kernel(part, values, upstream, gain, *rest):
        outs, scratch = rest[: 3 if gather else 2], rest[3 if gather else 2 :]
        result, gain_grad = outs[0], outs[1]
        held, (send, recv, local_sem, total) = scratch[:9], scratch[9:13]
        greet()
        from_tp, from_near = run_sum(part, total, held, send, recv, local_sem)
        gain_grad[...] = jnp.zeros_like(gain_grad)
        if gather:
            low, g_send, g_recv, own_sem = scratch[13:]

        def finish(at):
            grad = total[at] + from_tp[at].astype(jnp.float32)
            grad = grad + from_near[at].astype(jnp.float32)
            back, by_gain = norm_back(values[at].astype(jnp.float32), gain[...], grad)
            gain_grad[...] += by_gain.reshape(CHUNK // 8, 8, width).sum(axis=0)
            value = upstream[at].astype(jnp.float32) + back
            result[at] = value.astype(result.dtype)
            if gather:
                low[at] = value.astype(jnp.bfloat16)

        row_loop(rows, finish)
        if gather:
            run_gather(low, outs[2], g_send, g_recv, own_sem)

    out_shape = [
        jax.ShapeDtypeStruct((rows, width), jnp.float32 if gather else jnp.bfloat16),
        jax.ShapeDtypeStruct((8, width), jnp.float32),
    ]
    out_specs = [in_vmem(), in_vmem()]
    scratch_shapes = sum_scratch(rows, width) + [pltpu.VMEM((rows, width), jnp.float32)]
    if gather:
        out_shape.append(jax.ShapeDtypeStruct((NEAR, CORE, 2, rows, width), jnp.bfloat16))
        out_specs.append(anywhere())
        scratch_shapes += [pltpu.VMEM((rows, width), jnp.bfloat16)] + gather_scratch()
    outs = pl.pallas_call(
        kernel,
        name=name,
        out_shape=tuple(out_shape),
        in_specs=[anywhere()] + [in_vmem()] * 3,
        out_specs=tuple(out_specs),
        scratch_shapes=scratch_shapes,
        compiler_params=params(number),
        cost_estimate=link_cost(rows, width, 2 if gather else 1),
    )(spread(part, rows), values, upstream, gain.reshape(1, width))
    gain_grad = outs[1].sum(axis=0)
    if gather:
        return outs[0], gain_grad, outs[2].reshape(-1, width)
    return outs[0], gain_grad


def total_everywhere(values, outer_count, number, name):
    shape = values.shape

    def kernel(values, out, layer, outers, send, recv):
        near, core, tp = spots()
        outer = lax.axis_index("outer")
        partners = [
            {
                "near": 1 - near if a else near,
                "core": 1 - core if b else core,
                "tp": 1 - tp if c else tp,
            }
            for a in range(NEAR)
            for b in range(CORE)
            for c in range(2)
            if a + b + c
        ]
        partners += [{"outer": (outer + step) % outer_count} for step in range(1, outer_count)]
        barrier = pltpu.get_barrier_semaphore()
        for partner in partners:
            pl.semaphore_signal(barrier, inc=1, device_id=partner, device_id_type=MESH_ID)
        pl.semaphore_wait(barrier, len(partners))

        def share(slots, mine, first, count):
            copies = []
            for number in range(first, first + count):
                copy = pltpu.make_async_remote_copy(
                    src_ref=slots.at[mine],
                    dst_ref=slots.at[mine],
                    send_sem=send.at[number],
                    recv_sem=recv.at[number],
                    device_id=partners[number],
                    device_id_type=MESH_ID,
                )
                copy.start()
                copies.append(copy)
            for copy in copies:
                copy.wait()

        mine = near * (CORE * 2) + core * 2 + tp
        layer[mine] = values[...]
        share(layer, mine, 0, 7)
        total = layer[0]
        for slot in range(1, 8):
            total = total + layer[slot]
        outers[outer] = total
        share(outers, outer, 7, outer_count - 1)
        total = outers[0]
        for slot in range(1, outer_count):
            total = total + outers[slot]
        out[...] = total

    return pl.pallas_call(
        kernel,
        name=name,
        out_shape=jax.ShapeDtypeStruct(shape, jnp.float32),
        in_specs=[in_vmem()],
        out_specs=in_vmem(),
        scratch_shapes=[
            pltpu.VMEM((8,) + shape, jnp.float32),
            pltpu.VMEM((outer_count,) + shape, jnp.float32),
            pltpu.SemaphoreType.DMA((6 + outer_count,)),
            pltpu.SemaphoreType.DMA((6 + outer_count,)),
        ],
        compiler_params=params(number),
    )(values)


def head_scale(raw, gain, cos_full, sin_full):
    normed = raw * rms_scale(raw) * gain
    return (normed * cos_full + pltpu.roll(normed, HD // 2, 1) * sin_full).astype(jnp.bfloat16)


def head_back(raw, gain, grad, cos_full, sin_full):
    grad = grad * cos_full - pltpu.roll(grad, HD // 2, 1) * sin_full
    return norm_back(raw, gain, grad)


def columns(index):
    return pl.ds(index * HD, HD)


def head_inputs(proj, gains, cos_ref, sin_ref, queries, keys, values, heads):
    for head in range(heads):
        queries[head] = head_scale(
            proj[0, :, columns(head)], gains[0:1, :], cos_ref[...], sin_ref[...]
        )
    keys[...] = head_scale(
        proj[0, :, columns(heads)], gains[1:2, :], cos_ref[...], sin_ref[...]
    )
    values[...] = proj[0, :, columns(heads + 1)].astype(jnp.bfloat16)


def masked_scores(stacked, keys, step, length):
    scores = lax.dot_general(
        stacked, keys, (((1,), (1,)), ((), ())), preferred_element_type=jnp.float32
    ) * (HD ** (-0.5))
    row = lax.broadcasted_iota(jnp.int32, scores.shape, 0) % BLOCK + step * BLOCK
    column = lax.broadcasted_iota(jnp.int32, scores.shape, 1)
    return jnp.where((column <= row) & (column < length), scores, masked_score)


def stack_heads(ref, at, heads):
    return jnp.concatenate([ref[head, at] for head in range(heads)], axis=0)


def attend(projected, group_length, cos_full, sin_full, gains, heads):
    count, rows, width = projected.shape

    def kernel(lengths, proj, cos_ref, sin_ref, gains, out, logs, queries, keys, values):
        length = lengths[pl.program_id(0)]
        head_inputs(proj, gains, cos_ref, sin_ref, queries, keys, values, heads)
        lane = lax.broadcasted_iota(jnp.int32, (BLOCK, HD), 1)
        for step in range(rows // BLOCK):
            at = pl.ds(step * BLOCK, BLOCK)
            seen = pl.ds(0, (step + 1) * BLOCK)
            scores = masked_scores(stack_heads(queries, at, heads), keys[seen], step, length)
            top = jnp.max(scores, axis=-1, keepdims=True)
            exponent = jnp.exp(scores - top)
            total = jnp.sum(exponent, axis=-1, keepdims=True)
            probs = (exponent / total).astype(jnp.bfloat16)
            mixed = jnp.dot(probs, values[seen], preferred_element_type=jnp.float32)
            log_total = top + jnp.log(total)
            kept = jnp.zeros((BLOCK, HD), jnp.float32)
            for head in range(heads):
                mine = slice(head * BLOCK, (head + 1) * BLOCK)
                out[0, at, columns(head)] = mixed[mine].astype(jnp.bfloat16)
                kept = jnp.where(lane == head, log_total[mine], kept)
            logs[0, at] = kept

    return pl.pallas_call(
        kernel,
        name="attend",
        grid=(count,),
        out_shape=(
            jax.ShapeDtypeStruct((count, rows, heads * HD), jnp.bfloat16),
            jax.ShapeDtypeStruct((count, rows, HD), jnp.float32),
        ),
        in_specs=[
            pl.BlockSpec(memory_space=pltpu.SMEM),
            pl.BlockSpec((1, rows, width), lambda s: (s, 0, 0)),
            pl.BlockSpec((rows, HD), lambda s: (0, 0)),
            pl.BlockSpec((rows, HD), lambda s: (0, 0)),
            pl.BlockSpec((2, HD), lambda s: (0, 0)),
        ],
        out_specs=(
            pl.BlockSpec((1, rows, heads * HD), lambda s: (s, 0, 0)),
            pl.BlockSpec((1, rows, HD), lambda s: (s, 0, 0)),
        ),
        scratch_shapes=[
            pltpu.VMEM((heads, rows, HD), jnp.bfloat16),
            pltpu.VMEM((rows, HD), jnp.bfloat16),
            pltpu.VMEM((rows, HD), jnp.bfloat16),
        ],
        compiler_params=pltpu.CompilerParams(vmem_limit_bytes=VMEM_LIMIT),
        cost_estimate=pl.CostEstimate(flops=0, bytes_accessed=80 * 2**20, transcendentals=0),
    )(group_length, projected, cos_full, sin_full, gains)


def attend_back(projected, grad_attended, logs, group_length, cos_full, sin_full, gains, heads):
    count, rows, width = projected.shape

    def kernel(
        lengths, proj, grad, logs, cos_ref, sin_ref, gains, out, gain_grad, queries, keys, values, grad_q, grad_k, grad_v
    ):
        sequence = pl.program_id(0)
        length = lengths[sequence]
        head_inputs(proj, gains, cos_ref, sin_ref, queries, keys, values, heads)
        grad_k[...] = jnp.zeros_like(grad_k)
        grad_v[...] = jnp.zeros_like(grad_v)

        @pl.when(sequence == 0)
        def _():
            gain_grad[...] = jnp.zeros_like(gain_grad)

        for step in range(rows // BLOCK):
            at = pl.ds(step * BLOCK, BLOCK)
            seen = pl.ds(0, (step + 1) * BLOCK)
            stacked = stack_heads(queries, at, heads)
            above = jnp.concatenate([grad[0, at, columns(head)] for head in range(heads)], axis=0)
            log_total = jnp.concatenate(
                [logs[0, at, head : head + 1] for head in range(heads)], axis=0
            )
            probs = jnp.exp(masked_scores(stacked, keys[seen], step, length) - log_total)
            grad_probs = lax.dot_general(
                above, values[seen], (((1,), (1,)), ((), ())), preferred_element_type=jnp.float32
            )
            inner = jnp.sum(probs * grad_probs, axis=-1, keepdims=True)
            grad_scores = (probs * (grad_probs - inner)).astype(jnp.bfloat16)
            by_query = jnp.dot(grad_scores, keys[seen], preferred_element_type=jnp.float32)
            for head in range(heads):
                grad_q[head, at] = by_query[head * BLOCK : (head + 1) * BLOCK] * (HD ** (-0.5))
            grad_k[seen] += lax.dot_general(
                grad_scores, stacked, (((0,), (0,)), ((), ())), preferred_element_type=jnp.float32
            )
            grad_v[seen] += lax.dot_general(
                probs.astype(jnp.bfloat16),
                above,
                (((0,), (0,)), ((), ())),
                preferred_element_type=jnp.float32,
            )

        def finish(column, gain, value):
            back, by_gain = head_back(
                proj[0, :, columns(column)], gains[gain : gain + 1, :], value, cos_ref[...], sin_ref[...]
            )
            out[0, :, columns(column)] = back.astype(jnp.bfloat16)
            gain_grad[gain] += by_gain.reshape(rows // 8, 8, HD).sum(axis=0)

        for head in range(heads):
            finish(head, 0, grad_q[head])
        finish(heads, 1, grad_k[...] * (HD ** (-0.5)))
        out[0, :, columns(heads + 1)] = grad_v[...].astype(jnp.bfloat16)

    return pl.pallas_call(
        kernel,
        name="attend_back",
        grid=(count,),
        out_shape=(
            jax.ShapeDtypeStruct((count, rows, width), jnp.bfloat16),
            jax.ShapeDtypeStruct((2, 8, HD), jnp.float32),
        ),
        in_specs=[
            pl.BlockSpec(memory_space=pltpu.SMEM),
            pl.BlockSpec((1, rows, width), lambda s: (s, 0, 0)),
            pl.BlockSpec((1, rows, heads * HD), lambda s: (s, 0, 0)),
            pl.BlockSpec((1, rows, HD), lambda s: (s, 0, 0)),
            pl.BlockSpec((rows, HD), lambda s: (0, 0)),
            pl.BlockSpec((rows, HD), lambda s: (0, 0)),
            pl.BlockSpec((2, HD), lambda s: (0, 0)),
        ],
        out_specs=(
            pl.BlockSpec((1, rows, width), lambda s: (s, 0, 0)),
            pl.BlockSpec((2, 8, HD), lambda s: (0, 0, 0)),
        ),
        scratch_shapes=[
            pltpu.VMEM((heads, rows, HD), jnp.bfloat16),
            pltpu.VMEM((rows, HD), jnp.bfloat16),
            pltpu.VMEM((rows, HD), jnp.bfloat16),
            pltpu.VMEM((heads, rows, HD), jnp.float32),
            pltpu.VMEM((rows, HD), jnp.float32),
            pltpu.VMEM((rows, HD), jnp.float32),
        ],
        compiler_params=pltpu.CompilerParams(vmem_limit_bytes=VMEM_LIMIT),
        cost_estimate=pl.CostEstimate(flops=0, bytes_accessed=120 * 2**20, transcendentals=0),
    )(group_length, projected, grad_attended, logs, cos_full, sin_full, gains)


def team_swap(values, offset):
    pairs = [(member, member ^ offset) for member in range(TEAM)]
    return lax.ppermute(values, ("near", "core"), pairs)


def team_exchange(pieces):
    own = lax.axis_index("near") * CORE + lax.axis_index("core")
    buffer = jnp.zeros_like(pieces)
    buffer = put(buffer, pick(pieces, own), own)
    for offset in range(1, TEAM):
        there = own ^ offset
        buffer = put(buffer, team_swap(pick(pieces, there), offset), there)
    return buffer


def split_columns(values, widths):
    members = []
    for member in range(TEAM):
        start, parts = 0, []
        for width in widths:
            share = width // TEAM
            first = start + member * share
            parts.append(values[:, first : first + share])
            start += width
        members.append(jnp.concatenate(parts, axis=1))
    return jnp.stack(members)


def join_columns(pieces, widths):
    parts, start = [], 0
    for width in widths:
        share = width // TEAM
        parts += [pieces[member, :, start : start + share] for member in range(TEAM)]
        start += share
    return jnp.concatenate(parts, axis=1)


def gather_weight(shard, widths):
    mixed = team_exchange(split_columns(shard, widths))
    mixed = mixed.reshape(-1, mixed.shape[-1])
    return lax.all_gather(mixed, "outer", axis=0, tiled=True)


def sum_weight(gradient):
    return lax.psum_scatter(
        gradient.astype(jnp.bfloat16), "outer", scatter_dimension=0, tiled=True
    )


def return_weight(summed, widths):
    pieces = summed.reshape(TEAM, -1, summed.shape[-1])
    return join_columns(team_exchange(pieces), widths).astype(jnp.float32)


def adam_update(weight, gradient, moment_one, moment_two, factor, decay_rate, rate_value):
    clipped = gradient * factor
    moment_one = beta_first * moment_one + (1.0 - beta_first) * clipped
    moment_two = beta_second * moment_two + (1.0 - beta_second) * clipped * clipped
    first_fixed = moment_one / (1.0 - beta_first**STEP)
    second_fixed = moment_two / (1.0 - beta_second**STEP)
    weight = weight - rate_value * (
        first_fixed / (jnp.sqrt(second_fixed) + adam_epsilon) + decay_rate * weight
    )
    return (weight, moment_one, moment_two)


def dot(left, right, contract):
    return lax.dot_general(
        left, right, ((contract[0], contract[1]), ((), ())), preferred_element_type=jnp.float32
    )


def times(left, right):
    return dot(left, right, ((1,), (0,)))


def times_across(left, right):
    return dot(left, right, ((1,), (1,)))


def over_rows(left, right):
    return dot(left, right, ((0,), (0,)))


def local(
    inputs,
    cotangent,
    lengths,
    owners,
    qkv_weight,
    out_weight,
    gate_up_weight,
    down_weight,
    norm_gains,
    qkv_moment,
    out_moment,
    gate_up_moment,
    down_moment,
    gains_moment,
    qkv_square,
    out_square,
    gate_up_square,
    down_square,
    gains_square,
):
    tp_count = lax.axis_size("tp")
    half_rows = inputs.shape[0]
    row_count = half_rows * tp_count
    heads = H // tp_count // TEAM
    hidden_units = FF // tp_count // TEAM
    qkv_widths = (H * HD // tp_count, KV * HD // tp_count, KV * HD // tp_count)
    out_widths = (H * HD // tp_count,)
    gate_up_widths = (FF // tp_count, FF // tp_count)
    down_widths = (FF // tp_count,)

    first_group = lax.axis_index("outer") * TEAM
    group_ids = first_group + jnp.arange(TEAM)
    group_length = jnp.sum(
        jnp.where(owners[None, :] == group_ids[:, None], lengths[None, :], 0), axis=1
    )
    own_group = lax.axis_index("near") * CORE + lax.axis_index("core")
    own_rows = lax.axis_index("tp") * half_rows + jnp.arange(half_rows)
    valid_rows = (own_rows < pick(group_length, own_group))[:, None]
    half_width = HD // 2
    frequency = rope_base ** (-(jnp.arange(half_width, dtype=jnp.float32) * 2.0 / HD))
    angles = jnp.arange(row_count, dtype=jnp.float32)[:, None] * frequency[None, :]
    cosine, sine = jnp.cos(angles), jnp.sin(angles)
    cos_full = jnp.concatenate([cosine, cosine], axis=1)
    sin_full = jnp.concatenate([-sine, sine], axis=1)
    attn_gain = norm_gains[:D]
    mlp_gain = norm_gains[D : 2 * D]
    head_gains = norm_gains[2 * D :].reshape(2, HD)

    qkv_full = gather_weight(qkv_weight.astype(jnp.bfloat16), qkv_widths)
    out_full = gather_weight(out_weight.astype(jnp.bfloat16).T, out_widths)
    gate_up_full = gather_weight(gate_up_weight.astype(jnp.bfloat16), gate_up_widths)
    down_full = gather_weight(down_weight.astype(jnp.bfloat16).T, down_widths)

    residual_in = inputs.astype(jnp.float32)
    normed_attn = residual_in * rms_scale(residual_in) * attn_gain
    normed_attn = gather_rows(normed_attn.astype(jnp.bfloat16), 0, "gather_inputs")
    grad_low = jnp.where(valid_rows, cotangent, jnp.zeros_like(cotangent))
    grad_all = gather_rows(grad_low, 1, "gather_cotangent")
    projected = times(normed_attn, qkv_full)
    projected = projected.reshape(TEAM, row_count, projected.shape[1])
    attended, logs = attend(projected, group_length, cos_full, sin_full, head_gains, heads)
    attended = attended.reshape(-1, heads * HD)
    attn_branch = times_across(attended, out_full).astype(jnp.bfloat16)
    hidden, normed_mlp = branch_and_norm(attn_branch, inputs, mlp_gain, 2, "branch_and_norm")
    gate_up = times(normed_mlp, gate_up_full)
    gate_part = gate_up[:, :hidden_units]
    up_part = gate_up[:, hidden_units:]
    activated = swish_product(gate_part, up_part).astype(jnp.bfloat16)
    mlp_branch = sum_rows(activated, lambda rows: times_across(rows, down_full))
    output = (hidden + mlp_branch).astype(jnp.bfloat16)

    grad_activated = times(grad_all, down_full)
    swish_pull = jax.vjp(swish_product, gate_part, up_part)[1]
    grad_gate, grad_up = swish_pull(grad_activated)
    grad_gate_up = jnp.concatenate([grad_gate, grad_up], axis=1).astype(jnp.bfloat16)
    grad_normed_mlp = times_across(grad_gate_up, gate_up_full).astype(jnp.bfloat16)
    down_sum = sum_weight(over_rows(grad_all, activated))
    gate_up_sum = sum_weight(over_rows(normed_mlp, grad_gate_up))
    grad_hidden, grad_mlp_gain, grad_attn = norm_back_rows(
        grad_normed_mlp, hidden, grad_low, mlp_gain, 3, "norm_back_mlp", True
    )
    grad_attended = times(grad_attn, out_full).astype(jnp.bfloat16)
    grad_attended = grad_attended.reshape(TEAM, row_count, heads * HD)
    out_sum = sum_weight(over_rows(grad_attn, attended))
    grad_projected, grad_head_gains = attend_back(
        projected, grad_attended, logs, group_length, cos_full, sin_full, head_gains, heads
    )
    grad_projected = grad_projected.reshape(-1, projected.shape[2])
    qkv_sum = sum_weight(over_rows(normed_attn, grad_projected))
    grad_normed_attn = times_across(grad_projected, qkv_full).astype(jnp.bfloat16)
    input_grad, grad_attn_gain = norm_back_rows(
        grad_normed_attn, inputs, grad_hidden, attn_gain, 4, "norm_back_attn", False
    )
    gain_part = jnp.concatenate(
        [grad_attn_gain, grad_mlp_gain, grad_head_gains.sum(axis=1).reshape(-1)]
    )
    square_part = sum(
        jnp.sum(jnp.square(member.astype(jnp.float32)))
        for member in (qkv_sum, out_sum, gate_up_sum, down_sum)
    )
    gain_count = gain_part.shape[0]
    packed = jnp.concatenate([gain_part, square_part[None], jnp.zeros(PAD - 1, jnp.float32)])
    packed = packed.reshape(-1, HD)
    packed = jnp.pad(packed, ((0, -packed.shape[0] % 8), (0, 0)))
    packed = total_everywhere(packed, lax.axis_size("outer"), 5, "total_everywhere").reshape(-1)
    gain_grad, square_total = packed[:gain_count], packed[gain_count]
    down_grad = return_weight(down_sum, down_widths).T
    gate_up_grad = return_weight(gate_up_sum, gate_up_widths)
    out_grad = return_weight(out_sum, out_widths).T
    qkv_grad = return_weight(qkv_sum, qkv_widths)
    grad_norm = jnp.sqrt(square_total + jnp.sum(gain_grad * gain_grad))
    factor = jnp.minimum(1.0, clip_norm / (grad_norm + 1e-06))
    new_qkv, new_qkv_one, new_qkv_two = adam_update(
        qkv_weight, qkv_grad, qkv_moment, qkv_square, factor, weight_decay, learn_rate
    )
    new_out, new_out_one, new_out_two = adam_update(
        out_weight, out_grad, out_moment, out_square, factor, weight_decay, learn_rate
    )
    new_gate_up, new_gate_up_one, new_gate_up_two = adam_update(
        gate_up_weight,
        gate_up_grad,
        gate_up_moment,
        gate_up_square,
        factor,
        weight_decay,
        learn_rate,
    )
    new_down, new_down_one, new_down_two = adam_update(
        down_weight, down_grad, down_moment, down_square, factor, weight_decay, learn_rate
    )
    new_gains, new_gains_one, new_gains_two = adam_update(
        norm_gains, gain_grad, gains_moment, gains_square, factor, 0.0, gain_rate
    )
    return (
        output,
        input_grad,
        grad_norm,
        new_qkv,
        new_qkv_one,
        new_qkv_two,
        new_qkv.astype(jnp.bfloat16),
        new_out,
        new_out_one,
        new_out_two,
        new_out.astype(jnp.bfloat16),
        new_gate_up,
        new_gate_up_one,
        new_gate_up_two,
        new_gate_up.astype(jnp.bfloat16),
        new_down,
        new_down_one,
        new_down_two,
        new_down.astype(jnp.bfloat16),
        new_gains,
        new_gains_one,
        new_gains_two,
    )


def solution(mesh):
    fsdp_count, tp_count = mesh.shape["fsdp"], mesh.shape["tp"]
    cut = mesh.devices.reshape(fsdp_count // TEAM, NEAR, CORE, tp_count)
    cut_mesh = Mesh(cut, ("outer",) + LAYER)
    fsdp = ("outer", "near", "core")
    rows = P(fsdp + ("tp",), None)
    wide = P(fsdp, "tp")
    tall = P("tp", fsdp)
    weights = (wide, tall, wide, tall, P())
    return jax.shard_map(
        local,
        mesh=cut_mesh,
        in_specs=(rows, rows, P(), P()) + weights * 3,
        out_specs=(rows, rows, P()) + (wide,) * 4 + (tall,) * 4 + (wide,) * 4 + (tall,) * 4 + (P(),) * 3,
        check_vma=False,
    )
```

```python
import jax
import jax.numpy as jnp
from jax import lax
from jax.experimental import pallas as pl
from jax.experimental.pallas import tpu as pltpu
from jax.sharding import Mesh, PartitionSpec as P

D = 2048
H = 16
KV = 8
HD = 128
FF = 6144
STEP = 10


norm_epsilon = 1e-06
rope_base = 1000000.0
clip_norm = 1.0
learn_rate = 0.04
gain_rate = 0.8
beta_first = 0.9
beta_second = 0.999
adam_epsilon = 1e-08
weight_decay = 0.1
masked_score = -1e30

NEAR = 2
CORE = 2
TEAM = NEAR * CORE
LAYER = ("near", "core", "tp")
BLOCK = 128
PAD = 8 * 128


def rms_scale(values):
    return lax.rsqrt(jnp.mean(values * values, axis=-1, keepdims=True) + norm_epsilon)


def swish_product(gate_part, up_part):
    return jax.nn.silu(gate_part) * up_part


def pick(values, index):
    return lax.dynamic_index_in_dim(values, index, 0, keepdims=False)


MESH_ID = pl.DeviceIdType.MESH
VMEM_LIMIT = 60 * 1024 * 1024
CHUNK = 16
GATHER_COPIES = 13
SUM_COPIES = 10
NEIGHBOURS = ((1, 0, 0), (0, 1, 0), (0, 0, 1))
MATES = ((0, 1, 0), (1, 0, 0), (1, 1, 0))
EVERYONE_NEAR = NEIGHBOURS + ((1, 1, 0),)


def spots():
    return tuple(lax.axis_index(name) for name in LAYER)


def flipped(near_flip, core_flip, tp_flip):
    return {
        name: 1 - spot if flip else spot
        for name, spot, flip in zip(LAYER, spots(), (near_flip, core_flip, tp_flip))
    }


def greet(flips):
    barrier = pltpu.get_barrier_semaphore()
    for flip in flips:
        pl.semaphore_signal(barrier, inc=1, device_id=flipped(*flip), device_id_type=MESH_ID)
    pl.semaphore_wait(barrier, len(flips))


def link(source, target, send_sem, recv_sem, flip):
    return pltpu.make_async_remote_copy(
        src_ref=source,
        dst_ref=target,
        send_sem=send_sem,
        recv_sem=recv_sem,
        device_id=flipped(*flip),
        device_id_type=MESH_ID,
    )


TO_NEAR, TO_CORE, TO_TP = NEIGHBOURS


def plan_exchange(pieces, out, send, recv, own_sem):
    near, core, _ = spots()
    own = near * CORE + core
    copies = []
    for number, flip in enumerate(MATES):
        there = (1 - near if flip[0] else near) * CORE + (1 - core if flip[1] else core)
        copies.append(
            link(pieces.at[there], out.at[own], send.at[number], recv.at[number], flip)
        )
    copies.append(pltpu.make_async_copy(pieces.at[own], out.at[own], own_sem))
    return copies


def exchange_scratch():
    return [
        pltpu.SemaphoreType.DMA((len(MATES),)),
        pltpu.SemaphoreType.DMA((len(MATES),)),
        pltpu.SemaphoreType.DMA,
    ]


def plan_exchanges(pieces, mixed, sems):
    copies = []
    for place, (piece, result) in enumerate(zip(pieces, mixed)):
        copies += plan_exchange(piece, result, *sems[3 * place : 3 * place + 3])
    return copies


def plan_gather(own, out, send, recv, own_sem, cut):
    near, core, tp = spots()
    rows = own.shape[0]
    low, high = pl.ds(0, cut), pl.ds(cut, rows - cut)

    def make(number, source, target, flip):
        return link(source, target, send.at[number], recv.at[number], flip)

    def give(number, part, flip):
        return make(number, own.at[part], out.at[near, core, tp, part], flip)

    def relay(number, where_near, where_tp, part, flip):
        ref = out.at[where_near, core, where_tp, part]
        return make(number, ref, ref, flip)

    keep = pltpu.make_async_copy(own, out.at[near, core, tp], own_sem)
    twin_own = make(4, own, out.at[near, core, tp], TO_CORE)
    near_high = give(1, high, TO_NEAR)
    tp_high = give(2, high, TO_TP)
    far_high = relay(7, 1 - near, tp, high, TO_TP)
    twin_beside = relay(8, 1 - near, tp, high, TO_CORE)
    twin_across = relay(9, near, 1 - tp, high, TO_CORE)
    twin_far = relay(12, 1 - near, 1 - tp, high, TO_CORE)
    twins = [twin_own, twin_beside, twin_across, twin_far]
    ways = [near_high, tp_high, far_high]
    if cut:
        tp_low = give(0, low, TO_TP)
        near_low = give(3, low, TO_NEAR)
        far_low = relay(5, near, 1 - tp, low, TO_NEAR)
        twin_across_low = relay(6, near, 1 - tp, low, TO_CORE)
        twin_beside_low = relay(10, 1 - near, tp, low, TO_CORE)
        twin_far_low = relay(11, 1 - near, 1 - tp, low, TO_CORE)
        twins += [twin_across_low, twin_beside_low, twin_far_low]
        ways += [tp_low, near_low, far_low]

    def begin():
        if cut:
            tp_low.start()
        near_high.start()
        tp_high.start()
        if cut:
            near_low.start()
        twin_own.start()
        keep.start()

    def middle():
        if cut:
            tp_low.wait_recv()
            far_low.start()
            twin_across_low.start()
        near_high.wait_recv()
        far_high.start()
        twin_beside.start()

    def later():
        tp_high.wait_recv()
        twin_across.start()
        if cut:
            near_low.wait_recv()
            twin_beside_low.start()

    def finish():
        if cut:
            far_low.wait_recv()
            twin_far_low.start()
        far_high.wait_recv()
        twin_far.start()
        for copy in twins:
            copy.wait_recv()
        for copy in ways + twins:
            copy.wait_send()
        keep.wait()

    return [begin, middle, later, finish]


def gather_scratch():
    return [
        pltpu.SemaphoreType.DMA((GATHER_COPIES,)),
        pltpu.SemaphoreType.DMA((GATHER_COPIES,)),
        pltpu.SemaphoreType.DMA,
    ]


def add_rows(target, start, count, *sources):
    @pl.loop(0, count // CHUNK)
    def _(step):
        at = pl.ds(pl.multiple_of(start + step * CHUNK, CHUNK), CHUNK)
        total = None
        for source, shift in sources:
            where = pl.ds(pl.multiple_of(start - shift + step * CHUNK, CHUNK), CHUNK)
            value = source[where].astype(jnp.float32)
            total = value if total is None else total + value
        target[at] = total.astype(target.dtype)


def plan_sum(part, total, scratch, cut):
    mine, theirs, way_near, way_tp, from_tp, from_near, send, recv, local_sem = scratch
    near, core, tp = spots()
    rows = total.shape[0]
    low, high = pl.ds(0, cut), pl.ds(cut, rows - cut)
    order = [(1 - near, 1 - tp), (near, 1 - tp), (1 - near, tp), (near, tp)]
    twin, keep = [], []
    for number, (a, b) in enumerate(order):
        twin.append(
            link(
                part.at[a, 1 - core, b],
                theirs.at[number],
                send.at[number],
                recv.at[number],
                TO_CORE,
            )
        )
        keep.append(
            pltpu.make_async_copy(part.at[a, core, b], mine.at[number], local_sem.at[number])
        )

    def make(number, source, target, flip):
        return link(source, target, send.at[number], recv.at[number], flip)

    far, to_tp, to_near = mine.at[0], mine.at[1], mine.at[2]
    far_high = make(5, far.at[high], way_tp, TO_TP)
    tp_high = make(6, to_tp.at[high], from_tp.at[high], TO_TP)
    near_high = make(9, to_near.at[high], from_near.at[high], TO_NEAR)
    ways = [far_high, tp_high, near_high]
    if cut:
        far_low = make(4, far.at[low], way_near, TO_NEAR)
        near_low = make(7, to_near.at[low], from_near.at[low], TO_NEAR)
        tp_low = make(8, to_tp.at[low], from_tp.at[low], TO_TP)
        ways += [far_low, near_low, tp_low]

    def ready(number):
        keep[number].wait()
        twin[number].wait_recv()

    def both(number):
        return (mine.at[number], 0), (theirs.at[number], 0)

    def begin():
        for number in range(4):
            twin[number].start()
            keep[number].start()

    def first():
        ready(0)
        if cut:
            add_rows(far, 0, cut, *both(0))
            far_low.start()
        add_rows(far, cut, rows - cut, *both(0))
        far_high.start()
        ready(1)
        add_rows(to_tp, cut, rows - cut, *both(1))
        tp_high.start()
        ready(2)
        if cut:
            add_rows(to_near, 0, cut, *both(2))
            near_low.start()

    def second():
        if cut:
            far_low.wait_recv()
            add_rows(to_tp, 0, cut, *both(1), (way_near, 0))
            tp_low.start()
        far_high.wait_recv()
        add_rows(to_near, cut, rows - cut, *both(2), (way_tp, cut))
        near_high.start()
        ready(3)
        add_rows(total, 0, rows, *both(3))

    def finish():
        for copy in ways[1:]:
            if not cut or copy is not far_low:
                copy.wait_recv()
        for copy in twin + ways:
            copy.wait_send()

    return [begin, first, second, finish], from_tp, from_near


def sum_scratch(rows, width, cut):
    low = jnp.bfloat16
    return [
        pltpu.VMEM((4, rows, width), low),
        pltpu.VMEM((4, rows, width), low),
        pltpu.VMEM((max(cut, CHUNK), width), low),
        pltpu.VMEM((rows - cut, width), low),
        pltpu.VMEM((rows, width), low),
        pltpu.VMEM((rows, width), low),
        pltpu.SemaphoreType.DMA((SUM_COPIES,)),
        pltpu.SemaphoreType.DMA((SUM_COPIES,)),
        pltpu.SemaphoreType.DMA((4,)),
    ]


SUM_SCRATCH = 9


def params(number):
    return pltpu.CompilerParams(
        collective_id=number, has_side_effects=True, vmem_limit_bytes=VMEM_LIMIT
    )


def cost_of(microseconds):
    return pl.CostEstimate(
        flops=0, bytes_accessed=int(microseconds * 3.4e6), transcendentals=0
    )


def in_vmem():
    return pl.BlockSpec(memory_space=pltpu.VMEM)


def anywhere():
    return pl.BlockSpec(memory_space=pl.ANY)


def like(array):
    return jax.ShapeDtypeStruct(array.shape, array.dtype)


def layer_rows(rows, width):
    return jax.ShapeDtypeStruct((NEAR, CORE, 2, rows, width), jnp.bfloat16)


def exchange(pieces, number, name):
    def kernel(pieces, out, *sems):
        greet(MATES)
        copies = plan_exchange(pieces, out, *sems)
        for copy in copies:
            copy.start()
        for copy in copies:
            copy.wait()

    return pl.pallas_call(
        kernel,
        name=name,
        out_shape=like(pieces),
        in_specs=[anywhere()],
        out_specs=anywhere(),
        scratch_shapes=exchange_scratch(),
        compiler_params=params(number),
        cost_estimate=cost_of(12),
    )(pieces)


def gather_rows(values, extra, number, name):
    rows, width = values.shape
    extras = len(extra)

    def kernel(own, *rest):
        pieces, out, mixed = rest[:extras], rest[extras], rest[extras + 1 : 2 * extras + 1]
        sems = rest[2 * extras + 1 :]
        begin, *steps = plan_gather(own, out, *sems[:3], cut=0)
        copies = plan_exchanges(pieces, mixed, sems[3:])
        greet(EVERYONE_NEAR)
        begin()
        for copy in copies:
            copy.start()
        for step in steps:
            step()
        for copy in copies:
            copy.wait()

    outs = pl.pallas_call(
        kernel,
        name=name,
        out_shape=(layer_rows(rows, width),) + tuple(like(piece) for piece in extra),
        in_specs=[anywhere()] * (1 + extras),
        out_specs=(anywhere(),) * (1 + extras),
        scratch_shapes=gather_scratch() + exchange_scratch() * extras,
        compiler_params=params(number),
        cost_estimate=cost_of(60),
    )(values, *extra)
    return (outs[0].reshape(-1, width),) + tuple(outs[1:])


def row_loop(rows, body):
    @pl.loop(0, rows // CHUNK)
    def _(step):
        body(pl.ds(pl.multiple_of(step * CHUNK, CHUNK), CHUNK))


def spread(part, rows):
    return part.reshape(NEAR, CORE, 2, rows, part.shape[-1])


def read(ref, at):
    return ref[at].astype(jnp.float32)


def branch_and_norm(part, residual, gain, number, name):
    rows, width = residual.shape
    cut = rows // 2

    def kernel(part, residual, gain, hidden, out, *scratch):
        normed, sems = scratch[SUM_SCRATCH], scratch[SUM_SCRATCH + 1 :]
        steps, from_tp, from_near = plan_sum(part, hidden, scratch[:SUM_SCRATCH], cut)
        onward = plan_gather(normed, out, *sems, cut=cut)
        greet(NEIGHBOURS)
        for step in steps:
            step()

        def finish(at):
            value = hidden[at] + read(from_tp, at) + read(from_near, at)
            value = read(residual, at) + value
            hidden[at] = value
            normed[at] = (value * rms_scale(value) * gain[...]).astype(jnp.bfloat16)

        row_loop(rows, finish)
        for step in onward:
            step()

    hidden, full = pl.pallas_call(
        kernel,
        name=name,
        out_shape=(jax.ShapeDtypeStruct((rows, width), jnp.float32), layer_rows(rows, width)),
        in_specs=[anywhere(), in_vmem(), in_vmem()],
        out_specs=(in_vmem(), anywhere()),
        scratch_shapes=sum_scratch(rows, width, cut)
        + [pltpu.VMEM((rows, width), jnp.bfloat16)]
        + gather_scratch(),
        compiler_params=params(number),
        cost_estimate=cost_of(95),
    )(spread(part, rows), residual, gain.reshape(1, width))
    return hidden, full.reshape(-1, width)


def norm_back(value, gain, grad):
    scale = rms_scale(value)
    scaled = grad * gain
    inner = jnp.mean(scaled * value, axis=-1, keepdims=True)
    return scale * scaled - value * (scale * scale * scale * inner), grad * value * scale


def norm_back_gather(part, values, upstream, gain, number, name):
    rows, width = values.shape
    cut = rows // 2

    def kernel(part, values, upstream, gain, result, gain_grad, out, *scratch):
        (total, low), sems = (
            scratch[SUM_SCRATCH : SUM_SCRATCH + 2],
            scratch[SUM_SCRATCH + 2 :],
        )
        steps, from_tp, from_near = plan_sum(part, total, scratch[:SUM_SCRATCH], cut)
        onward = plan_gather(low, out, *sems, cut=cut)
        greet(NEIGHBOURS)
        for step in steps:
            step()
        gain_grad[...] = jnp.zeros_like(gain_grad)

        def finish(at):
            grad = total[at] + read(from_tp, at) + read(from_near, at)
            back, by_gain = norm_back(read(values, at), gain[...], grad)
            gain_grad[...] += by_gain.reshape(CHUNK // 8, 8, width).sum(axis=0)
            value = read(upstream, at) + back
            result[at] = value
            low[at] = value.astype(jnp.bfloat16)

        row_loop(rows, finish)
        for step in onward:
            step()

    result, gain_grad, full = pl.pallas_call(
        kernel,
        name=name,
        out_shape=(
            jax.ShapeDtypeStruct((rows, width), jnp.float32),
            jax.ShapeDtypeStruct((8, width), jnp.float32),
            layer_rows(rows, width),
        ),
        in_specs=[anywhere()] + [in_vmem()] * 3,
        out_specs=(in_vmem(), in_vmem(), anywhere()),
        scratch_shapes=sum_scratch(rows, width, cut)
        + [pltpu.VMEM((rows, width), jnp.float32), pltpu.VMEM((rows, width), jnp.bfloat16)]
        + gather_scratch(),
        compiler_params=params(number),
        cost_estimate=cost_of(100),
    )(spread(part, rows), values, upstream, gain.reshape(1, width))
    return result, gain_grad.sum(axis=0), full.reshape(-1, width)


def norm_back_last(part, values, upstream, gain, extra, number, name):
    rows, width = values.shape
    extras = len(extra)

    def kernel(part, values, upstream, gain, *rest):
        pieces, (result, gain_grad) = rest[:extras], rest[extras : extras + 2]
        mixed, rest = rest[extras + 2 : 2 * extras + 2], rest[2 * extras + 2 :]
        total, sems = rest[SUM_SCRATCH], rest[SUM_SCRATCH + 1 :]
        steps, from_tp, from_near = plan_sum(part, total, rest[:SUM_SCRATCH], 0)
        copies = plan_exchanges(pieces, mixed, sems)
        greet(EVERYONE_NEAR)
        steps[0]()
        for copy in copies:
            copy.start()
        for step in steps[1:]:
            step()
        gain_grad[...] = jnp.zeros_like(gain_grad)

        def finish(at):
            grad = total[at] + read(from_tp, at) + read(from_near, at)
            back, by_gain = norm_back(read(values, at), gain[...], grad)
            gain_grad[...] += by_gain.reshape(CHUNK // 8, 8, width).sum(axis=0)
            result[at] = (read(upstream, at) + back).astype(jnp.bfloat16)

        row_loop(rows, finish)
        for copy in copies:
            copy.wait()

    outs = pl.pallas_call(
        kernel,
        name=name,
        out_shape=(
            jax.ShapeDtypeStruct((rows, width), jnp.bfloat16),
            jax.ShapeDtypeStruct((8, width), jnp.float32),
        )
        + tuple(like(piece) for piece in extra),
        in_specs=[anywhere()] + [in_vmem()] * 3 + [anywhere()] * extras,
        out_specs=(in_vmem(), in_vmem()) + (anywhere(),) * extras,
        scratch_shapes=sum_scratch(rows, width, 0)
        + [pltpu.VMEM((rows, width), jnp.float32)]
        + exchange_scratch() * extras,
        compiler_params=params(number),
        cost_estimate=cost_of(65),
    )(spread(part, rows), values, upstream, gain.reshape(1, width), *extra)
    return (outs[0], outs[1].sum(axis=0)) + tuple(outs[2:])


def total_everywhere(values, pieces, outer_count, number, name):
    shape = values.shape

    def kernel(values, pieces, out, norm, factor, mixed, layer, outers, send, recv, *sems):
        near, core, tp = spots()
        outer = lax.axis_index("outer")
        partners = [
            flipped(a, b, c)
            for a in range(NEAR)
            for b in range(CORE)
            for c in range(2)
            if a + b + c
        ]
        partners += [{"outer": (outer + step) % outer_count} for step in range(1, outer_count)]
        barrier = pltpu.get_barrier_semaphore()
        for partner in partners:
            pl.semaphore_signal(barrier, inc=1, device_id=partner, device_id_type=MESH_ID)
        pl.semaphore_wait(barrier, len(partners))

        def share(slots, mine, first, count):
            copies = []
            for number in range(first, first + count):
                copy = pltpu.make_async_remote_copy(
                    src_ref=slots.at[mine],
                    dst_ref=slots.at[mine],
                    send_sem=send.at[number],
                    recv_sem=recv.at[number],
                    device_id=partners[number],
                    device_id_type=MESH_ID,
                )
                copy.start()
                copies.append(copy)
            return copies

        mine = near * (CORE * 2) + core * 2 + tp
        layer[mine] = values[...]
        copies = share(layer, mine, 0, 7)
        others = plan_exchange(pieces, mixed, *sems)
        for copy in others:
            copy.start()
        for copy in copies:
            copy.wait()
        total = layer[0]
        for slot in range(1, 8):
            total = total + layer[slot]
        outers[outer] = total
        for copy in share(outers, outer, 7, outer_count - 1):
            copy.wait()
        total = outers[0]
        for slot in range(1, outer_count):
            total = total + outers[slot]
        out[...] = total
        row = lax.broadcasted_iota(jnp.int32, shape, 0)
        squares = jnp.sum(jnp.where(row < shape[0] - 8, total * total, total), keepdims=True)
        root = jnp.sqrt(squares)
        norm[...] = jnp.broadcast_to(root, norm.shape)
        factor[...] = jnp.broadcast_to(
            jnp.minimum(1.0, clip_norm / (root + 1e-06)), factor.shape
        )
        for copy in others:
            copy.wait()

    tile = jax.ShapeDtypeStruct((8, HD), jnp.float32)
    return pl.pallas_call(
        kernel,
        name=name,
        out_shape=(jax.ShapeDtypeStruct(shape, jnp.float32), tile, tile, like(pieces)),
        in_specs=[in_vmem(), anywhere()],
        out_specs=(in_vmem(), in_vmem(), in_vmem(), anywhere()),
        scratch_shapes=[
            pltpu.VMEM((8,) + shape, jnp.float32),
            pltpu.VMEM((outer_count,) + shape, jnp.float32),
            pltpu.SemaphoreType.DMA((6 + outer_count,)),
            pltpu.SemaphoreType.DMA((6 + outer_count,)),
        ]
        + exchange_scratch(),
        compiler_params=params(number),
    )(values, pieces)


def head_scale(raw, gain, cos_full, sin_full):
    normed = raw * rms_scale(raw) * gain
    return (normed * cos_full + pltpu.roll(normed, HD // 2, 1) * sin_full).astype(jnp.bfloat16)


def head_back(raw, gain, grad, cos_full, sin_full):
    grad = grad * cos_full - pltpu.roll(grad, HD // 2, 1) * sin_full
    return norm_back(raw, gain, grad)


def columns(index):
    return pl.ds(index * HD, HD)


def head_inputs(proj, gains, cos_ref, sin_ref, queries, keys, values, heads):
    for head in range(heads):
        queries[head] = head_scale(
            proj[0, :, columns(head)], gains[0:1, :], cos_ref[...], sin_ref[...]
        )
    keys[...] = head_scale(
        proj[0, :, columns(heads)], gains[1:2, :], cos_ref[...], sin_ref[...]
    )
    values[...] = proj[0, :, columns(heads + 1)].astype(jnp.bfloat16)


def masked_scores(stacked, keys, step, length):
    scores = lax.dot_general(
        stacked, keys, (((1,), (1,)), ((), ())), preferred_element_type=jnp.float32
    ) * (HD ** (-0.5))
    row = lax.broadcasted_iota(jnp.int32, scores.shape, 0) % BLOCK + step * BLOCK
    column = lax.broadcasted_iota(jnp.int32, scores.shape, 1)
    return jnp.where((column <= row) & (column < length), scores, masked_score)


def stack_heads(ref, at, heads):
    return jnp.concatenate([ref[head, at] for head in range(heads)], axis=0)


def per_sequence(*shape):
    return pl.BlockSpec((1,) + shape, lambda s: (s,) + (0,) * len(shape))


def whole(*shape):
    return pl.BlockSpec(shape, lambda s: (0,) * len(shape), pipeline_mode=pl.Buffered(1))


def across_columns(left, weights, first, width, out):
    total = weights.shape[0]
    for start in range(0, total, 512):
        at = pl.ds(start, 512)
        out[0, :, at] = lax.dot_general(
            left,
            weights[at, first : first + width],
            (((1,), (1,)), ((), ())),
            preferred_element_type=jnp.float32,
        ).astype(out.dtype)


def attend(normed, weights, cotangent, extra, group_length, cos_full, sin_full, gains, heads, number):
    count, rows, width = normed.shape
    wide = (heads + 2) * HD
    extras = len(extra)
    own_rows = cotangent.shape[0]

    def kernel(lengths, normed, weights, cos_ref, sin_ref, gains, own, *rest):
        pieces, rest = rest[:extras], rest[extras:]
        (proj, out, logs, branch, gathered), rest = rest[:5], rest[5:]
        mixed, (queries, keys, values), sems = rest[:extras], rest[extras : extras + 3], rest[extras + 3 :]
        sequence = pl.program_id(0)
        steps = plan_gather(own, gathered, *sems[:3], cut=own_rows // 2)
        copies = plan_exchanges(pieces, mixed, sems[3:])

        @pl.when(sequence == 0)
        def _():
            greet(EVERYONE_NEAR)
            steps[0]()
            for copy in copies:
                copy.start()

        length = lengths[sequence]
        proj[0] = jnp.dot(
            normed[0], weights[:, :wide], preferred_element_type=jnp.float32
        )
        head_inputs(proj, gains, cos_ref, sin_ref, queries, keys, values, heads)
        lane = lax.broadcasted_iota(jnp.int32, (BLOCK, HD), 1)
        for step in range(rows // BLOCK):
            at = pl.ds(step * BLOCK, BLOCK)
            seen = pl.ds(0, (step + 1) * BLOCK)
            scores = masked_scores(stack_heads(queries, at, heads), keys[seen], step, length)
            top = jnp.max(scores, axis=-1, keepdims=True)
            exponent = jnp.exp(scores - top)
            total = jnp.sum(exponent, axis=-1, keepdims=True)
            probs = (exponent / total).astype(jnp.bfloat16)
            mixed_values = jnp.dot(probs, values[seen], preferred_element_type=jnp.float32)
            log_total = top + jnp.log(total)
            kept = jnp.zeros((BLOCK, HD), jnp.float32)
            for head in range(heads):
                mine = slice(head * BLOCK, (head + 1) * BLOCK)
                out[0, at, columns(head)] = mixed_values[mine].astype(jnp.bfloat16)
                kept = jnp.where(lane == head, log_total[mine], kept)
            logs[0, at] = kept
        across_columns(out[0], weights, wide, heads * HD, branch)

        @pl.when(sequence == 1)
        def _():
            steps[1]()

        @pl.when(sequence == 2)
        def _():
            steps[2]()

        @pl.when(sequence == count - 1)
        def _():
            steps[3]()
            for copy in copies:
                copy.wait()

    outs = pl.pallas_call(
        kernel,
        name="attend",
        grid=(count,),
        out_shape=(
            jax.ShapeDtypeStruct((count, rows, wide), jnp.float32),
            jax.ShapeDtypeStruct((count, rows, heads * HD), jnp.bfloat16),
            jax.ShapeDtypeStruct((count, rows, HD), jnp.float32),
            jax.ShapeDtypeStruct((count, rows, width), jnp.bfloat16),
            layer_rows(own_rows, width),
        )
        + tuple(like(piece) for piece in extra),
        in_specs=[
            pl.BlockSpec(memory_space=pltpu.SMEM),
            per_sequence(rows, width),
            whole(width, wide + heads * HD),
            whole(rows, HD),
            whole(rows, HD),
            whole(2, HD),
            anywhere(),
        ]
        + [anywhere()] * extras,
        out_specs=(
            per_sequence(rows, wide),
            per_sequence(rows, heads * HD),
            per_sequence(rows, HD),
            per_sequence(rows, width),
            anywhere(),
        )
        + (anywhere(),) * extras,
        scratch_shapes=[
            pltpu.VMEM((heads, rows, HD), jnp.bfloat16),
            pltpu.VMEM((rows, HD), jnp.bfloat16),
            pltpu.VMEM((rows, HD), jnp.bfloat16),
        ]
        + gather_scratch()
        + exchange_scratch() * extras,
        compiler_params=params(number),
        cost_estimate=cost_of(50),
    )(group_length, normed, weights, cos_full, sin_full, gains, cotangent, *extra)
    return outs[:4] + (outs[4].reshape(-1, width),) + tuple(outs[5:])


def attend_back(
    projected, grad_attn, logs, weights, part, hidden, group_length, cos_full, sin_full, gains, heads, number
):
    count, rows, wide = projected.shape
    own_rows, width = hidden.shape
    cut = own_rows // 2

    def kernel(
        lengths, proj, grad, logs, weights, cos_ref, sin_ref, gains, part, hidden, *rest
    ):
        (out, gain_grad, back_part, output), rest = rest[:4], rest[4:]
        (queries, keys, values, grad_att, grad_q, grad_k, grad_v, total, held, held_sem), rest = (
            rest[:10],
            rest[10:],
        )
        sequence = pl.program_id(0)
        steps, from_tp, from_near = plan_sum(part, total, rest, cut)
        fetch = pltpu.make_async_copy(hidden, held, held_sem)

        @pl.when(sequence == 0)
        def _():
            greet(NEIGHBOURS)
            steps[0]()
            fetch.start()
            gain_grad[...] = jnp.zeros_like(gain_grad)

        length = lengths[sequence]
        grad_att[...] = jnp.dot(
            grad[0], weights[:, wide:], preferred_element_type=jnp.float32
        ).astype(jnp.bfloat16)
        head_inputs(proj, gains, cos_ref, sin_ref, queries, keys, values, heads)
        grad_k[...] = jnp.zeros_like(grad_k)
        grad_v[...] = jnp.zeros_like(grad_v)

        @pl.when(sequence == 0)
        def _():
            steps[1]()

        for step in range(rows // BLOCK):
            at = pl.ds(step * BLOCK, BLOCK)
            seen = pl.ds(0, (step + 1) * BLOCK)
            stacked = stack_heads(queries, at, heads)
            above = jnp.concatenate([grad_att[at, columns(head)] for head in range(heads)], axis=0)
            log_total = jnp.concatenate(
                [logs[0, at, head : head + 1] for head in range(heads)], axis=0
            )
            probs = jnp.exp(masked_scores(stacked, keys[seen], step, length) - log_total)
            grad_probs = lax.dot_general(
                above, values[seen], (((1,), (1,)), ((), ())), preferred_element_type=jnp.float32
            )
            inner = jnp.sum(probs * grad_probs, axis=-1, keepdims=True)
            grad_scores = (probs * (grad_probs - inner)).astype(jnp.bfloat16)
            by_query = jnp.dot(grad_scores, keys[seen], preferred_element_type=jnp.float32)
            for head in range(heads):
                grad_q[head, at] = by_query[head * BLOCK : (head + 1) * BLOCK] * (HD ** (-0.5))
            grad_k[seen] += lax.dot_general(
                grad_scores, stacked, (((0,), (0,)), ((), ())), preferred_element_type=jnp.float32
            )
            grad_v[seen] += lax.dot_general(
                probs.astype(jnp.bfloat16),
                above,
                (((0,), (0,)), ((), ())),
                preferred_element_type=jnp.float32,
            )

        def settle(column, gain, value):
            back, by_gain = head_back(
                proj[0, :, columns(column)], gains[gain : gain + 1, :], value, cos_ref[...], sin_ref[...]
            )
            out[0, :, columns(column)] = back.astype(jnp.bfloat16)
            gain_grad[gain] += by_gain.reshape(rows // 8, 8, HD).sum(axis=0)

        for head in range(heads):
            settle(head, 0, grad_q[head])
        settle(heads, 1, grad_k[...] * (HD ** (-0.5)))
        out[0, :, columns(heads + 1)] = grad_v[...].astype(jnp.bfloat16)

        @pl.when(sequence == 2)
        def _():
            steps[2]()

        across_columns(out[0], weights, 0, wide, back_part)

        @pl.when(sequence == count - 1)
        def _():
            fetch.wait()
            steps[3]()

            def finish(at):
                value = total[at] + read(from_tp, at) + read(from_near, at)
                output[at] = (held[at] + value).astype(jnp.bfloat16)

            row_loop(own_rows, finish)

    return pl.pallas_call(
        kernel,
        name="attend_back",
        grid=(count,),
        out_shape=(
            jax.ShapeDtypeStruct((count, rows, wide), jnp.bfloat16),
            jax.ShapeDtypeStruct((2, 8, HD), jnp.float32),
            jax.ShapeDtypeStruct((count, rows, width), jnp.bfloat16),
            jax.ShapeDtypeStruct((own_rows, width), jnp.bfloat16),
        ),
        in_specs=[
            pl.BlockSpec(memory_space=pltpu.SMEM),
            per_sequence(rows, wide),
            per_sequence(rows, width),
            per_sequence(rows, HD),
            whole(width, wide + heads * HD),
            whole(rows, HD),
            whole(rows, HD),
            whole(2, HD),
            anywhere(),
            anywhere(),
        ],
        out_specs=(
            per_sequence(rows, wide),
            pl.BlockSpec((2, 8, HD), lambda s: (0, 0, 0)),
            per_sequence(rows, width),
            pl.BlockSpec((own_rows, width), lambda s: (0, 0)),
        ),
        scratch_shapes=[
            pltpu.VMEM((heads, rows, HD), jnp.bfloat16),
            pltpu.VMEM((rows, HD), jnp.bfloat16),
            pltpu.VMEM((rows, HD), jnp.bfloat16),
            pltpu.VMEM((rows, heads * HD), jnp.bfloat16),
            pltpu.VMEM((heads, rows, HD), jnp.float32),
            pltpu.VMEM((rows, HD), jnp.float32),
            pltpu.VMEM((rows, HD), jnp.float32),
            pltpu.VMEM((own_rows, width), jnp.float32),
            pltpu.VMEM((own_rows, width), jnp.float32),
            pltpu.SemaphoreType.DMA,
        ]
        + sum_scratch(own_rows, width, cut),
        compiler_params=params(number),
        cost_estimate=cost_of(50),
    )(
        group_length, projected, grad_attn, logs, weights, cos_full, sin_full, gains, spread(part, own_rows), hidden
    )


def adam_rows(weight, moment, square, pieces, factor, widths):
    rows, total = weight.shape
    height = 16

    def kernel(weight, moment, square, pieces, factor, new, one, two, low):
        scale = factor[0:1, 0:1]
        for member in range(TEAM):
            first, inside = 0, 0
            for width in widths:
                share = width // TEAM
                at = pl.ds(first + member * share, share)
                gradient = pieces[member, :, inside : inside + share].astype(jnp.float32)
                value, one[:, at], two[:, at] = adam_update(
                    weight[:, at], gradient, moment[:, at], square[:, at], scale, weight_decay, learn_rate
                )
                new[:, at] = value
                low[:, at] = value.astype(jnp.bfloat16)
                first += width
                inside += share

    block = pl.BlockSpec((height, total), lambda s: (s, 0))
    return pl.pallas_call(
        kernel,
        name="adam_rows",
        grid=(rows // height,),
        out_shape=(like(weight),) * 3 + (jax.ShapeDtypeStruct(weight.shape, jnp.bfloat16),),
        in_specs=[
            block,
            block,
            block,
            pl.BlockSpec((TEAM, height, pieces.shape[2]), lambda s: (0, s, 0)),
            whole(8, HD),
        ],
        out_specs=(block,) * 4,
        compiler_params=pltpu.CompilerParams(vmem_limit_bytes=VMEM_LIMIT),
        cost_estimate=cost_of(rows * total * 28 / 3.4e6),
    )(weight, moment, square, pieces, factor)


def adam_columns(weight, moment, square, pieces, factor):
    rows, total = weight.shape
    share = rows // TEAM

    def kernel(weight, moment, square, pieces, factor, new, one, two, low):
        gradient = pieces[0].astype(jnp.float32).T
        value, one[...], two[...] = adam_update(
            weight[...], gradient, moment[...], square[...], factor[0:1, 0:1], weight_decay, learn_rate
        )
        new[...] = value
        low[...] = value.astype(jnp.bfloat16)

    block = pl.BlockSpec((share, total), lambda s: (s, 0))
    return pl.pallas_call(
        kernel,
        name="adam_columns",
        grid=(TEAM,),
        out_shape=(like(weight),) * 3 + (jax.ShapeDtypeStruct(weight.shape, jnp.bfloat16),),
        in_specs=[block, block, block, per_sequence(*pieces.shape[1:]), whole(8, HD)],
        out_specs=(block,) * 4,
        compiler_params=pltpu.CompilerParams(vmem_limit_bytes=VMEM_LIMIT),
        cost_estimate=cost_of(rows * total * 28 / 3.4e6),
    )(weight, moment, square, pieces, factor)


def split_columns(values, widths):
    members = []
    for member in range(TEAM):
        start, parts = 0, []
        for width in widths:
            share = width // TEAM
            first = start + member * share
            parts.append(values[:, first : first + share])
            start += width
        members.append(jnp.concatenate(parts, axis=1))
    return jnp.stack(members)


def gather_outer(mixed):
    return lax.all_gather(mixed.reshape(-1, mixed.shape[2]), "outer", axis=0, tiled=True)


def team_pieces(summed):
    return summed.reshape(TEAM, -1, summed.shape[-1])


def sum_weight(gradient):
    return lax.psum_scatter(gradient, "outer", scatter_dimension=0, tiled=True)


def after(values, earlier):
    return lax.optimization_barrier((values, earlier))


def adam_update(weight, gradient, moment_one, moment_two, factor, decay_rate, rate_value):
    clipped = gradient * factor
    moment_one = beta_first * moment_one + (1.0 - beta_first) * clipped
    moment_two = beta_second * moment_two + (1.0 - beta_second) * clipped * clipped
    first_fixed = moment_one / (1.0 - beta_first**STEP)
    second_fixed = moment_two / (1.0 - beta_second**STEP)
    weight = weight - rate_value * (
        first_fixed / (jnp.sqrt(second_fixed) + adam_epsilon) + decay_rate * weight
    )
    return (weight, moment_one, moment_two)


def dot(left, right, contract):
    return lax.dot_general(
        left, right, ((contract[0], contract[1]), ((), ())), preferred_element_type=jnp.float32
    )


def times(left, right):
    return dot(left, right, ((1,), (0,)))


def times_across(left, right):
    return dot(left, right, ((1,), (1,)))


def over_rows(left, right):
    return dot(left, right, ((0,), (0,)))


def local(
    inputs,
    cotangent,
    lengths,
    owners,
    qkv_weight,
    out_weight,
    gate_up_weight,
    down_weight,
    norm_gains,
    qkv_moment,
    out_moment,
    gate_up_moment,
    down_moment,
    gains_moment,
    qkv_square,
    out_square,
    gate_up_square,
    down_square,
    gains_square,
):
    tp_count = lax.axis_size("tp")
    half_rows = inputs.shape[0]
    row_count = half_rows * tp_count
    heads = H // tp_count // TEAM
    hidden_units = FF // tp_count // TEAM
    qkv_widths = (H * HD // tp_count, KV * HD // tp_count, KV * HD // tp_count)
    out_widths = (H * HD // tp_count,)
    gate_up_widths = (FF // tp_count, FF // tp_count)
    down_widths = (FF // tp_count,)

    first_group = lax.axis_index("outer") * TEAM
    group_ids = first_group + jnp.arange(TEAM)
    group_length = jnp.sum(
        jnp.where(owners[None, :] == group_ids[:, None], lengths[None, :], 0), axis=1
    )
    own_group = lax.axis_index("near") * CORE + lax.axis_index("core")
    own_rows = lax.axis_index("tp") * half_rows + jnp.arange(half_rows)
    valid_rows = (own_rows < pick(group_length, own_group))[:, None]
    half_width = HD // 2
    frequency = rope_base ** (-(jnp.arange(half_width, dtype=jnp.float32) * 2.0 / HD))
    angles = jnp.arange(row_count, dtype=jnp.float32)[:, None] * frequency[None, :]
    cosine, sine = jnp.cos(angles), jnp.sin(angles)
    cos_full = jnp.concatenate([cosine, cosine], axis=1)
    sin_full = jnp.concatenate([-sine, sine], axis=1)
    attn_gain = norm_gains[:D]
    mlp_gain = norm_gains[D : 2 * D]
    head_gains = norm_gains[2 * D :].reshape(2, HD)

    first_pieces = jnp.concatenate(
        [
            split_columns(qkv_weight.astype(jnp.bfloat16), qkv_widths),
            split_columns(out_weight.astype(jnp.bfloat16).T, out_widths),
        ],
        axis=2,
    )
    gate_up_pieces = split_columns(gate_up_weight.astype(jnp.bfloat16), gate_up_widths)
    down_pieces = split_columns(down_weight.astype(jnp.bfloat16).T, down_widths)
    first_mixed = exchange(first_pieces, 6, "exchange_first")
    first_full = gather_outer(first_mixed)
    qkv_full = first_full[:, : (heads + 2) * HD]

    residual_in = inputs.astype(jnp.float32)
    normed_attn = residual_in * rms_scale(residual_in) * attn_gain
    normed_attn, first_mixed = lax.optimization_barrier(
        (normed_attn.astype(jnp.bfloat16), first_mixed)
    )
    normed_attn, gate_up_mixed = gather_rows(
        normed_attn, (gate_up_pieces,), 0, "gather_inputs"
    )
    gate_up_full = gather_outer(gate_up_mixed)
    grad_low = jnp.where(valid_rows, cotangent, jnp.zeros_like(cotangent))
    projected, attended, logs, attn_branch, grad_all, down_mixed = attend(
        normed_attn.reshape(TEAM, row_count, D),
        first_full,
        grad_low,
        (down_pieces,),
        group_length,
        cos_full,
        sin_full,
        head_gains,
        heads,
        1,
    )
    down_full = gather_outer(down_mixed)
    attended = attended.reshape(-1, heads * HD)
    hidden, normed_mlp = branch_and_norm(attn_branch, inputs, mlp_gain, 2, "branch_and_norm")
    gate_up = times(normed_mlp, gate_up_full)
    gate_part = gate_up[:, :hidden_units]
    up_part = gate_up[:, hidden_units:]
    activated = swish_product(gate_part, up_part).astype(jnp.bfloat16)
    mlp_part = times_across(activated, down_full).astype(jnp.bfloat16)

    grad_down = over_rows(grad_all, activated).astype(jnp.bfloat16)
    grad_all, grad_down = after(grad_all, grad_down)
    down_sum = sum_weight(grad_down)
    grad_activated = times(grad_all, down_full)
    swish_pull = jax.vjp(swish_product, gate_part, up_part)[1]
    grad_gate, grad_up = swish_pull(grad_activated)
    grad_gate_up = jnp.concatenate([grad_gate, grad_up], axis=1).astype(jnp.bfloat16)
    grad_normed_mlp = times_across(grad_gate_up, gate_up_full).astype(jnp.bfloat16)
    grad_gate_up_weight = over_rows(normed_mlp, grad_gate_up).astype(jnp.bfloat16)
    grad_normed_mlp, grad_gate_up_weight, down_sum = lax.optimization_barrier(
        (grad_normed_mlp, grad_gate_up_weight, down_sum)
    )
    gate_up_sum = sum_weight(grad_gate_up_weight)
    grad_hidden, grad_mlp_gain, grad_attn = norm_back_gather(
        grad_normed_mlp, hidden, grad_low, mlp_gain, 3, "norm_back_mlp"
    )
    grad_out_weight = over_rows(grad_attn, attended).astype(jnp.bfloat16)
    grad_out_weight, gate_up_sum = after(grad_out_weight, gate_up_sum)
    out_sum = sum_weight(grad_out_weight)
    grad_projected, grad_head_gains, grad_normed_attn, output = attend_back(
        projected,
        grad_attn.reshape(TEAM, row_count, D),
        logs,
        first_full,
        mlp_part,
        hidden,
        group_length,
        cos_full,
        sin_full,
        head_gains,
        heads,
        7,
    )
    grad_projected = grad_projected.reshape(-1, projected.shape[2])
    grad_qkv_weight = over_rows(normed_attn, grad_projected).astype(jnp.bfloat16)
    grad_qkv_weight, out_sum = after(grad_qkv_weight, out_sum)
    qkv_sum = sum_weight(grad_qkv_weight)
    input_grad, grad_attn_gain, down_mixed, gate_up_mixed, out_mixed = norm_back_last(
        grad_normed_attn,
        inputs,
        grad_hidden,
        attn_gain,
        (team_pieces(down_sum), team_pieces(gate_up_sum), team_pieces(out_sum)),
        4,
        "norm_back_attn",
    )
    gain_part = jnp.concatenate(
        [grad_attn_gain, grad_mlp_gain, grad_head_gains.sum(axis=1).reshape(-1)]
    )
    square_part = sum(
        jnp.sum(jnp.square(member.astype(jnp.float32)))
        for member in (qkv_sum, out_sum, gate_up_sum, down_sum)
    )
    gain_count = gain_part.shape[0]
    packed = jnp.pad(gain_part, (0, -gain_count % PAD))
    packed = jnp.concatenate([packed, jnp.pad(square_part[None], (0, PAD - 1))])
    packed, norm_tile, factor_tile, qkv_mixed = total_everywhere(
        packed.reshape(-1, HD), team_pieces(qkv_sum), lax.axis_size("outer"), 5, "total_everywhere"
    )
    gain_grad = packed.reshape(-1)[:gain_count]
    grad_norm, factor = norm_tile[0, 0], factor_tile[0, 0]
    new_qkv, new_qkv_one, new_qkv_two, qkv_copy = adam_rows(
        qkv_weight, qkv_moment, qkv_square, qkv_mixed, factor_tile, qkv_widths
    )
    new_out, new_out_one, new_out_two, out_copy = adam_columns(
        out_weight, out_moment, out_square, out_mixed, factor_tile
    )
    new_gate_up, new_gate_up_one, new_gate_up_two, gate_up_copy = adam_rows(
        gate_up_weight, gate_up_moment, gate_up_square, gate_up_mixed, factor_tile, gate_up_widths
    )
    new_down, new_down_one, new_down_two, down_copy = adam_columns(
        down_weight, down_moment, down_square, down_mixed, factor_tile
    )
    new_gains, new_gains_one, new_gains_two = adam_update(
        norm_gains, gain_grad, gains_moment, gains_square, factor, 0.0, gain_rate
    )
    return (
        output,
        input_grad,
        grad_norm,
        new_qkv,
        new_qkv_one,
        new_qkv_two,
        qkv_copy,
        new_out,
        new_out_one,
        new_out_two,
        out_copy,
        new_gate_up,
        new_gate_up_one,
        new_gate_up_two,
        gate_up_copy,
        new_down,
        new_down_one,
        new_down_two,
        down_copy,
        new_gains,
        new_gains_one,
        new_gains_two,
    )


def solution(mesh):
    fsdp_count, tp_count = mesh.shape["fsdp"], mesh.shape["tp"]
    cut = mesh.devices.reshape(fsdp_count // TEAM, NEAR, CORE, tp_count)
    cut_mesh = Mesh(cut, ("outer",) + LAYER)
    fsdp = ("outer", "near", "core")
    rows = P(fsdp + ("tp",), None)
    wide = P(fsdp, "tp")
    tall = P("tp", fsdp)
    weights = (wide, tall, wide, tall, P())
    return jax.shard_map(
        local,
        mesh=cut_mesh,
        in_specs=(rows, rows, P(), P()) + weights * 3,
        out_specs=(rows, rows, P()) + (wide,) * 4 + (tall,) * 4 + (wide,) * 4 + (tall,) * 4 + (P(),) * 3,
        check_vma=False,
    )
```

```python
import jax
import jax.numpy as jnp
from jax import lax
from jax.experimental import pallas as pl
from jax.experimental.pallas import tpu as pltpu
from jax.sharding import Mesh, PartitionSpec as P

D = 2048
H = 16
KV = 8
HD = 128
FF = 6144
STEP = 10


norm_epsilon = 1e-06
rope_base = 1000000.0
clip_norm = 1.0
learn_rate = 0.04
gain_rate = 0.8
beta_first = 0.9
beta_second = 0.999
adam_epsilon = 1e-08
weight_decay = 0.1
masked_score = -1e30

NEAR = 2
CORE = 2
TEAM = NEAR * CORE
LAYER = ("near", "core", "tp")
BLOCK = 128
PAD = 8 * 128


def rms_scale(values):
    return lax.rsqrt(jnp.mean(values * values, axis=-1, keepdims=True) + norm_epsilon)


def swish_product(gate_part, up_part):
    return jax.nn.silu(gate_part) * up_part


def pick(values, index):
    return lax.dynamic_index_in_dim(values, index, 0, keepdims=False)


MESH_ID = pl.DeviceIdType.MESH
VMEM_LIMIT = 60 * 1024 * 1024
CHUNK = 16
GATHER_COPIES = 13
SUM_COPIES = 10
NEIGHBOURS = ((1, 0, 0), (0, 1, 0), (0, 0, 1))
MATES = ((0, 1, 0), (1, 0, 0), (1, 1, 0))
EVERYONE_NEAR = NEIGHBOURS + ((1, 1, 0),)


def spots():
    return tuple(lax.axis_index(name) for name in LAYER)


def flipped(near_flip, core_flip, tp_flip):
    return {
        name: 1 - spot if flip else spot
        for name, spot, flip in zip(LAYER, spots(), (near_flip, core_flip, tp_flip))
    }


def greet(flips):
    barrier = pltpu.get_barrier_semaphore()
    for flip in flips:
        pl.semaphore_signal(barrier, inc=1, device_id=flipped(*flip), device_id_type=MESH_ID)
    pl.semaphore_wait(barrier, len(flips))


def link(source, target, send_sem, recv_sem, flip):
    return pltpu.make_async_remote_copy(
        src_ref=source,
        dst_ref=target,
        send_sem=send_sem,
        recv_sem=recv_sem,
        device_id=flipped(*flip),
        device_id_type=MESH_ID,
    )


TO_NEAR, TO_CORE, TO_TP = NEIGHBOURS


def plan_exchange(pieces, out, send, recv, own_sem):
    near, core, _ = spots()
    own = near * CORE + core
    copies = []
    for number, flip in enumerate(MATES):
        there = (1 - near if flip[0] else near) * CORE + (1 - core if flip[1] else core)
        copies.append(
            link(pieces.at[there], out.at[own], send.at[number], recv.at[number], flip)
        )
    copies.append(pltpu.make_async_copy(pieces.at[own], out.at[own], own_sem))
    return copies


def exchange_scratch():
    return [
        pltpu.SemaphoreType.DMA((len(MATES),)),
        pltpu.SemaphoreType.DMA((len(MATES),)),
        pltpu.SemaphoreType.DMA,
    ]


def crossing(pieces, width):
    return sum(2 * piece.shape[1] * piece.shape[2] for piece in pieces) // width


def plan_exchanges(pieces, mixed, sems):
    copies = []
    for place, (piece, result) in enumerate(zip(pieces, mixed)):
        copies += plan_exchange(piece, result, *sems[3 * place : 3 * place + 3])
    return copies


def plan_gather(own, out, send, recv, own_sem, cut, base=0, rows=None):
    near, core, tp = spots()
    rows = own.shape[0] if rows is None else rows
    low, high = pl.ds(base, cut), pl.ds(base + cut, rows - cut)
    all_rows = pl.ds(base, rows)

    def make(number, source, target, flip):
        return link(source, target, send.at[number], recv.at[number], flip)

    def give(number, part, flip):
        return make(number, own.at[part], out.at[near, core, tp, part], flip)

    def relay(number, where_near, where_tp, part, flip):
        ref = out.at[where_near, core, where_tp, part]
        return make(number, ref, ref, flip)

    keep = pltpu.make_async_copy(own.at[all_rows], out.at[near, core, tp, all_rows], own_sem)
    twin_own = give(4, all_rows, TO_CORE)
    near_high = give(1, high, TO_NEAR)
    tp_high = give(2, high, TO_TP)
    far_high = relay(7, 1 - near, tp, high, TO_TP)
    twin_beside = relay(8, 1 - near, tp, high, TO_CORE)
    twin_across = relay(9, near, 1 - tp, high, TO_CORE)
    twin_far = relay(12, 1 - near, 1 - tp, high, TO_CORE)
    twins = [twin_own, twin_beside, twin_across, twin_far]
    ways = [near_high, tp_high, far_high]
    if cut:
        tp_low = give(0, low, TO_TP)
        near_low = give(3, low, TO_NEAR)
        far_low = relay(5, near, 1 - tp, low, TO_NEAR)
        twin_across_low = relay(6, near, 1 - tp, low, TO_CORE)
        twin_beside_low = relay(10, 1 - near, tp, low, TO_CORE)
        twin_far_low = relay(11, 1 - near, 1 - tp, low, TO_CORE)
        twins += [twin_across_low, twin_beside_low, twin_far_low]
        ways += [tp_low, near_low, far_low]

    def begin():
        if cut:
            tp_low.start()
        near_high.start()
        tp_high.start()
        if cut:
            near_low.start()
        twin_own.start()
        keep.start()

    def middle():
        if cut:
            tp_low.wait_recv()
            far_low.start()
            twin_across_low.start()
        near_high.wait_recv()
        far_high.start()
        twin_beside.start()

    def later():
        tp_high.wait_recv()
        twin_across.start()
        if cut:
            near_low.wait_recv()
            twin_beside_low.start()

    def finish():
        if cut:
            far_low.wait_recv()
            twin_far_low.start()
        far_high.wait_recv()
        twin_far.start()
        for copy in twins:
            copy.wait_recv()
        for copy in ways + twins:
            copy.wait_send()
        keep.wait()

    return [begin, middle, later, finish]


def balanced(rows, beside):
    return max(0, (rows - beside) // 2 // CHUNK * CHUNK)


def gather_scratch():
    return [
        pltpu.SemaphoreType.DMA((GATHER_COPIES,)),
        pltpu.SemaphoreType.DMA((GATHER_COPIES,)),
        pltpu.SemaphoreType.DMA,
    ]


def add_rows(target, start, count, *sources):
    @pl.loop(0, count // CHUNK)
    def _(step):
        at = pl.ds(pl.multiple_of(start + step * CHUNK, CHUNK), CHUNK)
        total = None
        for source, shift in sources:
            where = pl.ds(pl.multiple_of(start - shift + step * CHUNK, CHUNK), CHUNK)
            value = source[where].astype(jnp.float32)
            total = value if total is None else total + value
        target[at] = total.astype(target.dtype)


def plan_sum(outgoing, mine, keep, total, scratch, cut):
    theirs, way_near, way_tp, from_tp, from_near, send, recv = scratch
    rows = total.shape[0]
    low, high = pl.ds(0, cut), pl.ds(cut, rows - cut)

    def make(number, source, target, flip):
        return link(source, target, send.at[number], recv.at[number], flip)

    twin = [make(number, outgoing[number], theirs.at[number], TO_CORE) for number in range(4)]
    far, to_tp, to_near, own = mine
    far_high = make(5, far.at[high], way_tp, TO_TP)
    tp_high = make(6, to_tp.at[high], from_tp.at[high], TO_TP)
    near_high = make(9, to_near.at[high], from_near.at[high], TO_NEAR)
    ways = [far_high, tp_high, near_high]
    if cut:
        far_low = make(4, far.at[low], way_near, TO_NEAR)
        near_low = make(7, to_near.at[low], from_near.at[low], TO_NEAR)
        tp_low = make(8, to_tp.at[low], from_tp.at[low], TO_TP)
        ways += [near_low, tp_low]

    def ready(number):
        if keep:
            keep[number].wait()
        twin[number].wait_recv()

    def both(number):
        return (mine[number], 0), (theirs.at[number], 0)

    def begin(numbers=range(4)):
        for number in numbers:
            twin[number].start()
            if keep:
                keep[number].start()

    def send_far():
        ready(0)
        if cut:
            add_rows(far, 0, cut, *both(0))
            far_low.start()
        add_rows(far, cut, rows - cut, *both(0))
        far_high.start()

    def send_tp():
        ready(1)
        add_rows(to_tp, cut, rows - cut, *both(1))
        tp_high.start()

    def send_near():
        ready(2)
        if cut:
            add_rows(to_near, 0, cut, *both(2))
            near_low.start()

    def first():
        send_far()
        send_tp()
        send_near()

    def second():
        if cut:
            far_low.wait_recv()
            add_rows(to_tp, 0, cut, *both(1), (way_near, 0))
            tp_low.start()
        far_high.wait_recv()
        add_rows(to_near, cut, rows - cut, *both(2), (way_tp, cut))
        near_high.start()
        ready(3)
        add_rows(total, 0, rows, *both(3))

    def finish():
        for copy in ways[1:]:
            copy.wait_recv()
        for copy in twin + ways + ([far_low] if cut else []):
            copy.wait_send()

    return [begin, first, second, finish], (send_far, send_tp, send_near)


def plan_sum_of(part, total, scratch, cut):
    mine, local_sem, *scratch = scratch
    near, core, tp = spots()
    order = [(1 - near, 1 - tp), (near, 1 - tp), (1 - near, tp), (near, tp)]
    outgoing = [part.at[a, 1 - core, b] for a, b in order]
    keep = [
        pltpu.make_async_copy(part.at[a, core, b], mine.at[number], local_sem.at[number])
        for number, (a, b) in enumerate(order)
    ]
    blocks = [mine.at[number] for number in range(4)]
    steps, _ = plan_sum(outgoing, blocks, keep, total, scratch, cut)
    return steps, scratch[3], scratch[4]


def sum_scratch(rows, width, cut, fetched=True):
    low = jnp.bfloat16
    fetch = [pltpu.VMEM((4, rows, width), low), pltpu.SemaphoreType.DMA((4,))]
    return (fetch if fetched else []) + [
        pltpu.VMEM((4, rows, width), low),
        pltpu.VMEM((max(cut, CHUNK), width), low),
        pltpu.VMEM((rows - cut, width), low),
        pltpu.VMEM((rows, width), low),
        pltpu.VMEM((rows, width), low),
        pltpu.SemaphoreType.DMA((SUM_COPIES,)),
        pltpu.SemaphoreType.DMA((SUM_COPIES,)),
    ]


SUM_SCRATCH = 9


def params(number):
    return pltpu.CompilerParams(
        collective_id=number, has_side_effects=True, vmem_limit_bytes=VMEM_LIMIT
    )


def cost_of(microseconds):
    return pl.CostEstimate(
        flops=0, bytes_accessed=int(microseconds * 3.4e6), transcendentals=0
    )


def in_vmem():
    return pl.BlockSpec(memory_space=pltpu.VMEM)


def anywhere():
    return pl.BlockSpec(memory_space=pl.ANY)


def like(array):
    return jax.ShapeDtypeStruct(array.shape, array.dtype)


def layer_rows(rows, width):
    return jax.ShapeDtypeStruct((NEAR, CORE, 2, rows, width), jnp.bfloat16)


def exchange(pieces, number, name):
    def kernel(pieces, out, *sems):
        greet(MATES)
        copies = plan_exchange(pieces, out, *sems)
        for copy in copies:
            copy.start()
        for copy in copies:
            copy.wait()

    return pl.pallas_call(
        kernel,
        name=name,
        out_shape=like(pieces),
        in_specs=[anywhere()],
        out_specs=anywhere(),
        scratch_shapes=exchange_scratch(),
        compiler_params=params(number),
        cost_estimate=cost_of(12),
    )(pieces)


def gather_rows(values, extra, number, name):
    rows, width = values.shape
    extras = len(extra)
    cut = balanced(rows, crossing(extra, width))

    def kernel(own, *rest):
        pieces, out, mixed = rest[:extras], rest[extras], rest[extras + 1 : 2 * extras + 1]
        sems = rest[2 * extras + 1 :]
        begin, *steps = plan_gather(own, out, *sems[:3], cut=cut)
        copies = plan_exchanges(pieces, mixed, sems[3:])
        greet(EVERYONE_NEAR)
        begin()
        for copy in copies:
            copy.start()
        for step in steps:
            step()
        for copy in copies:
            copy.wait()

    outs = pl.pallas_call(
        kernel,
        name=name,
        out_shape=(layer_rows(rows, width),) + tuple(like(piece) for piece in extra),
        in_specs=[anywhere()] * (1 + extras),
        out_specs=(anywhere(),) * (1 + extras),
        scratch_shapes=gather_scratch() + exchange_scratch() * extras,
        compiler_params=params(number),
        cost_estimate=cost_of(60),
    )(values, *extra)
    return (outs[0].reshape(-1, width),) + tuple(outs[1:])


def row_loop(rows, body):
    @pl.loop(0, rows // CHUNK)
    def _(step):
        body(pl.ds(pl.multiple_of(step * CHUNK, CHUNK), CHUNK))


def spread(part, rows):
    return part.reshape(NEAR, CORE, 2, rows, part.shape[-1])


def read(ref, at):
    return ref[at].astype(jnp.float32)


def branch_and_norm(part, residual, gain, number, name):
    rows, width = residual.shape
    cut = rows // 2

    def kernel(part, residual, gain, hidden, out, *scratch):
        normed, sems = scratch[SUM_SCRATCH], scratch[SUM_SCRATCH + 1 :]
        steps, from_tp, from_near = plan_sum_of(part, hidden, scratch[:SUM_SCRATCH], cut)
        onward = plan_gather(normed, out, *sems, cut=cut)
        greet(NEIGHBOURS)
        for step in steps:
            step()

        def finish(at):
            value = hidden[at] + read(from_tp, at) + read(from_near, at)
            value = read(residual, at) + value
            hidden[at] = value
            normed[at] = (value * rms_scale(value) * gain[...]).astype(jnp.bfloat16)

        row_loop(rows, finish)
        for step in onward:
            step()

    hidden, full = pl.pallas_call(
        kernel,
        name=name,
        out_shape=(jax.ShapeDtypeStruct((rows, width), jnp.float32), layer_rows(rows, width)),
        in_specs=[anywhere(), in_vmem(), in_vmem()],
        out_specs=(in_vmem(), anywhere()),
        scratch_shapes=sum_scratch(rows, width, cut)
        + [pltpu.VMEM((rows, width), jnp.bfloat16)]
        + gather_scratch(),
        compiler_params=params(number),
        cost_estimate=cost_of(95),
    )(spread(part, rows), residual, gain.reshape(1, width))
    return hidden, full.reshape(-1, width)


def norm_back(value, gain, grad):
    scale = rms_scale(value)
    scaled = grad * gain
    inner = jnp.mean(scaled * value, axis=-1, keepdims=True)
    return scale * scaled - value * (scale * scale * scale * inner), grad * value * scale


def sequence_order():
    near, core, _ = spots()
    return [
        (near if place >= 2 else 1 - near) * CORE + (core if place % 2 else 1 - core)
        for place in range(TEAM)
    ]


def halves_times(left, weights, target, rows):
    for start in range(0, weights.shape[0], 512):
        at = pl.ds(start, 512)
        product = lax.dot_general(
            left, weights[at, :], (((1,), (1,)), ((), ())), preferred_element_type=jnp.float32
        ).astype(target.dtype)
        target[0, :, at] = product[:rows]
        target[1, :, at] = product[rows:]


def feed_back_rest(
    grad_gate_up, weights, active, down, values, upstream, gain, number, name
):
    rows, width = values.shape
    count, both_rows, units = grad_gate_up.shape
    cut = rows // 2

    def kernel(
        grad, weights, active, down, values, upstream, gain, result, gain_grad, out, branch, *scratch
    ):
        (grad_v, weights_v, active_v, down_v, values_v, upstream_v, parts, total, low), rest = (
            scratch[:9],
            scratch[9:],
        )
        (load_sem, store_sem), rest = rest[:2], rest[2:]
        sums, sems = rest[:7], rest[7:]
        from_tp, from_near = sums[3], sums[4]
        near, core, tp = spots()
        members = sequence_order()
        outgoing = [parts.at[place, half] for place, half in ((0, 1 - tp), (2, 1 - tp), (0, tp), (2, tp))]
        mine = [parts.at[place, half] for place, half in ((1, 1 - tp), (3, 1 - tp), (1, tp), (3, tp))]
        steps, (send_far, send_tp, send_near) = plan_sum(outgoing, mine, (), total, sums, cut)
        onward = plan_gather(low, out, *sems, cut=cut)
        fetch = [
            pltpu.make_async_copy(grad.at[member], grad_v.at[place % 2], load_sem.at[place])
            for place, member in enumerate(members)
        ]
        fetch += [
            pltpu.make_async_copy(source, target, load_sem.at[4 + place])
            for place, (source, target) in enumerate(
                (
                    (weights, weights_v),
                    (values, values_v),
                    (upstream, upstream_v),
                    (active, active_v),
                    (down, down_v),
                )
            )
        ]
        for place in (0, 4, 1, 5, 6, 7, 8):
            fetch[place].start()
        greet(NEIGHBOURS)
        fetch[4].wait()
        for place in range(count):
            fetch[place].wait()
            halves_times(grad_v[place % 2], weights_v, parts.at[place], rows)
            if place + 2 < count:
                fetch[place + 2].start()
            if place == 0:
                steps[0]((0, 2))
            elif place == 1:
                send_far()
                send_near()
            elif place == 2:
                steps[0]((1, 3))
        send_tp()
        steps[2]()
        fetch[5].wait()
        fetch[6].wait()
        gain_grad[...] = jnp.zeros_like(gain_grad)
        steps[3]()

        def finish(at):
            grad = total[at] + read(from_tp, at) + read(from_near, at)
            back, by_gain = norm_back(values_v[at], gain[...], grad)
            gain_grad[...] += by_gain.reshape(CHUNK // 8, 8, width).sum(axis=0)
            value = read(upstream_v, at) + back
            total[at] = value
            low[at] = value.astype(jnp.bfloat16)

        row_loop(rows, finish)
        onward[0]()
        stores = [pltpu.make_async_copy(total, result, store_sem.at[count])]
        stores[0].start()
        fetch[7].wait()
        fetch[8].wait()
        for place in range(count):
            halves_times(active_v[place], down_v, parts.at[place], rows)
            store = pltpu.make_async_copy(parts.at[place], branch.at[place], store_sem.at[place])
            store.start()
            stores.append(store)
            if place == 1:
                onward[1]()
        onward[2]()
        onward[3]()
        for store in stores:
            store.wait()

    low_type = jnp.bfloat16
    result, gain_grad, full, branch = pl.pallas_call(
        kernel,
        name=name,
        out_shape=(
            jax.ShapeDtypeStruct((rows, width), jnp.float32),
            jax.ShapeDtypeStruct((8, width), jnp.float32),
            layer_rows(rows, width),
            jax.ShapeDtypeStruct((count, 2, rows, width), low_type),
        ),
        in_specs=[anywhere()] * 6 + [in_vmem()],
        out_specs=(anywhere(), in_vmem(), anywhere(), anywhere()),
        scratch_shapes=[
            pltpu.VMEM((2, both_rows, units), low_type),
            pltpu.VMEM(weights.shape, low_type),
            pltpu.VMEM(active.shape, low_type),
            pltpu.VMEM(down.shape, low_type),
            pltpu.VMEM((rows, width), values.dtype),
            pltpu.VMEM((rows, width), upstream.dtype),
            pltpu.VMEM((count, 2, rows, width), low_type),
            pltpu.VMEM((rows, width), jnp.float32),
            pltpu.VMEM((rows, width), low_type),
            pltpu.SemaphoreType.DMA((9,)),
            pltpu.SemaphoreType.DMA((count + 1,)),
        ]
        + sum_scratch(rows, width, cut, fetched=False)
        + gather_scratch(),
        compiler_params=params(number),
        cost_estimate=cost_of(105),
    )(grad_gate_up, weights, active, down, values, upstream, gain.reshape(1, width))
    return result, gain_grad.sum(axis=0), full.reshape(-1, width), branch.reshape(-1, width)


def norm_back_last(part, values, upstream, gain, extra, number, name):
    rows, width = values.shape
    extras = len(extra)
    cut = balanced(rows, crossing(extra, width))

    def kernel(part, values, upstream, gain, *rest):
        pieces, (result, gain_grad) = rest[:extras], rest[extras : extras + 2]
        mixed, rest = rest[extras + 2 : 2 * extras + 2], rest[2 * extras + 2 :]
        total, sems = rest[SUM_SCRATCH], rest[SUM_SCRATCH + 1 :]
        steps, from_tp, from_near = plan_sum_of(part, total, rest[:SUM_SCRATCH], cut)
        copies = plan_exchanges(pieces, mixed, sems)
        greet(EVERYONE_NEAR)
        steps[0]()
        for copy in copies:
            copy.start()
        for step in steps[1:]:
            step()
        gain_grad[...] = jnp.zeros_like(gain_grad)

        def finish(at):
            grad = total[at] + read(from_tp, at) + read(from_near, at)
            back, by_gain = norm_back(read(values, at), gain[...], grad)
            gain_grad[...] += by_gain.reshape(CHUNK // 8, 8, width).sum(axis=0)
            result[at] = (read(upstream, at) + back).astype(jnp.bfloat16)

        row_loop(rows, finish)
        for copy in copies:
            copy.wait()

    outs = pl.pallas_call(
        kernel,
        name=name,
        out_shape=(
            jax.ShapeDtypeStruct((rows, width), jnp.bfloat16),
            jax.ShapeDtypeStruct((8, width), jnp.float32),
        )
        + tuple(like(piece) for piece in extra),
        in_specs=[anywhere()] + [in_vmem()] * 3 + [anywhere()] * extras,
        out_specs=(in_vmem(), in_vmem()) + (anywhere(),) * extras,
        scratch_shapes=sum_scratch(rows, width, cut)
        + [pltpu.VMEM((rows, width), jnp.float32)]
        + exchange_scratch() * extras,
        compiler_params=params(number),
        cost_estimate=cost_of(65),
    )(spread(part, rows), values, upstream, gain.reshape(1, width), *extra)
    return (outs[0], outs[1].sum(axis=0)) + tuple(outs[2:])


def total_everywhere(values, pieces, outer_count, number, name):
    shape = values.shape

    def kernel(values, pieces, out, norm, factor, mixed, layer, outers, send, recv, *sems):
        near, core, tp = spots()
        outer = lax.axis_index("outer")
        partners = [
            flipped(a, b, c)
            for a in range(NEAR)
            for b in range(CORE)
            for c in range(2)
            if a + b + c
        ]
        partners += [{"outer": (outer + step) % outer_count} for step in range(1, outer_count)]
        barrier = pltpu.get_barrier_semaphore()
        for partner in partners:
            pl.semaphore_signal(barrier, inc=1, device_id=partner, device_id_type=MESH_ID)
        pl.semaphore_wait(barrier, len(partners))

        def share(slots, mine, first, count):
            copies = []
            for number in range(first, first + count):
                copy = pltpu.make_async_remote_copy(
                    src_ref=slots.at[mine],
                    dst_ref=slots.at[mine],
                    send_sem=send.at[number],
                    recv_sem=recv.at[number],
                    device_id=partners[number],
                    device_id_type=MESH_ID,
                )
                copy.start()
                copies.append(copy)
            return copies

        mine = near * (CORE * 2) + core * 2 + tp
        layer[mine] = values[...]
        copies = share(layer, mine, 0, 7)
        others = plan_exchange(pieces, mixed, *sems)
        for copy in others:
            copy.start()
        for copy in copies:
            copy.wait()
        total = layer[0]
        for slot in range(1, 8):
            total = total + layer[slot]
        outers[outer] = total
        for copy in share(outers, outer, 7, outer_count - 1):
            copy.wait()
        total = outers[0]
        for slot in range(1, outer_count):
            total = total + outers[slot]
        out[...] = total
        row = lax.broadcasted_iota(jnp.int32, shape, 0)
        squares = jnp.sum(jnp.where(row < shape[0] - 8, total * total, total), keepdims=True)
        root = jnp.sqrt(squares)
        norm[...] = jnp.broadcast_to(root, norm.shape)
        factor[...] = jnp.broadcast_to(
            jnp.minimum(1.0, clip_norm / (root + 1e-06)), factor.shape
        )
        for copy in others:
            copy.wait()

    tile = jax.ShapeDtypeStruct((8, HD), jnp.float32)
    return pl.pallas_call(
        kernel,
        name=name,
        out_shape=(jax.ShapeDtypeStruct(shape, jnp.float32), tile, tile, like(pieces)),
        in_specs=[in_vmem(), anywhere()],
        out_specs=(in_vmem(), in_vmem(), in_vmem(), anywhere()),
        scratch_shapes=[
            pltpu.VMEM((8,) + shape, jnp.float32),
            pltpu.VMEM((outer_count,) + shape, jnp.float32),
            pltpu.SemaphoreType.DMA((6 + outer_count,)),
            pltpu.SemaphoreType.DMA((6 + outer_count,)),
        ]
        + exchange_scratch(),
        compiler_params=params(number),
    )(values, pieces)


def head_scale(raw, gain, cos_full, sin_full):
    normed = raw * rms_scale(raw) * gain
    return (normed * cos_full + pltpu.roll(normed, HD // 2, 1) * sin_full).astype(jnp.bfloat16)


def head_back(raw, gain, grad, cos_full, sin_full):
    grad = grad * cos_full - pltpu.roll(grad, HD // 2, 1) * sin_full
    return norm_back(raw, gain, grad)


def columns(index):
    return pl.ds(index * HD, HD)


def head_inputs(proj, gains, cos_ref, sin_ref, queries, keys, values, heads):
    for head in range(heads):
        queries[head] = head_scale(
            proj[0, :, columns(head)], gains[0:1, :], cos_ref[...], sin_ref[...]
        )
    keys[...] = head_scale(
        proj[0, :, columns(heads)], gains[1:2, :], cos_ref[...], sin_ref[...]
    )
    values[...] = proj[0, :, columns(heads + 1)].astype(jnp.bfloat16)


def masked_scores(stacked, keys, step, length):
    scores = lax.dot_general(
        stacked, keys, (((1,), (1,)), ((), ())), preferred_element_type=jnp.float32
    ) * (HD ** (-0.5))
    row = lax.broadcasted_iota(jnp.int32, scores.shape, 0) % BLOCK + step * BLOCK
    column = lax.broadcasted_iota(jnp.int32, scores.shape, 1)
    return jnp.where((column <= row) & (column < length), scores, masked_score)


def stack_heads(ref, at, heads):
    return jnp.concatenate([ref[head, at] for head in range(heads)], axis=0)


def per_sequence(*shape):
    return pl.BlockSpec((1,) + shape, lambda s: (s,) + (0,) * len(shape))


def whole(*shape):
    return pl.BlockSpec(shape, lambda s: (0,) * len(shape), pipeline_mode=pl.Buffered(1))


def across_columns(left, weights, first, width, out):
    total = weights.shape[0]
    for start in range(0, total, 512):
        at = pl.ds(start, 512)
        out[0, :, at] = lax.dot_general(
            left,
            weights[at, first : first + width],
            (((1,), (1,)), ((), ())),
            preferred_element_type=jnp.float32,
        ).astype(out.dtype)


def attend(normed, weights, cotangent, extra, group_length, cos_full, sin_full, gains, heads, early, number):
    count, rows, width = normed.shape
    wide = (heads + 2) * HD
    extras = len(extra)
    own_rows = cotangent.shape[0]
    cut = balanced(early, crossing(extra, width))

    def kernel(lengths, normed, weights, cos_ref, sin_ref, gains, own, *rest):
        pieces, rest = rest[:extras], rest[extras:]
        (proj, out, logs, branch, gathered), rest = rest[:5], rest[5:]
        mixed, (queries, keys, values), sems = rest[:extras], rest[extras : extras + 3], rest[extras + 3 :]
        sequence = pl.program_id(0)
        steps = plan_gather(own, gathered, *sems[:3], cut=cut, rows=early)
        copies = plan_exchanges(pieces, mixed, sems[3:])

        @pl.when(sequence == 0)
        def _():
            greet(EVERYONE_NEAR)
            steps[0]()
            for copy in copies:
                copy.start()

        length = lengths[sequence]
        proj[0] = jnp.dot(
            normed[0], weights[:, :wide], preferred_element_type=jnp.float32
        )
        head_inputs(proj, gains, cos_ref, sin_ref, queries, keys, values, heads)
        lane = lax.broadcasted_iota(jnp.int32, (BLOCK, HD), 1)
        for step in range(rows // BLOCK):
            at = pl.ds(step * BLOCK, BLOCK)
            seen = pl.ds(0, (step + 1) * BLOCK)
            scores = masked_scores(stack_heads(queries, at, heads), keys[seen], step, length)
            top = jnp.max(scores, axis=-1, keepdims=True)
            exponent = jnp.exp(scores - top)
            total = jnp.sum(exponent, axis=-1, keepdims=True)
            probs = (exponent / total).astype(jnp.bfloat16)
            mixed_values = jnp.dot(probs, values[seen], preferred_element_type=jnp.float32)
            log_total = top + jnp.log(total)
            kept = jnp.zeros((BLOCK, HD), jnp.float32)
            for head in range(heads):
                mine = slice(head * BLOCK, (head + 1) * BLOCK)
                out[0, at, columns(head)] = mixed_values[mine].astype(jnp.bfloat16)
                kept = jnp.where(lane == head, log_total[mine], kept)
            logs[0, at] = kept
        across_columns(out[0], weights, wide, heads * HD, branch)

        @pl.when(sequence == 1)
        def _():
            steps[1]()

        @pl.when(sequence == 2)
        def _():
            steps[2]()

        @pl.when(sequence == count - 1)
        def _():
            steps[3]()
            for copy in copies:
                copy.wait()

    outs = pl.pallas_call(
        kernel,
        name="attend",
        grid=(count,),
        out_shape=(
            jax.ShapeDtypeStruct((count, rows, wide), jnp.float32),
            jax.ShapeDtypeStruct((count, rows, heads * HD), jnp.bfloat16),
            jax.ShapeDtypeStruct((count, rows, HD), jnp.float32),
            jax.ShapeDtypeStruct((count, rows, width), jnp.bfloat16),
            layer_rows(own_rows, width),
        )
        + tuple(like(piece) for piece in extra),
        in_specs=[
            pl.BlockSpec(memory_space=pltpu.SMEM),
            per_sequence(rows, width),
            whole(width, wide + heads * HD),
            whole(rows, HD),
            whole(rows, HD),
            whole(2, HD),
            anywhere(),
        ]
        + [anywhere()] * extras,
        out_specs=(
            per_sequence(rows, wide),
            per_sequence(rows, heads * HD),
            per_sequence(rows, HD),
            per_sequence(rows, width),
            anywhere(),
        )
        + (anywhere(),) * extras,
        scratch_shapes=[
            pltpu.VMEM((heads, rows, HD), jnp.bfloat16),
            pltpu.VMEM((rows, HD), jnp.bfloat16),
            pltpu.VMEM((rows, HD), jnp.bfloat16),
        ]
        + gather_scratch()
        + exchange_scratch() * extras,
        compiler_params=params(number),
        cost_estimate=cost_of(50),
    )(group_length, normed, weights, cos_full, sin_full, gains, cotangent, *extra)
    return outs


def attend_back(
    projected,
    grad_attn,
    logs,
    weights,
    part,
    hidden,
    extra,
    group_length,
    cos_full,
    sin_full,
    gains,
    heads,
    number,
):
    count, rows, wide = projected.shape
    own_rows, width = hidden.shape
    extras = len(extra)
    cut = balanced(own_rows, crossing(extra, width))

    def kernel(
        lengths, proj, grad, logs, weights, cos_ref, sin_ref, gains, part, hidden, *rest
    ):
        pieces, rest = rest[:extras], rest[extras:]
        (out, gain_grad, back_part, output), rest = rest[:4], rest[4:]
        mixed, rest = rest[:extras], rest[extras:]
        (queries, keys, values, grad_att, grad_q, grad_k, grad_v, total, held, held_sem), rest = (
            rest[:10],
            rest[10:],
        )
        sequence = pl.program_id(0)
        steps, from_tp, from_near = plan_sum_of(part, total, rest[:SUM_SCRATCH], cut)
        copies = plan_exchanges(pieces, mixed, rest[SUM_SCRATCH:])
        fetch = pltpu.make_async_copy(hidden, held, held_sem)

        @pl.when(sequence == 0)
        def _():
            greet(EVERYONE_NEAR)
            steps[0]()
            for copy in copies:
                copy.start()
            fetch.start()
            gain_grad[...] = jnp.zeros_like(gain_grad)

        length = lengths[sequence]
        grad_att[...] = jnp.dot(
            grad[0], weights[:, wide:], preferred_element_type=jnp.float32
        ).astype(jnp.bfloat16)
        head_inputs(proj, gains, cos_ref, sin_ref, queries, keys, values, heads)
        grad_k[...] = jnp.zeros_like(grad_k)
        grad_v[...] = jnp.zeros_like(grad_v)

        @pl.when(sequence == 0)
        def _():
            steps[1]()

        for step in range(rows // BLOCK):
            at = pl.ds(step * BLOCK, BLOCK)
            seen = pl.ds(0, (step + 1) * BLOCK)
            stacked = stack_heads(queries, at, heads)
            above = jnp.concatenate([grad_att[at, columns(head)] for head in range(heads)], axis=0)
            log_total = jnp.concatenate(
                [logs[0, at, head : head + 1] for head in range(heads)], axis=0
            )
            probs = jnp.exp(masked_scores(stacked, keys[seen], step, length) - log_total)
            grad_probs = lax.dot_general(
                above, values[seen], (((1,), (1,)), ((), ())), preferred_element_type=jnp.float32
            )
            inner = jnp.sum(probs * grad_probs, axis=-1, keepdims=True)
            grad_scores = (probs * (grad_probs - inner)).astype(jnp.bfloat16)
            by_query = jnp.dot(grad_scores, keys[seen], preferred_element_type=jnp.float32)
            for head in range(heads):
                grad_q[head, at] = by_query[head * BLOCK : (head + 1) * BLOCK] * (HD ** (-0.5))
            grad_k[seen] += lax.dot_general(
                grad_scores, stacked, (((0,), (0,)), ((), ())), preferred_element_type=jnp.float32
            )
            grad_v[seen] += lax.dot_general(
                probs.astype(jnp.bfloat16),
                above,
                (((0,), (0,)), ((), ())),
                preferred_element_type=jnp.float32,
            )

        def settle(column, gain, value):
            back, by_gain = head_back(
                proj[0, :, columns(column)], gains[gain : gain + 1, :], value, cos_ref[...], sin_ref[...]
            )
            out[0, :, columns(column)] = back.astype(jnp.bfloat16)
            gain_grad[gain] += by_gain.reshape(rows // 8, 8, HD).sum(axis=0)

        for head in range(heads):
            settle(head, 0, grad_q[head])
        settle(heads, 1, grad_k[...] * (HD ** (-0.5)))
        out[0, :, columns(heads + 1)] = grad_v[...].astype(jnp.bfloat16)

        across_columns(out[0], weights, 0, wide, back_part)

        @pl.when(sequence == 1)
        def _():
            steps[2]()

        @pl.when(sequence == count - 1)
        def _():
            fetch.wait()
            steps[3]()

            def finish(at):
                value = total[at] + read(from_tp, at) + read(from_near, at)
                output[at] = (held[at] + value).astype(jnp.bfloat16)

            row_loop(own_rows, finish)
            for copy in copies:
                copy.wait()

    return pl.pallas_call(
        kernel,
        name="attend_back",
        grid=(count,),
        out_shape=(
            jax.ShapeDtypeStruct((count, rows, wide), jnp.bfloat16),
            jax.ShapeDtypeStruct((2, 8, HD), jnp.float32),
            jax.ShapeDtypeStruct((count, rows, width), jnp.bfloat16),
            jax.ShapeDtypeStruct((own_rows, width), jnp.bfloat16),
        )
        + tuple(like(piece) for piece in extra),
        in_specs=[
            pl.BlockSpec(memory_space=pltpu.SMEM),
            per_sequence(rows, wide),
            per_sequence(rows, width),
            per_sequence(rows, HD),
            whole(width, wide + heads * HD),
            whole(rows, HD),
            whole(rows, HD),
            whole(2, HD),
            anywhere(),
            anywhere(),
        ]
        + [anywhere()] * extras,
        out_specs=(
            per_sequence(rows, wide),
            pl.BlockSpec((2, 8, HD), lambda s: (0, 0, 0)),
            per_sequence(rows, width),
            pl.BlockSpec((own_rows, width), lambda s: (0, 0)),
        )
        + (anywhere(),) * extras,
        scratch_shapes=[
            pltpu.VMEM((heads, rows, HD), jnp.bfloat16),
            pltpu.VMEM((rows, HD), jnp.bfloat16),
            pltpu.VMEM((rows, HD), jnp.bfloat16),
            pltpu.VMEM((rows, heads * HD), jnp.bfloat16),
            pltpu.VMEM((heads, rows, HD), jnp.float32),
            pltpu.VMEM((rows, HD), jnp.float32),
            pltpu.VMEM((rows, HD), jnp.float32),
            pltpu.VMEM((own_rows, width), jnp.float32),
            pltpu.VMEM((own_rows, width), jnp.float32),
            pltpu.SemaphoreType.DMA,
        ]
        + sum_scratch(own_rows, width, cut)
        + exchange_scratch() * extras,
        compiler_params=params(number),
        cost_estimate=cost_of(50),
    )(
        group_length,
        projected,
        grad_attn,
        logs,
        weights,
        cos_full,
        sin_full,
        gains,
        spread(part, own_rows),
        hidden,
        *extra,
    )


def feed(normed, weights, cotangent, gathered, early, number):
    count, rows, width = normed.shape
    units = weights.shape[1] // 2
    late = cotangent.shape[0] - early

    def kernel(normed, weights, own, _, product, active, out, *sems):
        steps = plan_gather(
            own, out, *sems, cut=balanced(late, 0), base=early, rows=late
        )
        sequence = pl.program_id(0)

        @pl.when(sequence == 0)
        def _():
            greet(NEIGHBOURS)
            steps[0]()

        for start in range(0, units, 256):
            gate_at, up_at = pl.ds(start, 256), pl.ds(units + start, 256)
            gate = jnp.dot(normed[0], weights[:, gate_at], preferred_element_type=jnp.float32)
            up = jnp.dot(normed[0], weights[:, up_at], preferred_element_type=jnp.float32)
            product[0, :, gate_at] = gate
            product[0, :, up_at] = up
            active[0, :, gate_at] = swish_product(gate, up).astype(jnp.bfloat16)

        for place in (1, 2, 3):

            @pl.when(sequence == count - 4 + place)
            def _(place=place):
                steps[place]()

    return pl.pallas_call(
        kernel,
        name="feed",
        grid=(count,),
        out_shape=(
            jax.ShapeDtypeStruct((count, rows, 2 * units), jnp.float32),
            jax.ShapeDtypeStruct((count, rows, units), jnp.bfloat16),
            like(gathered),
        ),
        in_specs=[
            per_sequence(rows, width),
            whole(*weights.shape),
            anywhere(),
            anywhere(),
        ],
        out_specs=(per_sequence(rows, 2 * units), per_sequence(rows, units), anywhere()),
        scratch_shapes=gather_scratch(),
        input_output_aliases={3: 2},
        compiler_params=params(number),
        cost_estimate=cost_of(28),
    )(normed, weights, cotangent, gathered)


def feed_back(grads, weights, product):
    count, rows, width = grads.shape
    units = weights.shape[1]

    def kernel(grads, weights, product, out):
        for start in range(0, units, 256):
            gate_at, up_at = pl.ds(start, 256), pl.ds(units + start, 256)
            grad = jnp.dot(grads[0], weights[:, gate_at], preferred_element_type=jnp.float32)
            gate, up = product[0, :, gate_at], product[0, :, up_at]
            share = jax.nn.sigmoid(gate)
            by_gate = grad * up * share * (1.0 + gate * (1.0 - share))
            out[0, :, gate_at] = by_gate.astype(jnp.bfloat16)
            out[0, :, up_at] = (grad * gate * share).astype(jnp.bfloat16)

    return pl.pallas_call(
        kernel,
        name="feed_back",
        grid=(count,),
        out_shape=jax.ShapeDtypeStruct((count, rows, 2 * units), jnp.bfloat16),
        in_specs=[
            per_sequence(rows, width),
            whole(*weights.shape),
            per_sequence(rows, 2 * units),
        ],
        out_specs=per_sequence(rows, 2 * units),
        compiler_params=pltpu.CompilerParams(vmem_limit_bytes=VMEM_LIMIT),
        cost_estimate=cost_of(18),
    )(grads, weights, product)


def adam_all(sets, factor):
    jobs = []
    for weight, _, _, pieces, widths in sets:
        rows = weight.shape[0]
        height = rows // TEAM if widths is None else max(CHUNK, rows // 4)
        jobs.append((height, rows // height, widths))
    count = sum(job[1] for job in jobs)
    total = len(sets)

    def kernel(*refs):
        inputs, factor, outputs = refs[: 4 * total], refs[4 * total], refs[4 * total + 1 : 8 * total + 1]
        held = refs[8 * total + 1 : 13 * total + 1]
        piece_sem, in_sem, out_sem = refs[13 * total + 1 :]
        scale = factor[0:1, 0:1]
        loads, stores = [], []
        for place in range(total):
            load = pltpu.make_async_copy(
                inputs[4 * place + 3], held[5 * place + 3], piece_sem.at[place]
            )
            load.start()
            loads.append(load)
        work, slot = [], 0
        for place, (height, steps, widths) in enumerate(jobs):
            for step in range(steps):
                at = pl.ds(step * height, height)
                arrive = []
                for kind in range(3):
                    copy = pltpu.make_async_copy(
                        inputs[4 * place + kind].at[at],
                        held[5 * place + kind].at[at],
                        in_sem.at[3 * slot + kind],
                    )
                    copy.start()
                    arrive.append(copy)
                work.append((place, step, at, slot, arrive))
                slot += 1
        for place, step, at, slot, arrive in work:
            height, _, widths = jobs[place]
            weight, moment, square, pieces, low = held[5 * place : 5 * place + 5]
            if step == 0:
                loads[place].wait()
            for copy in arrive:
                copy.wait()

            def update(rows, across, gradient):
                where = (rows, across)
                value, one, two = adam_update(
                    weight[where], gradient, moment[where], square[where], scale, weight_decay, learn_rate
                )
                weight[where], moment[where], square[where] = value, one, two
                low[where] = value.astype(jnp.bfloat16)

            if widths is None:
                update(at, slice(None), pieces[step].astype(jnp.float32).T)
            else:

                @pl.loop(0, height // CHUNK)
                def _(row):
                    rows = pl.ds(pl.multiple_of(step * height + row * CHUNK, CHUNK), CHUNK)
                    for member in range(TEAM):
                        first, inside = 0, 0
                        for width in widths:
                            share = width // TEAM
                            update(
                                rows,
                                pl.ds(first + member * share, share),
                                pieces[member, rows, pl.ds(inside, share)].astype(jnp.float32),
                            )
                            first += width
                            inside += share

            for kind, source in enumerate((weight, moment, square, low)):
                copy = pltpu.make_async_copy(
                    source.at[at], outputs[4 * place + kind].at[at], out_sem.at[4 * slot + kind]
                )
                copy.start()
                stores.append(copy)
        for copy in stores:
            copy.wait()

    args, shapes, scratch, moved = [], [], [], 0
    for weight, moment, square, pieces, _ in sets:
        args += [weight, moment, square, pieces]
        low = jax.ShapeDtypeStruct(weight.shape, jnp.bfloat16)
        shapes += [like(weight)] * 3 + [low]
        scratch += [pltpu.VMEM(each.shape, each.dtype) for each in (weight, moment, square, pieces, low)]
        moved += weight.size * 28
    outs = pl.pallas_call(
        kernel,
        name="adam_all",
        out_shape=tuple(shapes),
        in_specs=[anywhere()] * (4 * total) + [in_vmem()],
        out_specs=(anywhere(),) * (4 * total),
        scratch_shapes=scratch
        + [
            pltpu.SemaphoreType.DMA((total,)),
            pltpu.SemaphoreType.DMA((3 * count,)),
            pltpu.SemaphoreType.DMA((4 * count,)),
        ],
        compiler_params=pltpu.CompilerParams(vmem_limit_bytes=VMEM_LIMIT),
        cost_estimate=cost_of(moved / 3.4e6),
    )(*args, factor)
    return [outs[4 * place : 4 * place + 4] for place in range(total)]


def split_columns(values, widths):
    members = []
    for member in range(TEAM):
        start, parts = 0, []
        for width in widths:
            share = width // TEAM
            first = start + member * share
            parts.append(values[:, first : first + share])
            start += width
        members.append(jnp.concatenate(parts, axis=1))
    return jnp.stack(members)


def gather_outer(mixed):
    return lax.all_gather(mixed.reshape(-1, mixed.shape[2]), "outer", axis=0, tiled=True)


def team_pieces(summed):
    return summed.reshape(TEAM, -1, summed.shape[-1])


def sum_weight(gradient):
    return lax.psum_scatter(gradient, "outer", scatter_dimension=0, tiled=True)


def after(values, earlier):
    return lax.optimization_barrier((values, earlier))


def adam_update(weight, gradient, moment_one, moment_two, factor, decay_rate, rate_value):
    clipped = gradient * factor
    moment_one = beta_first * moment_one + (1.0 - beta_first) * clipped
    moment_two = beta_second * moment_two + (1.0 - beta_second) * clipped * clipped
    first_fixed = moment_one / (1.0 - beta_first**STEP)
    second_fixed = moment_two / (1.0 - beta_second**STEP)
    weight = weight - rate_value * (
        first_fixed / (jnp.sqrt(second_fixed) + adam_epsilon) + decay_rate * weight
    )
    return (weight, moment_one, moment_two)


def dot(left, right, contract):
    return lax.dot_general(
        left, right, ((contract[0], contract[1]), ((), ())), preferred_element_type=jnp.float32
    )


def times(left, right):
    return dot(left, right, ((1,), (0,)))


def times_across(left, right):
    return dot(left, right, ((1,), (1,)))


def over_rows(left, right):
    return dot(left, right, ((0,), (0,)))


def local(
    inputs,
    cotangent,
    lengths,
    owners,
    qkv_weight,
    out_weight,
    gate_up_weight,
    down_weight,
    norm_gains,
    qkv_moment,
    out_moment,
    gate_up_moment,
    down_moment,
    gains_moment,
    qkv_square,
    out_square,
    gate_up_square,
    down_square,
    gains_square,
):
    tp_count = lax.axis_size("tp")
    half_rows = inputs.shape[0]
    row_count = half_rows * tp_count
    heads = H // tp_count // TEAM
    hidden_units = FF // tp_count // TEAM
    qkv_widths = (H * HD // tp_count, KV * HD // tp_count, KV * HD // tp_count)
    out_widths = (H * HD // tp_count,)
    gate_up_widths = (FF // tp_count, FF // tp_count)
    down_widths = (FF // tp_count,)

    first_group = lax.axis_index("outer") * TEAM
    group_ids = first_group + jnp.arange(TEAM)
    group_length = jnp.sum(
        jnp.where(owners[None, :] == group_ids[:, None], lengths[None, :], 0), axis=1
    )
    own_group = lax.axis_index("near") * CORE + lax.axis_index("core")
    own_rows = lax.axis_index("tp") * half_rows + jnp.arange(half_rows)
    valid_rows = (own_rows < pick(group_length, own_group))[:, None]
    half_width = HD // 2
    frequency = rope_base ** (-(jnp.arange(half_width, dtype=jnp.float32) * 2.0 / HD))
    angles = jnp.arange(row_count, dtype=jnp.float32)[:, None] * frequency[None, :]
    cosine, sine = jnp.cos(angles), jnp.sin(angles)
    cos_full = jnp.concatenate([cosine, cosine], axis=1)
    sin_full = jnp.concatenate([-sine, sine], axis=1)
    attn_gain = norm_gains[:D]
    mlp_gain = norm_gains[D : 2 * D]
    head_gains = norm_gains[2 * D :].reshape(2, HD)

    first_pieces = jnp.concatenate(
        [
            split_columns(qkv_weight.astype(jnp.bfloat16), qkv_widths),
            split_columns(out_weight.astype(jnp.bfloat16).T, out_widths),
        ],
        axis=2,
    )
    gate_up_pieces = split_columns(gate_up_weight.astype(jnp.bfloat16), gate_up_widths)
    down_pieces = split_columns(down_weight.astype(jnp.bfloat16).T, down_widths)
    first_mixed = exchange(first_pieces, 6, "exchange_first")
    first_full = gather_outer(first_mixed)
    qkv_full = first_full[:, : (heads + 2) * HD]

    residual_in = inputs.astype(jnp.float32)
    normed_attn = residual_in * rms_scale(residual_in) * attn_gain
    grad_low = jnp.where(valid_rows, cotangent, jnp.zeros_like(cotangent))
    normed_attn, first_mixed, grad_low, down_pieces, cos_full, sin_full = (
        lax.optimization_barrier(
            (
                normed_attn.astype(jnp.bfloat16),
                first_mixed,
                grad_low,
                down_pieces,
                cos_full,
                sin_full,
            )
        )
    )
    normed_attn, gate_up_mixed = gather_rows(
        normed_attn, (gate_up_pieces,), 0, "gather_inputs"
    )
    gate_up_full = gather_outer(gate_up_mixed)
    early = half_rows * 3 // 5 // CHUNK * CHUNK
    projected, attended, logs, attn_branch, grad_all, down_mixed = attend(
        normed_attn.reshape(TEAM, row_count, D),
        first_full,
        grad_low,
        (down_pieces,),
        group_length,
        cos_full,
        sin_full,
        head_gains,
        heads,
        early,
        1,
    )
    down_full = gather_outer(down_mixed)
    attended = attended.reshape(-1, heads * HD)
    hidden, normed_mlp = branch_and_norm(attn_branch, inputs, mlp_gain, 2, "branch_and_norm")
    gate_up, activated, grad_all = feed(
        normed_mlp.reshape(TEAM, row_count, D), gate_up_full, grad_low, grad_all, early, 8
    )
    grad_down = over_rows(grad_all.reshape(-1, D), activated.reshape(-1, hidden_units))
    grad_all, grad_down = after(grad_all, grad_down.astype(jnp.bfloat16))
    down_sum = sum_weight(grad_down)
    grad_gate_up = feed_back(grad_all.reshape(TEAM, row_count, D), down_full, gate_up)
    grad_gate_up_weight = over_rows(normed_mlp, grad_gate_up.reshape(-1, 2 * hidden_units))
    grad_gate_up, grad_gate_up_weight, down_sum = lax.optimization_barrier(
        (grad_gate_up, grad_gate_up_weight.astype(jnp.bfloat16), down_sum)
    )
    gate_up_sum = sum_weight(grad_gate_up_weight)
    grad_hidden, grad_mlp_gain, grad_attn, mlp_part = feed_back_rest(
        grad_gate_up, gate_up_full, activated, down_full, hidden, grad_low, mlp_gain, 3, "feed_back_rest"
    )
    grad_out_weight = over_rows(grad_attn, attended).astype(jnp.bfloat16)
    grad_out_weight, gate_up_sum = after(grad_out_weight, gate_up_sum)
    out_sum = sum_weight(grad_out_weight)
    grad_projected, grad_head_gains, grad_normed_attn, output, down_mixed = attend_back(
        projected,
        grad_attn.reshape(TEAM, row_count, D),
        logs,
        first_full,
        mlp_part,
        hidden,
        (team_pieces(down_sum),),
        group_length,
        cos_full,
        sin_full,
        head_gains,
        heads,
        7,
    )
    grad_projected = grad_projected.reshape(-1, projected.shape[2])
    grad_qkv_weight = over_rows(normed_attn, grad_projected).astype(jnp.bfloat16)
    grad_qkv_weight, out_sum = after(grad_qkv_weight, out_sum)
    qkv_sum = sum_weight(grad_qkv_weight)
    input_grad, grad_attn_gain, gate_up_mixed, out_mixed = norm_back_last(
        grad_normed_attn,
        inputs,
        grad_hidden,
        attn_gain,
        (team_pieces(gate_up_sum), team_pieces(out_sum)),
        4,
        "norm_back_attn",
    )
    gain_part = jnp.concatenate(
        [grad_attn_gain, grad_mlp_gain, grad_head_gains.sum(axis=1).reshape(-1)]
    )
    square_part = sum(
        jnp.sum(jnp.square(member.astype(jnp.float32)))
        for member in (qkv_sum, out_sum, gate_up_sum, down_sum)
    )
    gain_count = gain_part.shape[0]
    packed = jnp.pad(gain_part, (0, -gain_count % PAD))
    packed = jnp.concatenate([packed, jnp.pad(square_part[None], (0, PAD - 1))])
    packed, norm_tile, factor_tile, qkv_mixed = total_everywhere(
        packed.reshape(-1, HD), team_pieces(qkv_sum), lax.axis_size("outer"), 5, "total_everywhere"
    )
    gain_grad = packed.reshape(-1)[:gain_count]
    grad_norm, factor = norm_tile[0, 0], factor_tile[0, 0]
    (
        (new_gate_up, new_gate_up_one, new_gate_up_two, gate_up_copy),
        (new_down, new_down_one, new_down_two, down_copy),
        (new_out, new_out_one, new_out_two, out_copy),
        (new_qkv, new_qkv_one, new_qkv_two, qkv_copy),
    ) = adam_all(
        [
            (gate_up_weight, gate_up_moment, gate_up_square, gate_up_mixed, gate_up_widths),
            (down_weight, down_moment, down_square, down_mixed, None),
            (out_weight, out_moment, out_square, out_mixed, None),
            (qkv_weight, qkv_moment, qkv_square, qkv_mixed, qkv_widths),
        ],
        factor_tile,
    )
    new_gains, new_gains_one, new_gains_two = adam_update(
        norm_gains, gain_grad, gains_moment, gains_square, factor, 0.0, gain_rate
    )
    return (
        output,
        input_grad,
        grad_norm,
        new_qkv,
        new_qkv_one,
        new_qkv_two,
        qkv_copy,
        new_out,
        new_out_one,
        new_out_two,
        out_copy,
        new_gate_up,
        new_gate_up_one,
        new_gate_up_two,
        gate_up_copy,
        new_down,
        new_down_one,
        new_down_two,
        down_copy,
        new_gains,
        new_gains_one,
        new_gains_two,
    )


def solution(mesh):
    fsdp_count, tp_count = mesh.shape["fsdp"], mesh.shape["tp"]
    cut = mesh.devices.reshape(fsdp_count // TEAM, NEAR, CORE, tp_count)
    cut_mesh = Mesh(cut, ("outer",) + LAYER)
    fsdp = ("outer", "near", "core")
    rows = P(fsdp + ("tp",), None)
    wide = P(fsdp, "tp")
    tall = P("tp", fsdp)
    weights = (wide, tall, wide, tall, P())
    return jax.shard_map(
        local,
        mesh=cut_mesh,
        in_specs=(rows, rows, P(), P()) + weights * 3,
        out_specs=(rows, rows, P()) + (wide,) * 4 + (tall,) * 4 + (wide,) * 4 + (tall,) * 4 + (P(),) * 3,
        check_vma=False,
    )
```

```python
import jax
import jax.numpy as jnp
from jax import lax
from jax.experimental import pallas as pl
from jax.experimental.pallas import tpu as pltpu
from jax.sharding import Mesh, PartitionSpec as P

D = 2048
H = 16
KV = 8
HD = 128
FF = 6144
STEP = 10


norm_epsilon = 1e-06
rope_base = 1000000.0
clip_norm = 1.0
learn_rate = 0.04
gain_rate = 0.8
beta_first = 0.9
beta_second = 0.999
adam_epsilon = 1e-08
weight_decay = 0.1
masked_score = -1e30

NEAR = 2
CORE = 2
TEAM = NEAR * CORE
LAYER = ("near", "core", "tp")
BLOCK = 128
PAD = 8 * 128


def rms_scale(values):
    return lax.rsqrt(jnp.mean(values * values, axis=-1, keepdims=True) + norm_epsilon)


def swish_product(gate_part, up_part):
    return jax.nn.silu(gate_part) * up_part


def pick(values, index):
    return lax.dynamic_index_in_dim(values, index, 0, keepdims=False)


MESH_ID = pl.DeviceIdType.MESH
VMEM_LIMIT = 60 * 1024 * 1024
CHUNK = 16
GATHER_COPIES = 13
SUM_COPIES = 10
NEIGHBOURS = ((1, 0, 0), (0, 1, 0), (0, 0, 1))
MATES = ((0, 1, 0), (1, 0, 0), (1, 1, 0))
EVERYONE_NEAR = NEIGHBOURS + ((1, 1, 0),)


def spots():
    return tuple(lax.axis_index(name) for name in LAYER)


def flipped(near_flip, core_flip, tp_flip):
    return {
        name: 1 - spot if flip else spot
        for name, spot, flip in zip(LAYER, spots(), (near_flip, core_flip, tp_flip))
    }


def greet(flips):
    barrier = pltpu.get_barrier_semaphore()
    for flip in flips:
        pl.semaphore_signal(barrier, inc=1, device_id=flipped(*flip), device_id_type=MESH_ID)
    pl.semaphore_wait(barrier, len(flips))


def link(source, target, send_sem, recv_sem, flip):
    return pltpu.make_async_remote_copy(
        src_ref=source,
        dst_ref=target,
        send_sem=send_sem,
        recv_sem=recv_sem,
        device_id=flipped(*flip),
        device_id_type=MESH_ID,
    )


TO_NEAR, TO_CORE, TO_TP = NEIGHBOURS


def plan_exchange(pieces, out, send, recv, own_sem):
    near, core, _ = spots()
    own = near * CORE + core
    copies = []
    for number, flip in enumerate(MATES):
        there = (1 - near if flip[0] else near) * CORE + (1 - core if flip[1] else core)
        copies.append(
            link(pieces.at[there], out.at[own], send.at[number], recv.at[number], flip)
        )
    copies.append(pltpu.make_async_copy(pieces.at[own], out.at[own], own_sem))
    return copies


def exchange_scratch():
    return [
        pltpu.SemaphoreType.DMA((len(MATES),)),
        pltpu.SemaphoreType.DMA((len(MATES),)),
        pltpu.SemaphoreType.DMA,
    ]


def crossing(pieces, width):
    return sum(2 * piece.shape[1] * piece.shape[2] for piece in pieces) // width


def plan_exchanges(pieces, mixed, sems):
    copies = []
    for place, (piece, result) in enumerate(zip(pieces, mixed)):
        copies += plan_exchange(piece, result, *sems[3 * place : 3 * place + 3])
    return copies


def plan_gather(own, out, send, recv, own_sem, cut, base=0, rows=None):
    near, core, tp = spots()
    rows = own.shape[0] if rows is None else rows
    low, high = pl.ds(base, cut), pl.ds(base + cut, rows - cut)
    all_rows = pl.ds(base, rows)

    def make(number, source, target, flip):
        return link(source, target, send.at[number], recv.at[number], flip)

    def give(number, part, flip):
        return make(number, own.at[part], out.at[near, core, tp, part], flip)

    def relay(number, where_near, where_tp, part, flip):
        ref = out.at[where_near, core, where_tp, part]
        return make(number, ref, ref, flip)

    keep = pltpu.make_async_copy(own.at[all_rows], out.at[near, core, tp, all_rows], own_sem)
    twin_own = give(4, all_rows, TO_CORE)
    near_high = give(1, high, TO_NEAR)
    tp_high = give(2, high, TO_TP)
    far_high = relay(7, 1 - near, tp, high, TO_TP)
    twin_beside = relay(8, 1 - near, tp, high, TO_CORE)
    twin_across = relay(9, near, 1 - tp, high, TO_CORE)
    twin_far = relay(12, 1 - near, 1 - tp, high, TO_CORE)
    twins = [twin_own, twin_beside, twin_across, twin_far]
    ways = [near_high, tp_high, far_high]
    if cut:
        tp_low = give(0, low, TO_TP)
        near_low = give(3, low, TO_NEAR)
        far_low = relay(5, near, 1 - tp, low, TO_NEAR)
        twin_across_low = relay(6, near, 1 - tp, low, TO_CORE)
        twin_beside_low = relay(10, 1 - near, tp, low, TO_CORE)
        twin_far_low = relay(11, 1 - near, 1 - tp, low, TO_CORE)
        twins += [twin_across_low, twin_beside_low, twin_far_low]
        ways += [tp_low, near_low, far_low]

    def begin():
        if cut:
            tp_low.start()
        near_high.start()
        tp_high.start()
        if cut:
            near_low.start()
        twin_own.start()
        keep.start()

    def middle():
        if cut:
            tp_low.wait_recv()
            far_low.start()
            twin_across_low.start()
        near_high.wait_recv()
        far_high.start()
        twin_beside.start()

    def later():
        tp_high.wait_recv()
        twin_across.start()
        if cut:
            near_low.wait_recv()
            twin_beside_low.start()

    def finish():
        if cut:
            far_low.wait_recv()
            twin_far_low.start()
        far_high.wait_recv()
        twin_far.start()
        for copy in twins:
            copy.wait_recv()
        for copy in ways + twins:
            copy.wait_send()
        keep.wait()

    return [begin, middle, later, finish]


def balanced(rows, beside):
    return max(0, (rows - beside) // 2 // CHUNK * CHUNK)


def gather_scratch():
    return [
        pltpu.SemaphoreType.DMA((GATHER_COPIES,)),
        pltpu.SemaphoreType.DMA((GATHER_COPIES,)),
        pltpu.SemaphoreType.DMA,
    ]


def add_rows(target, start, count, *sources):
    @pl.loop(0, count // CHUNK)
    def _(step):
        at = pl.ds(pl.multiple_of(start + step * CHUNK, CHUNK), CHUNK)
        total = None
        for source, shift in sources:
            where = pl.ds(pl.multiple_of(start - shift + step * CHUNK, CHUNK), CHUNK)
            value = source[where].astype(jnp.float32)
            total = value if total is None else total + value
        target[at] = total.astype(target.dtype)


def plan_sum(outgoing, mine, keep, total, scratch, cut):
    theirs, way_near, way_tp, from_tp, from_near, send, recv = scratch
    rows = total.shape[0]
    low, high = pl.ds(0, cut), pl.ds(cut, rows - cut)

    def make(number, source, target, flip):
        return link(source, target, send.at[number], recv.at[number], flip)

    twin = [make(number, outgoing[number], theirs.at[number], TO_CORE) for number in range(4)]
    far, to_tp, to_near, own = mine
    far_high = make(5, far.at[high], way_tp, TO_TP)
    tp_high = make(6, to_tp.at[high], from_tp.at[high], TO_TP)
    near_high = make(9, to_near.at[high], from_near.at[high], TO_NEAR)
    ways = [far_high, tp_high, near_high]
    if cut:
        far_low = make(4, far.at[low], way_near, TO_NEAR)
        near_low = make(7, to_near.at[low], from_near.at[low], TO_NEAR)
        tp_low = make(8, to_tp.at[low], from_tp.at[low], TO_TP)
        ways += [near_low, tp_low]

    def ready(number):
        if keep:
            keep[number].wait()
        twin[number].wait_recv()

    def both(number):
        return (mine[number], 0), (theirs.at[number], 0)

    def begin(numbers=range(4)):
        for number in numbers:
            twin[number].start()
            if keep:
                keep[number].start()

    def send_far():
        ready(0)
        if cut:
            add_rows(far, 0, cut, *both(0))
            far_low.start()
        add_rows(far, cut, rows - cut, *both(0))
        far_high.start()

    def send_tp():
        ready(1)
        add_rows(to_tp, cut, rows - cut, *both(1))
        tp_high.start()

    def send_near():
        ready(2)
        if cut:
            add_rows(to_near, 0, cut, *both(2))
            near_low.start()

    def first():
        send_far()
        send_tp()
        send_near()

    def second():
        if cut:
            far_low.wait_recv()
            add_rows(to_tp, 0, cut, *both(1), (way_near, 0))
            tp_low.start()
        far_high.wait_recv()
        add_rows(to_near, cut, rows - cut, *both(2), (way_tp, cut))
        near_high.start()
        ready(3)
        add_rows(total, 0, rows, *both(3))

    def finish():
        for copy in ways[1:]:
            copy.wait_recv()
        for copy in twin + ways + ([far_low] if cut else []):
            copy.wait_send()

    return [begin, first, second, finish], (send_far, send_tp, send_near)


def plan_sum_of(part, total, scratch, cut):
    mine, local_sem, *scratch = scratch
    near, core, tp = spots()
    order = [(1 - near, 1 - tp), (near, 1 - tp), (1 - near, tp), (near, tp)]
    outgoing = [part.at[a, 1 - core, b] for a, b in order]
    keep = [
        pltpu.make_async_copy(part.at[a, core, b], mine.at[number], local_sem.at[number])
        for number, (a, b) in enumerate(order)
    ]
    blocks = [mine.at[number] for number in range(4)]
    steps, _ = plan_sum(outgoing, blocks, keep, total, scratch, cut)
    return steps, scratch[3], scratch[4]


def sum_scratch(rows, width, cut, fetched=True):
    low = jnp.bfloat16
    fetch = [pltpu.VMEM((4, rows, width), low), pltpu.SemaphoreType.DMA((4,))]
    return (fetch if fetched else []) + [
        pltpu.VMEM((4, rows, width), low),
        pltpu.VMEM((max(cut, CHUNK), width), low),
        pltpu.VMEM((rows - cut, width), low),
        pltpu.VMEM((rows, width), low),
        pltpu.VMEM((rows, width), low),
        pltpu.SemaphoreType.DMA((SUM_COPIES,)),
        pltpu.SemaphoreType.DMA((SUM_COPIES,)),
    ]


SUM_SCRATCH = 9
COST_SHARE = 1e5


def params(number):
    return pltpu.CompilerParams(
        collective_id=number, has_side_effects=True, vmem_limit_bytes=VMEM_LIMIT
    )


def cost_of(microseconds):
    return pl.CostEstimate(
        flops=0, bytes_accessed=int(microseconds * COST_SHARE), transcendentals=0
    )


def in_vmem():
    return pl.BlockSpec(memory_space=pltpu.VMEM)


def anywhere():
    return pl.BlockSpec(memory_space=pl.ANY)


def like(array):
    return jax.ShapeDtypeStruct(array.shape, array.dtype)


def layer_rows(rows, width):
    return jax.ShapeDtypeStruct((NEAR, CORE, 2, rows, width), jnp.bfloat16)


def exchange(pieces, number, name):
    def kernel(pieces, out, *sems):
        greet(MATES)
        copies = plan_exchange(pieces, out, *sems)
        for copy in copies:
            copy.start()
        for copy in copies:
            copy.wait()

    return pl.pallas_call(
        kernel,
        name=name,
        out_shape=like(pieces),
        in_specs=[anywhere()],
        out_specs=anywhere(),
        scratch_shapes=exchange_scratch(),
        compiler_params=params(number),
        cost_estimate=cost_of(12),
    )(pieces)


def gather_rows(values, extra, number, name):
    rows, width = values.shape
    extras = len(extra)
    cut = balanced(rows, crossing(extra, width))

    def kernel(own, *rest):
        pieces, out, mixed = rest[:extras], rest[extras], rest[extras + 1 : 2 * extras + 1]
        sems = rest[2 * extras + 1 :]
        begin, *steps = plan_gather(own, out, *sems[:3], cut=cut)
        copies = plan_exchanges(pieces, mixed, sems[3:])
        greet(EVERYONE_NEAR)
        begin()
        for copy in copies:
            copy.start()
        for step in steps:
            step()
        for copy in copies:
            copy.wait()

    outs = pl.pallas_call(
        kernel,
        name=name,
        out_shape=(layer_rows(rows, width),) + tuple(like(piece) for piece in extra),
        in_specs=[anywhere()] * (1 + extras),
        out_specs=(anywhere(),) * (1 + extras),
        scratch_shapes=gather_scratch() + exchange_scratch() * extras,
        compiler_params=params(number),
        cost_estimate=cost_of(60),
    )(values, *extra)
    return (outs[0].reshape(-1, width),) + tuple(outs[1:])


def row_loop(rows, body):
    @pl.loop(0, rows // CHUNK)
    def _(step):
        body(pl.ds(pl.multiple_of(step * CHUNK, CHUNK), CHUNK))


def spread(part, rows):
    return part.reshape(NEAR, CORE, 2, rows, part.shape[-1])


def read(ref, at):
    return ref[at].astype(jnp.float32)


def branch_and_norm(part, residual, gain, number, name):
    rows, width = residual.shape
    cut = rows // 2

    def kernel(part, residual, gain, hidden, out, *scratch):
        normed, sems = scratch[SUM_SCRATCH], scratch[SUM_SCRATCH + 1 :]
        steps, from_tp, from_near = plan_sum_of(part, hidden, scratch[:SUM_SCRATCH], cut)
        onward = plan_gather(normed, out, *sems, cut=cut)
        greet(NEIGHBOURS)
        for step in steps:
            step()

        def finish(at):
            value = hidden[at] + read(from_tp, at) + read(from_near, at)
            value = read(residual, at) + value
            hidden[at] = value
            normed[at] = (value * rms_scale(value) * gain[...]).astype(jnp.bfloat16)

        row_loop(rows, finish)
        for step in onward:
            step()

    hidden, full = pl.pallas_call(
        kernel,
        name=name,
        out_shape=(jax.ShapeDtypeStruct((rows, width), jnp.float32), layer_rows(rows, width)),
        in_specs=[anywhere(), in_vmem(), in_vmem()],
        out_specs=(in_vmem(), anywhere()),
        scratch_shapes=sum_scratch(rows, width, cut)
        + [pltpu.VMEM((rows, width), jnp.bfloat16)]
        + gather_scratch(),
        compiler_params=params(number),
        cost_estimate=cost_of(95),
    )(spread(part, rows), residual, gain.reshape(1, width))
    return hidden, full.reshape(-1, width)


def norm_back(value, gain, grad):
    scale = rms_scale(value)
    scaled = grad * gain
    inner = jnp.mean(scaled * value, axis=-1, keepdims=True)
    return scale * scaled - value * (scale * scale * scale * inner), grad * value * scale


def sequence_order():
    near, core, _ = spots()
    return [
        (near if place >= 2 else 1 - near) * CORE + (core if place % 2 else 1 - core)
        for place in range(TEAM)
    ]


def halves_times(left, weights, target, rows):
    for start in range(0, weights.shape[0], 512):
        at = pl.ds(start, 512)
        product = lax.dot_general(
            left, weights[at, :], (((1,), (1,)), ((), ())), preferred_element_type=jnp.float32
        ).astype(target.dtype)
        target[0, :, at] = product[:rows]
        target[1, :, at] = product[rows:]


def feed_back_rest(
    grad_gate_up, weights, active, down, values, upstream, gain, number, name
):
    rows, width = values.shape
    count, both_rows, units = grad_gate_up.shape
    cut = rows // 2

    def kernel(
        grad, weights, active, down, values, upstream, gain, result, gain_grad, out, branch, *scratch
    ):
        (grad_v, weights_v, active_v, down_v, values_v, upstream_v, parts, total, low), rest = (
            scratch[:9],
            scratch[9:],
        )
        (load_sem, store_sem), rest = rest[:2], rest[2:]
        sums, sems = rest[:7], rest[7:]
        from_tp, from_near = sums[3], sums[4]
        near, core, tp = spots()
        members = sequence_order()
        outgoing = [parts.at[place, half] for place, half in ((0, 1 - tp), (2, 1 - tp), (0, tp), (2, tp))]
        mine = [parts.at[place, half] for place, half in ((1, 1 - tp), (3, 1 - tp), (1, tp), (3, tp))]
        steps, (send_far, send_tp, send_near) = plan_sum(outgoing, mine, (), total, sums, cut)
        onward = plan_gather(low, out, *sems, cut=cut)
        fetch = [
            pltpu.make_async_copy(grad.at[member], grad_v.at[place % 2], load_sem.at[place])
            for place, member in enumerate(members)
        ]
        fetch += [
            pltpu.make_async_copy(source, target, load_sem.at[4 + place])
            for place, (source, target) in enumerate(
                (
                    (weights, weights_v),
                    (values, values_v),
                    (upstream, upstream_v),
                    (active, active_v),
                    (down, down_v),
                )
            )
        ]
        for place in (0, 4, 1, 5, 6, 7, 8):
            fetch[place].start()
        greet(NEIGHBOURS)
        fetch[4].wait()
        for place in range(count):
            fetch[place].wait()
            halves_times(grad_v[place % 2], weights_v, parts.at[place], rows)
            if place + 2 < count:
                fetch[place + 2].start()
            if place == 0:
                steps[0]((0, 2))
            elif place == 1:
                send_far()
                send_near()
            elif place == 2:
                steps[0]((1, 3))
        send_tp()
        steps[2]()
        fetch[5].wait()
        fetch[6].wait()
        gain_grad[...] = jnp.zeros_like(gain_grad)
        steps[3]()

        def finish(at):
            grad = total[at] + read(from_tp, at) + read(from_near, at)
            back, by_gain = norm_back(values_v[at], gain[...], grad)
            gain_grad[...] += by_gain.reshape(CHUNK // 8, 8, width).sum(axis=0)
            value = read(upstream_v, at) + back
            total[at] = value
            low[at] = value.astype(jnp.bfloat16)

        row_loop(rows, finish)
        onward[0]()
        stores = [pltpu.make_async_copy(total, result, store_sem.at[count])]
        stores[0].start()
        fetch[7].wait()
        fetch[8].wait()
        for place in range(count):
            halves_times(active_v[place], down_v, parts.at[place], rows)
            store = pltpu.make_async_copy(parts.at[place], branch.at[place], store_sem.at[place])
            store.start()
            stores.append(store)
            if place == 1:
                onward[1]()
        onward[2]()
        onward[3]()
        for store in stores:
            store.wait()

    low_type = jnp.bfloat16
    result, gain_grad, full, branch = pl.pallas_call(
        kernel,
        name=name,
        out_shape=(
            jax.ShapeDtypeStruct((rows, width), jnp.float32),
            jax.ShapeDtypeStruct((8, width), jnp.float32),
            layer_rows(rows, width),
            jax.ShapeDtypeStruct((count, 2, rows, width), low_type),
        ),
        in_specs=[anywhere()] * 6 + [in_vmem()],
        out_specs=(anywhere(), in_vmem(), anywhere(), anywhere()),
        scratch_shapes=[
            pltpu.VMEM((2, both_rows, units), low_type),
            pltpu.VMEM(weights.shape, low_type),
            pltpu.VMEM(active.shape, low_type),
            pltpu.VMEM(down.shape, low_type),
            pltpu.VMEM((rows, width), values.dtype),
            pltpu.VMEM((rows, width), upstream.dtype),
            pltpu.VMEM((count, 2, rows, width), low_type),
            pltpu.VMEM((rows, width), jnp.float32),
            pltpu.VMEM((rows, width), low_type),
            pltpu.SemaphoreType.DMA((9,)),
            pltpu.SemaphoreType.DMA((count + 1,)),
        ]
        + sum_scratch(rows, width, cut, fetched=False)
        + gather_scratch(),
        compiler_params=params(number),
        cost_estimate=cost_of(105),
    )(grad_gate_up, weights, active, down, values, upstream, gain.reshape(1, width))
    return result, gain_grad.sum(axis=0), full.reshape(-1, width), branch.reshape(-1, width)


def norm_back_last(part, values, upstream, gain, extra, number, name):
    rows, width = values.shape
    extras = len(extra)
    cut = balanced(rows, crossing(extra, width))

    def kernel(part, values, upstream, gain, *rest):
        pieces, (result, gain_grad) = rest[:extras], rest[extras : extras + 2]
        mixed, rest = rest[extras + 2 : 2 * extras + 2], rest[2 * extras + 2 :]
        total, sems = rest[SUM_SCRATCH], rest[SUM_SCRATCH + 1 :]
        steps, from_tp, from_near = plan_sum_of(part, total, rest[:SUM_SCRATCH], cut)
        copies = plan_exchanges(pieces, mixed, sems)
        greet(EVERYONE_NEAR)
        steps[0]()
        for copy in copies:
            copy.start()
        for step in steps[1:]:
            step()
        gain_grad[...] = jnp.zeros_like(gain_grad)

        def finish(at):
            grad = total[at] + read(from_tp, at) + read(from_near, at)
            back, by_gain = norm_back(read(values, at), gain[...], grad)
            gain_grad[...] += by_gain.reshape(CHUNK // 8, 8, width).sum(axis=0)
            result[at] = (read(upstream, at) + back).astype(jnp.bfloat16)

        row_loop(rows, finish)
        for copy in copies:
            copy.wait()

    outs = pl.pallas_call(
        kernel,
        name=name,
        out_shape=(
            jax.ShapeDtypeStruct((rows, width), jnp.bfloat16),
            jax.ShapeDtypeStruct((8, width), jnp.float32),
        )
        + tuple(like(piece) for piece in extra),
        in_specs=[anywhere()] + [in_vmem()] * 3 + [anywhere()] * extras,
        out_specs=(in_vmem(), in_vmem()) + (anywhere(),) * extras,
        scratch_shapes=sum_scratch(rows, width, cut)
        + [pltpu.VMEM((rows, width), jnp.float32)]
        + exchange_scratch() * extras,
        compiler_params=params(number),
        cost_estimate=cost_of(65),
    )(spread(part, rows), values, upstream, gain.reshape(1, width), *extra)
    return outs


def total_everywhere(values, first, pieces, outer_count, number, name):
    shape = values.shape
    width = first.shape[1]

    def kernel(values, first, square_of, pieces, out, norm, factor, mixed, layer, outers, send, recv, *sems):
        near, core, tp = spots()
        outer = lax.axis_index("outer")
        partners = [
            flipped(a, b, c)
            for a in range(NEAR)
            for b in range(CORE)
            for c in range(2)
            if a + b + c
        ]
        partners += [{"outer": (outer + step) % outer_count} for step in range(1, outer_count)]
        barrier = pltpu.get_barrier_semaphore()
        for partner in partners:
            pl.semaphore_signal(barrier, inc=1, device_id=partner, device_id_type=MESH_ID)
        pl.semaphore_wait(barrier, len(partners))

        def share(slots, mine, first, count):
            copies = []
            for number in range(first, first + count):
                copy = pltpu.make_async_remote_copy(
                    src_ref=slots.at[mine],
                    dst_ref=slots.at[mine],
                    send_sem=send.at[number],
                    recv_sem=recv.at[number],
                    device_id=partners[number],
                    device_id_type=MESH_ID,
                )
                copy.start()
                copies.append(copy)
            return copies

        mine = near * (CORE * 2) + core * 2 + tp
        row = lax.broadcasted_iota(jnp.int32, shape, 0)
        column = lax.broadcasted_iota(jnp.int32, shape, 1)
        flat = square_of[...].astype(jnp.float32)
        squares = jnp.sum(flat * flat, keepdims=True)
        squares = jnp.where((row == shape[0] - 8) & (column == 0), squares, 0.0)
        layer[mine] = values[...] + squares
        sums = jnp.sum(first[...], axis=0, keepdims=True)
        for place in range(width // HD):
            layer[mine, place : place + 1] = sums[:, place * HD : (place + 1) * HD]
        copies = share(layer, mine, 0, 7)
        others = plan_exchange(pieces, mixed, *sems)
        for copy in others:
            copy.start()
        for copy in copies:
            copy.wait()
        total = layer[0]
        for slot in range(1, 8):
            total = total + layer[slot]
        outers[outer] = total
        for copy in share(outers, outer, 7, outer_count - 1):
            copy.wait()
        total = outers[0]
        for slot in range(1, outer_count):
            total = total + outers[slot]
        out[...] = total
        squares = jnp.sum(jnp.where(row < shape[0] - 8, total * total, total), keepdims=True)
        root = jnp.sqrt(squares)
        norm[...] = jnp.broadcast_to(root, norm.shape)
        factor[...] = jnp.broadcast_to(
            jnp.minimum(1.0, clip_norm / (root + 1e-06)), factor.shape
        )
        for copy in others:
            copy.wait()

    tile = jax.ShapeDtypeStruct((8, HD), jnp.float32)
    return pl.pallas_call(
        kernel,
        name=name,
        out_shape=(jax.ShapeDtypeStruct(shape, jnp.float32), tile, tile, like(pieces)),
        in_specs=[in_vmem(), in_vmem(), in_vmem(), anywhere()],
        out_specs=(in_vmem(), in_vmem(), in_vmem(), anywhere()),
        scratch_shapes=[
            pltpu.VMEM((8,) + shape, jnp.float32),
            pltpu.VMEM((outer_count,) + shape, jnp.float32),
            pltpu.SemaphoreType.DMA((6 + outer_count,)),
            pltpu.SemaphoreType.DMA((6 + outer_count,)),
        ]
        + exchange_scratch(),
        compiler_params=params(number),
    )(values, first, pieces.reshape(-1, pieces.shape[2]), pieces)


def head_scale(raw, gain, cos_full, sin_full):
    normed = raw * rms_scale(raw) * gain
    return (normed * cos_full + pltpu.roll(normed, HD // 2, 1) * sin_full).astype(jnp.bfloat16)


def head_back(raw, gain, grad, cos_full, sin_full):
    grad = grad * cos_full - pltpu.roll(grad, HD // 2, 1) * sin_full
    return norm_back(raw, gain, grad)


def columns(index):
    return pl.ds(index * HD, HD)


def head_inputs(proj, gains, cos_ref, sin_ref, queries, keys, values, heads):
    for head in range(heads):
        queries[head] = head_scale(
            proj[0, :, columns(head)], gains[0:1, :], cos_ref[...], sin_ref[...]
        )
    keys[...] = head_scale(
        proj[0, :, columns(heads)], gains[1:2, :], cos_ref[...], sin_ref[...]
    )
    values[...] = proj[0, :, columns(heads + 1)].astype(jnp.bfloat16)


def masked_scores(stacked, keys, step, length):
    scores = lax.dot_general(
        stacked, keys, (((1,), (1,)), ((), ())), preferred_element_type=jnp.float32
    ) * (HD ** (-0.5))
    row = lax.broadcasted_iota(jnp.int32, scores.shape, 0) % BLOCK + step * BLOCK
    column = lax.broadcasted_iota(jnp.int32, scores.shape, 1)
    return jnp.where((column <= row) & (column < length), scores, masked_score)


def stack_heads(ref, at, heads):
    return jnp.concatenate([ref[head, at] for head in range(heads)], axis=0)


def per_sequence(*shape):
    return pl.BlockSpec((1,) + shape, lambda s: (s,) + (0,) * len(shape))


def whole(*shape):
    return pl.BlockSpec(shape, lambda s: (0,) * len(shape), pipeline_mode=pl.Buffered(1))


def across_columns(left, weights, first, width, out):
    total = weights.shape[0]
    for start in range(0, total, 512):
        at = pl.ds(start, 512)
        out[0, :, at] = lax.dot_general(
            left,
            weights[at, first : first + width],
            (((1,), (1,)), ((), ())),
            preferred_element_type=jnp.float32,
        ).astype(out.dtype)


def attend(normed, weights, cotangent, extra, group_length, cos_full, sin_full, gains, heads, early, number):
    count, rows, width = normed.shape
    wide = (heads + 2) * HD
    extras = len(extra)
    own_rows = cotangent.shape[0]
    cut = balanced(early, crossing(extra, width))

    def kernel(lengths, normed, weights, cos_ref, sin_ref, gains, own, *rest):
        pieces, rest = rest[:extras], rest[extras:]
        (proj, out, logs, branch, gathered), rest = rest[:5], rest[5:]
        mixed, (queries, keys, values), sems = rest[:extras], rest[extras : extras + 3], rest[extras + 3 :]
        sequence = pl.program_id(0)
        steps = plan_gather(own, gathered, *sems[:3], cut=cut, rows=early)
        copies = plan_exchanges(pieces, mixed, sems[3:])

        @pl.when(sequence == 0)
        def _():
            greet(EVERYONE_NEAR)
            steps[0]()
            for copy in copies:
                copy.start()

        length = lengths[sequence]
        proj[0] = jnp.dot(
            normed[0], weights[:, :wide], preferred_element_type=jnp.float32
        )
        head_inputs(proj, gains, cos_ref, sin_ref, queries, keys, values, heads)
        lane = lax.broadcasted_iota(jnp.int32, (BLOCK, HD), 1)
        for step in range(rows // BLOCK):
            at = pl.ds(step * BLOCK, BLOCK)
            seen = pl.ds(0, (step + 1) * BLOCK)
            scores = masked_scores(stack_heads(queries, at, heads), keys[seen], step, length)
            top = jnp.max(scores, axis=-1, keepdims=True)
            exponent = jnp.exp(scores - top)
            total = jnp.sum(exponent, axis=-1, keepdims=True)
            probs = (exponent / total).astype(jnp.bfloat16)
            mixed_values = jnp.dot(probs, values[seen], preferred_element_type=jnp.float32)
            log_total = top + jnp.log(total)
            kept = jnp.zeros((BLOCK, HD), jnp.float32)
            for head in range(heads):
                mine = slice(head * BLOCK, (head + 1) * BLOCK)
                out[0, at, columns(head)] = mixed_values[mine].astype(jnp.bfloat16)
                kept = jnp.where(lane == head, log_total[mine], kept)
            logs[0, at] = kept
        across_columns(out[0], weights, wide, heads * HD, branch)

        @pl.when(sequence == 1)
        def _():
            steps[1]()

        @pl.when(sequence == 2)
        def _():
            steps[2]()

        @pl.when(sequence == count - 1)
        def _():
            steps[3]()
            for copy in copies:
                copy.wait()

    outs = pl.pallas_call(
        kernel,
        name="attend",
        grid=(count,),
        out_shape=(
            jax.ShapeDtypeStruct((count, rows, wide), jnp.float32),
            jax.ShapeDtypeStruct((count, rows, heads * HD), jnp.bfloat16),
            jax.ShapeDtypeStruct((count, rows, HD), jnp.float32),
            jax.ShapeDtypeStruct((count, rows, width), jnp.bfloat16),
            layer_rows(own_rows, width),
        )
        + tuple(like(piece) for piece in extra),
        in_specs=[
            pl.BlockSpec(memory_space=pltpu.SMEM),
            per_sequence(rows, width),
            whole(width, wide + heads * HD),
            whole(rows, HD),
            whole(rows, HD),
            whole(2, HD),
            anywhere(),
        ]
        + [anywhere()] * extras,
        out_specs=(
            per_sequence(rows, wide),
            per_sequence(rows, heads * HD),
            per_sequence(rows, HD),
            per_sequence(rows, width),
            anywhere(),
        )
        + (anywhere(),) * extras,
        scratch_shapes=[
            pltpu.VMEM((heads, rows, HD), jnp.bfloat16),
            pltpu.VMEM((rows, HD), jnp.bfloat16),
            pltpu.VMEM((rows, HD), jnp.bfloat16),
        ]
        + gather_scratch()
        + exchange_scratch() * extras,
        compiler_params=params(number),
        cost_estimate=cost_of(50),
    )(group_length, normed, weights, cos_full, sin_full, gains, cotangent, *extra)
    return outs


def team_split(width, outer_count):
    split = TEAM if width // outer_count % (TEAM * HD) == 0 else 1
    return split, width // outer_count // split


def attend_back(
    projected,
    normed,
    attended,
    grad_attn,
    logs,
    weights,
    part,
    hidden,
    extra,
    outer_count,
    group_length,
    cos_full,
    sin_full,
    gains,
    heads,
    number,
):
    count, rows, wide = projected.shape
    own_rows, width = hidden.shape
    extras = len(extra)
    cut = balanced(own_rows, crossing(extra, width))

    every = wide + heads * HD
    split, share = team_split(width, outer_count)

    def kernel(
        lengths, proj, normed, attended, grad, logs, weights, cos_ref, sin_ref, gains, part, hidden, *rest
    ):
        pieces, rest = rest[:extras], rest[extras:]
        (out, gain_grad, back_part, output, grad_weights), rest = rest[:5], rest[5:]
        mixed, rest = rest[:extras], rest[extras:]
        (queries, keys, values, grad_att, grad_q, grad_k, grad_v, summed), rest = rest[:8], rest[8:]
        (total, held, held_sem), rest = rest[:3], rest[3:]
        sequence = pl.program_id(0)
        steps, from_tp, from_near = plan_sum_of(part, total, rest[:SUM_SCRATCH], cut)
        copies = plan_exchanges(pieces, mixed, rest[SUM_SCRATCH:])
        fetch = pltpu.make_async_copy(hidden, held, held_sem)

        @pl.when(sequence == 0)
        def _():
            greet(EVERYONE_NEAR)
            steps[0]()
            for copy in copies:
                copy.start()
            fetch.start()
            gain_grad[...] = jnp.zeros_like(gain_grad)
            summed[...] = jnp.zeros_like(summed)

        length = lengths[sequence]
        grad_att[...] = jnp.dot(
            grad[0], weights[:, wide:], preferred_element_type=jnp.float32
        ).astype(jnp.bfloat16)
        head_inputs(proj, gains, cos_ref, sin_ref, queries, keys, values, heads)
        grad_k[...] = jnp.zeros_like(grad_k)
        grad_v[...] = jnp.zeros_like(grad_v)

        @pl.when(sequence == 0)
        def _():
            steps[1]()

        for step in range(rows // BLOCK):
            at = pl.ds(step * BLOCK, BLOCK)
            seen = pl.ds(0, (step + 1) * BLOCK)
            stacked = stack_heads(queries, at, heads)
            above = jnp.concatenate([grad_att[at, columns(head)] for head in range(heads)], axis=0)
            log_total = jnp.concatenate(
                [logs[0, at, head : head + 1] for head in range(heads)], axis=0
            )
            probs = jnp.exp(masked_scores(stacked, keys[seen], step, length) - log_total)
            grad_probs = lax.dot_general(
                above, values[seen], (((1,), (1,)), ((), ())), preferred_element_type=jnp.float32
            )
            inner = jnp.sum(probs * grad_probs, axis=-1, keepdims=True)
            grad_scores = (probs * (grad_probs - inner)).astype(jnp.bfloat16)
            by_query = jnp.dot(grad_scores, keys[seen], preferred_element_type=jnp.float32)
            for head in range(heads):
                grad_q[head, at] = by_query[head * BLOCK : (head + 1) * BLOCK] * (HD ** (-0.5))
            grad_k[seen] += lax.dot_general(
                grad_scores, stacked, (((0,), (0,)), ((), ())), preferred_element_type=jnp.float32
            )
            grad_v[seen] += lax.dot_general(
                probs.astype(jnp.bfloat16),
                above,
                (((0,), (0,)), ((), ())),
                preferred_element_type=jnp.float32,
            )

        def settle(column, gain, value):
            back, by_gain = head_back(
                proj[0, :, columns(column)], gains[gain : gain + 1, :], value, cos_ref[...], sin_ref[...]
            )
            out[0, :, columns(column)] = back.astype(jnp.bfloat16)
            gain_grad[gain] += by_gain.reshape(rows // 8, 8, HD).sum(axis=0)

        for head in range(heads):
            settle(head, 0, grad_q[head])
        settle(heads, 1, grad_k[...] * (HD ** (-0.5)))
        out[0, :, columns(heads + 1)] = grad_v[...].astype(jnp.bfloat16)

        across_columns(out[0], weights, 0, wide, back_part)

        @pl.when(sequence == 1)
        def _():
            steps[2]()

        by_projected, by_attended = out[0].T, attended[0].T
        for start in range(0, width, 512):
            at = pl.ds(start, 512)
            summed[:wide, at] += jnp.dot(
                by_projected, normed[0, :, at], preferred_element_type=jnp.float32
            )
            summed[wide:, at] += jnp.dot(
                by_attended, grad[0, :, at], preferred_element_type=jnp.float32
            )

        @pl.when(sequence == count - 1)
        def _():
            fetch.wait()
            steps[3]()

            def finish(at):
                value = total[at] + read(from_tp, at) + read(from_near, at)
                output[at] = (held[at] + value).astype(jnp.bfloat16)

            row_loop(own_rows, finish)
            for outer in range(outer_count):
                for member in range(split):
                    start = (outer * split + member) * share
                    grad_weights[outer, member] = summed[:, start : start + share].astype(
                        jnp.bfloat16
                    )
            for copy in copies:
                copy.wait()

    return pl.pallas_call(
        kernel,
        name="attend_back",
        grid=(count,),
        out_shape=(
            jax.ShapeDtypeStruct((count, rows, wide), jnp.bfloat16),
            jax.ShapeDtypeStruct((2, 8, HD), jnp.float32),
            jax.ShapeDtypeStruct((count, rows, width), jnp.bfloat16),
            jax.ShapeDtypeStruct((own_rows, width), jnp.bfloat16),
            jax.ShapeDtypeStruct((outer_count, split, every, share), jnp.bfloat16),
        )
        + tuple(like(piece) for piece in extra),
        in_specs=[
            pl.BlockSpec(memory_space=pltpu.SMEM),
            per_sequence(rows, wide),
            per_sequence(rows, width),
            per_sequence(rows, heads * HD),
            per_sequence(rows, width),
            per_sequence(rows, HD),
            whole(width, wide + heads * HD),
            whole(rows, HD),
            whole(rows, HD),
            whole(2, HD),
            anywhere(),
            anywhere(),
        ]
        + [anywhere()] * extras,
        out_specs=(
            per_sequence(rows, wide),
            pl.BlockSpec((2, 8, HD), lambda s: (0, 0, 0)),
            per_sequence(rows, width),
            whole(own_rows, width),
            whole(outer_count, split, every, share),
        )
        + (anywhere(),) * extras,
        scratch_shapes=[
            pltpu.VMEM((heads, rows, HD), jnp.bfloat16),
            pltpu.VMEM((rows, HD), jnp.bfloat16),
            pltpu.VMEM((rows, HD), jnp.bfloat16),
            pltpu.VMEM((rows, heads * HD), jnp.bfloat16),
            pltpu.VMEM((heads, rows, HD), jnp.float32),
            pltpu.VMEM((rows, HD), jnp.float32),
            pltpu.VMEM((rows, HD), jnp.float32),
            pltpu.VMEM((every, width), jnp.float32),
            pltpu.VMEM((own_rows, width), jnp.float32),
            pltpu.VMEM((own_rows, width), jnp.float32),
            pltpu.SemaphoreType.DMA,
        ]
        + sum_scratch(own_rows, width, cut)
        + exchange_scratch() * extras,
        compiler_params=params(number),
        cost_estimate=cost_of(50),
    )(
        group_length,
        projected,
        normed,
        attended,
        grad_attn,
        logs,
        weights,
        cos_full,
        sin_full,
        gains,
        spread(part, own_rows),
        hidden,
        *extra,
    )


def feed(normed, weights, cotangent, gathered, early, number):
    count, rows, width = normed.shape
    units = weights.shape[1] // 2
    late = cotangent.shape[0] - early

    def kernel(normed, weights, own, _, product, active, out, *sems):
        steps = plan_gather(
            own, out, *sems, cut=balanced(late, 0), base=early, rows=late
        )
        sequence = pl.program_id(0)

        @pl.when(sequence == 0)
        def _():
            greet(NEIGHBOURS)
            steps[0]()

        for start in range(0, units, 256):
            gate_at, up_at = pl.ds(start, 256), pl.ds(units + start, 256)
            gate = jnp.dot(normed[0], weights[:, gate_at], preferred_element_type=jnp.float32)
            up = jnp.dot(normed[0], weights[:, up_at], preferred_element_type=jnp.float32)
            product[0, :, gate_at] = gate
            product[0, :, up_at] = up
            active[0, :, gate_at] = swish_product(gate, up).astype(jnp.bfloat16)

        for place in (1, 2, 3):

            @pl.when(sequence == count - 4 + place)
            def _(place=place):
                steps[place]()

    return pl.pallas_call(
        kernel,
        name="feed",
        grid=(count,),
        out_shape=(
            jax.ShapeDtypeStruct((count, rows, 2 * units), jnp.float32),
            jax.ShapeDtypeStruct((count, rows, units), jnp.bfloat16),
            like(gathered),
        ),
        in_specs=[
            per_sequence(rows, width),
            whole(*weights.shape),
            anywhere(),
            anywhere(),
        ],
        out_specs=(per_sequence(rows, 2 * units), per_sequence(rows, units), anywhere()),
        scratch_shapes=gather_scratch(),
        input_output_aliases={3: 2},
        compiler_params=params(number),
        cost_estimate=cost_of(28),
    )(normed, weights, cotangent, gathered)


def feed_back(grads, weights, product):
    count, rows, width = grads.shape
    units = weights.shape[1]

    def kernel(grads, weights, product, out):
        for start in range(0, units, 256):
            gate_at, up_at = pl.ds(start, 256), pl.ds(units + start, 256)
            grad = jnp.dot(grads[0], weights[:, gate_at], preferred_element_type=jnp.float32)
            gate, up = product[0, :, gate_at], product[0, :, up_at]
            share = jax.nn.sigmoid(gate)
            by_gate = grad * up * share * (1.0 + gate * (1.0 - share))
            out[0, :, gate_at] = by_gate.astype(jnp.bfloat16)
            out[0, :, up_at] = (grad * gate * share).astype(jnp.bfloat16)

    return pl.pallas_call(
        kernel,
        name="feed_back",
        grid=(count,),
        out_shape=jax.ShapeDtypeStruct((count, rows, 2 * units), jnp.bfloat16),
        in_specs=[
            per_sequence(rows, width),
            whole(*weights.shape),
            per_sequence(rows, 2 * units),
        ],
        out_specs=per_sequence(rows, 2 * units),
        compiler_params=pltpu.CompilerParams(vmem_limit_bytes=VMEM_LIMIT),
        cost_estimate=cost_of(18),
    )(grads, weights, product)


def adam_all(sets, pieces, factor):
    jobs = []
    for weight, _, _, source, kind, detail in sets:
        rows = weight.shape[0]
        height = {"columns": max(CHUNK, rows // 4), "across": rows}.get(kind, rows // TEAM)
        jobs.append((height, rows // height, source, kind, detail))
    count = sum(job[1] for job in jobs)
    total, sources = len(sets), len(pieces)

    def kernel(*refs):
        inputs, refs = refs[: 3 * total], refs[3 * total :]
        piece_refs, factor, refs = refs[:sources], refs[sources], refs[sources + 1 :]
        outputs, refs = refs[: 4 * total], refs[4 * total :]
        held, refs = refs[: 4 * total], refs[4 * total :]
        held_pieces, (piece_sem, in_sem, out_sem) = refs[:sources], refs[sources:]
        scale = factor[0:1, 0:1]
        loads, stores, work, slot = [], [], [], 0
        for place in range(sources):
            loads.append(
                pltpu.make_async_copy(piece_refs[place], held_pieces[place], piece_sem.at[place])
            )
            loads[place].start()
        for place, (height, steps, *_) in enumerate(jobs):
            for step in range(steps):
                at = pl.ds(step * height, height)
                arrive = []
                for number in range(3):
                    copy = pltpu.make_async_copy(
                        inputs[3 * place + number].at[at],
                        held[4 * place + number].at[at],
                        in_sem.at[3 * slot + number],
                    )
                    copy.start()
                    arrive.append(copy)
                work.append((place, step, at, slot, arrive))
                slot += 1
        arrived = set()
        for place, step, at, slot, arrive in work:
            height, _, source, kind, detail = jobs[place]
            weight, moment, square, low = held[4 * place : 4 * place + 4]
            gradients = held_pieces[source]
            if source not in arrived:
                loads[source].wait()
                arrived.add(source)
            for copy in arrive:
                copy.wait()

            def update(rows, across, gradient):
                where = (rows, across)
                value, one, two = adam_update(
                    weight[where], gradient, moment[where], square[where], scale, weight_decay, learn_rate
                )
                weight[where], moment[where], square[where] = value, one, two
                low[where] = value.astype(jnp.bfloat16)

            def spans(widths):
                for member in range(TEAM):
                    first, inside = 0, 0
                    for width in widths:
                        share = width // TEAM
                        yield member, pl.ds(first + member * share, share), pl.ds(inside, share)
                        first += width
                        inside += share

            if kind == "rows":
                update(at, slice(None), gradients[step].astype(jnp.float32).T)
            elif kind == "below":
                update(
                    at, slice(None), gradients[step, pl.ds(detail, height)].astype(jnp.float32)
                )
            elif kind == "across":
                for member, across, inside in spans(detail):
                    update(at, across, gradients[member, inside].astype(jnp.float32).T)
            else:

                @pl.loop(0, height // CHUNK)
                def _(row):
                    rows = pl.ds(pl.multiple_of(step * height + row * CHUNK, CHUNK), CHUNK)
                    for member, across, inside in spans(detail):
                        update(rows, across, gradients[member, rows, inside].astype(jnp.float32))

            for number, origin in enumerate((weight, moment, square, low)):
                copy = pltpu.make_async_copy(
                    origin.at[at], outputs[4 * place + number].at[at], out_sem.at[4 * slot + number]
                )
                copy.start()
                stores.append(copy)
        for copy in stores:
            copy.wait()

    args, shapes, scratch = [], [], []
    for weight, moment, square, *_ in sets:
        args += [weight, moment, square]
        low = jax.ShapeDtypeStruct(weight.shape, jnp.bfloat16)
        shapes += [like(weight)] * 3 + [low]
        scratch += [pltpu.VMEM(each.shape, each.dtype) for each in (weight, moment, square, low)]
    outs = pl.pallas_call(
        kernel,
        name="adam_all",
        out_shape=tuple(shapes),
        in_specs=[anywhere()] * (3 * total + sources) + [in_vmem()],
        out_specs=(anywhere(),) * (4 * total),
        scratch_shapes=scratch
        + [pltpu.VMEM(piece.shape, piece.dtype) for piece in pieces]
        + [
            pltpu.SemaphoreType.DMA((sources,)),
            pltpu.SemaphoreType.DMA((3 * count,)),
            pltpu.SemaphoreType.DMA((4 * count,)),
        ],
        compiler_params=pltpu.CompilerParams(vmem_limit_bytes=VMEM_LIMIT),
        cost_estimate=cost_of(15),
    )(*args, *pieces, factor)
    return [outs[4 * place : 4 * place + 4] for place in range(total)]


def split_columns(values, widths):
    members = []
    for member in range(TEAM):
        start, parts = 0, []
        for width in widths:
            share = width // TEAM
            first = start + member * share
            parts.append(values[:, first : first + share])
            start += width
        members.append(jnp.concatenate(parts, axis=1))
    return jnp.stack(members)


def gather_outer(mixed):
    return lax.all_gather(mixed.reshape(-1, mixed.shape[2]), "outer", axis=0, tiled=True)


def team_pieces(summed):
    return summed.reshape(TEAM, -1, summed.shape[-1])


def sum_weight(gradient):
    return lax.psum_scatter(gradient, "outer", scatter_dimension=0, tiled=True)


def after(values, earlier):
    return lax.optimization_barrier((values, earlier))


def adam_update(weight, gradient, moment_one, moment_two, factor, decay_rate, rate_value):
    clipped = gradient * factor
    moment_one = beta_first * moment_one + (1.0 - beta_first) * clipped
    moment_two = beta_second * moment_two + (1.0 - beta_second) * clipped * clipped
    first_fixed = moment_one / (1.0 - beta_first**STEP)
    second_fixed = moment_two / (1.0 - beta_second**STEP)
    weight = weight - rate_value * (
        first_fixed / (jnp.sqrt(second_fixed) + adam_epsilon) + decay_rate * weight
    )
    return (weight, moment_one, moment_two)


def dot(left, right, contract):
    return lax.dot_general(
        left, right, ((contract[0], contract[1]), ((), ())), preferred_element_type=jnp.float32
    )


def times(left, right):
    return dot(left, right, ((1,), (0,)))


def times_across(left, right):
    return dot(left, right, ((1,), (1,)))


def over_rows(left, right):
    return dot(left, right, ((0,), (0,)))


def local(
    inputs,
    cotangent,
    lengths,
    owners,
    qkv_weight,
    out_weight,
    gate_up_weight,
    down_weight,
    norm_gains,
    qkv_moment,
    out_moment,
    gate_up_moment,
    down_moment,
    gains_moment,
    qkv_square,
    out_square,
    gate_up_square,
    down_square,
    gains_square,
):
    tp_count = lax.axis_size("tp")
    half_rows = inputs.shape[0]
    row_count = half_rows * tp_count
    heads = H // tp_count // TEAM
    hidden_units = FF // tp_count // TEAM
    qkv_widths = (H * HD // tp_count, KV * HD // tp_count, KV * HD // tp_count)
    out_widths = (H * HD // tp_count,)
    gate_up_widths = (FF // tp_count, FF // tp_count)
    down_widths = (FF // tp_count,)

    first_group = lax.axis_index("outer") * TEAM
    group_ids = first_group + jnp.arange(TEAM)
    group_length = jnp.sum(
        jnp.where(owners[None, :] == group_ids[:, None], lengths[None, :], 0), axis=1
    )
    own_group = lax.axis_index("near") * CORE + lax.axis_index("core")
    own_rows = lax.axis_index("tp") * half_rows + jnp.arange(half_rows)
    valid_rows = (own_rows < pick(group_length, own_group))[:, None]
    half_width = HD // 2
    frequency = rope_base ** (-(jnp.arange(half_width, dtype=jnp.float32) * 2.0 / HD))
    angles = jnp.arange(row_count, dtype=jnp.float32)[:, None] * frequency[None, :]
    cosine, sine = jnp.cos(angles), jnp.sin(angles)
    cos_full = jnp.concatenate([cosine, cosine], axis=1)
    sin_full = jnp.concatenate([-sine, sine], axis=1)
    attn_gain = norm_gains[:D]
    mlp_gain = norm_gains[D : 2 * D]
    head_gains = norm_gains[2 * D :].reshape(2, HD)

    first_pieces = jnp.concatenate(
        [
            split_columns(qkv_weight.astype(jnp.bfloat16), qkv_widths),
            split_columns(out_weight.astype(jnp.bfloat16).T, out_widths),
        ],
        axis=2,
    )
    gate_up_pieces = split_columns(gate_up_weight.astype(jnp.bfloat16), gate_up_widths)
    down_pieces = split_columns(down_weight.astype(jnp.bfloat16).T, down_widths)
    first_mixed = exchange(first_pieces, 6, "exchange_first")
    first_full = gather_outer(first_mixed)
    qkv_full = first_full[:, : (heads + 2) * HD]

    residual_in = inputs.astype(jnp.float32)
    normed_attn = residual_in * rms_scale(residual_in) * attn_gain
    grad_low = jnp.where(valid_rows, cotangent, jnp.zeros_like(cotangent))
    normed_attn, first_mixed, grad_low, down_pieces, cos_full, sin_full = (
        lax.optimization_barrier(
            (
                normed_attn.astype(jnp.bfloat16),
                first_mixed,
                grad_low,
                down_pieces,
                cos_full,
                sin_full,
            )
        )
    )
    normed_attn, gate_up_mixed = gather_rows(
        normed_attn, (gate_up_pieces,), 0, "gather_inputs"
    )
    gate_up_full = gather_outer(gate_up_mixed)
    early = half_rows * 3 // 5 // CHUNK * CHUNK
    projected, attended, logs, attn_branch, grad_all, down_mixed = attend(
        normed_attn.reshape(TEAM, row_count, D),
        first_full,
        grad_low,
        (down_pieces,),
        group_length,
        cos_full,
        sin_full,
        head_gains,
        heads,
        early,
        1,
    )
    down_full = gather_outer(down_mixed)
    hidden, normed_mlp = branch_and_norm(attn_branch, inputs, mlp_gain, 2, "branch_and_norm")
    gate_up, activated, grad_all = feed(
        normed_mlp.reshape(TEAM, row_count, D), gate_up_full, grad_low, grad_all, early, 8
    )
    grad_down = over_rows(grad_all.reshape(-1, D), activated.reshape(-1, hidden_units))
    grad_all, grad_down = after(grad_all, grad_down.astype(jnp.bfloat16))
    down_sum = sum_weight(grad_down)
    grad_gate_up = feed_back(grad_all.reshape(TEAM, row_count, D), down_full, gate_up)
    grad_gate_up_weight = over_rows(normed_mlp, grad_gate_up.reshape(-1, 2 * hidden_units))
    grad_gate_up, grad_gate_up_weight = after(
        grad_gate_up, grad_gate_up_weight.astype(jnp.bfloat16)
    )
    gate_up_sum = sum_weight(grad_gate_up_weight)
    grad_hidden, grad_mlp_gain, grad_attn, mlp_part = feed_back_rest(
        grad_gate_up, gate_up_full, activated, down_full, hidden, grad_low, mlp_gain, 3, "feed_back_rest"
    )
    _, grad_head_gains, grad_normed_attn, output, grad_first, down_mixed = attend_back(
        projected,
        normed_attn.reshape(TEAM, row_count, D),
        attended,
        grad_attn.reshape(TEAM, row_count, D),
        logs,
        first_full,
        mlp_part,
        hidden,
        (team_pieces(down_sum),),
        lax.axis_size("outer"),
        group_length,
        cos_full,
        sin_full,
        head_gains,
        heads,
        7,
    )
    first_sum = sum_weight(grad_first.reshape(-1, grad_first.shape[3]))
    if grad_first.shape[1] == TEAM:
        first_sum = team_pieces(first_sum)
    else:
        first_sum = first_sum.reshape(first_sum.shape[0], TEAM, -1).transpose(1, 0, 2)
    input_grad, attn_gain_parts, gate_up_mixed = norm_back_last(
        grad_normed_attn,
        inputs,
        grad_hidden,
        attn_gain,
        (team_pieces(gate_up_sum),),
        4,
        "norm_back_attn",
    )
    gain_part = jnp.concatenate(
        [jnp.zeros_like(grad_mlp_gain), grad_mlp_gain, grad_head_gains.sum(axis=1).reshape(-1)]
    )
    square_part = sum(
        jnp.sum(jnp.square(member.astype(jnp.float32))) for member in (gate_up_sum, down_sum)
    )
    gain_count = gain_part.shape[0]
    packed = jnp.pad(gain_part, (0, -gain_count % PAD))
    packed = jnp.concatenate([packed, jnp.pad(square_part[None], (0, PAD - 1))])
    packed, norm_tile, factor_tile, first_mixed = total_everywhere(
        packed.reshape(-1, HD),
        attn_gain_parts,
        first_sum,
        lax.axis_size("outer"),
        5,
        "total_everywhere",
    )
    gain_grad = packed.reshape(-1)[:gain_count]
    grad_norm, factor = norm_tile[0, 0], factor_tile[0, 0]
    (
        (new_gate_up, new_gate_up_one, new_gate_up_two, gate_up_copy),
        (new_down, new_down_one, new_down_two, down_copy),
        (new_out, new_out_one, new_out_two, out_copy),
        (new_qkv, new_qkv_one, new_qkv_two, qkv_copy),
    ) = adam_all(
        [
            (gate_up_weight, gate_up_moment, gate_up_square, 0, "columns", gate_up_widths),
            (down_weight, down_moment, down_square, 1, "rows", None),
            (out_weight, out_moment, out_square, 2, "below", (heads + 2) * HD),
            (qkv_weight, qkv_moment, qkv_square, 2, "across", qkv_widths),
        ],
        (gate_up_mixed, down_mixed, first_mixed),
        factor_tile,
    )
    new_gains, new_gains_one, new_gains_two = adam_update(
        norm_gains, gain_grad, gains_moment, gains_square, factor, 0.0, gain_rate
    )
    return (
        output,
        input_grad,
        grad_norm,
        new_qkv,
        new_qkv_one,
        new_qkv_two,
        qkv_copy,
        new_out,
        new_out_one,
        new_out_two,
        out_copy,
        new_gate_up,
        new_gate_up_one,
        new_gate_up_two,
        gate_up_copy,
        new_down,
        new_down_one,
        new_down_two,
        down_copy,
        new_gains,
        new_gains_one,
        new_gains_two,
    )


def solution(mesh):
    fsdp_count, tp_count = mesh.shape["fsdp"], mesh.shape["tp"]
    cut = mesh.devices.reshape(fsdp_count // TEAM, NEAR, CORE, tp_count)
    cut_mesh = Mesh(cut, ("outer",) + LAYER)
    fsdp = ("outer", "near", "core")
    rows = P(fsdp + ("tp",), None)
    wide = P(fsdp, "tp")
    tall = P("tp", fsdp)
    weights = (wide, tall, wide, tall, P())
    return jax.shard_map(
        local,
        mesh=cut_mesh,
        in_specs=(rows, rows, P(), P()) + weights * 3,
        out_specs=(rows, rows, P()) + (wide,) * 4 + (tall,) * 4 + (wide,) * 4 + (tall,) * 4 + (P(),) * 3,
        check_vma=False,
    )
```

```python
import jax
import jax.numpy as jnp
from jax import lax
from jax.experimental import pallas as pl
from jax.experimental.pallas import tpu as pltpu
from jax.sharding import Mesh, PartitionSpec as P

D = 2048
H = 16
KV = 8
HD = 128
FF = 6144
STEP = 10


norm_epsilon = 1e-06
rope_base = 1000000.0
clip_norm = 1.0
learn_rate = 0.04
gain_rate = 0.8
beta_first = 0.9
beta_second = 0.999
adam_epsilon = 1e-08
weight_decay = 0.1
masked_score = -1e30

NEAR = 2
CORE = 2
TEAM = NEAR * CORE
LAYER = ("near", "core", "tp")
BLOCK = 128
PAD = 8 * 128


def rms_scale(values):
    return lax.rsqrt(jnp.mean(values * values, axis=-1, keepdims=True) + norm_epsilon)


def swish_product(gate_part, up_part):
    return jax.nn.silu(gate_part) * up_part


def pick(values, index):
    return lax.dynamic_index_in_dim(values, index, 0, keepdims=False)


MESH_ID = pl.DeviceIdType.MESH
VMEM_LIMIT = 60 * 1024 * 1024
CHUNK = 16
GATHER_COPIES = 13
AHEAD = 4
SUM_COPIES = 10
NEIGHBOURS = ((1, 0, 0), (0, 1, 0), (0, 0, 1))
MATES = ((0, 1, 0), (1, 0, 0), (1, 1, 0))
EVERYONE_NEAR = NEIGHBOURS + ((1, 1, 0),)


def spots():
    return tuple(lax.axis_index(name) for name in LAYER)


def flipped(near_flip, core_flip, tp_flip):
    return {
        name: 1 - spot if flip else spot
        for name, spot, flip in zip(LAYER, spots(), (near_flip, core_flip, tp_flip))
    }


def greet(flips):
    barrier = pltpu.get_barrier_semaphore()
    for flip in flips:
        pl.semaphore_signal(barrier, inc=1, device_id=flipped(*flip), device_id_type=MESH_ID)
    pl.semaphore_wait(barrier, len(flips))


def link(source, target, send_sem, recv_sem, flip):
    return pltpu.make_async_remote_copy(
        src_ref=source,
        dst_ref=target,
        send_sem=send_sem,
        recv_sem=recv_sem,
        device_id=flipped(*flip),
        device_id_type=MESH_ID,
    )


TO_NEAR, TO_CORE, TO_TP = NEIGHBOURS


def plan_exchange(pieces, out, send, recv, own_sem):
    near, core, _ = spots()
    own = near * CORE + core
    copies = []
    for number, flip in enumerate(MATES):
        there = (1 - near if flip[0] else near) * CORE + (1 - core if flip[1] else core)
        copies.append(
            link(pieces.at[there], out.at[own], send.at[number], recv.at[number], flip)
        )
    copies.append(pltpu.make_async_copy(pieces.at[own], out.at[own], own_sem))
    return copies


def exchange_scratch():
    return [
        pltpu.SemaphoreType.DMA((len(MATES),)),
        pltpu.SemaphoreType.DMA((len(MATES),)),
        pltpu.SemaphoreType.DMA,
    ]


def crossing(pieces, width):
    return sum(2 * piece.shape[1] * piece.shape[2] for piece in pieces) // width


def plan_exchanges(pieces, mixed, sems):
    copies = []
    for place, (piece, result) in enumerate(zip(pieces, mixed)):
        copies += plan_exchange(piece, result, *sems[3 * place : 3 * place + 3])
    return copies


def plan_gather(own, out, send, recv, own_sem, cut, base=0, rows=None, parts=False):
    near, core, tp = spots()
    rows = own.shape[0] if rows is None else rows
    low, high = pl.ds(base, cut), pl.ds(base + cut, rows - cut)
    all_rows = pl.ds(base, rows)

    def make(number, source, target, flip):
        return link(source, target, send.at[number], recv.at[number], flip)

    def give(number, part, flip):
        return make(number, own.at[part], out.at[near, core, tp, part], flip)

    def relay(number, where_near, where_tp, part, flip):
        ref = out.at[where_near, core, where_tp, part]
        return make(number, ref, ref, flip)

    keep = pltpu.make_async_copy(own.at[all_rows], out.at[near, core, tp, all_rows], own_sem)
    twin_own = give(4, all_rows, TO_CORE)
    near_high = give(1, high, TO_NEAR)
    tp_high = give(2, high, TO_TP)
    far_high = relay(7, 1 - near, tp, high, TO_TP)
    twin_beside = relay(8, 1 - near, tp, high, TO_CORE)
    twin_across = relay(9, near, 1 - tp, high, TO_CORE)
    twin_far = relay(12, 1 - near, 1 - tp, high, TO_CORE)
    twins = [twin_own, twin_beside, twin_across, twin_far]
    ways = [near_high, tp_high, far_high]
    if cut:
        tp_low = give(0, low, TO_TP)
        near_low = give(3, low, TO_NEAR)
        far_low = relay(5, near, 1 - tp, low, TO_NEAR)
        twin_across_low = relay(6, near, 1 - tp, low, TO_CORE)
        twin_beside_low = relay(10, 1 - near, tp, low, TO_CORE)
        twin_far_low = relay(11, 1 - near, 1 - tp, low, TO_CORE)
        twins += [twin_across_low, twin_beside_low, twin_far_low]
        ways += [tp_low, near_low, far_low]

    def begin():
        if cut:
            tp_low.start()
        near_high.start()
        tp_high.start()
        if cut:
            near_low.start()
        twin_own.start()
        keep.start()

    def middle():
        if cut:
            tp_low.wait_recv()
            far_low.start()
            twin_across_low.start()
        near_high.wait_recv()
        far_high.start()
        twin_beside.start()

    def later():
        tp_high.wait_recv()
        twin_across.start()
        if cut:
            near_low.wait_recv()
            twin_beside_low.start()

    def own_there():
        keep.wait()

    def twin_there():
        twin_own.wait_recv()
        twin_across.wait_recv()
        if cut:
            twin_across_low.wait_recv()

    def far_there():
        if cut:
            far_low.wait_recv()
            twin_far_low.start()
        far_high.wait_recv()
        twin_far.start()

    def rest_there():
        twin_beside.wait_recv()
        twin_far.wait_recv()
        if cut:
            twin_beside_low.wait_recv()
            twin_far_low.wait_recv()
        for copy in ways + twins:
            copy.wait_send()

    def finish():
        own_there()
        twin_there()
        far_there()
        rest_there()

    if parts:
        return [begin, middle, later, own_there, twin_there, far_there, rest_there]
    return [begin, middle, later, finish]


def balanced(rows, beside):
    return max(0, (rows - beside) // 2 // CHUNK * CHUNK)


def gather_scratch():
    return [
        pltpu.SemaphoreType.DMA((GATHER_COPIES,)),
        pltpu.SemaphoreType.DMA((GATHER_COPIES,)),
        pltpu.SemaphoreType.DMA,
    ]


def add_rows(target, start, count, *sources):
    @pl.loop(0, count // CHUNK)
    def _(step):
        at = pl.ds(pl.multiple_of(start + step * CHUNK, CHUNK), CHUNK)
        total = None
        for source, shift in sources:
            where = pl.ds(pl.multiple_of(start - shift + step * CHUNK, CHUNK), CHUNK)
            value = source[where].astype(jnp.float32)
            total = value if total is None else total + value
        target[at] = total.astype(target.dtype)


def plan_sum(outgoing, mine, keep, total, scratch, cut):
    theirs, way_near, way_tp, from_tp, from_near, send, recv = scratch
    rows = total.shape[0]
    low, high = pl.ds(0, cut), pl.ds(cut, rows - cut)

    def make(number, source, target, flip):
        return link(source, target, send.at[number], recv.at[number], flip)

    twin = [make(number, outgoing[number], theirs.at[number], TO_CORE) for number in range(4)]
    far, to_tp, to_near, own = mine
    far_high = make(5, far.at[high], way_tp, TO_TP)
    tp_high = make(6, to_tp.at[high], from_tp.at[high], TO_TP)
    near_high = make(9, to_near.at[high], from_near.at[high], TO_NEAR)
    ways = [far_high, tp_high, near_high]
    if cut:
        far_low = make(4, far.at[low], way_near, TO_NEAR)
        near_low = make(7, to_near.at[low], from_near.at[low], TO_NEAR)
        tp_low = make(8, to_tp.at[low], from_tp.at[low], TO_TP)
        ways += [near_low, tp_low]

    def ready(number):
        if keep:
            keep[number].wait()
        twin[number].wait_recv()

    def both(number):
        return (mine[number], 0), (theirs.at[number], 0)

    def begin(numbers=range(4)):
        for number in numbers:
            twin[number].start()
            if keep:
                keep[number].start()

    def send_far():
        ready(0)
        if cut:
            add_rows(far, 0, cut, *both(0))
            far_low.start()
        add_rows(far, cut, rows - cut, *both(0))
        far_high.start()

    def send_tp():
        ready(1)
        add_rows(to_tp, cut, rows - cut, *both(1))
        tp_high.start()

    def send_near():
        ready(2)
        if cut:
            add_rows(to_near, 0, cut, *both(2))
            near_low.start()

    def first():
        send_far()
        send_tp()
        send_near()

    def second():
        if cut:
            far_low.wait_recv()
            add_rows(to_tp, 0, cut, *both(1), (way_near, 0))
            tp_low.start()
        far_high.wait_recv()
        add_rows(to_near, cut, rows - cut, *both(2), (way_tp, cut))
        near_high.start()
        ready(3)
        add_rows(total, 0, rows, *both(3))

    def finish():
        for copy in ways[1:]:
            copy.wait_recv()
        for copy in twin + ways + ([far_low] if cut else []):
            copy.wait_send()

    return [begin, first, second, finish], (send_far, send_tp, send_near)


def plan_sum_of(part, total, scratch, cut):
    mine, local_sem, *scratch = scratch
    near, core, tp = spots()
    order = [(1 - near, 1 - tp), (near, 1 - tp), (1 - near, tp), (near, tp)]
    outgoing = [part.at[a, 1 - core, b] for a, b in order]
    keep = [
        pltpu.make_async_copy(part.at[a, core, b], mine.at[number], local_sem.at[number])
        for number, (a, b) in enumerate(order)
    ]
    blocks = [mine.at[number] for number in range(4)]
    steps, _ = plan_sum(outgoing, blocks, keep, total, scratch, cut)
    return steps, scratch[3], scratch[4]


def sum_scratch(rows, width, cut, fetched=True):
    low = jnp.bfloat16
    fetch = [pltpu.VMEM((4, rows, width), low), pltpu.SemaphoreType.DMA((4,))]
    return (fetch if fetched else []) + [
        pltpu.VMEM((4, rows, width), low),
        pltpu.VMEM((max(cut, CHUNK), width), low),
        pltpu.VMEM((rows - cut, width), low),
        pltpu.VMEM((rows, width), low),
        pltpu.VMEM((rows, width), low),
        pltpu.SemaphoreType.DMA((SUM_COPIES,)),
        pltpu.SemaphoreType.DMA((SUM_COPIES,)),
    ]


SUM_SCRATCH = 9
COST_SHARE = 1e5


def params(number):
    return pltpu.CompilerParams(
        collective_id=number, has_side_effects=True, vmem_limit_bytes=VMEM_LIMIT
    )


def cost_of(microseconds):
    return pl.CostEstimate(
        flops=0, bytes_accessed=int(microseconds * COST_SHARE), transcendentals=0
    )


def in_vmem():
    return pl.BlockSpec(memory_space=pltpu.VMEM)


def anywhere():
    return pl.BlockSpec(memory_space=pl.ANY)


def like(array):
    return jax.ShapeDtypeStruct(array.shape, array.dtype)


def layer_rows(rows, width):
    return jax.ShapeDtypeStruct((NEAR, CORE, 2, rows, width), jnp.bfloat16)


def exchange(pieces, number, name):
    def kernel(pieces, out, *sems):
        greet(MATES)
        copies = plan_exchange(pieces, out, *sems)
        for copy in copies:
            copy.start()
        for copy in copies:
            copy.wait()

    return pl.pallas_call(
        kernel,
        name=name,
        out_shape=like(pieces),
        in_specs=[anywhere()],
        out_specs=anywhere(),
        scratch_shapes=exchange_scratch(),
        compiler_params=params(number),
        cost_estimate=cost_of(12),
    )(pieces)


def gather_rows(values, extra, number, name):
    rows, width = values.shape
    extras = len(extra)
    cut = balanced(rows, crossing(extra, width))

    def kernel(own, *rest):
        pieces, out, mixed = rest[:extras], rest[extras], rest[extras + 1 : 2 * extras + 1]
        sems = rest[2 * extras + 1 :]
        begin, *steps = plan_gather(own, out, *sems[:3], cut=cut)
        copies = plan_exchanges(pieces, mixed, sems[3:])
        greet(EVERYONE_NEAR)
        begin()
        for copy in copies:
            copy.start()
        for step in steps:
            step()
        for copy in copies:
            copy.wait()

    outs = pl.pallas_call(
        kernel,
        name=name,
        out_shape=(layer_rows(rows, width),) + tuple(like(piece) for piece in extra),
        in_specs=[anywhere()] * (1 + extras),
        out_specs=(anywhere(),) * (1 + extras),
        scratch_shapes=gather_scratch() + exchange_scratch() * extras,
        compiler_params=params(number),
        cost_estimate=cost_of(60),
    )(values, *extra)
    return (outs[0].reshape(-1, width),) + tuple(outs[1:])


def row_loop(rows, body):
    @pl.loop(0, rows // CHUNK)
    def _(step):
        body(pl.ds(pl.multiple_of(step * CHUNK, CHUNK), CHUNK))


def spread(part, rows):
    return part.reshape(NEAR, CORE, 2, rows, part.shape[-1])


def read(ref, at):
    return ref[at].astype(jnp.float32)


def branch_and_norm(part, residual, gain, number, name):
    rows, width = residual.shape
    cut = rows // 2

    def kernel(part, residual, gain, hidden, out, *scratch):
        normed, sems = scratch[SUM_SCRATCH], scratch[SUM_SCRATCH + 1 :]
        steps, from_tp, from_near = plan_sum_of(part, hidden, scratch[:SUM_SCRATCH], cut)
        onward = plan_gather(normed, out, *sems, cut=cut)
        greet(NEIGHBOURS)
        for step in steps:
            step()

        def finish(at):
            value = hidden[at] + read(from_tp, at) + read(from_near, at)
            value = read(residual, at) + value
            hidden[at] = value
            normed[at] = (value * rms_scale(value) * gain[...]).astype(jnp.bfloat16)

        row_loop(rows, finish)
        for step in onward:
            step()

    hidden, full = pl.pallas_call(
        kernel,
        name=name,
        out_shape=(jax.ShapeDtypeStruct((rows, width), jnp.float32), layer_rows(rows, width)),
        in_specs=[anywhere(), in_vmem(), in_vmem()],
        out_specs=(in_vmem(), anywhere()),
        scratch_shapes=sum_scratch(rows, width, cut)
        + [pltpu.VMEM((rows, width), jnp.bfloat16)]
        + gather_scratch(),
        compiler_params=params(number),
        cost_estimate=cost_of(95),
    )(spread(part, rows), residual, gain.reshape(1, width))
    return hidden, full.reshape(-1, width)


def norm_back(value, gain, grad):
    scale = rms_scale(value)
    scaled = grad * gain
    inner = jnp.mean(scaled * value, axis=-1, keepdims=True)
    return scale * scaled - value * (scale * scale * scale * inner), grad * value * scale


def sequence_order():
    near, core, _ = spots()
    return [
        (near if place >= 2 else 1 - near) * CORE + (core if place % 2 else 1 - core)
        for place in range(TEAM)
    ]


def times_turned(left, weights, target):
    for start in range(0, weights.shape[0], 512):
        at = pl.ds(start, 512)
        target[:, at] = lax.dot_general(
            left, weights[at, :], (((1,), (1,)), ((), ())), preferred_element_type=jnp.float32
        ).astype(target.dtype)


def feed_back_rest(
    grad_gate, grad_up, weights, active, down, normed, values, upstream, gain, outer_count, number, name
):
    rows, width = values.shape
    count, both_rows, units = grad_gate.shape
    all_rows = count * both_rows
    past = all_rows - width
    cut = rows // 2
    split, share = team_split(width, outer_count)
    turns = width // 512

    def kernel(
        gate, ups, weights, active, down, normed, values, upstream, gain,
        result, gain_grad, low, branch, grad_weight, *scratch
    ):
        (grad_v, weights_v, active_v, down_v, values_v, upstream_v, parts, total), rest = (
            scratch[:8],
            scratch[8:],
        )
        (shares, staged, load_sem, store_sem, chunk_sem, piece_sem), sums = rest[:6], rest[6:]
        from_tp, from_near = sums[3], sums[4]
        near, core, tp = spots()
        members = sequence_order()
        outgoing = [parts.at[place, half] for place, half in ((0, 1 - tp), (2, 1 - tp), (0, tp), (2, tp))]
        mine = [parts.at[place, half] for place, half in ((1, 1 - tp), (3, 1 - tp), (1, tp), (3, tp))]
        steps, (send_far, send_tp, send_near) = plan_sum(outgoing, mine, (), total, sums, cut)
        stores = [
            pltpu.make_async_copy(shares.at[place % 2], branch.at[place], store_sem.at[place])
            for place in range(count)
        ]
        fetch = [
            pltpu.make_async_copy(source, target, load_sem.at[place])
            for place, (source, target) in enumerate(
                (
                    (weights, weights_v),
                    (values, values_v),
                    (upstream, upstream_v),
                    (active, active_v),
                    (down, down_v),
                    (ups, active_v),
                )
            )
        ]
        grads = []
        for place, member in enumerate(members):
            for side, source in enumerate((gate, ups)):
                grads.append(
                    pltpu.make_async_copy(
                        source.at[member],
                        grad_v.at[place % 2, :, :, pl.ds(side * units, units)],
                        load_sem.at[6 + 2 * place + side],
                    )
                )

        def bring(place):
            grads[2 * place].start()
            grads[2 * place + 1].start()

        def brought(place):
            grads[2 * place].wait()
            grads[2 * place + 1].wait()

        def back(place, half):
            times_turned(grad_v[place % 2, half], weights_v, parts.at[place, half])

        def chunk(turn):
            at, slot = pl.ds(turn * 512, 512), turn % 2
            return [
                pltpu.make_async_copy(
                    normed.at[pl.ds(0, width), at],
                    weights_v.at[:, pl.ds(slot * 1024, 512)],
                    chunk_sem.at[slot, 0],
                ),
                pltpu.make_async_copy(
                    normed.at[pl.ds(width, past), at],
                    weights_v.at[pl.ds(slot * past, past), pl.ds(512, 512)],
                    chunk_sem.at[slot, 1],
                ),
            ]

        def pieces(turn):
            slot = turn % 2
            return [
                pltpu.make_async_copy(
                    staged.at[slot, :, pl.ds(place * share, share)],
                    grad_weight.at[turn * (512 // share) + place],
                    piece_sem.at[slot, place],
                )
                for place in range(512 // share)
            ]

        fetch[0].start()
        bring(0)
        bring(1)
        greet(NEIGHBOURS)
        fetch[0].wait()
        brought(0)
        back(0, 1 - tp)
        steps[0]((0,))
        brought(1)
        back(1, 1 - tp)
        send_far()
        back(0, tp)
        steps[0]((2,))
        bring(2)
        for place in (3, 4, 1, 2):
            fetch[place].start()
        back(1, tp)
        send_near()
        bring(3)
        brought(2)
        back(2, 1 - tp)
        steps[0]((1,))
        brought(3)
        back(3, 1 - tp)
        send_tp()
        back(2, tp)
        steps[0]((3,))
        back(3, tp)
        for turn in (0, 1):
            for copy in chunk(turn):
                copy.start()
        fetch[3].wait()
        fetch[4].wait()
        for place in range(count):
            if place >= 2:
                stores[place - 2].wait()
            for half in range(2):
                times_turned(active_v[place, half], down_v, shares.at[place % 2, half])
            stores[place].start()
        fetch[5].start()
        steps[2]()
        fetch[5].wait()
        for turn in range(turns):
            slot = turn % 2
            for copy in chunk(turn):
                copy.wait()
            left = active_v[...].reshape(all_rows, units)
            product = lax.dot_general(
                left[:width],
                weights_v[:, slot * 1024 : slot * 1024 + 512],
                (((0,), (0,)), ((), ())),
                preferred_element_type=jnp.float32,
            ) + lax.dot_general(
                left[width:],
                weights_v[slot * past : (slot + 1) * past, 512:1024],
                (((0,), (0,)), ((), ())),
                preferred_element_type=jnp.float32,
            )
            if turn >= 2:
                for copy in pieces(turn - 2):
                    copy.wait()
            staged[slot] = product.astype(staged.dtype)
            for copy in pieces(turn):
                copy.start()
            if turn + 2 < turns:
                for copy in chunk(turn + 2):
                    copy.start()
        fetch[1].wait()
        fetch[2].wait()
        gain_grad[...] = jnp.zeros_like(gain_grad)
        steps[3]()

        def finish(at):
            grad = total[at] + read(from_tp, at) + read(from_near, at)
            turned, by_gain = norm_back(values_v[at], gain[...], grad)
            gain_grad[...] += by_gain.reshape(CHUNK // 8, 8, width).sum(axis=0)
            value = read(upstream_v, at) + turned
            total[at] = value
            low[at] = value.astype(jnp.bfloat16)

        row_loop(rows, finish)
        store = pltpu.make_async_copy(total, result, store_sem.at[count])
        store.start()
        for turn in range(max(0, turns - 2), turns):
            for copy in pieces(turn):
                copy.wait()
        for copy in [store] + stores[2:]:
            copy.wait()

    low_type = jnp.bfloat16
    halves = (count, 2, rows, units)
    result, gain_grad, rounded, branch, grad_weight = pl.pallas_call(
        kernel,
        name=name,
        out_shape=(
            jax.ShapeDtypeStruct((rows, width), jnp.float32),
            jax.ShapeDtypeStruct((8, width), jnp.float32),
            jax.ShapeDtypeStruct((rows, width), low_type),
            jax.ShapeDtypeStruct((count, 2, rows, width), low_type),
            jax.ShapeDtypeStruct((outer_count * split, units, share), low_type),
        ),
        in_specs=[anywhere()] * 8 + [in_vmem()],
        out_specs=(anywhere(), in_vmem(), in_vmem(), anywhere(), anywhere()),
        scratch_shapes=[
            pltpu.VMEM((2, 2, rows, 2 * units), low_type),
            pltpu.VMEM(weights.shape, low_type),
            pltpu.VMEM(halves, low_type),
            pltpu.VMEM(down.shape, low_type),
            pltpu.VMEM((rows, width), values.dtype),
            pltpu.VMEM((rows, width), upstream.dtype),
            pltpu.VMEM((count, 2, rows, width), low_type),
            pltpu.VMEM((rows, width), jnp.float32),
            pltpu.VMEM((2, 2, rows, width), low_type),
            pltpu.VMEM((2, units, 512), low_type),
            pltpu.SemaphoreType.DMA((6 + 2 * count,)),
            pltpu.SemaphoreType.DMA((count + 1,)),
            pltpu.SemaphoreType.DMA((2, 2)),
            pltpu.SemaphoreType.DMA((2, 512 // share)),
        ]
        + sum_scratch(rows, width, cut, fetched=False),
        compiler_params=params(number),
        cost_estimate=cost_of(60),
    )(
        grad_gate.reshape(halves),
        grad_up.reshape(halves),
        weights,
        active.reshape(halves),
        down,
        normed,
        values,
        upstream,
        gain.reshape(1, width),
    )
    return result, gain_grad.sum(axis=0), rounded, branch.reshape(-1, width), grad_weight


def square_sum(values):
    values = values.reshape(-1, values.shape[-1]).astype(jnp.float32)
    return jnp.sum(values * values, keepdims=True)


def corner(value):
    row = lax.broadcasted_iota(jnp.int32, (8, HD), 0)
    column = lax.broadcasted_iota(jnp.int32, (8, HD), 1)
    return jnp.where((row == 0) & (column == 0), value, 0.0)


def norm_back_last(part, values, upstream, gain, extra, squared, number, name):
    rows, width = values.shape
    extras, count = len(extra), len(squared)
    cut = balanced(rows, crossing(extra, width))

    def kernel(part, values, upstream, gain, *rest):
        pieces, rest = rest[:extras], rest[extras:]
        squared, (result, gain_grad, squares), rest = (
            rest[:count],
            rest[count : count + 3],
            rest[count + 3 :],
        )
        mixed, rest = rest[:extras], rest[extras:]
        sums, rest = rest[:SUM_SCRATCH], rest[SUM_SCRATCH:]
        (total, values_v, upstream_v, load_sem), rest = rest[:4], rest[4:]
        squared_v, sems = rest[:count], rest[count:]
        steps, from_tp, from_near = plan_sum_of(part, total, sums, cut)
        copies = plan_exchanges(pieces, mixed, sems)
        fetch = [
            pltpu.make_async_copy(source, target, load_sem.at[place])
            for place, (source, target) in enumerate(
                zip((values, upstream) + tuple(squared), (values_v, upstream_v) + tuple(squared_v))
            )
        ]
        greet(EVERYONE_NEAR)
        steps[0]()
        for copy in copies:
            copy.start()
        for copy in fetch:
            copy.start()
        steps[1]()
        for copy in fetch:
            copy.wait()
        squares[...] = corner(sum(square_sum(ref[...]) for ref in squared_v))
        steps[2]()
        gain_grad[...] = jnp.zeros_like(gain_grad)
        steps[3]()

        def finish(at):
            grad = total[at] + read(from_tp, at) + read(from_near, at)
            back, by_gain = norm_back(read(values_v, at), gain[...], grad)
            gain_grad[...] += by_gain.reshape(CHUNK // 8, 8, width).sum(axis=0)
            result[at] = (upstream_v[at] + back).astype(jnp.bfloat16)

        row_loop(rows, finish)
        for copy in copies:
            copy.wait()

    return pl.pallas_call(
        kernel,
        name=name,
        out_shape=(
            jax.ShapeDtypeStruct((rows, width), jnp.bfloat16),
            jax.ShapeDtypeStruct((8, width), jnp.float32),
            jax.ShapeDtypeStruct((8, HD), jnp.float32),
        )
        + tuple(like(piece) for piece in extra),
        in_specs=[anywhere()] * 3 + [in_vmem()] * (1 + extras) + [anywhere()] * count,
        out_specs=(in_vmem(), in_vmem(), in_vmem()) + (anywhere(),) * extras,
        scratch_shapes=sum_scratch(rows, width, cut)
        + [
            pltpu.VMEM((rows, width), jnp.float32),
            pltpu.VMEM((rows, width), values.dtype),
            pltpu.VMEM((rows, width), upstream.dtype),
            pltpu.SemaphoreType.DMA((2 + count,)),
        ]
        + [pltpu.VMEM(each.shape, each.dtype) for each in squared]
        + exchange_scratch() * extras,
        compiler_params=params(number),
        cost_estimate=cost_of(65),
    )(spread(part, rows), values, upstream, gain.reshape(1, width), *extra, *squared)


def total_everywhere(values, first, squares, pieces, outer_count, number, name):
    gains = values.shape[0]
    shape = (gains + 8, HD)
    width = first.shape[1]

    def kernel(values, first, squares, pieces, out, norm, factor, mixed, layer, outers, send, recv, *sems):
        near, core, tp = spots()
        outer = lax.axis_index("outer")
        partners = [
            flipped(a, b, c)
            for a in range(NEAR)
            for b in range(CORE)
            for c in range(2)
            if a + b + c
        ]
        partners += [{"outer": (outer + step) % outer_count} for step in range(1, outer_count)]
        barrier = pltpu.get_barrier_semaphore()
        for partner in partners:
            pl.semaphore_signal(barrier, inc=1, device_id=partner, device_id_type=MESH_ID)
        pl.semaphore_wait(barrier, len(partners))

        def share(slots, mine, first, count):
            copies = []
            for number in range(first, first + count):
                copy = pltpu.make_async_remote_copy(
                    src_ref=slots.at[mine],
                    dst_ref=slots.at[mine],
                    send_sem=send.at[number],
                    recv_sem=recv.at[number],
                    device_id=partners[number],
                    device_id_type=MESH_ID,
                )
                copy.start()
                copies.append(copy)
            return copies

        mine = near * (CORE * 2) + core * 2 + tp
        layer[mine, :gains] = values[...]
        layer[mine, gains:] = squares[...] + corner(square_sum(pieces[...]))
        sums = jnp.sum(first[...], axis=0, keepdims=True)
        for place in range(width // HD):
            layer[mine, place : place + 1] = sums[:, place * HD : (place + 1) * HD]
        copies = share(layer, mine, 0, 7)
        others = plan_exchange(pieces, mixed, *sems)
        for copy in others:
            copy.start()
        for copy in copies:
            copy.wait()
        total = layer[0]
        for slot in range(1, 8):
            total = total + layer[slot]
        outers[outer] = total
        for copy in share(outers, outer, 7, outer_count - 1):
            copy.wait()
        total = outers[0]
        for slot in range(1, outer_count):
            total = total + outers[slot]
        out[...] = total
        gain_part = total[:gains]
        root = jnp.sqrt(
            jnp.sum(gain_part * gain_part, keepdims=True) + jnp.sum(total[gains:], keepdims=True)
        )
        norm[...] = jnp.broadcast_to(root, norm.shape)
        factor[...] = jnp.broadcast_to(
            jnp.minimum(1.0, clip_norm / (root + 1e-06)), factor.shape
        )
        for copy in others:
            copy.wait()

    tile = jax.ShapeDtypeStruct((8, HD), jnp.float32)
    return pl.pallas_call(
        kernel,
        name=name,
        out_shape=(jax.ShapeDtypeStruct(shape, jnp.float32), tile, tile, like(pieces)),
        in_specs=[in_vmem()] * 4,
        out_specs=(in_vmem(), in_vmem(), in_vmem(), anywhere()),
        scratch_shapes=[
            pltpu.VMEM((8,) + shape, jnp.float32),
            pltpu.VMEM((outer_count,) + shape, jnp.float32),
            pltpu.SemaphoreType.DMA((6 + outer_count,)),
            pltpu.SemaphoreType.DMA((6 + outer_count,)),
        ]
        + exchange_scratch(),
        compiler_params=params(number),
    )(values, first, squares, pieces)


def head_scale(raw, gain, cos_full, sin_full):
    normed = raw * rms_scale(raw) * gain
    return (normed * cos_full + pltpu.roll(normed, HD // 2, 1) * sin_full).astype(jnp.bfloat16)


def head_back(raw, gain, grad, cos_full, sin_full):
    grad = grad * cos_full - pltpu.roll(grad, HD // 2, 1) * sin_full
    return norm_back(raw, gain, grad)


def columns(index):
    return pl.ds(index * HD, HD)


def head_inputs(proj, gains, cos_ref, sin_ref, queries, keys, values, heads):
    for head in range(heads):
        queries[head] = head_scale(
            proj[0, :, columns(head)], gains[0:1, :], cos_ref[...], sin_ref[...]
        )
    keys[...] = head_scale(
        proj[0, :, columns(heads)], gains[1:2, :], cos_ref[...], sin_ref[...]
    )
    values[...] = proj[0, :, columns(heads + 1)].astype(jnp.bfloat16)


def masked_scores(stacked, keys, step, length):
    scores = lax.dot_general(
        stacked, keys, (((1,), (1,)), ((), ())), preferred_element_type=jnp.float32
    ) * (HD ** (-0.5))
    row = lax.broadcasted_iota(jnp.int32, scores.shape, 0) % BLOCK + step * BLOCK
    column = lax.broadcasted_iota(jnp.int32, scores.shape, 1)
    return jnp.where((column <= row) & (column < length), scores, masked_score)


def stack_heads(ref, at, heads):
    return jnp.concatenate([ref[head, at] for head in range(heads)], axis=0)


def per_sequence(*shape):
    return pl.BlockSpec((1,) + shape, lambda s: (s,) + (0,) * len(shape))


def whole(*shape):
    return pl.BlockSpec(shape, lambda s: (0,) * len(shape), pipeline_mode=pl.Buffered(1))


def across_columns(left, weights, first, width, out):
    total = weights.shape[0]
    for start in range(0, total, 512):
        at = pl.ds(start, 512)
        out[0, :, at] = lax.dot_general(
            left,
            weights[at, first : first + width],
            (((1,), (1,)), ((), ())),
            preferred_element_type=jnp.float32,
        ).astype(out.dtype)


def attend(normed, weights, cotangent, extra, group_length, cos_full, sin_full, gains, heads, early, number):
    count, rows, width = normed.shape
    wide = (heads + 2) * HD
    extras = len(extra)
    own_rows = cotangent.shape[0]
    cut = balanced(early, crossing(extra, width))

    def kernel(lengths, normed, weights, cos_ref, sin_ref, gains, own, *rest):
        pieces, rest = rest[:extras], rest[extras:]
        (proj, out, logs, branch, gathered), rest = rest[:5], rest[5:]
        mixed, (queries, keys, values), sems = rest[:extras], rest[extras : extras + 3], rest[extras + 3 :]
        sequence = pl.program_id(0)
        steps = plan_gather(own, gathered, *sems[:3], cut=cut, rows=early)
        copies = plan_exchanges(pieces, mixed, sems[3:])

        @pl.when(sequence == 0)
        def _():
            greet(EVERYONE_NEAR)
            steps[0]()
            for copy in copies:
                copy.start()

        length = lengths[sequence]
        proj[0] = jnp.dot(
            normed[0], weights[:, :wide], preferred_element_type=jnp.float32
        )
        head_inputs(proj, gains, cos_ref, sin_ref, queries, keys, values, heads)
        lane = lax.broadcasted_iota(jnp.int32, (BLOCK, HD), 1)
        for step in range(rows // BLOCK):
            at = pl.ds(step * BLOCK, BLOCK)
            seen = pl.ds(0, (step + 1) * BLOCK)
            scores = masked_scores(stack_heads(queries, at, heads), keys[seen], step, length)
            top = jnp.max(scores, axis=-1, keepdims=True)
            exponent = jnp.exp(scores - top)
            total = jnp.sum(exponent, axis=-1, keepdims=True)
            probs = (exponent / total).astype(jnp.bfloat16)
            mixed_values = jnp.dot(probs, values[seen], preferred_element_type=jnp.float32)
            log_total = top + jnp.log(total)
            kept = jnp.zeros((BLOCK, HD), jnp.float32)
            for head in range(heads):
                mine = slice(head * BLOCK, (head + 1) * BLOCK)
                out[0, at, columns(head)] = mixed_values[mine].astype(jnp.bfloat16)
                kept = jnp.where(lane == head, log_total[mine], kept)
            logs[0, at] = kept
        across_columns(out[0], weights, wide, heads * HD, branch)

        @pl.when(sequence == 1)
        def _():
            steps[1]()

        @pl.when(sequence == 2)
        def _():
            steps[2]()

        @pl.when(sequence == count - 1)
        def _():
            steps[3]()
            for copy in copies:
                copy.wait()

    outs = pl.pallas_call(
        kernel,
        name="attend",
        grid=(count,),
        out_shape=(
            jax.ShapeDtypeStruct((count, rows, wide), jnp.float32),
            jax.ShapeDtypeStruct((count, rows, heads * HD), jnp.bfloat16),
            jax.ShapeDtypeStruct((count, rows, HD), jnp.float32),
            jax.ShapeDtypeStruct((count, rows, width), jnp.bfloat16),
            layer_rows(own_rows, width),
        )
        + tuple(like(piece) for piece in extra),
        in_specs=[
            pl.BlockSpec(memory_space=pltpu.SMEM),
            per_sequence(rows, width),
            whole(width, wide + heads * HD),
            whole(rows, HD),
            whole(rows, HD),
            whole(2, HD),
            whole(own_rows, width),
        ]
        + [whole(*piece.shape) for piece in extra],
        out_specs=(
            per_sequence(rows, wide),
            per_sequence(rows, heads * HD),
            per_sequence(rows, HD),
            per_sequence(rows, width),
            anywhere(),
        )
        + (anywhere(),) * extras,
        scratch_shapes=[
            pltpu.VMEM((heads, rows, HD), jnp.bfloat16),
            pltpu.VMEM((rows, HD), jnp.bfloat16),
            pltpu.VMEM((rows, HD), jnp.bfloat16),
        ]
        + gather_scratch()
        + exchange_scratch() * extras,
        compiler_params=params(number),
        cost_estimate=cost_of(50),
    )(group_length, normed, weights, cos_full, sin_full, gains, cotangent, *extra)
    return outs


def team_split(width, outer_count):
    split = TEAM if width // outer_count % (TEAM * HD) == 0 else 1
    return split, width // outer_count // split


def local_first(place):
    near, core, _ = spots()
    other_near, other_core = place // 2, place % 2
    return (near + other_near * (1 - 2 * near)) * CORE + core + other_core * (1 - 2 * core)


def ordered(*shape):
    return pl.BlockSpec((1,) + shape, lambda s: (local_first(s),) + (0,) * len(shape))


def attend_back(
    projected,
    normed,
    attended,
    own_grad,
    logs,
    weights,
    part,
    hidden,
    extra,
    outer_count,
    group_length,
    cos_full,
    sin_full,
    gains,
    heads,
    number,
):
    count, rows, wide = projected.shape
    own_rows, width = hidden.shape
    extras = len(extra)
    cut = balanced(own_rows, crossing(extra, width))

    every = wide + heads * HD
    split, share = team_split(width, outer_count)

    def kernel(
        lengths, proj, normed, attended, own_grad, logs, weights_any, cos_ref, sin_ref, gains, part, hidden, *rest
    ):
        pieces, rest = rest[:extras], rest[extras:]
        (gathered, gain_grad, back_part, output, grad_weights), rest = rest[:5], rest[5:]
        mixed, rest = rest[:extras], rest[extras:]
        (queries, keys, values, grad_att, grad_q, grad_k, grad_v_sum, summed), rest = rest[:8], rest[8:]
        (total, held, held_sem, out, grad_v, grad_sem), rest = rest[:6], rest[6:]
        (weights, staged, weights_sem, store_sem), rest = rest[:4], rest[4:]
        sums, sems, rest = rest[:SUM_SCRATCH], rest[SUM_SCRATCH : SUM_SCRATCH + 3], rest[SUM_SCRATCH + 3 :]
        place = pl.program_id(0)
        sequence = local_first(place)
        steps, from_tp, from_near = plan_sum_of(part, total, sums, cut)
        gather = plan_gather(own_grad, gathered, *sems, cut=own_rows // 2, parts=True)
        copies = plan_exchanges(pieces, mixed, rest)
        fetch_weights = pltpu.make_async_copy(weights_any, weights, weights_sem)
        store = pltpu.make_async_copy(staged, grad_weights, store_sem)

        def arrival(which):
            member = local_first(which)
            return pltpu.make_async_copy(
                gathered.at[member // CORE, member % CORE],
                grad_v.at[which % 2],
                grad_sem.at[which % 2],
            )

        fetch = pltpu.make_async_copy(hidden, held, held_sem)

        @pl.when(place == 0)
        def _():
            greet(EVERYONE_NEAR)
            gather[0]()
            steps[0]()
            fetch.start()
            fetch_weights.start()
            gain_grad[...] = jnp.zeros_like(gain_grad)
            summed[...] = jnp.zeros_like(summed)
            gather[1]()
            gather[2]()
            gather[3]()
            arrival(0).start()
            fetch_weights.wait()

        @pl.when(place == 2)
        def _():
            arrival(3).start()

        head_inputs(proj, gains, cos_ref, sin_ref, queries, keys, values, heads)
        grad_k[...] = jnp.zeros_like(grad_k)
        grad_v_sum[...] = jnp.zeros_like(grad_v_sum)
        arrival(place).wait()
        grad = grad_v[place % 2].reshape(rows, width)
        length = lengths[sequence]
        grad_att[...] = jnp.dot(
            grad, weights[:, wide:], preferred_element_type=jnp.float32
        ).astype(jnp.bfloat16)

        for step in range(rows // BLOCK):
            at = pl.ds(step * BLOCK, BLOCK)
            seen = pl.ds(0, (step + 1) * BLOCK)
            stacked = stack_heads(queries, at, heads)
            above = jnp.concatenate([grad_att[at, columns(head)] for head in range(heads)], axis=0)
            log_total = jnp.concatenate(
                [logs[0, at, head : head + 1] for head in range(heads)], axis=0
            )
            probs = jnp.exp(masked_scores(stacked, keys[seen], step, length) - log_total)
            grad_probs = lax.dot_general(
                above, values[seen], (((1,), (1,)), ((), ())), preferred_element_type=jnp.float32
            )
            inner = jnp.sum(probs * grad_probs, axis=-1, keepdims=True)
            grad_scores = (probs * (grad_probs - inner)).astype(jnp.bfloat16)
            by_query = jnp.dot(grad_scores, keys[seen], preferred_element_type=jnp.float32)
            for head in range(heads):
                grad_q[head, at] = by_query[head * BLOCK : (head + 1) * BLOCK] * (HD ** (-0.5))
            grad_k[seen] += lax.dot_general(
                grad_scores, stacked, (((0,), (0,)), ((), ())), preferred_element_type=jnp.float32
            )
            grad_v_sum[seen] += lax.dot_general(
                probs.astype(jnp.bfloat16),
                above,
                (((0,), (0,)), ((), ())),
                preferred_element_type=jnp.float32,
            )

        def settle(column, gain, value):
            back, by_gain = head_back(
                proj[0, :, columns(column)], gains[gain : gain + 1, :], value, cos_ref[...], sin_ref[...]
            )
            out[:, columns(column)] = back.astype(jnp.bfloat16)
            gain_grad[gain] += by_gain.reshape(rows // 8, 8, HD).sum(axis=0)

        for head in range(heads):
            settle(head, 0, grad_q[head])
        settle(heads, 1, grad_k[...] * (HD ** (-0.5)))
        out[:, columns(heads + 1)] = grad_v_sum[...].astype(jnp.bfloat16)

        across_columns(out[...], weights, 0, wide, back_part)

        by_projected, by_attended = out[...].T, attended[0].T
        for start in range(0, width, 512):
            at = pl.ds(start, 512)
            summed[:wide, at] += jnp.dot(
                by_projected, normed[0, :, at], preferred_element_type=jnp.float32
            )
            summed[wide:, at] += jnp.dot(
                by_attended, grad[:, start : start + 512], preferred_element_type=jnp.float32
            )

        @pl.when(place == 0)
        def _():
            gather[5]()
            steps[1]()
            for copy in copies:
                copy.start()
            gather[4]()
            arrival(1).start()

        @pl.when(place == 1)
        def _():
            steps[2]()
            gather[6]()
            arrival(2).start()

        @pl.when(place == count - 1)
        def _():
            for outer in range(outer_count):
                for member in range(split):
                    start = (outer * split + member) * share
                    staged[outer, member] = summed[:, start : start + share].astype(jnp.bfloat16)
            store.start()
            fetch.wait()
            steps[3]()

            def finish(at):
                value = total[at] + read(from_tp, at) + read(from_near, at)
                output[at] = (held[at] + value).astype(jnp.bfloat16)

            row_loop(own_rows, finish)
            store.wait()
            for copy in copies:
                copy.wait()

    return pl.pallas_call(
        kernel,
        name="attend_back",
        grid=(count,),
        out_shape=(
            layer_rows(own_rows, width),
            jax.ShapeDtypeStruct((2, 8, HD), jnp.float32),
            jax.ShapeDtypeStruct((count, rows, width), jnp.bfloat16),
            jax.ShapeDtypeStruct((own_rows, width), jnp.bfloat16),
            jax.ShapeDtypeStruct((outer_count, split, every, share), jnp.bfloat16),
        )
        + tuple(like(piece) for piece in extra),
        in_specs=[
            pl.BlockSpec(memory_space=pltpu.SMEM),
            ordered(rows, wide),
            ordered(rows, width),
            ordered(rows, heads * HD),
            whole(own_rows, width),
            ordered(rows, HD),
            anywhere(),
            whole(rows, HD),
            whole(rows, HD),
            whole(2, HD),
            anywhere(),
            anywhere(),
        ]
        + [whole(*piece.shape) for piece in extra],
        out_specs=(
            anywhere(),
            pl.BlockSpec((2, 8, HD), lambda s: (0, 0, 0)),
            ordered(rows, width),
            whole(own_rows, width),
            anywhere(),
        )
        + (anywhere(),) * extras,
        scratch_shapes=[
            pltpu.VMEM((heads, rows, HD), jnp.bfloat16),
            pltpu.VMEM((rows, HD), jnp.bfloat16),
            pltpu.VMEM((rows, HD), jnp.bfloat16),
            pltpu.VMEM((rows, heads * HD), jnp.bfloat16),
            pltpu.VMEM((heads, rows, HD), jnp.float32),
            pltpu.VMEM((rows, HD), jnp.float32),
            pltpu.VMEM((rows, HD), jnp.float32),
            pltpu.VMEM((every, width), jnp.float32),
            pltpu.VMEM((own_rows, width), jnp.float32),
            pltpu.VMEM((own_rows, width), jnp.float32),
            pltpu.SemaphoreType.DMA,
            pltpu.VMEM((rows, wide), jnp.bfloat16),
            pltpu.VMEM((2, 2, own_rows, width), jnp.bfloat16),
            pltpu.SemaphoreType.DMA((2,)),
            pltpu.VMEM(weights.shape, weights.dtype),
            pltpu.VMEM((outer_count, split, every, share), jnp.bfloat16),
            pltpu.SemaphoreType.DMA,
            pltpu.SemaphoreType.DMA,
        ]
        + sum_scratch(own_rows, width, cut)
        + gather_scratch()
        + exchange_scratch() * extras,
        compiler_params=params(number),
        cost_estimate=cost_of(50),
    )(
        group_length,
        projected,
        normed,
        attended,
        own_grad,
        logs,
        weights,
        cos_full,
        sin_full,
        gains,
        spread(part, own_rows),
        hidden,
        *extra,
    )


def feed(normed, weights, cotangent, gathered, early, number):
    count, rows, width = normed.shape
    units = weights.shape[1] // 2
    late = cotangent.shape[0] - early

    def kernel(normed, weights, own, _, product, active, out, *sems):
        steps = plan_gather(
            own, out, *sems, cut=balanced(late, 0), base=early, rows=late
        )
        sequence = pl.program_id(0)

        @pl.when(sequence == 0)
        def _():
            greet(NEIGHBOURS)
            steps[0]()

        for start in range(0, units, 256):
            gate_at, up_at = pl.ds(start, 256), pl.ds(units + start, 256)
            gate = jnp.dot(normed[0], weights[:, gate_at], preferred_element_type=jnp.float32)
            up = jnp.dot(normed[0], weights[:, up_at], preferred_element_type=jnp.float32)
            product[0, :, gate_at] = gate
            product[0, :, up_at] = up
            active[0, :, gate_at] = swish_product(gate, up).astype(jnp.bfloat16)

        for place in (1, 2, 3):

            @pl.when(sequence == count - 4 + place)
            def _(place=place):
                steps[place]()

    return pl.pallas_call(
        kernel,
        name="feed",
        grid=(count,),
        out_shape=(
            jax.ShapeDtypeStruct((count, rows, 2 * units), jnp.float32),
            jax.ShapeDtypeStruct((count, rows, units), jnp.bfloat16),
            like(gathered),
        ),
        in_specs=[
            per_sequence(rows, width),
            whole(*weights.shape),
            whole(*cotangent.shape),
            anywhere(),
        ],
        out_specs=(per_sequence(rows, 2 * units), per_sequence(rows, units), anywhere()),
        scratch_shapes=gather_scratch(),
        input_output_aliases={3: 2},
        compiler_params=params(number),
        cost_estimate=cost_of(28),
    )(normed, weights, cotangent, gathered)


def feed_back(grads, weights, product):
    count, rows, width = grads.shape
    units = weights.shape[1]

    def kernel(grads, weights, product, by_gate, by_up):
        for start in range(0, units, 256):
            gate_at, up_at = pl.ds(start, 256), pl.ds(units + start, 256)
            grad = jnp.dot(grads[0], weights[:, gate_at], preferred_element_type=jnp.float32)
            gate, up = product[0, :, gate_at], product[0, :, up_at]
            share = jax.nn.sigmoid(gate)
            slope = grad * up * share * (1.0 + gate * (1.0 - share))
            by_gate[0, :, gate_at] = slope.astype(jnp.bfloat16)
            by_up[0, :, gate_at] = (grad * gate * share).astype(jnp.bfloat16)

    return pl.pallas_call(
        kernel,
        name="feed_back",
        grid=(count,),
        out_shape=(jax.ShapeDtypeStruct((count, rows, units), jnp.bfloat16),) * 2,
        in_specs=[
            per_sequence(rows, width),
            whole(*weights.shape),
            per_sequence(rows, 2 * units),
        ],
        out_specs=(per_sequence(rows, units),) * 2,
        compiler_params=pltpu.CompilerParams(vmem_limit_bytes=VMEM_LIMIT),
        cost_estimate=cost_of(18),
    )(grads, weights, product)


def spans(widths, base=0):
    for member in range(TEAM):
        first, inside = base, 0
        for width in widths:
            share = width // TEAM
            yield member, pl.ds(first + member * share, share), pl.ds(inside, share)
            first += width
            inside += share


def by_columns(start, height, widths, source):
    def run(pieces, update):
        @pl.loop(0, height // CHUNK)
        def _(row):
            rows = pl.ds(pl.multiple_of(start + row * CHUNK, CHUNK), CHUNK)
            for member, across, inside in spans(widths):
                update(rows, across, pieces[member, rows, inside])

    return source, pl.ds(start, height), pl.ds(0, sum(widths)), run


def by_turned(height, base, widths, source, members=range(TEAM)):
    parts = [part for part in spans(widths, base) if part[0] in members]

    def run(pieces, update):
        for member, across, inside in parts:
            update(pl.ds(0, height), across, pieces[member, inside].astype(jnp.float32).T)

    if len(members) == 1:
        columns = parts[0][1]
    else:
        columns = pl.ds(base, sum(widths))
    return source, pl.ds(0, height), columns, run


def by_rows(member, height, width, inside, source):
    at, across = pl.ds(member * height, height), pl.ds(0, width)

    def run(pieces, update):
        if inside is None:
            update(at, across, pieces[member].astype(jnp.float32).T)
        else:
            update(at, across, pieces[member, pl.ds(inside, height)])

    return source, at, across, run


def adam_all(sets, pieces, factor, gain_grad, gains, passed):
    jobs = [(place,) + job for place, group in enumerate(sets) for job in group[3]]
    count, total, sources, others = len(jobs), len(sets), len(pieces), len(passed)

    def kernel(*refs):
        inputs, refs = refs[: 3 * total], refs[3 * total :]
        piece_refs, factor, refs = refs[:sources], refs[sources], refs[sources + 1 :]
        (gain_grad, *gains), refs = refs[:4], refs[4:]
        passed, refs = refs[:others], refs[others:]
        outputs, refs = refs[: 4 * total], refs[4 * total :]
        new_gains, refs = refs[:3], refs[3:]
        onward, refs = refs[:others], refs[others:]
        held, refs = refs[: 4 * total], refs[4 * total :]
        held_pieces, refs = refs[:sources], refs[sources:]
        between, (piece_sem, in_sem, out_sem, pass_sem) = refs[:others], refs[others:]
        scale = factor[0:1, 0:1]
        loads = [
            pltpu.make_async_copy(piece_refs[place], held_pieces[place], piece_sem.at[place])
            for place in range(sources)
        ]
        arrivals, stores = [], []
        kept = [
            pltpu.make_async_copy(source, target, pass_sem.at[0, place])
            for place, (source, target) in enumerate(zip(passed, between))
        ]
        kept_on = [
            pltpu.make_async_copy(source, target, pass_sem.at[1, place])
            for place, (source, target) in enumerate(zip(between, onward))
        ]
        for slot, (place, source, at, across, _) in enumerate(jobs):
            arrivals.append(
                [
                    pltpu.make_async_copy(
                        inputs[3 * place + number].at[at, across],
                        held[4 * place + number].at[at, across],
                        in_sem.at[3 * slot + number],
                    )
                    for number in range(3)
                ]
            )
        first_use = {}
        for slot, job in enumerate(jobs):
            first_use.setdefault(job[1], slot)

        def bring(slot):
            if slot < count:
                if first_use[jobs[slot][1]] == slot:
                    loads[jobs[slot][1]].start()
                for copy in arrivals[slot]:
                    copy.start()

        for slot in range(AHEAD):
            bring(slot)
        gain_step = adam_update(
            gains[0][...],
            gain_grad[: gains[0].shape[0]],
            gains[1][...],
            gains[2][...],
            scale,
            0.0,
            gain_rate,
        )
        for target, value in zip(new_gains, gain_step):
            target[...] = value
        for slot, (place, source, at, across, run) in enumerate(jobs):
            weight, moment, square, low = held[4 * place : 4 * place + 4]
            if first_use[source] == slot:
                loads[source].wait()
            for copy in arrivals[slot]:
                copy.wait()
            bring(slot + AHEAD)
            if slot == 0:
                for copy in kept:
                    copy.start()

            def update(rows, columns, gradient):
                where = (rows, columns)
                value, one, two = adam_update(
                    weight[where],
                    gradient.astype(jnp.float32),
                    moment[where],
                    square[where],
                    scale,
                    weight_decay,
                    learn_rate,
                )
                weight[where], moment[where], square[where] = value, one, two
                low[where] = value.astype(jnp.bfloat16)

            run(held_pieces[source], update)
            for number, origin in enumerate((weight, moment, square, low)):
                copy = pltpu.make_async_copy(
                    origin.at[at, across],
                    outputs[4 * place + number].at[at, across],
                    out_sem.at[4 * slot + number],
                )
                copy.start()
                stores.append(copy)
            if slot == 4:
                for arrived, copy in zip(kept, kept_on):
                    arrived.wait()
                    copy.start()
        for copy in stores + kept_on:
            copy.wait()

    args, shapes, scratch = [], [], []
    for weight, moment, square, _ in sets:
        args += [weight, moment, square]
        low = jax.ShapeDtypeStruct(weight.shape, jnp.bfloat16)
        shapes += [like(weight)] * 3 + [low]
        scratch += [pltpu.VMEM(each.shape, each.dtype) for each in (weight, moment, square, low)]
    outs = pl.pallas_call(
        kernel,
        name="adam_all",
        out_shape=tuple(shapes) + (like(gains[0]),) * 3 + tuple(like(each) for each in passed),
        in_specs=[anywhere()] * (3 * total + sources) + [in_vmem()] * 5 + [anywhere()] * others,
        out_specs=(anywhere(),) * (4 * total) + (in_vmem(),) * 3 + (anywhere(),) * others,
        scratch_shapes=scratch
        + [pltpu.VMEM(each.shape, each.dtype) for each in tuple(pieces) + tuple(passed)]
        + [
            pltpu.SemaphoreType.DMA((sources,)),
            pltpu.SemaphoreType.DMA((3 * count,)),
            pltpu.SemaphoreType.DMA((4 * count,)),
            pltpu.SemaphoreType.DMA((2, others)),
        ],
        compiler_params=pltpu.CompilerParams(vmem_limit_bytes=VMEM_LIMIT),
        cost_estimate=cost_of(15),
    )(*args, *pieces, factor, gain_grad, *gains, *passed)
    steps = [outs[4 * place : 4 * place + 4] for place in range(total)]
    return steps + [outs[4 * total : 4 * total + 3], outs[4 * total + 3 :]]


def split_columns(values, widths):
    members = []
    for member in range(TEAM):
        start, parts = 0, []
        for width in widths:
            share = width // TEAM
            first = start + member * share
            parts.append(values[:, first : first + share])
            start += width
        members.append(jnp.concatenate(parts, axis=1))
    return jnp.stack(members)


def gather_outer(mixed):
    return lax.all_gather(mixed.reshape(-1, mixed.shape[2]), "outer", axis=0, tiled=True)


def team_pieces(summed):
    return summed.reshape(TEAM, -1, summed.shape[-1])


def turned_pieces(summed):
    if summed.shape[1] * TEAM * lax.axis_size("outer") == D:
        return team_pieces(summed)
    return summed.reshape(summed.shape[0], TEAM, -1).transpose(1, 0, 2)


def sum_weight(gradient):
    return lax.psum_scatter(gradient, "outer", scatter_dimension=0, tiled=True)


def after(values, earlier):
    return lax.optimization_barrier((values, earlier))


def adam_update(weight, gradient, moment_one, moment_two, factor, decay_rate, rate_value):
    clipped = gradient * factor
    moment_one = beta_first * moment_one + (1.0 - beta_first) * clipped
    moment_two = beta_second * moment_two + (1.0 - beta_second) * clipped * clipped
    first_fixed = moment_one / (1.0 - beta_first**STEP)
    second_fixed = moment_two / (1.0 - beta_second**STEP)
    weight = weight - rate_value * (
        first_fixed / (jnp.sqrt(second_fixed) + adam_epsilon) + decay_rate * weight
    )
    return (weight, moment_one, moment_two)


def dot(left, right, contract):
    return lax.dot_general(
        left, right, ((contract[0], contract[1]), ((), ())), preferred_element_type=jnp.float32
    )


def times(left, right):
    return dot(left, right, ((1,), (0,)))


def times_across(left, right):
    return dot(left, right, ((1,), (1,)))


def over_rows(left, right):
    return dot(left, right, ((0,), (0,)))


def local(
    inputs,
    cotangent,
    lengths,
    owners,
    qkv_weight,
    out_weight,
    gate_up_weight,
    down_weight,
    norm_gains,
    qkv_moment,
    out_moment,
    gate_up_moment,
    down_moment,
    gains_moment,
    qkv_square,
    out_square,
    gate_up_square,
    down_square,
    gains_square,
):
    tp_count = lax.axis_size("tp")
    half_rows = inputs.shape[0]
    row_count = half_rows * tp_count
    heads = H // tp_count // TEAM
    hidden_units = FF // tp_count // TEAM
    qkv_widths = (H * HD // tp_count, KV * HD // tp_count, KV * HD // tp_count)
    out_widths = (H * HD // tp_count,)
    part_rows = qkv_weight.shape[0]
    gate_up_widths = (FF // tp_count, FF // tp_count)
    down_widths = (FF // tp_count,)

    first_group = lax.axis_index("outer") * TEAM
    group_ids = first_group + jnp.arange(TEAM)
    group_length = jnp.sum(
        jnp.where(owners[None, :] == group_ids[:, None], lengths[None, :], 0), axis=1
    )
    own_group = lax.axis_index("near") * CORE + lax.axis_index("core")
    own_rows = lax.axis_index("tp") * half_rows + jnp.arange(half_rows)
    valid_rows = (own_rows < pick(group_length, own_group))[:, None]
    half_width = HD // 2
    frequency = rope_base ** (-(jnp.arange(half_width, dtype=jnp.float32) * 2.0 / HD))
    angles = jnp.arange(row_count, dtype=jnp.float32)[:, None] * frequency[None, :]
    cosine, sine = jnp.cos(angles), jnp.sin(angles)
    cos_full = jnp.concatenate([cosine, cosine], axis=1)
    sin_full = jnp.concatenate([-sine, sine], axis=1)
    attn_gain = norm_gains[:D]
    mlp_gain = norm_gains[D : 2 * D]
    head_gains = norm_gains[2 * D :].reshape(2, HD)

    first_pieces = jnp.concatenate(
        [
            split_columns(qkv_weight.astype(jnp.bfloat16), qkv_widths),
            split_columns(out_weight.astype(jnp.bfloat16).T, out_widths),
        ],
        axis=2,
    )
    gate_up_pieces = split_columns(gate_up_weight.astype(jnp.bfloat16), gate_up_widths)
    down_pieces = split_columns(down_weight.astype(jnp.bfloat16).T, down_widths)
    first_mixed = exchange(first_pieces, 6, "exchange_first")
    first_full = gather_outer(first_mixed)
    qkv_full = first_full[:, : (heads + 2) * HD]

    residual_in = inputs.astype(jnp.float32)
    normed_attn = residual_in * rms_scale(residual_in) * attn_gain
    grad_low = jnp.where(valid_rows, cotangent, jnp.zeros_like(cotangent))
    normed_attn, first_mixed, grad_low, down_pieces, cos_full, sin_full = (
        lax.optimization_barrier(
            (
                normed_attn.astype(jnp.bfloat16),
                first_mixed,
                grad_low,
                down_pieces,
                cos_full,
                sin_full,
            )
        )
    )
    normed_attn, gate_up_mixed = gather_rows(
        normed_attn, (gate_up_pieces,), 0, "gather_inputs"
    )
    gate_up_full = gather_outer(gate_up_mixed)
    early = half_rows * 2 // 5 // CHUNK * CHUNK
    projected, attended, logs, attn_branch, grad_all, down_mixed = attend(
        normed_attn.reshape(TEAM, row_count, D),
        first_full,
        grad_low,
        (down_pieces,),
        group_length,
        cos_full,
        sin_full,
        head_gains,
        heads,
        early,
        1,
    )
    down_full = gather_outer(down_mixed)
    hidden, normed_mlp = branch_and_norm(attn_branch, inputs, mlp_gain, 2, "branch_and_norm")
    gate_up, activated, grad_all = feed(
        normed_mlp.reshape(TEAM, row_count, D), gate_up_full, grad_low, grad_all, early, 8
    )
    grad_down = over_rows(grad_all.reshape(-1, D), activated.reshape(-1, hidden_units))
    grad_all, grad_down = after(grad_all, grad_down.astype(jnp.bfloat16))
    down_sum = sum_weight(grad_down)
    grad_gate, grad_up = feed_back(
        grad_all.reshape(TEAM, row_count, D), down_full, gate_up
    )
    grad_gate_weight = over_rows(normed_mlp, grad_gate.reshape(-1, hidden_units))
    grad_gate, grad_gate_weight = after(grad_gate, grad_gate_weight.astype(jnp.bfloat16))
    gate_sum = sum_weight(grad_gate_weight)
    grad_hidden, grad_mlp_gain, own_grad, mlp_part, grad_up_weight = feed_back_rest(
        grad_gate,
        grad_up,
        gate_up_full,
        activated,
        down_full,
        normed_mlp,
        hidden,
        grad_low,
        mlp_gain,
        lax.axis_size("outer"),
        3,
        "feed_back_rest",
    )
    up_sum = turned_pieces(sum_weight(grad_up_weight.reshape(-1, grad_up_weight.shape[2])))
    _, grad_head_gains, grad_normed_attn, output, grad_first, down_mixed = attend_back(
        projected,
        normed_attn.reshape(TEAM, row_count, D),
        attended,
        own_grad,
        logs,
        first_full,
        mlp_part,
        hidden,
        (team_pieces(down_sum),),
        lax.axis_size("outer"),
        group_length,
        cos_full,
        sin_full,
        head_gains,
        heads,
        7,
    )
    grad_first, gate_sum = after(grad_first, gate_sum)
    first_sum = turned_pieces(sum_weight(grad_first.reshape(-1, grad_first.shape[3])))
    input_grad, attn_gain_parts, squares, gate_mixed, up_mixed = norm_back_last(
        grad_normed_attn,
        inputs,
        grad_hidden,
        attn_gain,
        (team_pieces(gate_sum), up_sum),
        (gate_sum, up_sum, down_sum),
        4,
        "norm_back_attn",
    )
    gain_part = jnp.concatenate(
        [jnp.zeros_like(grad_mlp_gain), grad_mlp_gain, grad_head_gains.sum(axis=1).reshape(-1)]
    )
    gain_count = gain_part.shape[0]
    packed = jnp.pad(gain_part, (0, -gain_count % PAD))
    packed, norm_tile, factor_tile, first_mixed = total_everywhere(
        packed.reshape(-1, HD),
        attn_gain_parts,
        squares,
        first_sum,
        lax.axis_size("outer"),
        5,
        "total_everywhere",
    )
    grad_norm = norm_tile[0, 0]
    (
        (new_gate_up, new_gate_up_one, new_gate_up_two, gate_up_copy),
        (new_down, new_down_one, new_down_two, down_copy),
        (new_out, new_out_one, new_out_two, out_copy),
        (new_qkv, new_qkv_one, new_qkv_two, qkv_copy),
        new_gains,
        (output, input_grad),
    ) = adam_all(
        [
            (
                gate_up_weight,
                gate_up_moment,
                gate_up_square,
                [
                    by_columns(start, max(CHUNK, part_rows // 4), gate_up_widths[:1], 0)
                    for start in range(0, part_rows, max(CHUNK, part_rows // 4))
                ]
                + [
                    by_turned(part_rows, gate_up_widths[0], gate_up_widths[1:], 1, (member,))
                    for member in range(TEAM)
                ],
            ),
            (
                down_weight,
                down_moment,
                down_square,
                [by_rows(member, hidden_units, part_rows, None, 2) for member in range(TEAM)],
            ),
            (
                out_weight,
                out_moment,
                out_square,
                [
                    by_rows(member, heads * HD, part_rows, (heads + 2) * HD, 3)
                    for member in range(TEAM)
                ],
            ),
            (
                qkv_weight,
                qkv_moment,
                qkv_square,
                [by_turned(part_rows, 0, qkv_widths, 3)],
            ),
        ],
        (gate_mixed, up_mixed, down_mixed, first_mixed),
        factor_tile,
        packed,
        [each.reshape(-1, HD) for each in (norm_gains, gains_moment, gains_square)],
        (output, input_grad),
    )
    new_gains, new_gains_one, new_gains_two = (each.reshape(-1) for each in new_gains)
    return (
        output,
        input_grad,
        grad_norm,
        new_qkv,
        new_qkv_one,
        new_qkv_two,
        qkv_copy,
        new_out,
        new_out_one,
        new_out_two,
        out_copy,
        new_gate_up,
        new_gate_up_one,
        new_gate_up_two,
        gate_up_copy,
        new_down,
        new_down_one,
        new_down_two,
        down_copy,
        new_gains,
        new_gains_one,
        new_gains_two,
    )


def solution(mesh):
    fsdp_count, tp_count = mesh.shape["fsdp"], mesh.shape["tp"]
    cut = mesh.devices.reshape(fsdp_count // TEAM, NEAR, CORE, tp_count)
    cut_mesh = Mesh(cut, ("outer",) + LAYER)
    fsdp = ("outer", "near", "core")
    rows = P(fsdp + ("tp",), None)
    wide = P(fsdp, "tp")
    tall = P("tp", fsdp)
    weights = (wide, tall, wide, tall, P())
    return jax.shard_map(
        local,
        mesh=cut_mesh,
        in_specs=(rows, rows, P(), P()) + weights * 3,
        out_specs=(rows, rows, P()) + (wide,) * 4 + (tall,) * 4 + (wide,) * 4 + (tall,) * 4 + (P(),) * 3,
        check_vma=False,
    )
```

```python
from functools import partial

import jax
import jax.numpy as jnp
import numpy as np
from jax import lax
from jax.experimental import pallas as pl
from jax.experimental.pallas import tpu as pltpu
from jax.sharding import Mesh, PartitionSpec as P

D = 2048
H = 16
KV = 8
HD = 128
FF = 6144
STEP = 10


norm_epsilon = 1e-06
rope_base = 1000000.0
clip_norm = 1.0
learn_rate = 0.04
gain_rate = 0.8
beta_first = 0.9
beta_second = 0.999
adam_epsilon = 1e-08
weight_decay = 0.1
masked_score = -1e30

NEAR = 2
CORE = 2
TEAM = NEAR * CORE
LAYER = ("near", "core", "tp")
BLOCK = 128
PAD = 8 * 128


def rms_scale(values):
    return lax.rsqrt(jnp.mean(values * values, axis=-1, keepdims=True) + norm_epsilon)


def swish_product(gate_part, up_part):
    return jax.nn.silu(gate_part) * up_part


MESH_ID = pl.DeviceIdType.MESH
VMEM_LIMIT = 60 * 1024 * 1024
CHUNK = 16
GATHER_COPIES = 16
AHEAD = 1000
SUM_COPIES = 10
NEIGHBOURS = ((1, 0, 0), (0, 1, 0), (0, 0, 1))
MATES = ((0, 1, 0), (1, 0, 0), (1, 1, 0))
EVERYONE_NEAR = NEIGHBOURS + ((1, 1, 0),)


def spots():
    return tuple(lax.axis_index(name) for name in LAYER)


def flipped(near_flip, core_flip, tp_flip):
    return {
        name: 1 - spot if flip else spot
        for name, spot, flip in zip(LAYER, spots(), (near_flip, core_flip, tp_flip))
    }


def greet(flips):
    barrier = pltpu.get_barrier_semaphore()
    for flip in flips:
        pl.semaphore_signal(barrier, inc=1, device_id=flipped(*flip), device_id_type=MESH_ID)
    pl.semaphore_wait(barrier, len(flips))


def link(source, target, send_sem, recv_sem, flip):
    return pltpu.make_async_remote_copy(
        src_ref=source,
        dst_ref=target,
        send_sem=send_sem,
        recv_sem=recv_sem,
        device_id=flipped(*flip),
        device_id_type=MESH_ID,
    )


TO_NEAR, TO_CORE, TO_TP = NEIGHBOURS


def plan_exchange(pieces, out, send, recv, own_sem):
    near, core, _ = spots()
    own = near * CORE + core
    copies = []
    for number, flip in enumerate(MATES):
        there = (1 - near if flip[0] else near) * CORE + (1 - core if flip[1] else core)
        copies.append(
            link(pieces.at[there], out.at[own], send.at[number], recv.at[number], flip)
        )
    copies.append(pltpu.make_async_copy(pieces.at[own], out.at[own], own_sem))
    return copies


def exchange_scratch():
    return [
        pltpu.SemaphoreType.DMA((len(MATES),)),
        pltpu.SemaphoreType.DMA((len(MATES),)),
        pltpu.SemaphoreType.DMA,
    ]


def crossing(pieces, width):
    return sum(2 * piece.shape[1] * piece.shape[2] for piece in pieces) // width


def plan_exchanges(pieces, mixed, sems):
    copies = []
    for place, (piece, result) in enumerate(zip(pieces, mixed)):
        copies += plan_exchange(piece, result, *sems[3 * place : 3 * place + 3])
    return copies


def plan_gather(own, out, send, recv, own_sem, cut, base=0, rows=None, parts=False, apart=False):
    near, core, tp = spots()
    rows = own.shape[0] if rows is None else rows
    low, high = pl.ds(base, cut), pl.ds(base + cut, rows - cut)
    all_rows = pl.ds(base, rows)

    def make(number, source, target, flip):
        return link(source, target, send.at[number], recv.at[number], flip)

    def give(number, part, flip):
        return make(number, own.at[part], out.at[near, core, tp, part], flip)

    def relay(number, where_near, where_tp, part, flip):
        ref = out.at[where_near, core, where_tp, part]
        return make(number, ref, ref, flip)

    keep = pltpu.make_async_copy(own.at[all_rows], out.at[near, core, tp, all_rows], own_sem)
    twin_own = give(4, all_rows, TO_CORE)
    first_rows = (rows - cut) // 2 // CHUNK * CHUNK
    high_parts = [
        (pl.ds(base + cut, first_rows), 1, 7, 8),
        (pl.ds(base + cut + first_rows, rows - cut - first_rows), 13, 14, 15),
    ]
    near_high = [give(number, part, TO_NEAR) for part, number, _, _ in high_parts]
    tp_high = give(2, high, TO_TP)
    far_high = [relay(number, 1 - near, tp, part, TO_TP) for part, _, number, _ in high_parts]
    twin_beside = [relay(number, 1 - near, tp, part, TO_CORE) for part, _, _, number in high_parts]
    twin_across = relay(9, near, 1 - tp, high, TO_CORE)
    twin_far = relay(12, 1 - near, 1 - tp, high, TO_CORE)
    twins = [twin_own, twin_across, twin_far] + twin_beside
    ways = near_high + far_high + [tp_high]
    if cut:
        tp_low = give(0, low, TO_TP)
        near_low = give(3, low, TO_NEAR)
        far_low = relay(5, near, 1 - tp, low, TO_NEAR)
        twin_across_low = relay(6, near, 1 - tp, low, TO_CORE)
        twin_beside_low = relay(10, 1 - near, tp, low, TO_CORE)
        twin_far_low = relay(11, 1 - near, 1 - tp, low, TO_CORE)
        twins += [twin_across_low, twin_beside_low, twin_far_low]
        ways += [tp_low, near_low, far_low]

    def begin_tp():
        if cut:
            tp_low.start()
        tp_high.start()
        twin_own.start()
        keep.start()

    def begin_near():
        for copy in near_high:
            copy.start()
        if cut:
            near_low.start()

    def begin():
        begin_near()
        begin_tp()

    def pass_on(part):
        near_high[part].wait_recv()
        far_high[part].start()
        twin_beside[part].start()

    def middle():
        if cut:
            tp_low.wait_recv()
            far_low.start()
            twin_across_low.start()
        pass_on(0)
        if not apart:
            pass_on(1)

    def later():
        tp_high.wait_recv()
        twin_across.start()
        if cut:
            near_low.wait_recv()
            twin_beside_low.start()

    def own_there():
        keep.wait()

    def twin_there():
        twin_own.wait_recv()
        twin_across.wait_recv()
        if cut:
            twin_across_low.wait_recv()

    def far_there():
        if cut:
            far_low.wait_recv()
            twin_far_low.start()
        for copy in far_high:
            copy.wait_recv()
        twin_far.start()

    def rest_there():
        for copy in twin_beside:
            copy.wait_recv()
        twin_far.wait_recv()
        if cut:
            twin_beside_low.wait_recv()
            twin_far_low.wait_recv()
        for copy in ways + twins:
            copy.wait_send()

    def finish():
        own_there()
        twin_there()
        far_there()
        rest_there()

    if parts:
        return [begin, middle, later, own_there, twin_there, far_there, rest_there]
    if apart:
        return [begin_tp, begin_near, middle, partial(pass_on, 1), later, finish]
    return [begin, middle, later, finish]


def balanced(rows, beside):
    return max(0, (rows - beside) // 2 // CHUNK * CHUNK)


def gather_scratch():
    return [
        pltpu.SemaphoreType.DMA((GATHER_COPIES,)),
        pltpu.SemaphoreType.DMA((GATHER_COPIES,)),
        pltpu.SemaphoreType.DMA,
    ]


def add_rows(target, start, count, *sources):
    @pl.loop(0, count // CHUNK)
    def _(step):
        at = pl.ds(pl.multiple_of(start + step * CHUNK, CHUNK), CHUNK)
        total = None
        for source, shift in sources:
            where = pl.ds(pl.multiple_of(start - shift + step * CHUNK, CHUNK), CHUNK)
            value = source[where].astype(jnp.float32)
            total = value if total is None else total + value
        target[at] = total.astype(target.dtype)


def plan_sum(outgoing, mine, keep, total, scratch, cut):
    theirs, way_near, way_tp, from_tp, from_near, send, recv = scratch
    rows = total.shape[0]
    low, high = pl.ds(0, cut), pl.ds(cut, rows - cut)

    def make(number, source, target, flip):
        return link(source, target, send.at[number], recv.at[number], flip)

    twin = [make(number, outgoing[number], theirs.at[number], TO_CORE) for number in range(4)]
    far, to_tp, to_near, own = mine
    far_high = make(5, far.at[high], way_tp, TO_TP)
    tp_high = make(6, to_tp.at[high], from_tp.at[high], TO_TP)
    near_high = make(9, to_near.at[high], from_near.at[high], TO_NEAR)
    ways = [far_high, tp_high, near_high]
    if cut:
        far_low = make(4, far.at[low], way_near, TO_NEAR)
        near_low = make(7, to_near.at[low], from_near.at[low], TO_NEAR)
        tp_low = make(8, to_tp.at[low], from_tp.at[low], TO_TP)
        ways += [near_low, tp_low]

    def ready(number):
        if keep:
            keep[number].wait()
        twin[number].wait_recv()

    def both(number):
        return (mine[number], 0), (theirs.at[number], 0)

    def begin(numbers=range(4)):
        for number in numbers:
            twin[number].start()
            if keep:
                keep[number].start()

    def send_far():
        ready(0)
        if cut:
            add_rows(far, 0, cut, *both(0))
            far_low.start()
        add_rows(far, cut, rows - cut, *both(0))
        far_high.start()

    def send_tp():
        ready(1)
        add_rows(to_tp, cut, rows - cut, *both(1))
        tp_high.start()

    def send_near():
        ready(2)
        if cut:
            add_rows(to_near, 0, cut, *both(2))
            near_low.start()

    def first():
        send_far()
        send_tp()
        send_near()

    def second():
        if cut:
            far_low.wait_recv()
            add_rows(to_tp, 0, cut, *both(1), (way_near, 0))
            tp_low.start()
        far_high.wait_recv()
        add_rows(to_near, cut, rows - cut, *both(2), (way_tp, cut))
        near_high.start()
        ready(3)
        add_rows(total, 0, rows, *both(3))

    def finish():
        for copy in ways[1:]:
            copy.wait_recv()
        for copy in twin + ways + ([far_low] if cut else []):
            copy.wait_send()

    return [begin, first, second, finish], (send_far, send_tp, send_near)


def plan_sum_of(part, total, scratch, cut):
    mine, local_sem, *scratch = scratch
    near, core, tp = spots()
    order = [(1 - near, 1 - tp), (near, 1 - tp), (1 - near, tp), (near, tp)]
    outgoing = [part.at[a, 1 - core, b] for a, b in order]
    keep = [
        pltpu.make_async_copy(part.at[a, core, b], mine.at[number], local_sem.at[number])
        for number, (a, b) in enumerate(order)
    ]
    blocks = [mine.at[number] for number in range(4)]
    steps, _ = plan_sum(outgoing, blocks, keep, total, scratch, cut)
    return steps, scratch[3], scratch[4]


def sum_scratch(rows, width, cut, fetched=True):
    low = jnp.bfloat16
    fetch = [pltpu.VMEM((4, rows, width), low), pltpu.SemaphoreType.DMA((4,))]
    return (fetch if fetched else []) + [
        pltpu.VMEM((4, rows, width), low),
        pltpu.VMEM((max(cut, CHUNK), width), low),
        pltpu.VMEM((rows - cut, width), low),
        pltpu.VMEM((rows, width), low),
        pltpu.VMEM((rows, width), low),
        pltpu.SemaphoreType.DMA((SUM_COPIES,)),
        pltpu.SemaphoreType.DMA((SUM_COPIES,)),
    ]


SUM_SCRATCH = 9
COST_SHARE = 1e5


def params(number):
    return pltpu.CompilerParams(
        collective_id=number, has_side_effects=True, vmem_limit_bytes=VMEM_LIMIT
    )


def cost_of(microseconds):
    return pl.CostEstimate(
        flops=0, bytes_accessed=int(microseconds * COST_SHARE), transcendentals=0
    )


def in_vmem():
    return pl.BlockSpec(memory_space=pltpu.VMEM)


def anywhere():
    return pl.BlockSpec(memory_space=pl.ANY)


def like(array):
    return jax.ShapeDtypeStruct(array.shape, array.dtype)


def layer_rows(rows, width):
    return jax.ShapeDtypeStruct((NEAR, CORE, 2, rows, width), jnp.bfloat16)


def row_loop(rows, body):
    @pl.loop(0, rows // CHUNK)
    def _(step):
        body(pl.ds(pl.multiple_of(step * CHUNK, CHUNK), CHUNK))


def plan_line(blocks, send, recv, count):
    own = lax.axis_index("outer")

    def message(side, number):
        block = blocks.at[own - number if side == 0 else own + number]
        return pltpu.make_async_remote_copy(
            src_ref=block,
            dst_ref=block,
            send_sem=send.at[side, number],
            recv_sem=recv.at[side, number],
            device_id={"outer": own + 1 if side == 0 else own - 1},
            device_id_type=MESH_ID,
        )

    def arrival(side, number):
        block = blocks.at[own - 1 - number if side == 0 else own + 1 + number]
        return pltpu.make_async_remote_copy(
            src_ref=block,
            dst_ref=block,
            send_sem=send.at[side, number],
            recv_sem=recv.at[side, number],
            device_id={"outer": own + 1 if side == 0 else own - 1},
            device_id_type=MESH_ID,
        )

    def sends(side, number):
        if side == 0:
            return (own < count - 1) & (own >= number)
        return (own > 0) & (own + number < count)

    def gets(side, number):
        return own >= number + 1 if side == 0 else own + 1 + number < count

    def push(number):
        for side in range(2):

            @pl.when(sends(side, number))
            def _(side=side):
                message(side, number).start()

    def take(number):
        for side in range(2):

            @pl.when(gets(side, number))
            def _(side=side):
                arrival(side, number).wait_recv()

            if number + 2 < count:

                @pl.when(sends(side, number + 1))
                def _(side=side):
                    message(side, number + 1).start()

    def settle():
        for number in range(count - 1):
            for side in range(2):

                @pl.when(sends(side, number))
                def _(side=side, number=number):
                    message(side, number).wait_send()

    return push, take, settle


def greet_all(flips, count):
    barrier = pltpu.get_barrier_semaphore()
    own = lax.axis_index("outer")
    for flip in flips:
        pl.semaphore_signal(barrier, inc=1, device_id=flipped(*flip), device_id_type=MESH_ID)
    for there, neighbour in ((own < count - 1, own + 1), (own > 0, own - 1)):

        @pl.when(there)
        def _(neighbour=neighbour):
            pl.semaphore_signal(
                barrier, inc=1, device_id={"outer": neighbour}, device_id_type=MESH_ID
            )

    beside = jnp.where(own < count - 1, 1, 0) + jnp.where(own > 0, 1, 0)
    pl.semaphore_wait(barrier, len(flips) + beside)


def sequence_length(lengths, owners, group):
    total = jnp.int32(0)
    for place in range(lengths.shape[0]):
        total += jnp.where(owners[place] == group, lengths[place], 0)
    return total


def opening(
    qkv, out_weight, gate_up, down, inputs, gain, cotangent, lengths, owners, outer_count, number
):
    rows, width = inputs.shape
    part_rows, wide = qkv.shape
    tall, units = out_weight.shape[0], down.shape[0]
    widths = (wide // 2, wide // 4, wide // 4)
    first_shape = jax.ShapeDtypeStruct((TEAM, part_rows, (wide + tall) // TEAM), jnp.bfloat16)
    gate_up_shape = jax.ShapeDtypeStruct((TEAM, part_rows, 2 * units // TEAM), jnp.bfloat16)
    down_shape = jax.ShapeDtypeStruct((TEAM, part_rows, units // TEAM), jnp.bfloat16)
    cut = balanced(rows, crossing((first_shape, gate_up_shape), width))

    def kernel(
        lengths, owners, qkv, out_weight, inputs, gain, gate_up, down, cotangent,
        out, mixed, full, low, down_pieces,
        normed, first, pieces, gate_up_v, down_v, cotangent_v, load_sem, line_send, line_recv, *sems
    ):
        near, core, tp = spots()
        outer = lax.axis_index("outer")
        begin_tp, begin_near, middle, middle_rest, later, finish = plan_gather(
            normed, out, *sems[:3], cut=cut, apart=True
        )
        team = plan_exchange(first, full.at[outer], *sems[3:6])
        others = plan_exchange(pieces, mixed, *sems[6:9])
        push, take, settle = plan_line(full, line_send, line_recv, outer_count)
        fetch = [
            pltpu.make_async_copy(source, target, load_sem.at[place])
            for place, (source, target) in enumerate(
                ((cotangent, cotangent_v), (gate_up, gate_up_v), (down, down_v))
            )
        ]
        for copy in fetch:
            copy.start()
        for member, across, inside in spans(widths):
            first[member, :, inside] = qkv[:, across].astype(jnp.bfloat16)
        for member in range(TEAM):
            at = pl.ds(member * (tall // TEAM), tall // TEAM)
            first[member, :, wide // TEAM :] = out_weight[at].astype(jnp.bfloat16).T
        greet_all(EVERYONE_NEAR, outer_count)
        for copy in team:
            copy.start()

        def prepare(at):
            value = inputs[at].astype(jnp.float32)
            normed[at] = (value * rms_scale(value) * gain[...]).astype(jnp.bfloat16)

        row_loop(rows, prepare)
        begin_tp()
        fetch[1].wait()
        for member, across, inside in spans((units, units)):
            pieces[member, :, inside] = gate_up_v[:, across].astype(jnp.bfloat16)
        for copy in team:
            copy.wait()
        push(0)
        begin_near()
        length = sequence_length(lengths, owners, outer * TEAM + near * CORE + core)
        fetch[0].wait()

        def mask(at):
            row = lax.broadcasted_iota(jnp.int32, (CHUNK, width), 0) + at.start + tp * rows
            value = jnp.where(row < length, cotangent_v[at].astype(jnp.float32), 0.0)
            low[at] = value.astype(jnp.bfloat16)

        row_loop(rows, mask)
        fetch[2].wait()
        for member in range(TEAM):
            at = pl.ds(member * (units // TEAM), units // TEAM)
            down_pieces[member] = down_v[at].astype(jnp.bfloat16).T
        middle()
        take(0)
        middle_rest()
        for copy in others:
            copy.start()
        later()
        for step in range(1, outer_count - 1):
            take(step)
        finish()
        settle()
        for copy in others:
            copy.wait()

    scalars = pl.BlockSpec(memory_space=pltpu.SMEM)
    outs = pl.pallas_call(
        kernel,
        name="opening",
        out_shape=(
            layer_rows(rows, width),
            gate_up_shape,
            jax.ShapeDtypeStruct((outer_count,) + first_shape.shape, jnp.bfloat16),
            jax.ShapeDtypeStruct((rows, width), jnp.bfloat16),
            down_shape,
        ),
        in_specs=[scalars] * 2 + [in_vmem()] * 4 + [anywhere()] * 3,
        out_specs=(anywhere(),) * 3 + (in_vmem(),) * 2,
        scratch_shapes=[
            pltpu.VMEM((rows, width), jnp.bfloat16),
            pltpu.VMEM(first_shape.shape, jnp.bfloat16),
            pltpu.VMEM(gate_up_shape.shape, jnp.bfloat16),
            pltpu.VMEM(gate_up.shape, gate_up.dtype),
            pltpu.VMEM(down.shape, down.dtype),
            pltpu.VMEM(cotangent.shape, cotangent.dtype),
            pltpu.SemaphoreType.DMA((3,)),
            pltpu.SemaphoreType.DMA((2, outer_count)),
            pltpu.SemaphoreType.DMA((2, outer_count)),
        ]
        + gather_scratch()
        + exchange_scratch() * 2,
        compiler_params=params(number),
        cost_estimate=cost_of(60),
    )(
        lengths,
        owners,
        qkv,
        out_weight,
        inputs,
        gain.reshape(1, width),
        gate_up,
        down,
        cotangent,
    )
    gathered, mixed, full, low, down_pieces = outs
    return (
        gathered.reshape(-1, width),
        mixed,
        full.reshape(-1, first_shape.shape[2]),
        low,
        down_pieces,
    )


def spread(part, rows):
    return part.reshape(NEAR, CORE, 2, rows, part.shape[-1])


def read(ref, at):
    return ref[at].astype(jnp.float32)


def branch_and_norm(part, residual, gain, number, name):
    rows, width = residual.shape
    cut = rows // 2

    def kernel(part, residual, gain, hidden, out, *scratch):
        normed, sems = scratch[SUM_SCRATCH], scratch[SUM_SCRATCH + 1 :]
        steps, from_tp, from_near = plan_sum_of(part, hidden, scratch[:SUM_SCRATCH], cut)
        onward = plan_gather(normed, out, *sems, cut=cut)
        greet(NEIGHBOURS)
        for step in steps:
            step()

        def finish(at):
            value = hidden[at] + read(from_tp, at) + read(from_near, at)
            value = read(residual, at) + value
            hidden[at] = value
            normed[at] = (value * rms_scale(value) * gain[...]).astype(jnp.bfloat16)

        row_loop(rows, finish)
        for step in onward:
            step()

    hidden, full = pl.pallas_call(
        kernel,
        name=name,
        out_shape=(jax.ShapeDtypeStruct((rows, width), jnp.float32), layer_rows(rows, width)),
        in_specs=[anywhere(), in_vmem(), in_vmem()],
        out_specs=(in_vmem(), anywhere()),
        scratch_shapes=sum_scratch(rows, width, cut)
        + [pltpu.VMEM((rows, width), jnp.bfloat16)]
        + gather_scratch(),
        compiler_params=params(number),
        cost_estimate=cost_of(95),
    )(spread(part, rows), residual, gain.reshape(1, width))
    return hidden, full.reshape(-1, width)


def norm_back(value, gain, grad):
    scale = rms_scale(value)
    scaled = grad * gain
    inner = jnp.mean(scaled * value, axis=-1, keepdims=True)
    return scale * scaled - value * (scale * scale * scale * inner), grad * value * scale


def sequence_order():
    near, core, _ = spots()
    return [
        (near if place >= 2 else 1 - near) * CORE + (core if place % 2 else 1 - core)
        for place in range(TEAM)
    ]


def times_turned(left, weights, target):
    for start in range(0, weights.shape[0], 512):
        at = pl.ds(start, 512)
        target[:, at] = lax.dot_general(
            left, weights[at, :], (((1,), (1,)), ((), ())), preferred_element_type=jnp.float32
        ).astype(target.dtype)


def feed_back_rest(
    grad_gate, grad_up, weights, active, down, normed, values, upstream, gain, outer_count, number, name
):
    rows, width = values.shape
    count, both_rows, units = grad_gate.shape
    all_rows = count * both_rows
    past = all_rows - width
    cut = rows // 2
    split, share = team_split(width, outer_count)
    turns = width // 512

    def kernel(
        gate, ups, weights, active, down, normed, values, upstream, gain,
        result, gain_grad, low, branch, grad_weight, *scratch
    ):
        (grad_v, weights_v, active_v, down_v, values_v, upstream_v, parts, total), rest = (
            scratch[:8],
            scratch[8:],
        )
        (shares, staged, load_sem, store_sem, chunk_sem, piece_sem), sums = rest[:6], rest[6:]
        from_tp, from_near = sums[3], sums[4]
        near, core, tp = spots()
        members = sequence_order()
        outgoing = [parts.at[place, half] for place, half in ((0, 1 - tp), (2, 1 - tp), (0, tp), (2, tp))]
        mine = [parts.at[place, half] for place, half in ((1, 1 - tp), (3, 1 - tp), (1, tp), (3, tp))]
        steps, (send_far, send_tp, send_near) = plan_sum(outgoing, mine, (), total, sums, cut)
        stores = [
            pltpu.make_async_copy(shares.at[place % 2], branch.at[place], store_sem.at[place])
            for place in range(count)
        ]
        fetch = [
            pltpu.make_async_copy(source, target, load_sem.at[place])
            for place, (source, target) in enumerate(
                (
                    (weights, weights_v),
                    (values, values_v),
                    (upstream, upstream_v),
                    (active, active_v),
                    (down, down_v),
                    (ups, active_v),
                )
            )
        ]
        grads = []
        for place, member in enumerate(members):
            for side, source in enumerate((gate, ups)):
                grads.append(
                    pltpu.make_async_copy(
                        source.at[member],
                        grad_v.at[place % 2, :, :, pl.ds(side * units, units)],
                        load_sem.at[6 + 2 * place + side],
                    )
                )

        def bring(place):
            grads[2 * place].start()
            grads[2 * place + 1].start()

        def brought(place):
            grads[2 * place].wait()
            grads[2 * place + 1].wait()

        def back(place, half):
            times_turned(grad_v[place % 2, half], weights_v, parts.at[place, half])

        def chunk(turn):
            at, slot = pl.ds(turn * 512, 512), turn % 2
            return [
                pltpu.make_async_copy(
                    normed.at[pl.ds(0, width), at],
                    weights_v.at[:, pl.ds(slot * 1024, 512)],
                    chunk_sem.at[slot, 0],
                ),
                pltpu.make_async_copy(
                    normed.at[pl.ds(width, past), at],
                    weights_v.at[pl.ds(slot * past, past), pl.ds(512, 512)],
                    chunk_sem.at[slot, 1],
                ),
            ]

        def pieces(turn):
            slot = turn % 2
            return [
                pltpu.make_async_copy(
                    staged.at[slot, :, pl.ds(place * share, share)],
                    grad_weight.at[turn * (512 // share) + place],
                    piece_sem.at[slot, place],
                )
                for place in range(512 // share)
            ]

        fetch[0].start()
        bring(0)
        bring(1)
        greet(NEIGHBOURS)
        fetch[0].wait()
        brought(0)
        back(0, 1 - tp)
        steps[0]((0,))
        brought(1)
        back(1, 1 - tp)
        send_far()
        back(0, tp)
        steps[0]((2,))
        bring(2)
        for place in (3, 4, 1, 2):
            fetch[place].start()
        back(1, tp)
        send_near()
        bring(3)
        brought(2)
        back(2, 1 - tp)
        steps[0]((1,))
        brought(3)
        back(3, 1 - tp)
        send_tp()
        back(2, tp)
        steps[0]((3,))
        back(3, tp)
        for turn in (0, 1):
            for copy in chunk(turn):
                copy.start()
        fetch[3].wait()
        fetch[4].wait()
        for place in range(count):
            if place >= 2:
                stores[place - 2].wait()
            for half in range(2):
                times_turned(active_v[place, half], down_v, shares.at[place % 2, half])
            stores[place].start()
        fetch[5].start()
        steps[2]()
        fetch[5].wait()
        for turn in range(turns):
            slot = turn % 2
            for copy in chunk(turn):
                copy.wait()
            left = active_v[...].reshape(all_rows, units)
            product = lax.dot_general(
                left[:width],
                weights_v[:, slot * 1024 : slot * 1024 + 512],
                (((0,), (0,)), ((), ())),
                preferred_element_type=jnp.float32,
            ) + lax.dot_general(
                left[width:],
                weights_v[slot * past : (slot + 1) * past, 512:1024],
                (((0,), (0,)), ((), ())),
                preferred_element_type=jnp.float32,
            )
            if turn >= 2:
                for copy in pieces(turn - 2):
                    copy.wait()
            staged[slot] = product.astype(staged.dtype)
            for copy in pieces(turn):
                copy.start()
            if turn + 2 < turns:
                for copy in chunk(turn + 2):
                    copy.start()
        fetch[1].wait()
        fetch[2].wait()
        gain_grad[...] = jnp.zeros_like(gain_grad)
        steps[3]()

        def finish(at):
            grad = total[at] + read(from_tp, at) + read(from_near, at)
            turned, by_gain = norm_back(values_v[at], gain[...], grad)
            gain_grad[...] += by_gain.reshape(CHUNK // 8, 8, width).sum(axis=0)
            value = read(upstream_v, at) + turned
            total[at] = value
            low[at] = value.astype(jnp.bfloat16)

        row_loop(rows, finish)
        store = pltpu.make_async_copy(total, result, store_sem.at[count])
        store.start()
        for turn in range(max(0, turns - 2), turns):
            for copy in pieces(turn):
                copy.wait()
        for copy in [store] + stores[2:]:
            copy.wait()

    low_type = jnp.bfloat16
    halves = (count, 2, rows, units)
    result, gain_grad, rounded, branch, grad_weight = pl.pallas_call(
        kernel,
        name=name,
        out_shape=(
            jax.ShapeDtypeStruct((rows, width), jnp.float32),
            jax.ShapeDtypeStruct((8, width), jnp.float32),
            jax.ShapeDtypeStruct((rows, width), low_type),
            jax.ShapeDtypeStruct((count, 2, rows, width), low_type),
            jax.ShapeDtypeStruct((outer_count * split, units, share), low_type),
        ),
        in_specs=[anywhere()] * 8 + [in_vmem()],
        out_specs=(anywhere(), in_vmem(), in_vmem(), anywhere(), anywhere()),
        scratch_shapes=[
            pltpu.VMEM((2, 2, rows, 2 * units), low_type),
            pltpu.VMEM(weights.shape, low_type),
            pltpu.VMEM(halves, low_type),
            pltpu.VMEM(down.shape, low_type),
            pltpu.VMEM((rows, width), values.dtype),
            pltpu.VMEM((rows, width), upstream.dtype),
            pltpu.VMEM((count, 2, rows, width), low_type),
            pltpu.VMEM((rows, width), jnp.float32),
            pltpu.VMEM((2, 2, rows, width), low_type),
            pltpu.VMEM((2, units, 512), low_type),
            pltpu.SemaphoreType.DMA((6 + 2 * count,)),
            pltpu.SemaphoreType.DMA((count + 1,)),
            pltpu.SemaphoreType.DMA((2, 2)),
            pltpu.SemaphoreType.DMA((2, 512 // share)),
        ]
        + sum_scratch(rows, width, cut, fetched=False),
        compiler_params=params(number),
        cost_estimate=cost_of(60),
    )(
        grad_gate.reshape(halves),
        grad_up.reshape(halves),
        weights,
        active.reshape(halves),
        down,
        normed,
        values,
        upstream,
        gain.reshape(1, width),
    )
    return result, gain_grad.sum(axis=0), rounded, branch.reshape(-1, width), grad_weight


def square_sum(values):
    values = values.reshape(-1, values.shape[-1]).astype(jnp.float32)
    return jnp.sum(values * values, keepdims=True)


def corner(value):
    row = lax.broadcasted_iota(jnp.int32, (8, HD), 0)
    column = lax.broadcasted_iota(jnp.int32, (8, HD), 1)
    return jnp.where((row == 0) & (column == 0), value, 0.0)


def norm_back_last(part, values, upstream, gain, extra, squared, number, name):
    rows, width = values.shape
    extras, count = len(extra), len(squared)
    cut = balanced(rows, crossing(extra, width))

    def kernel(part, values, upstream, gain, *rest):
        pieces, rest = rest[:extras], rest[extras:]
        squared, (result, gain_grad, squares), rest = (
            rest[:count],
            rest[count : count + 3],
            rest[count + 3 :],
        )
        mixed, rest = rest[:extras], rest[extras:]
        sums, rest = rest[:SUM_SCRATCH], rest[SUM_SCRATCH:]
        (total, values_v, upstream_v, load_sem), rest = rest[:4], rest[4:]
        squared_v, sems = rest[:count], rest[count:]
        steps, from_tp, from_near = plan_sum_of(part, total, sums, cut)
        copies = plan_exchanges(pieces, mixed, sems)
        fetch = [
            pltpu.make_async_copy(source, target, load_sem.at[place])
            for place, (source, target) in enumerate(
                zip((values, upstream) + tuple(squared), (values_v, upstream_v) + tuple(squared_v))
            )
        ]
        greet(EVERYONE_NEAR)
        steps[0]()
        for copy in copies:
            copy.start()
        for copy in fetch:
            copy.start()
        steps[1]()
        for copy in fetch:
            copy.wait()
        squares[...] = corner(sum(square_sum(ref[...]) for ref in squared_v))
        steps[2]()
        gain_grad[...] = jnp.zeros_like(gain_grad)
        steps[3]()

        def finish(at):
            grad = total[at] + read(from_tp, at) + read(from_near, at)
            back, by_gain = norm_back(read(values_v, at), gain[...], grad)
            gain_grad[...] += by_gain.reshape(CHUNK // 8, 8, width).sum(axis=0)
            result[at] = (upstream_v[at] + back).astype(jnp.bfloat16)

        row_loop(rows, finish)
        for copy in copies:
            copy.wait()

    return pl.pallas_call(
        kernel,
        name=name,
        out_shape=(
            jax.ShapeDtypeStruct((rows, width), jnp.bfloat16),
            jax.ShapeDtypeStruct((8, width), jnp.float32),
            jax.ShapeDtypeStruct((8, HD), jnp.float32),
        )
        + tuple(like(piece) for piece in extra),
        in_specs=[anywhere()] * 3 + [in_vmem()] * (1 + extras) + [anywhere()] * count,
        out_specs=(in_vmem(), in_vmem(), in_vmem()) + (anywhere(),) * extras,
        scratch_shapes=sum_scratch(rows, width, cut)
        + [
            pltpu.VMEM((rows, width), jnp.float32),
            pltpu.VMEM((rows, width), values.dtype),
            pltpu.VMEM((rows, width), upstream.dtype),
            pltpu.SemaphoreType.DMA((2 + count,)),
        ]
        + [pltpu.VMEM(each.shape, each.dtype) for each in squared]
        + exchange_scratch() * extras,
        compiler_params=params(number),
        cost_estimate=cost_of(65),
    )(spread(part, rows), values, upstream, gain.reshape(1, width), *extra, *squared)


def total_everywhere(values, first, squares, pieces, outer_count, number, name):
    gains = values.shape[0]
    shape = (gains + 8, HD)
    width = first.shape[1]

    def kernel(values, first, squares, pieces, out, norm, factor, mixed, layer, outers, send, recv, *sems):
        near, core, tp = spots()
        outer = lax.axis_index("outer")
        partners = [
            flipped(a, b, c)
            for a in range(NEAR)
            for b in range(CORE)
            for c in range(2)
            if a + b + c
        ]
        partners += [{"outer": (outer + step) % outer_count} for step in range(1, outer_count)]
        barrier = pltpu.get_barrier_semaphore()
        for partner in partners:
            pl.semaphore_signal(barrier, inc=1, device_id=partner, device_id_type=MESH_ID)
        pl.semaphore_wait(barrier, len(partners))

        def share(slots, mine, first, count):
            copies = []
            for number in range(first, first + count):
                copy = pltpu.make_async_remote_copy(
                    src_ref=slots.at[mine],
                    dst_ref=slots.at[mine],
                    send_sem=send.at[number],
                    recv_sem=recv.at[number],
                    device_id=partners[number],
                    device_id_type=MESH_ID,
                )
                copy.start()
                copies.append(copy)
            return copies

        mine = near * (CORE * 2) + core * 2 + tp
        layer[mine, :gains] = values[...]
        layer[mine, gains:] = squares[...] + corner(square_sum(pieces[...]))
        sums = jnp.sum(first[...], axis=0, keepdims=True)
        for place in range(width // HD):
            layer[mine, place : place + 1] = sums[:, place * HD : (place + 1) * HD]
        copies = share(layer, mine, 0, 7)
        others = plan_exchange(pieces, mixed, *sems)
        for copy in others:
            copy.start()
        for copy in copies:
            copy.wait()
        total = layer[0]
        for slot in range(1, 8):
            total = total + layer[slot]
        outers[outer] = total
        for copy in share(outers, outer, 7, outer_count - 1):
            copy.wait()
        total = outers[0]
        for slot in range(1, outer_count):
            total = total + outers[slot]
        out[...] = total
        gain_part = total[:gains]
        root = jnp.sqrt(
            jnp.sum(gain_part * gain_part, keepdims=True) + jnp.sum(total[gains:], keepdims=True)
        )
        norm[...] = jnp.broadcast_to(root, norm.shape)
        factor[...] = jnp.broadcast_to(
            jnp.minimum(1.0, clip_norm / (root + 1e-06)), factor.shape
        )
        for copy in others:
            copy.wait()

    tile = jax.ShapeDtypeStruct((8, HD), jnp.float32)
    return pl.pallas_call(
        kernel,
        name=name,
        out_shape=(jax.ShapeDtypeStruct(shape, jnp.float32), tile, tile, like(pieces)),
        in_specs=[in_vmem()] * 4,
        out_specs=(in_vmem(), in_vmem(), in_vmem(), anywhere()),
        scratch_shapes=[
            pltpu.VMEM((8,) + shape, jnp.float32),
            pltpu.VMEM((outer_count,) + shape, jnp.float32),
            pltpu.SemaphoreType.DMA((6 + outer_count,)),
            pltpu.SemaphoreType.DMA((6 + outer_count,)),
        ]
        + exchange_scratch(),
        compiler_params=params(number),
    )(values, first, squares, pieces)


def head_scale(raw, gain, cos_full, sin_full):
    normed = raw * rms_scale(raw) * gain
    return (normed * cos_full + pltpu.roll(normed, HD // 2, 1) * sin_full).astype(jnp.bfloat16)


def head_back(raw, gain, grad, cos_full, sin_full):
    grad = grad * cos_full - pltpu.roll(grad, HD // 2, 1) * sin_full
    return norm_back(raw, gain, grad)


def columns(index):
    return pl.ds(index * HD, HD)


def head_inputs(proj, gains, cos_ref, sin_ref, queries, keys, values, heads):
    for head in range(heads):
        queries[head] = head_scale(
            proj[0, :, columns(head)], gains[0:1, :], cos_ref[...], sin_ref[...]
        )
    keys[...] = head_scale(
        proj[0, :, columns(heads)], gains[1:2, :], cos_ref[...], sin_ref[...]
    )
    values[...] = proj[0, :, columns(heads + 1)].astype(jnp.bfloat16)


def masked_scores(stacked, keys, step, length):
    scores = lax.dot_general(
        stacked, keys, (((1,), (1,)), ((), ())), preferred_element_type=jnp.float32
    ) * (HD ** (-0.5))
    row = lax.broadcasted_iota(jnp.int32, scores.shape, 0) % BLOCK + step * BLOCK
    column = lax.broadcasted_iota(jnp.int32, scores.shape, 1)
    return jnp.where((column <= row) & (column < length), scores, masked_score)


def stack_heads(ref, at, heads):
    return jnp.concatenate([ref[head, at] for head in range(heads)], axis=0)


def per_sequence(*shape):
    return pl.BlockSpec((1,) + shape, lambda s: (s,) + (0,) * len(shape))


def whole(*shape):
    return pl.BlockSpec(shape, lambda s: (0,) * len(shape), pipeline_mode=pl.Buffered(1))


def across_columns(left, weights, first, width, out):
    total = weights.shape[0]
    for start in range(0, total, 512):
        at = pl.ds(start, 512)
        out[0, :, at] = lax.dot_general(
            left,
            weights[at, first : first + width],
            (((1,), (1,)), ((), ())),
            preferred_element_type=jnp.float32,
        ).astype(out.dtype)


def attend(normed, weights, cotangent, extra, lengths, owners, cos_full, sin_full, gains, heads, early, number):
    count, rows, width = normed.shape
    wide = (heads + 2) * HD
    extras = len(extra)
    own_rows = cotangent.shape[0]
    cut = balanced(early, crossing(extra, width))

    def kernel(lengths, owners, normed, weights, cos_ref, sin_ref, gains, own, *rest):
        pieces, rest = rest[:extras], rest[extras:]
        (proj, out, logs, branch, gathered), rest = rest[:5], rest[5:]
        mixed, (queries, keys, values), sems = rest[:extras], rest[extras : extras + 3], rest[extras + 3 :]
        sequence = pl.program_id(0)
        steps = plan_gather(own, gathered, *sems[:3], cut=cut, rows=early)
        copies = plan_exchanges(pieces, mixed, sems[3:])

        @pl.when(sequence == 0)
        def _():
            greet(EVERYONE_NEAR)
            steps[0]()
            for copy in copies:
                copy.start()

        group = lax.axis_index("outer") * TEAM + sequence
        length = sequence_length(lengths, owners, group)
        proj[0] = jnp.dot(
            normed[0], weights[:, :wide], preferred_element_type=jnp.float32
        )
        head_inputs(proj, gains, cos_ref, sin_ref, queries, keys, values, heads)
        lane = lax.broadcasted_iota(jnp.int32, (BLOCK, HD), 1)
        for step in range(rows // BLOCK):
            at = pl.ds(step * BLOCK, BLOCK)
            seen = pl.ds(0, (step + 1) * BLOCK)
            scores = masked_scores(stack_heads(queries, at, heads), keys[seen], step, length)
            top = jnp.max(scores, axis=-1, keepdims=True)
            exponent = jnp.exp(scores - top)
            total = jnp.sum(exponent, axis=-1, keepdims=True)
            probs = (exponent / total).astype(jnp.bfloat16)
            mixed_values = jnp.dot(probs, values[seen], preferred_element_type=jnp.float32)
            log_total = top + jnp.log(total)
            kept = jnp.zeros((BLOCK, HD), jnp.float32)
            for head in range(heads):
                mine = slice(head * BLOCK, (head + 1) * BLOCK)
                out[0, at, columns(head)] = mixed_values[mine].astype(jnp.bfloat16)
                kept = jnp.where(lane == head, log_total[mine], kept)
            logs[0, at] = kept
        across_columns(out[0], weights, wide, heads * HD, branch)

        @pl.when(sequence == 1)
        def _():
            steps[1]()

        @pl.when(sequence == 2)
        def _():
            steps[2]()

        @pl.when(sequence == count - 1)
        def _():
            steps[3]()
            for copy in copies:
                copy.wait()

    outs = pl.pallas_call(
        kernel,
        name="attend",
        grid=(count,),
        out_shape=(
            jax.ShapeDtypeStruct((count, rows, wide), jnp.float32),
            jax.ShapeDtypeStruct((count, rows, heads * HD), jnp.bfloat16),
            jax.ShapeDtypeStruct((count, rows, HD), jnp.float32),
            jax.ShapeDtypeStruct((count, rows, width), jnp.bfloat16),
            layer_rows(own_rows, width),
        )
        + tuple(like(piece) for piece in extra),
        in_specs=[
            pl.BlockSpec(memory_space=pltpu.SMEM),
            pl.BlockSpec(memory_space=pltpu.SMEM),
            per_sequence(rows, width),
            whole(width, wide + heads * HD),
            whole(rows, HD),
            whole(rows, HD),
            whole(2, HD),
            whole(own_rows, width),
        ]
        + [whole(*piece.shape) for piece in extra],
        out_specs=(
            per_sequence(rows, wide),
            per_sequence(rows, heads * HD),
            per_sequence(rows, HD),
            per_sequence(rows, width),
            anywhere(),
        )
        + (anywhere(),) * extras,
        scratch_shapes=[
            pltpu.VMEM((heads, rows, HD), jnp.bfloat16),
            pltpu.VMEM((rows, HD), jnp.bfloat16),
            pltpu.VMEM((rows, HD), jnp.bfloat16),
        ]
        + gather_scratch()
        + exchange_scratch() * extras,
        compiler_params=params(number),
        cost_estimate=cost_of(50),
    )(lengths, owners, normed, weights, cos_full, sin_full, gains, cotangent, *extra)
    return outs


def team_split(width, outer_count):
    split = TEAM if width // outer_count % (TEAM * HD) == 0 else 1
    return split, width // outer_count // split


def local_first(place):
    near, core, _ = spots()
    other_near, other_core = place // 2, place % 2
    return (near + other_near * (1 - 2 * near)) * CORE + core + other_core * (1 - 2 * core)


def ordered(*shape):
    return pl.BlockSpec((1,) + shape, lambda s: (local_first(s),) + (0,) * len(shape))


def attend_back(
    projected,
    normed,
    attended,
    own_grad,
    logs,
    weights,
    part,
    hidden,
    extra,
    outer_count,
    lengths,
    owners,
    cos_full,
    sin_full,
    gains,
    heads,
    number,
):
    count, rows, wide = projected.shape
    own_rows, width = hidden.shape
    extras = len(extra)
    cut = balanced(own_rows, crossing(extra, width))

    every = wide + heads * HD
    split, share = team_split(width, outer_count)

    def kernel(
        lengths, owners, proj, normed, attended, own_grad, logs, weights_any, cos_ref, sin_ref, gains, part, hidden, *rest
    ):
        pieces, rest = rest[:extras], rest[extras:]
        (gathered, gain_grad, back_part, output, grad_weights), rest = rest[:5], rest[5:]
        mixed, rest = rest[:extras], rest[extras:]
        (queries, keys, values, grad_att, grad_q, grad_k, grad_v_sum, summed), rest = rest[:8], rest[8:]
        (total, held, held_sem, out, grad_v, grad_sem), rest = rest[:6], rest[6:]
        (weights, staged, weights_sem, store_sem), rest = rest[:4], rest[4:]
        sums, sems, rest = rest[:SUM_SCRATCH], rest[SUM_SCRATCH : SUM_SCRATCH + 3], rest[SUM_SCRATCH + 3 :]
        place = pl.program_id(0)
        sequence = local_first(place)
        steps, from_tp, from_near = plan_sum_of(part, total, sums, cut)
        gather = plan_gather(own_grad, gathered, *sems, cut=own_rows // 2, parts=True)
        copies = plan_exchanges(pieces, mixed, rest)
        fetch_weights = pltpu.make_async_copy(weights_any, weights, weights_sem)
        store = pltpu.make_async_copy(staged, grad_weights, store_sem)

        def arrival(which):
            member = local_first(which)
            return pltpu.make_async_copy(
                gathered.at[member // CORE, member % CORE],
                grad_v.at[which % 2],
                grad_sem.at[which % 2],
            )

        fetch = pltpu.make_async_copy(hidden, held, held_sem)

        @pl.when(place == 0)
        def _():
            greet(EVERYONE_NEAR)
            gather[0]()
            steps[0]()
            fetch.start()
            fetch_weights.start()
            gain_grad[...] = jnp.zeros_like(gain_grad)
            summed[...] = jnp.zeros_like(summed)
            gather[1]()
            gather[2]()
            gather[3]()
            arrival(0).start()
            fetch_weights.wait()

        @pl.when(place == 2)
        def _():
            arrival(3).start()

        head_inputs(proj, gains, cos_ref, sin_ref, queries, keys, values, heads)
        grad_k[...] = jnp.zeros_like(grad_k)
        grad_v_sum[...] = jnp.zeros_like(grad_v_sum)
        arrival(place).wait()
        grad = grad_v[place % 2].reshape(rows, width)
        group = lax.axis_index("outer") * TEAM + sequence
        length = sequence_length(lengths, owners, group)
        grad_att[...] = jnp.dot(
            grad, weights[:, wide:], preferred_element_type=jnp.float32
        ).astype(jnp.bfloat16)

        for step in range(rows // BLOCK):
            at = pl.ds(step * BLOCK, BLOCK)
            seen = pl.ds(0, (step + 1) * BLOCK)
            stacked = stack_heads(queries, at, heads)
            above = jnp.concatenate([grad_att[at, columns(head)] for head in range(heads)], axis=0)
            log_total = jnp.concatenate(
                [logs[0, at, head : head + 1] for head in range(heads)], axis=0
            )
            probs = jnp.exp(masked_scores(stacked, keys[seen], step, length) - log_total)
            grad_probs = lax.dot_general(
                above, values[seen], (((1,), (1,)), ((), ())), preferred_element_type=jnp.float32
            )
            inner = jnp.sum(probs * grad_probs, axis=-1, keepdims=True)
            grad_scores = (probs * (grad_probs - inner)).astype(jnp.bfloat16)
            by_query = jnp.dot(grad_scores, keys[seen], preferred_element_type=jnp.float32)
            for head in range(heads):
                grad_q[head, at] = by_query[head * BLOCK : (head + 1) * BLOCK] * (HD ** (-0.5))
            grad_k[seen] += lax.dot_general(
                grad_scores, stacked, (((0,), (0,)), ((), ())), preferred_element_type=jnp.float32
            )
            grad_v_sum[seen] += lax.dot_general(
                probs.astype(jnp.bfloat16),
                above,
                (((0,), (0,)), ((), ())),
                preferred_element_type=jnp.float32,
            )

        def settle(column, gain, value):
            back, by_gain = head_back(
                proj[0, :, columns(column)], gains[gain : gain + 1, :], value, cos_ref[...], sin_ref[...]
            )
            out[:, columns(column)] = back.astype(jnp.bfloat16)
            gain_grad[gain] += by_gain.reshape(rows // 8, 8, HD).sum(axis=0)

        for head in range(heads):
            settle(head, 0, grad_q[head])
        settle(heads, 1, grad_k[...] * (HD ** (-0.5)))
        out[:, columns(heads + 1)] = grad_v_sum[...].astype(jnp.bfloat16)

        across_columns(out[...], weights, 0, wide, back_part)

        by_projected, by_attended = out[...].T, attended[0].T
        for start in range(0, width, 512):
            at = pl.ds(start, 512)
            summed[:wide, at] += jnp.dot(
                by_projected, normed[0, :, at], preferred_element_type=jnp.float32
            )
            summed[wide:, at] += jnp.dot(
                by_attended, grad[:, start : start + 512], preferred_element_type=jnp.float32
            )

        @pl.when(place == 0)
        def _():
            gather[5]()
            steps[1]()
            for copy in copies:
                copy.start()
            gather[4]()
            arrival(1).start()

        @pl.when(place == 1)
        def _():
            steps[2]()
            gather[6]()
            arrival(2).start()

        @pl.when(place == count - 1)
        def _():
            for outer in range(outer_count):
                for member in range(split):
                    start = (outer * split + member) * share
                    staged[outer, member] = summed[:, start : start + share].astype(jnp.bfloat16)
            store.start()
            fetch.wait()
            steps[3]()

            def finish(at):
                value = total[at] + read(from_tp, at) + read(from_near, at)
                output[at] = (held[at] + value).astype(jnp.bfloat16)

            row_loop(own_rows, finish)
            store.wait()
            for copy in copies:
                copy.wait()

    return pl.pallas_call(
        kernel,
        name="attend_back",
        grid=(count,),
        out_shape=(
            layer_rows(own_rows, width),
            jax.ShapeDtypeStruct((2, 8, HD), jnp.float32),
            jax.ShapeDtypeStruct((count, rows, width), jnp.bfloat16),
            jax.ShapeDtypeStruct((own_rows, width), jnp.bfloat16),
            jax.ShapeDtypeStruct((outer_count, split, every, share), jnp.bfloat16),
        )
        + tuple(like(piece) for piece in extra),
        in_specs=[
            pl.BlockSpec(memory_space=pltpu.SMEM),
            pl.BlockSpec(memory_space=pltpu.SMEM),
            ordered(rows, wide),
            ordered(rows, width),
            ordered(rows, heads * HD),
            whole(own_rows, width),
            ordered(rows, HD),
            anywhere(),
            whole(rows, HD),
            whole(rows, HD),
            whole(2, HD),
            anywhere(),
            anywhere(),
        ]
        + [whole(*piece.shape) for piece in extra],
        out_specs=(
            anywhere(),
            pl.BlockSpec((2, 8, HD), lambda s: (0, 0, 0)),
            ordered(rows, width),
            whole(own_rows, width),
            anywhere(),
        )
        + (anywhere(),) * extras,
        scratch_shapes=[
            pltpu.VMEM((heads, rows, HD), jnp.bfloat16),
            pltpu.VMEM((rows, HD), jnp.bfloat16),
            pltpu.VMEM((rows, HD), jnp.bfloat16),
            pltpu.VMEM((rows, heads * HD), jnp.bfloat16),
            pltpu.VMEM((heads, rows, HD), jnp.float32),
            pltpu.VMEM((rows, HD), jnp.float32),
            pltpu.VMEM((rows, HD), jnp.float32),
            pltpu.VMEM((every, width), jnp.float32),
            pltpu.VMEM((own_rows, width), jnp.float32),
            pltpu.VMEM((own_rows, width), jnp.float32),
            pltpu.SemaphoreType.DMA,
            pltpu.VMEM((rows, wide), jnp.bfloat16),
            pltpu.VMEM((2, 2, own_rows, width), jnp.bfloat16),
            pltpu.SemaphoreType.DMA((2,)),
            pltpu.VMEM(weights.shape, weights.dtype),
            pltpu.VMEM((outer_count, split, every, share), jnp.bfloat16),
            pltpu.SemaphoreType.DMA,
            pltpu.SemaphoreType.DMA,
        ]
        + sum_scratch(own_rows, width, cut)
        + gather_scratch()
        + exchange_scratch() * extras,
        compiler_params=params(number),
        cost_estimate=cost_of(50),
    )(
        lengths,
        owners,
        projected,
        normed,
        attended,
        own_grad,
        logs,
        weights,
        cos_full,
        sin_full,
        gains,
        spread(part, own_rows),
        hidden,
        *extra,
    )


def feed(normed, weights, cotangent, gathered, early, number):
    count, rows, width = normed.shape
    units = weights.shape[1] // 2
    late = cotangent.shape[0] - early

    def kernel(normed, weights, own, _, product, active, out, *sems):
        steps = plan_gather(
            own, out, *sems, cut=balanced(late, 0), base=early, rows=late
        )
        sequence = pl.program_id(0)

        @pl.when(sequence == 0)
        def _():
            greet(NEIGHBOURS)
            steps[0]()

        for start in range(0, units, 256):
            gate_at, up_at = pl.ds(start, 256), pl.ds(units + start, 256)
            gate = jnp.dot(normed[0], weights[:, gate_at], preferred_element_type=jnp.float32)
            up = jnp.dot(normed[0], weights[:, up_at], preferred_element_type=jnp.float32)
            product[0, :, gate_at] = gate
            product[0, :, up_at] = up
            active[0, :, gate_at] = swish_product(gate, up).astype(jnp.bfloat16)

        for place in (1, 2, 3):

            @pl.when(sequence == count - 4 + place)
            def _(place=place):
                steps[place]()

    return pl.pallas_call(
        kernel,
        name="feed",
        grid=(count,),
        out_shape=(
            jax.ShapeDtypeStruct((count, rows, 2 * units), jnp.float32),
            jax.ShapeDtypeStruct((count, rows, units), jnp.bfloat16),
            like(gathered),
        ),
        in_specs=[
            per_sequence(rows, width),
            whole(*weights.shape),
            whole(*cotangent.shape),
            anywhere(),
        ],
        out_specs=(per_sequence(rows, 2 * units), per_sequence(rows, units), anywhere()),
        scratch_shapes=gather_scratch(),
        input_output_aliases={3: 2},
        compiler_params=params(number),
        cost_estimate=cost_of(28),
    )(normed, weights, cotangent, gathered)


def feed_back(grads, weights, product):
    count, rows, width = grads.shape
    units = weights.shape[1]

    def kernel(grads, weights, product, by_gate, by_up):
        for start in range(0, units, 256):
            gate_at, up_at = pl.ds(start, 256), pl.ds(units + start, 256)
            grad = jnp.dot(grads[0], weights[:, gate_at], preferred_element_type=jnp.float32)
            gate, up = product[0, :, gate_at], product[0, :, up_at]
            share = jax.nn.sigmoid(gate)
            slope = grad * up * share * (1.0 + gate * (1.0 - share))
            by_gate[0, :, gate_at] = slope.astype(jnp.bfloat16)
            by_up[0, :, gate_at] = (grad * gate * share).astype(jnp.bfloat16)

    return pl.pallas_call(
        kernel,
        name="feed_back",
        grid=(count,),
        out_shape=(jax.ShapeDtypeStruct((count, rows, units), jnp.bfloat16),) * 2,
        in_specs=[
            per_sequence(rows, width),
            whole(*weights.shape),
            per_sequence(rows, 2 * units),
        ],
        out_specs=(per_sequence(rows, units),) * 2,
        compiler_params=pltpu.CompilerParams(vmem_limit_bytes=VMEM_LIMIT),
        cost_estimate=cost_of(18),
    )(grads, weights, product)


def spans(widths, base=0):
    for member in range(TEAM):
        first, inside = base, 0
        for width in widths:
            share = width // TEAM
            yield member, pl.ds(first + member * share, share), pl.ds(inside, share)
            first += width
            inside += share


def by_columns(start, height, widths, source):
    def run(pieces, update):
        @pl.loop(0, height // CHUNK)
        def _(row):
            rows = pl.ds(pl.multiple_of(start + row * CHUNK, CHUNK), CHUNK)
            for member, across, inside in spans(widths):
                update(rows, across, pieces[member, rows, inside])

    return source, pl.ds(start, height), pl.ds(0, sum(widths)), run


def by_turned(height, base, widths, source, members=range(TEAM)):
    parts = [part for part in spans(widths, base) if part[0] in members]

    def run(pieces, update):
        for member, across, inside in parts:
            update(pl.ds(0, height), across, pieces[member, inside].T)

    if len(members) == 1:
        columns = parts[0][1]
    else:
        columns = pl.ds(base, sum(widths))
    return source, pl.ds(0, height), columns, run


def by_rows(member, height, width, inside, source):
    at, across = pl.ds(member * height, height), pl.ds(0, width)

    def run(pieces, update):
        if inside is None:
            update(at, across, pieces[member].T)
        else:
            update(at, across, pieces[member, pl.ds(inside, height)])

    return source, at, across, run


def adam_all(sets, pieces, factor, gain_grad, gains, passed):
    jobs = [(place,) + job for place, group in enumerate(sets) for job in group[3]]
    count, total, sources, others = len(jobs), len(sets), len(pieces), len(passed)

    def kernel(*refs):
        inputs, refs = refs[: 3 * total], refs[3 * total :]
        piece_refs, factor, refs = refs[:sources], refs[sources], refs[sources + 1 :]
        (gain_grad, *gains), refs = refs[:4], refs[4:]
        passed, refs = refs[:others], refs[others:]
        outputs, refs = refs[: 4 * total], refs[4 * total :]
        new_gains, refs = refs[:3], refs[3:]
        onward, refs = refs[:others], refs[others:]
        held, refs = refs[: 4 * total], refs[4 * total :]
        held_pieces, refs = refs[:sources], refs[sources:]
        between, (piece_sem, in_sem, out_sem, pass_sem) = refs[:others], refs[others:]
        scale = factor[0:1, 0:1]
        loads = [
            pltpu.make_async_copy(piece_refs[place], held_pieces[place], piece_sem.at[place])
            for place in range(sources)
        ]
        arrivals, stores = [], []
        kept = [
            pltpu.make_async_copy(source, target, pass_sem.at[0, place])
            for place, (source, target) in enumerate(zip(passed, between))
        ]
        kept_on = [
            pltpu.make_async_copy(source, target, pass_sem.at[1, place])
            for place, (source, target) in enumerate(zip(between, onward))
        ]
        for slot, (place, source, at, across, _) in enumerate(jobs):
            arrivals.append(
                [
                    pltpu.make_async_copy(
                        inputs[3 * place + number].at[at, across],
                        held[4 * place + number].at[at, across],
                        in_sem.at[3 * slot + number],
                    )
                    for number in range(3)
                ]
            )
        first_use = {}
        for slot, job in enumerate(jobs):
            first_use.setdefault(job[1], slot)

        def bring(slot):
            if slot < count:
                if first_use[jobs[slot][1]] == slot:
                    loads[jobs[slot][1]].start()
                for copy in arrivals[slot]:
                    copy.start()

        for slot in range(AHEAD):
            bring(slot)
        gain_step = adam_update(
            gains[0][...],
            gain_grad[: gains[0].shape[0]],
            gains[1][...],
            gains[2][...],
            scale,
            0.0,
            gain_rate,
        )
        for target, value in zip(new_gains, gain_step):
            target[...] = value
        for slot, (place, source, at, across, run) in enumerate(jobs):
            weight, moment, square, low = held[4 * place : 4 * place + 4]
            if first_use[source] == slot:
                loads[source].wait()
            for copy in arrivals[slot]:
                copy.wait()
            bring(slot + AHEAD)
            if slot == 0:
                for copy in kept:
                    copy.start()

            def update(rows, columns, gradient):
                where = (rows, columns)
                value, one, two = adam_update(
                    weight[where],
                    gradient.astype(jnp.float32),
                    moment[where],
                    square[where],
                    scale,
                    weight_decay,
                    learn_rate,
                )
                weight[where], moment[where], square[where] = value, one, two
                low[where] = value.astype(jnp.bfloat16)

            run(held_pieces[source], update)
            for number, origin in enumerate((weight, moment, square, low)):
                copy = pltpu.make_async_copy(
                    origin.at[at, across],
                    outputs[4 * place + number].at[at, across],
                    out_sem.at[4 * slot + number],
                )
                copy.start()
                stores.append(copy)
            if slot == 4:
                for arrived, copy in zip(kept, kept_on):
                    arrived.wait()
                    copy.start()
        for copy in stores + kept_on:
            copy.wait()

    args, shapes, scratch = [], [], []
    for weight, moment, square, _ in sets:
        args += [weight, moment, square]
        low = jax.ShapeDtypeStruct(weight.shape, jnp.bfloat16)
        shapes += [like(weight)] * 3 + [low]
        scratch += [pltpu.VMEM(each.shape, each.dtype) for each in (weight, moment, square, low)]
    outs = pl.pallas_call(
        kernel,
        name="adam_all",
        out_shape=tuple(shapes) + (like(gains[0]),) * 3 + tuple(like(each) for each in passed),
        in_specs=[anywhere()] * (3 * total + sources) + [in_vmem()] * 5 + [anywhere()] * others,
        out_specs=(anywhere(),) * (4 * total) + (in_vmem(),) * 3 + (anywhere(),) * others,
        scratch_shapes=scratch
        + [pltpu.VMEM(each.shape, each.dtype) for each in tuple(pieces) + tuple(passed)]
        + [
            pltpu.SemaphoreType.DMA((sources,)),
            pltpu.SemaphoreType.DMA((3 * count,)),
            pltpu.SemaphoreType.DMA((4 * count,)),
            pltpu.SemaphoreType.DMA((2, others)),
        ],
        compiler_params=pltpu.CompilerParams(vmem_limit_bytes=VMEM_LIMIT),
        cost_estimate=cost_of(15),
    )(*args, *pieces, factor, gain_grad, *gains, *passed)
    steps = [outs[4 * place : 4 * place + 4] for place in range(total)]
    return steps + [outs[4 * total : 4 * total + 3], outs[4 * total + 3 :]]


def rotary(count):
    frequency = rope_base ** (-(np.arange(HD // 2) * 2.0 / HD))
    angles = np.arange(count)[:, None] * frequency[None, :]
    cosine, sine = np.cos(angles), np.sin(angles)
    full = [np.concatenate(pair, axis=1) for pair in ((cosine, cosine), (-sine, sine))]
    return [jnp.asarray(table, jnp.float32) for table in full]


def gather_outer(mixed):
    return lax.all_gather(mixed.reshape(-1, mixed.shape[2]), "outer", axis=0, tiled=True)


def team_pieces(summed):
    return summed.reshape(TEAM, -1, summed.shape[-1])


def turned_pieces(summed):
    if summed.shape[1] * TEAM * lax.axis_size("outer") == D:
        return team_pieces(summed)
    return summed.reshape(summed.shape[0], TEAM, -1).transpose(1, 0, 2)


def sum_weight(gradient):
    return lax.psum_scatter(gradient, "outer", scatter_dimension=0, tiled=True)


def after(values, earlier):
    return lax.optimization_barrier((values, earlier))


def adam_update(weight, gradient, moment_one, moment_two, factor, decay_rate, rate_value):
    clipped = gradient * factor
    moment_one = beta_first * moment_one + (1.0 - beta_first) * clipped
    moment_two = beta_second * moment_two + (1.0 - beta_second) * clipped * clipped
    first_fixed = moment_one * (rate_value / (1.0 - beta_first**STEP))
    root_fixed = jnp.sqrt(moment_two) * (1.0 - beta_second**STEP) ** (-0.5)
    kept = weight * (1.0 - rate_value * decay_rate) if decay_rate else weight
    weight = kept - first_fixed / (root_fixed + adam_epsilon)
    return (weight, moment_one, moment_two)


def dot(left, right, contract):
    return lax.dot_general(
        left, right, ((contract[0], contract[1]), ((), ())), preferred_element_type=jnp.float32
    )


def times(left, right):
    return dot(left, right, ((1,), (0,)))


def times_across(left, right):
    return dot(left, right, ((1,), (1,)))


def over_rows(left, right):
    return dot(left, right, ((0,), (0,)))


def local(
    inputs,
    cotangent,
    lengths,
    owners,
    qkv_weight,
    out_weight,
    gate_up_weight,
    down_weight,
    norm_gains,
    qkv_moment,
    out_moment,
    gate_up_moment,
    down_moment,
    gains_moment,
    qkv_square,
    out_square,
    gate_up_square,
    down_square,
    gains_square,
):
    tp_count = lax.axis_size("tp")
    half_rows = inputs.shape[0]
    row_count = half_rows * tp_count
    heads = H // tp_count // TEAM
    hidden_units = FF // tp_count // TEAM
    qkv_widths = (H * HD // tp_count, KV * HD // tp_count, KV * HD // tp_count)
    out_widths = (H * HD // tp_count,)
    part_rows = qkv_weight.shape[0]
    gate_up_widths = (FF // tp_count, FF // tp_count)
    down_widths = (FF // tp_count,)

    cos_full, sin_full = rotary(row_count)
    attn_gain = norm_gains[:D]
    mlp_gain = norm_gains[D : 2 * D]
    head_gains = norm_gains[2 * D :].reshape(2, HD)

    normed_attn, gate_up_mixed, first_full, grad_low, down_pieces = opening(
        qkv_weight,
        out_weight,
        gate_up_weight,
        down_weight,
        inputs,
        attn_gain,
        cotangent,
        lengths,
        owners,
        lax.axis_size("outer"),
        0,
    )
    gate_up_full = gather_outer(gate_up_mixed)
    early = half_rows * 2 // 5 // CHUNK * CHUNK
    projected, attended, logs, attn_branch, grad_all, down_mixed = attend(
        normed_attn.reshape(TEAM, row_count, D),
        first_full,
        grad_low,
        (down_pieces,),
        lengths,
        owners,
        cos_full,
        sin_full,
        head_gains,
        heads,
        early,
        1,
    )
    down_full = gather_outer(down_mixed)
    hidden, normed_mlp = branch_and_norm(attn_branch, inputs, mlp_gain, 2, "branch_and_norm")
    gate_up, activated, grad_all = feed(
        normed_mlp.reshape(TEAM, row_count, D), gate_up_full, grad_low, grad_all, early, 8
    )
    grad_down = over_rows(grad_all.reshape(-1, D), activated.reshape(-1, hidden_units))
    grad_all, grad_down = after(grad_all, grad_down.astype(jnp.bfloat16))
    down_sum = sum_weight(grad_down)
    grad_gate, grad_up = feed_back(
        grad_all.reshape(TEAM, row_count, D), down_full, gate_up
    )
    grad_gate_weight = over_rows(normed_mlp, grad_gate.reshape(-1, hidden_units))
    grad_gate, grad_gate_weight = after(grad_gate, grad_gate_weight.astype(jnp.bfloat16))
    gate_sum = sum_weight(grad_gate_weight)
    grad_hidden, grad_mlp_gain, own_grad, mlp_part, grad_up_weight = feed_back_rest(
        grad_gate,
        grad_up,
        gate_up_full,
        activated,
        down_full,
        normed_mlp,
        hidden,
        grad_low,
        mlp_gain,
        lax.axis_size("outer"),
        3,
        "feed_back_rest",
    )
    up_sum = turned_pieces(sum_weight(grad_up_weight.reshape(-1, grad_up_weight.shape[2])))
    _, grad_head_gains, grad_normed_attn, output, grad_first, down_mixed = attend_back(
        projected,
        normed_attn.reshape(TEAM, row_count, D),
        attended,
        own_grad,
        logs,
        first_full,
        mlp_part,
        hidden,
        (team_pieces(down_sum),),
        lax.axis_size("outer"),
        lengths,
        owners,
        cos_full,
        sin_full,
        head_gains,
        heads,
        7,
    )
    grad_first, gate_sum = after(grad_first, gate_sum)
    first_sum = turned_pieces(sum_weight(grad_first.reshape(-1, grad_first.shape[3])))
    input_grad, attn_gain_parts, squares, gate_mixed, up_mixed = norm_back_last(
        grad_normed_attn,
        inputs,
        grad_hidden,
        attn_gain,
        (team_pieces(gate_sum), up_sum),
        (gate_sum, up_sum, down_sum),
        4,
        "norm_back_attn",
    )
    gain_part = jnp.concatenate(
        [jnp.zeros_like(grad_mlp_gain), grad_mlp_gain, grad_head_gains.sum(axis=1).reshape(-1)]
    )
    gain_count = gain_part.shape[0]
    packed = jnp.pad(gain_part, (0, -gain_count % PAD))
    packed, norm_tile, factor_tile, first_mixed = total_everywhere(
        packed.reshape(-1, HD),
        attn_gain_parts,
        squares,
        first_sum,
        lax.axis_size("outer"),
        5,
        "total_everywhere",
    )
    grad_norm = norm_tile[0, 0]
    (
        (new_gate_up, new_gate_up_one, new_gate_up_two, gate_up_copy),
        (new_down, new_down_one, new_down_two, down_copy),
        (new_out, new_out_one, new_out_two, out_copy),
        (new_qkv, new_qkv_one, new_qkv_two, qkv_copy),
        new_gains,
        (output, input_grad),
    ) = adam_all(
        [
            (
                gate_up_weight,
                gate_up_moment,
                gate_up_square,
                [
                    by_columns(start, max(CHUNK, part_rows // 4), gate_up_widths[:1], 0)
                    for start in range(0, part_rows, max(CHUNK, part_rows // 4))
                ]
                + [
                    by_turned(part_rows, gate_up_widths[0], gate_up_widths[1:], 1, (member,))
                    for member in range(TEAM)
                ],
            ),
            (
                down_weight,
                down_moment,
                down_square,
                [by_rows(member, hidden_units, part_rows, None, 2) for member in range(TEAM)],
            ),
            (
                out_weight,
                out_moment,
                out_square,
                [
                    by_rows(member, heads * HD, part_rows, (heads + 2) * HD, 3)
                    for member in range(TEAM)
                ],
            ),
            (
                qkv_weight,
                qkv_moment,
                qkv_square,
                [by_turned(part_rows, 0, qkv_widths, 3)],
            ),
        ],
        (gate_mixed, up_mixed, down_mixed, first_mixed),
        factor_tile,
        packed,
        [each.reshape(-1, HD) for each in (norm_gains, gains_moment, gains_square)],
        (output, input_grad),
    )
    new_gains, new_gains_one, new_gains_two = (each.reshape(-1) for each in new_gains)
    return (
        output,
        input_grad,
        grad_norm,
        new_qkv,
        new_qkv_one,
        new_qkv_two,
        qkv_copy,
        new_out,
        new_out_one,
        new_out_two,
        out_copy,
        new_gate_up,
        new_gate_up_one,
        new_gate_up_two,
        gate_up_copy,
        new_down,
        new_down_one,
        new_down_two,
        down_copy,
        new_gains,
        new_gains_one,
        new_gains_two,
    )


def solution(mesh):
    fsdp_count, tp_count = mesh.shape["fsdp"], mesh.shape["tp"]
    cut = mesh.devices.reshape(fsdp_count // TEAM, NEAR, CORE, tp_count)
    cut_mesh = Mesh(cut, ("outer",) + LAYER)
    fsdp = ("outer", "near", "core")
    rows = P(fsdp + ("tp",), None)
    wide = P(fsdp, "tp")
    tall = P("tp", fsdp)
    weights = (wide, tall, wide, tall, P())
    return jax.shard_map(
        local,
        mesh=cut_mesh,
        in_specs=(rows, rows, P(), P()) + weights * 3,
        out_specs=(rows, rows, P()) + (wide,) * 4 + (tall,) * 4 + (wide,) * 4 + (tall,) * 4 + (P(),) * 3,
        check_vma=False,
    )
```

```python
from functools import partial

import jax
import jax.numpy as jnp
import numpy as np
from jax import lax
from jax.experimental import pallas as pl
from jax.experimental.pallas import tpu as pltpu
from jax.sharding import Mesh, PartitionSpec as P

D = 2048
H = 16
KV = 8
HD = 128
FF = 6144
STEP = 10


norm_epsilon = 1e-06
rope_base = 1000000.0
clip_norm = 1.0
learn_rate = 0.04
gain_rate = 0.8
beta_first = 0.9
beta_second = 0.999
adam_epsilon = 1e-08
weight_decay = 0.1
masked_score = -1e30

NEAR = 2
CORE = 2
TEAM = NEAR * CORE
LAYER = ("near", "core", "tp")
BLOCK = 128
PAD = 8 * 128


def rms_scale(values):
    return lax.rsqrt(jnp.mean(values * values, axis=-1, keepdims=True) + norm_epsilon)


def swish_product(gate_part, up_part):
    return jax.nn.silu(gate_part) * up_part


MESH_ID = pl.DeviceIdType.MESH
VMEM_LIMIT = 60 * 1024 * 1024
CHUNK = 16
GATHER_COPIES = 16
AHEAD = 1000
PART = TEAM // 2
SUM_COPIES = 12
NEIGHBOURS = ((1, 0, 0), (0, 1, 0), (0, 0, 1))
MATES = ((0, 1, 0), (1, 0, 0), (1, 1, 0))
EVERYONE_NEAR = NEIGHBOURS + ((1, 1, 0),)


def spots():
    return tuple(lax.axis_index(name) for name in LAYER)


def flipped(near_flip, core_flip, tp_flip):
    return {
        name: 1 - spot if flip else spot
        for name, spot, flip in zip(LAYER, spots(), (near_flip, core_flip, tp_flip))
    }


def greet(flips):
    barrier = pltpu.get_barrier_semaphore()
    for flip in flips:
        pl.semaphore_signal(barrier, inc=1, device_id=flipped(*flip), device_id_type=MESH_ID)
    pl.semaphore_wait(barrier, len(flips))


def link(source, target, send_sem, recv_sem, flip):
    return pltpu.make_async_remote_copy(
        src_ref=source,
        dst_ref=target,
        send_sem=send_sem,
        recv_sem=recv_sem,
        device_id=flipped(*flip),
        device_id_type=MESH_ID,
    )


TO_NEAR, TO_CORE, TO_TP = NEIGHBOURS


def plan_exchange(pieces, out, send, recv, own_sem):
    near, core, _ = spots()
    own = near * CORE + core
    copies = []
    for number, flip in enumerate(MATES):
        there = (1 - near if flip[0] else near) * CORE + (1 - core if flip[1] else core)
        copies.append(
            link(pieces.at[there], out.at[own], send.at[number], recv.at[number], flip)
        )
    copies.append(pltpu.make_async_copy(pieces.at[own], out.at[own], own_sem))
    return copies


def exchange_scratch():
    return [
        pltpu.SemaphoreType.DMA((len(MATES),)),
        pltpu.SemaphoreType.DMA((len(MATES),)),
        pltpu.SemaphoreType.DMA,
    ]


def crossing(pieces, width):
    return sum(2 * piece.shape[1] * piece.shape[2] for piece in pieces) // width


def plan_exchanges(pieces, mixed, sems):
    copies = []
    for place, (piece, result) in enumerate(zip(pieces, mixed)):
        copies += plan_exchange(piece, result, *sems[3 * place : 3 * place + 3])
    return copies


def plan_gather(own, out, send, recv, own_sem, cut, base=0, rows=None, parts=False, apart=False):
    near, core, tp = spots()
    rows = own.shape[0] if rows is None else rows
    low, high = pl.ds(base, cut), pl.ds(base + cut, rows - cut)
    all_rows = pl.ds(base, rows)

    def make(number, source, target, flip):
        return link(source, target, send.at[number], recv.at[number], flip)

    def give(number, part, flip):
        return make(number, own.at[part], out.at[near, core, tp, part], flip)

    def relay(number, where_near, where_tp, part, flip):
        ref = out.at[where_near, core, where_tp, part]
        return make(number, ref, ref, flip)

    keep = pltpu.make_async_copy(own.at[all_rows], out.at[near, core, tp, all_rows], own_sem)
    twin_own = give(4, all_rows, TO_CORE)
    first_rows = (rows - cut) // 2 // CHUNK * CHUNK
    high_parts = [
        (pl.ds(base + cut, first_rows), 1, 7, 8),
        (pl.ds(base + cut + first_rows, rows - cut - first_rows), 13, 14, 15),
    ]
    near_high = [give(number, part, TO_NEAR) for part, number, _, _ in high_parts]
    tp_high = give(2, high, TO_TP)
    far_high = [relay(number, 1 - near, tp, part, TO_TP) for part, _, number, _ in high_parts]
    twin_beside = [relay(number, 1 - near, tp, part, TO_CORE) for part, _, _, number in high_parts]
    twin_across = relay(9, near, 1 - tp, high, TO_CORE)
    twin_far = relay(12, 1 - near, 1 - tp, high, TO_CORE)
    twins = [twin_own, twin_across, twin_far] + twin_beside
    ways = near_high + far_high + [tp_high]
    if cut:
        tp_low = give(0, low, TO_TP)
        near_low = give(3, low, TO_NEAR)
        far_low = relay(5, near, 1 - tp, low, TO_NEAR)
        twin_across_low = relay(6, near, 1 - tp, low, TO_CORE)
        twin_beside_low = relay(10, 1 - near, tp, low, TO_CORE)
        twin_far_low = relay(11, 1 - near, 1 - tp, low, TO_CORE)
        twins += [twin_across_low, twin_beside_low, twin_far_low]
        ways += [tp_low, near_low, far_low]

    def begin_tp():
        if cut:
            tp_low.start()
        tp_high.start()
        twin_own.start()
        keep.start()

    def begin_near():
        for copy in near_high:
            copy.start()
        if cut:
            near_low.start()

    def begin():
        begin_near()
        begin_tp()

    def pass_on(part):
        near_high[part].wait_recv()
        far_high[part].start()
        twin_beside[part].start()

    def middle():
        if cut:
            tp_low.wait_recv()
            far_low.start()
            twin_across_low.start()
        pass_on(0)
        if not apart:
            pass_on(1)

    def later():
        tp_high.wait_recv()
        twin_across.start()
        if cut:
            near_low.wait_recv()
            twin_beside_low.start()

    def own_there():
        keep.wait()

    def twin_there():
        twin_own.wait_recv()
        twin_across.wait_recv()
        if cut:
            twin_across_low.wait_recv()

    def far_there():
        if cut:
            far_low.wait_recv()
            twin_far_low.start()
        for copy in far_high:
            copy.wait_recv()
        twin_far.start()

    def rest_there():
        for copy in twin_beside:
            copy.wait_recv()
        twin_far.wait_recv()
        if cut:
            twin_beside_low.wait_recv()
            twin_far_low.wait_recv()
        for copy in ways + twins:
            copy.wait_send()

    def finish():
        own_there()
        twin_there()
        far_there()
        rest_there()

    if parts:
        return [begin, middle, later, own_there, twin_there, far_there, rest_there]
    if apart:
        return [begin_tp, begin_near, middle, partial(pass_on, 1), later, finish]
    return [begin, middle, later, finish]


def balanced(rows, beside):
    return max(0, (rows - beside) // 2 // CHUNK * CHUNK)


def gather_scratch():
    return [
        pltpu.SemaphoreType.DMA((GATHER_COPIES,)),
        pltpu.SemaphoreType.DMA((GATHER_COPIES,)),
        pltpu.SemaphoreType.DMA,
    ]


def add_rows(target, start, count, *sources):
    @pl.loop(0, count // CHUNK)
    def _(step):
        at = pl.ds(pl.multiple_of(start + step * CHUNK, CHUNK), CHUNK)
        total = None
        for source, shift in sources:
            where = pl.ds(pl.multiple_of(start - shift + step * CHUNK, CHUNK), CHUNK)
            value = source[where].astype(jnp.float32)
            total = value if total is None else total + value
        target[at] = total.astype(target.dtype)


def halved(start, count):
    half = count // 2 // CHUNK * CHUNK
    return (start, half), (start + half, count - half)


def plan_sum(outgoing, mine, keep, total, scratch, cut):
    theirs, way_near, way_tp, from_tp, from_near, send, recv = scratch
    rows = total.shape[0]
    low, high = pl.ds(0, cut), pl.ds(cut, rows - cut)

    def make(number, source, target, flip):
        return link(source, target, send.at[number], recv.at[number], flip)

    twin = [make(number, outgoing[number], theirs.at[number], TO_CORE) for number in range(4)]
    far, to_tp, to_near, own = mine
    low_parts = halved(0, cut)
    high_parts = halved(cut, rows - cut)
    far_high = make(5, far.at[high], way_tp, TO_TP)
    tp_high = make(6, to_tp.at[high], from_tp.at[high], TO_TP)
    near_high = [
        make(9 + 2 * place, to_near.at[pl.ds(*part)], from_near.at[pl.ds(*part)], TO_NEAR)
        for place, part in enumerate(high_parts)
    ]
    ways = [far_high, tp_high] + near_high
    tp_low = []
    if cut:
        far_low = make(4, far.at[low], way_near, TO_NEAR)
        near_low = make(7, to_near.at[low], from_near.at[low], TO_NEAR)
        tp_low = [
            make(8 + 2 * place, to_tp.at[pl.ds(*part)], from_tp.at[pl.ds(*part)], TO_TP)
            for place, part in enumerate(low_parts)
        ]
        ways += [far_low, near_low] + tp_low

    def ready(number):
        if keep:
            keep[number].wait()
        twin[number].wait_recv()

    def both(number):
        return (mine[number], 0), (theirs.at[number], 0)

    def begin(numbers=range(4)):
        for number in numbers:
            twin[number].start()
            if keep:
                keep[number].start()

    def send_far():
        ready(0)
        if cut:
            add_rows(far, 0, cut, *both(0))
            far_low.start()
        add_rows(far, cut, rows - cut, *both(0))
        far_high.start()

    def send_tp():
        ready(1)
        add_rows(to_tp, cut, rows - cut, *both(1))
        tp_high.start()

    def send_near():
        ready(2)
        if cut:
            add_rows(to_near, 0, cut, *both(2))
            near_low.start()

    def first():
        send_far()
        send_tp()
        send_near()

    def second():
        if cut:
            far_low.wait_recv()
        far_high.wait_recv()
        for place, part in enumerate(high_parts):
            if cut:
                add_rows(to_tp, *low_parts[place], *both(1), (way_near, 0))
                tp_low[place].start()
            add_rows(to_near, *part, *both(2), (way_tp, cut))
            near_high[place].start()
        ready(3)
        add_rows(total, 0, rows, *both(3))

    def finish(body):
        tp_high.wait_recv()
        if cut:
            near_low.wait_recv()
        for place, part in enumerate(high_parts):
            if cut:
                tp_low[place].wait_recv()
                row_loop(*low_parts[place], body)
            near_high[place].wait_recv()
            row_loop(*part, body)
        for copy in twin + ways:
            copy.wait_send()

    return [begin, first, second, finish], (send_far, send_tp, send_near)


def plan_sum_of(part, total, scratch, cut):
    mine, local_sem, *scratch = scratch
    near, core, tp = spots()
    order = [(1 - near, 1 - tp), (near, 1 - tp), (1 - near, tp), (near, tp)]
    outgoing = [part.at[a, 1 - core, b] for a, b in order]
    keep = [
        pltpu.make_async_copy(part.at[a, core, b], mine.at[number], local_sem.at[number])
        for number, (a, b) in enumerate(order)
    ]
    blocks = [mine.at[number] for number in range(4)]
    steps, _ = plan_sum(outgoing, blocks, keep, total, scratch, cut)
    return steps, scratch[3], scratch[4]


def sum_scratch(rows, width, cut, fetched=True):
    low = jnp.bfloat16
    fetch = [pltpu.VMEM((4, rows, width), low), pltpu.SemaphoreType.DMA((4,))]
    return (fetch if fetched else []) + [
        pltpu.VMEM((4, rows, width), low),
        pltpu.VMEM((max(cut, CHUNK), width), low),
        pltpu.VMEM((rows - cut, width), low),
        pltpu.VMEM((rows, width), low),
        pltpu.VMEM((rows, width), low),
        pltpu.SemaphoreType.DMA((SUM_COPIES,)),
        pltpu.SemaphoreType.DMA((SUM_COPIES,)),
    ]


SUM_SCRATCH = 9
COST_SHARE = 1e5


def params(number):
    return pltpu.CompilerParams(
        collective_id=number, has_side_effects=True, vmem_limit_bytes=VMEM_LIMIT
    )


def cost_of(microseconds):
    return pl.CostEstimate(
        flops=0, bytes_accessed=int(microseconds * COST_SHARE), transcendentals=0
    )


def in_vmem():
    return pl.BlockSpec(memory_space=pltpu.VMEM)


def anywhere():
    return pl.BlockSpec(memory_space=pl.ANY)


def like(array):
    return jax.ShapeDtypeStruct(array.shape, array.dtype)


def layer_rows(rows, width):
    return jax.ShapeDtypeStruct((NEAR, CORE, 2, rows, width), jnp.bfloat16)


def row_loop(start, count, body):
    @pl.loop(0, count // CHUNK)
    def _(step):
        body(pl.ds(pl.multiple_of(start + step * CHUNK, CHUNK), CHUNK))


def plan_line(blocks, send, recv, count):
    own = lax.axis_index("outer")

    def handle(side, number, half, there):
        block = blocks.at[there, pl.ds(half * PART, PART)]
        return pltpu.make_async_remote_copy(
            src_ref=block,
            dst_ref=block,
            send_sem=send.at[side, number, half],
            recv_sem=recv.at[side, number, half],
            device_id={"outer": own + 1 if side == 0 else own - 1},
            device_id_type=MESH_ID,
        )

    def message(side, number, half):
        return handle(side, number, half, own - number if side == 0 else own + number)

    def arrival(side, number, half):
        return handle(side, number, half, own - 1 - number if side == 0 else own + 1 + number)

    def sends(side, number):
        if side == 0:
            return (own < count - 1) & (own >= number)
        return (own > 0) & (own + number < count)

    def gets(side, number):
        return own >= number + 1 if side == 0 else own + 1 + number < count

    def push(number):
        for side in range(2):

            @pl.when(sends(side, number))
            def _(side=side):
                for half in range(2):
                    message(side, number, half).start()

    def take(number):
        for half in range(2):
            for side in range(2):

                @pl.when(gets(side, number))
                def _(side=side, half=half):
                    arrival(side, number, half).wait_recv()

                if number + 2 < count:

                    @pl.when(sends(side, number + 1))
                    def _(side=side, half=half):
                        message(side, number + 1, half).start()

    def settle():
        for number in range(count - 1):
            for side in range(2):

                @pl.when(sends(side, number))
                def _(side=side, number=number):
                    for half in range(2):
                        message(side, number, half).wait_send()

    return push, take, settle


def greet_all(flips, count):
    barrier = pltpu.get_barrier_semaphore()
    own = lax.axis_index("outer")
    for flip in flips:
        pl.semaphore_signal(barrier, inc=1, device_id=flipped(*flip), device_id_type=MESH_ID)
    for there, neighbour in ((own < count - 1, own + 1), (own > 0, own - 1)):

        @pl.when(there)
        def _(neighbour=neighbour):
            pl.semaphore_signal(
                barrier, inc=1, device_id={"outer": neighbour}, device_id_type=MESH_ID
            )

    beside = jnp.where(own < count - 1, 1, 0) + jnp.where(own > 0, 1, 0)
    pl.semaphore_wait(barrier, len(flips) + beside)


def sequence_length(lengths, owners, group):
    total = jnp.int32(0)
    for place in range(lengths.shape[0]):
        total += jnp.where(owners[place] == group, lengths[place], 0)
    return total


def opening(
    qkv, out_weight, gate_up, down, inputs, gain, cotangent, lengths, owners, outer_count, number
):
    rows, width = inputs.shape
    part_rows, wide = qkv.shape
    tall, units = out_weight.shape[0], down.shape[0]
    widths = (wide // 2, wide // 4, wide // 4)
    first_shape = jax.ShapeDtypeStruct((TEAM, part_rows, (wide + tall) // TEAM), jnp.bfloat16)
    gate_up_shape = jax.ShapeDtypeStruct((TEAM, part_rows, 2 * units // TEAM), jnp.bfloat16)
    down_shape = jax.ShapeDtypeStruct((TEAM, part_rows, units // TEAM), jnp.bfloat16)
    cut = balanced(rows, crossing((first_shape, gate_up_shape), width))

    def kernel(
        lengths, owners, qkv, out_weight, inputs, gain, gate_up, down, cotangent,
        out, mixed, full, low, down_pieces,
        normed, first, pieces, gate_up_v, down_v, cotangent_v, load_sem, line_send, line_recv, *sems
    ):
        near, core, tp = spots()
        outer = lax.axis_index("outer")
        begin_tp, begin_near, middle, middle_rest, later, finish = plan_gather(
            normed, out, *sems[:3], cut=cut, apart=True
        )
        team = plan_exchange(first, full.at[outer], *sems[3:6])
        others = plan_exchange(pieces, mixed, *sems[6:9])
        push, take, settle = plan_line(full, line_send, line_recv, outer_count)
        fetch = [
            pltpu.make_async_copy(source, target, load_sem.at[place])
            for place, (source, target) in enumerate(
                ((cotangent, cotangent_v), (gate_up, gate_up_v), (down, down_v))
            )
        ]
        for copy in fetch:
            copy.start()
        for member, across, inside in spans(widths):
            first[member, :, inside] = qkv[:, across].astype(jnp.bfloat16)
        for member in range(TEAM):
            at = pl.ds(member * (tall // TEAM), tall // TEAM)
            first[member, :, wide // TEAM :] = out_weight[at].astype(jnp.bfloat16).T
        greet_all(EVERYONE_NEAR, outer_count)
        for copy in team:
            copy.start()

        def prepare(at):
            value = inputs[at].astype(jnp.float32)
            normed[at] = (value * rms_scale(value) * gain[...]).astype(jnp.bfloat16)

        row_loop(0, rows, prepare)
        begin_tp()
        fetch[1].wait()
        for member, across, inside in spans((units, units)):
            pieces[member, :, inside] = gate_up_v[:, across].astype(jnp.bfloat16)
        for copy in team:
            copy.wait()
        push(0)
        begin_near()
        length = sequence_length(lengths, owners, outer * TEAM + near * CORE + core)
        fetch[0].wait()

        def mask(at):
            row = lax.broadcasted_iota(jnp.int32, (CHUNK, width), 0) + at.start + tp * rows
            value = jnp.where(row < length, cotangent_v[at].astype(jnp.float32), 0.0)
            low[at] = value.astype(jnp.bfloat16)

        row_loop(0, rows, mask)
        fetch[2].wait()
        for member in range(TEAM):
            at = pl.ds(member * (units // TEAM), units // TEAM)
            down_pieces[member] = down_v[at].astype(jnp.bfloat16).T
        middle()
        take(0)
        middle_rest()
        for copy in others:
            copy.start()
        later()
        for step in range(1, outer_count - 1):
            take(step)
        finish()
        settle()
        for copy in others:
            copy.wait()

    scalars = pl.BlockSpec(memory_space=pltpu.SMEM)
    outs = pl.pallas_call(
        kernel,
        name="opening",
        out_shape=(
            layer_rows(rows, width),
            gate_up_shape,
            jax.ShapeDtypeStruct((outer_count,) + first_shape.shape, jnp.bfloat16),
            jax.ShapeDtypeStruct((rows, width), jnp.bfloat16),
            down_shape,
        ),
        in_specs=[scalars] * 2 + [in_vmem()] * 4 + [anywhere()] * 3,
        out_specs=(anywhere(),) * 3 + (in_vmem(),) * 2,
        scratch_shapes=[
            pltpu.VMEM((rows, width), jnp.bfloat16),
            pltpu.VMEM(first_shape.shape, jnp.bfloat16),
            pltpu.VMEM(gate_up_shape.shape, jnp.bfloat16),
            pltpu.VMEM(gate_up.shape, gate_up.dtype),
            pltpu.VMEM(down.shape, down.dtype),
            pltpu.VMEM(cotangent.shape, cotangent.dtype),
            pltpu.SemaphoreType.DMA((3,)),
            pltpu.SemaphoreType.DMA((2, outer_count, 2)),
            pltpu.SemaphoreType.DMA((2, outer_count, 2)),
        ]
        + gather_scratch()
        + exchange_scratch() * 2,
        compiler_params=params(number),
        cost_estimate=cost_of(60),
    )(
        lengths,
        owners,
        qkv,
        out_weight,
        inputs,
        gain.reshape(1, width),
        gate_up,
        down,
        cotangent,
    )
    gathered, mixed, full, low, down_pieces = outs
    return (
        gathered.reshape(-1, width),
        mixed,
        full.reshape(-1, first_shape.shape[2]),
        low,
        down_pieces,
    )


def spread(part, rows):
    return part.reshape(NEAR, CORE, 2, rows, part.shape[-1])


def read(ref, at):
    return ref[at].astype(jnp.float32)


def branch_and_norm(part, residual, gain, number, name):
    rows, width = residual.shape
    cut = rows // 2

    def kernel(part, residual, gain, hidden, out, *scratch):
        normed, sems = scratch[SUM_SCRATCH], scratch[SUM_SCRATCH + 1 :]
        steps, from_tp, from_near = plan_sum_of(part, hidden, scratch[:SUM_SCRATCH], cut)
        onward = plan_gather(normed, out, *sems, cut=cut)
        greet(NEIGHBOURS)
        for step in steps[:3]:
            step()

        def finish(at):
            value = hidden[at] + read(from_tp, at) + read(from_near, at)
            value = read(residual, at) + value
            hidden[at] = value
            normed[at] = (value * rms_scale(value) * gain[...]).astype(jnp.bfloat16)

        steps[3](finish)
        for step in onward:
            step()

    hidden, full = pl.pallas_call(
        kernel,
        name=name,
        out_shape=(jax.ShapeDtypeStruct((rows, width), jnp.float32), layer_rows(rows, width)),
        in_specs=[anywhere(), in_vmem(), in_vmem()],
        out_specs=(in_vmem(), anywhere()),
        scratch_shapes=sum_scratch(rows, width, cut)
        + [pltpu.VMEM((rows, width), jnp.bfloat16)]
        + gather_scratch(),
        compiler_params=params(number),
        cost_estimate=cost_of(95),
    )(spread(part, rows), residual, gain.reshape(1, width))
    return hidden, full.reshape(-1, width)


def norm_back(value, gain, grad):
    scale = rms_scale(value)
    scaled = grad * gain
    inner = jnp.mean(scaled * value, axis=-1, keepdims=True)
    return scale * scaled - value * (scale * scale * scale * inner), grad * value * scale


def sequence_order():
    near, core, _ = spots()
    return [
        (near if place >= 2 else 1 - near) * CORE + (core if place % 2 else 1 - core)
        for place in range(TEAM)
    ]


def times_turned(left, weights, target):
    for start in range(0, weights.shape[0], 512):
        at = pl.ds(start, 512)
        target[:, at] = lax.dot_general(
            left, weights[at, :], (((1,), (1,)), ((), ())), preferred_element_type=jnp.float32
        ).astype(target.dtype)


def feed_back_rest(
    grad_gate, grad_up, weights, active, down, normed, values, upstream, gain, outer_count, number, name
):
    rows, width = values.shape
    count, both_rows, units = grad_gate.shape
    all_rows = count * both_rows
    past = all_rows - width
    cut = rows // 2
    split, share = team_split(width, outer_count)
    turns = width // 512

    def kernel(
        gate, ups, weights, active, down, normed, values, upstream, gain,
        result, gain_grad, low, branch, grad_weight, *scratch
    ):
        (grad_v, weights_v, active_v, down_v, values_v, upstream_v, parts, total), rest = (
            scratch[:8],
            scratch[8:],
        )
        (shares, staged, load_sem, store_sem, chunk_sem, piece_sem), sums = rest[:6], rest[6:]
        from_tp, from_near = sums[3], sums[4]
        near, core, tp = spots()
        members = sequence_order()
        outgoing = [parts.at[place, half] for place, half in ((0, 1 - tp), (2, 1 - tp), (0, tp), (2, tp))]
        mine = [parts.at[place, half] for place, half in ((1, 1 - tp), (3, 1 - tp), (1, tp), (3, tp))]
        steps, (send_far, send_tp, send_near) = plan_sum(outgoing, mine, (), total, sums, cut)
        stores = [
            pltpu.make_async_copy(shares.at[place % 2], branch.at[place], store_sem.at[place])
            for place in range(count)
        ]
        fetch = [
            pltpu.make_async_copy(source, target, load_sem.at[place])
            for place, (source, target) in enumerate(
                (
                    (weights, weights_v),
                    (values, values_v),
                    (upstream, upstream_v),
                    (active, active_v),
                    (down, down_v),
                    (ups, active_v),
                )
            )
        ]
        grads = []
        for place, member in enumerate(members):
            for side, source in enumerate((gate, ups)):
                grads.append(
                    pltpu.make_async_copy(
                        source.at[member],
                        grad_v.at[place % 2, :, :, pl.ds(side * units, units)],
                        load_sem.at[6 + 2 * place + side],
                    )
                )

        def bring(place):
            grads[2 * place].start()
            grads[2 * place + 1].start()

        def brought(place):
            grads[2 * place].wait()
            grads[2 * place + 1].wait()

        def back(place, half):
            times_turned(grad_v[place % 2, half], weights_v, parts.at[place, half])

        def chunk(turn):
            at, slot = pl.ds(turn * 512, 512), turn % 2
            return [
                pltpu.make_async_copy(
                    normed.at[pl.ds(0, width), at],
                    weights_v.at[:, pl.ds(slot * 1024, 512)],
                    chunk_sem.at[slot, 0],
                ),
                pltpu.make_async_copy(
                    normed.at[pl.ds(width, past), at],
                    weights_v.at[pl.ds(slot * past, past), pl.ds(512, 512)],
                    chunk_sem.at[slot, 1],
                ),
            ]

        def pieces(turn):
            slot = turn % 2
            return [
                pltpu.make_async_copy(
                    staged.at[slot, :, pl.ds(place * share, share)],
                    grad_weight.at[turn * (512 // share) + place],
                    piece_sem.at[slot, place],
                )
                for place in range(512 // share)
            ]

        fetch[0].start()
        bring(0)
        bring(1)
        greet(NEIGHBOURS)
        fetch[0].wait()
        brought(0)
        back(0, 1 - tp)
        steps[0]((0,))
        brought(1)
        back(1, 1 - tp)
        send_far()
        back(0, tp)
        steps[0]((2,))
        bring(2)
        for place in (3, 4, 1, 2):
            fetch[place].start()
        back(1, tp)
        send_near()
        bring(3)
        brought(2)
        back(2, 1 - tp)
        steps[0]((1,))
        brought(3)
        back(3, 1 - tp)
        send_tp()
        back(2, tp)
        steps[0]((3,))
        back(3, tp)
        for turn in (0, 1):
            for copy in chunk(turn):
                copy.start()
        fetch[3].wait()
        fetch[4].wait()
        for place in range(count):
            if place >= 2:
                stores[place - 2].wait()
            for half in range(2):
                times_turned(active_v[place, half], down_v, shares.at[place % 2, half])
            stores[place].start()
        fetch[5].start()
        steps[2]()
        fetch[5].wait()
        for turn in range(turns):
            slot = turn % 2
            for copy in chunk(turn):
                copy.wait()
            left = active_v[...].reshape(all_rows, units)
            product = lax.dot_general(
                left[:width],
                weights_v[:, slot * 1024 : slot * 1024 + 512],
                (((0,), (0,)), ((), ())),
                preferred_element_type=jnp.float32,
            ) + lax.dot_general(
                left[width:],
                weights_v[slot * past : (slot + 1) * past, 512:1024],
                (((0,), (0,)), ((), ())),
                preferred_element_type=jnp.float32,
            )
            if turn >= 2:
                for copy in pieces(turn - 2):
                    copy.wait()
            staged[slot] = product.astype(staged.dtype)
            for copy in pieces(turn):
                copy.start()
            if turn + 2 < turns:
                for copy in chunk(turn + 2):
                    copy.start()
        fetch[1].wait()
        fetch[2].wait()
        gain_grad[...] = jnp.zeros_like(gain_grad)

        def finish(at):
            grad = total[at] + read(from_tp, at) + read(from_near, at)
            turned, by_gain = norm_back(values_v[at], gain[...], grad)
            gain_grad[...] += by_gain.reshape(CHUNK // 8, 8, width).sum(axis=0)
            value = read(upstream_v, at) + turned
            total[at] = value
            low[at] = value.astype(jnp.bfloat16)

        steps[3](finish)
        store = pltpu.make_async_copy(total, result, store_sem.at[count])
        store.start()
        for turn in range(max(0, turns - 2), turns):
            for copy in pieces(turn):
                copy.wait()
        for copy in [store] + stores[2:]:
            copy.wait()

    low_type = jnp.bfloat16
    halves = (count, 2, rows, units)
    result, gain_grad, rounded, branch, grad_weight = pl.pallas_call(
        kernel,
        name=name,
        out_shape=(
            jax.ShapeDtypeStruct((rows, width), jnp.float32),
            jax.ShapeDtypeStruct((8, width), jnp.float32),
            jax.ShapeDtypeStruct((rows, width), low_type),
            jax.ShapeDtypeStruct((count, 2, rows, width), low_type),
            jax.ShapeDtypeStruct((outer_count * split, units, share), low_type),
        ),
        in_specs=[anywhere()] * 8 + [in_vmem()],
        out_specs=(anywhere(), in_vmem(), in_vmem(), anywhere(), anywhere()),
        scratch_shapes=[
            pltpu.VMEM((2, 2, rows, 2 * units), low_type),
            pltpu.VMEM(weights.shape, low_type),
            pltpu.VMEM(halves, low_type),
            pltpu.VMEM(down.shape, low_type),
            pltpu.VMEM((rows, width), values.dtype),
            pltpu.VMEM((rows, width), upstream.dtype),
            pltpu.VMEM((count, 2, rows, width), low_type),
            pltpu.VMEM((rows, width), jnp.float32),
            pltpu.VMEM((2, 2, rows, width), low_type),
            pltpu.VMEM((2, units, 512), low_type),
            pltpu.SemaphoreType.DMA((6 + 2 * count,)),
            pltpu.SemaphoreType.DMA((count + 1,)),
            pltpu.SemaphoreType.DMA((2, 2)),
            pltpu.SemaphoreType.DMA((2, 512 // share)),
        ]
        + sum_scratch(rows, width, cut, fetched=False),
        compiler_params=params(number),
        cost_estimate=cost_of(60),
    )(
        grad_gate.reshape(halves),
        grad_up.reshape(halves),
        weights,
        active.reshape(halves),
        down,
        normed,
        values,
        upstream,
        gain.reshape(1, width),
    )
    return result, gain_grad.sum(axis=0), rounded, branch.reshape(-1, width), grad_weight


def square_sum(values):
    values = values.reshape(-1, values.shape[-1]).astype(jnp.float32)
    return jnp.sum(values * values, keepdims=True)


def corner(value):
    row = lax.broadcasted_iota(jnp.int32, (8, HD), 0)
    column = lax.broadcasted_iota(jnp.int32, (8, HD), 1)
    return jnp.where((row == 0) & (column == 0), value, 0.0)


def norm_back_last(part, values, upstream, gain, extra, squared, number, name):
    rows, width = values.shape
    extras, count = len(extra), len(squared)
    cut = balanced(rows, crossing(extra, width))

    def kernel(part, values, upstream, gain, *rest):
        pieces, rest = rest[:extras], rest[extras:]
        squared, (result, gain_grad, squares), rest = (
            rest[:count],
            rest[count : count + 3],
            rest[count + 3 :],
        )
        mixed, rest = rest[:extras], rest[extras:]
        sums, rest = rest[:SUM_SCRATCH], rest[SUM_SCRATCH:]
        (total, values_v, upstream_v, load_sem), rest = rest[:4], rest[4:]
        squared_v, sems = rest[:count], rest[count:]
        steps, from_tp, from_near = plan_sum_of(part, total, sums, cut)
        copies = plan_exchanges(pieces, mixed, sems)
        fetch = [
            pltpu.make_async_copy(source, target, load_sem.at[place])
            for place, (source, target) in enumerate(
                zip((values, upstream) + tuple(squared), (values_v, upstream_v) + tuple(squared_v))
            )
        ]
        greet(EVERYONE_NEAR)
        steps[0]()
        for copy in copies:
            copy.start()
        for copy in fetch:
            copy.start()
        steps[1]()
        for copy in fetch:
            copy.wait()
        squares[...] = corner(sum(square_sum(ref[...]) for ref in squared_v))
        steps[2]()
        gain_grad[...] = jnp.zeros_like(gain_grad)

        def finish(at):
            grad = total[at] + read(from_tp, at) + read(from_near, at)
            back, by_gain = norm_back(read(values_v, at), gain[...], grad)
            gain_grad[...] += by_gain.reshape(CHUNK // 8, 8, width).sum(axis=0)
            result[at] = (upstream_v[at] + back).astype(jnp.bfloat16)

        steps[3](finish)
        for copy in copies:
            copy.wait()

    return pl.pallas_call(
        kernel,
        name=name,
        out_shape=(
            jax.ShapeDtypeStruct((rows, width), jnp.bfloat16),
            jax.ShapeDtypeStruct((8, width), jnp.float32),
            jax.ShapeDtypeStruct((8, HD), jnp.float32),
        )
        + tuple(like(piece) for piece in extra),
        in_specs=[anywhere()] * 3 + [in_vmem()] * (1 + extras) + [anywhere()] * count,
        out_specs=(in_vmem(), in_vmem(), in_vmem()) + (anywhere(),) * extras,
        scratch_shapes=sum_scratch(rows, width, cut)
        + [
            pltpu.VMEM((rows, width), jnp.float32),
            pltpu.VMEM((rows, width), values.dtype),
            pltpu.VMEM((rows, width), upstream.dtype),
            pltpu.SemaphoreType.DMA((2 + count,)),
        ]
        + [pltpu.VMEM(each.shape, each.dtype) for each in squared]
        + exchange_scratch() * extras,
        compiler_params=params(number),
        cost_estimate=cost_of(65),
    )(spread(part, rows), values, upstream, gain.reshape(1, width), *extra, *squared)


def total_everywhere(values, first, squares, pieces, outer_count, number, name):
    gains = values.shape[0]
    shape = (gains + 8, HD)
    width = first.shape[1]

    def kernel(values, first, squares, pieces, out, norm, factor, mixed, layer, outers, send, recv, *sems):
        near, core, tp = spots()
        outer = lax.axis_index("outer")
        partners = [
            flipped(a, b, c)
            for a in range(NEAR)
            for b in range(CORE)
            for c in range(2)
            if a + b + c
        ]
        partners += [{"outer": (outer + step) % outer_count} for step in range(1, outer_count)]
        barrier = pltpu.get_barrier_semaphore()
        for partner in partners:
            pl.semaphore_signal(barrier, inc=1, device_id=partner, device_id_type=MESH_ID)
        pl.semaphore_wait(barrier, len(partners))

        def share(slots, mine, first, count):
            copies = []
            for number in range(first, first + count):
                copy = pltpu.make_async_remote_copy(
                    src_ref=slots.at[mine],
                    dst_ref=slots.at[mine],
                    send_sem=send.at[number],
                    recv_sem=recv.at[number],
                    device_id=partners[number],
                    device_id_type=MESH_ID,
                )
                copy.start()
                copies.append(copy)
            return copies

        mine = near * (CORE * 2) + core * 2 + tp
        layer[mine, :gains] = values[...]
        layer[mine, gains:] = squares[...] + corner(square_sum(pieces[...]))
        sums = jnp.sum(first[...], axis=0, keepdims=True)
        for place in range(width // HD):
            layer[mine, place : place + 1] = sums[:, place * HD : (place + 1) * HD]
        copies = share(layer, mine, 0, 7)
        others = plan_exchange(pieces, mixed, *sems)
        for copy in others:
            copy.start()
        for copy in copies:
            copy.wait()
        total = layer[0]
        for slot in range(1, 8):
            total = total + layer[slot]
        outers[outer] = total
        for copy in share(outers, outer, 7, outer_count - 1):
            copy.wait()
        total = outers[0]
        for slot in range(1, outer_count):
            total = total + outers[slot]
        out[...] = total
        gain_part = total[:gains]
        root = jnp.sqrt(
            jnp.sum(gain_part * gain_part, keepdims=True) + jnp.sum(total[gains:], keepdims=True)
        )
        norm[...] = jnp.broadcast_to(root, norm.shape)
        factor[...] = jnp.broadcast_to(
            jnp.minimum(1.0, clip_norm / (root + 1e-06)), factor.shape
        )
        for copy in others:
            copy.wait()

    tile = jax.ShapeDtypeStruct((8, HD), jnp.float32)
    return pl.pallas_call(
        kernel,
        name=name,
        out_shape=(jax.ShapeDtypeStruct(shape, jnp.float32), tile, tile, like(pieces)),
        in_specs=[in_vmem()] * 4,
        out_specs=(in_vmem(), in_vmem(), in_vmem(), anywhere()),
        scratch_shapes=[
            pltpu.VMEM((8,) + shape, jnp.float32),
            pltpu.VMEM((outer_count,) + shape, jnp.float32),
            pltpu.SemaphoreType.DMA((6 + outer_count,)),
            pltpu.SemaphoreType.DMA((6 + outer_count,)),
        ]
        + exchange_scratch(),
        compiler_params=params(number),
    )(values, first, squares, pieces)


def head_scale(raw, gain, cos_full, sin_full):
    normed = raw * rms_scale(raw) * gain
    return (normed * cos_full + pltpu.roll(normed, HD // 2, 1) * sin_full).astype(jnp.bfloat16)


def head_back(raw, gain, grad, cos_full, sin_full):
    grad = grad * cos_full - pltpu.roll(grad, HD // 2, 1) * sin_full
    return norm_back(raw, gain, grad)


def columns(index):
    return pl.ds(index * HD, HD)


def head_inputs(proj, gains, cos_ref, sin_ref, queries, keys, values, heads):
    for head in range(heads):
        queries[head] = head_scale(
            proj[0, :, columns(head)], gains[0:1, :], cos_ref[...], sin_ref[...]
        )
    keys[...] = head_scale(
        proj[0, :, columns(heads)], gains[1:2, :], cos_ref[...], sin_ref[...]
    )
    values[...] = proj[0, :, columns(heads + 1)].astype(jnp.bfloat16)


def masked_scores(stacked, keys, step, length):
    scores = lax.dot_general(
        stacked, keys, (((1,), (1,)), ((), ())), preferred_element_type=jnp.float32
    ) * (HD ** (-0.5))
    row = lax.broadcasted_iota(jnp.int32, scores.shape, 0) % BLOCK + step * BLOCK
    column = lax.broadcasted_iota(jnp.int32, scores.shape, 1)
    return jnp.where((column <= row) & (column < length), scores, masked_score)


def stack_heads(ref, at, heads):
    return jnp.concatenate([ref[head, at] for head in range(heads)], axis=0)


def per_sequence(*shape):
    return pl.BlockSpec((1,) + shape, lambda s: (s,) + (0,) * len(shape))


def whole(*shape):
    return pl.BlockSpec(shape, lambda s: (0,) * len(shape), pipeline_mode=pl.Buffered(1))


def across_columns(left, weights, first, width, out):
    total = weights.shape[0]
    for start in range(0, total, 512):
        at = pl.ds(start, 512)
        out[0, :, at] = lax.dot_general(
            left,
            weights[at, first : first + width],
            (((1,), (1,)), ((), ())),
            preferred_element_type=jnp.float32,
        ).astype(out.dtype)


def attend(normed, weights, cotangent, extra, lengths, owners, cos_full, sin_full, gains, heads, early, number):
    count, rows, width = normed.shape
    wide = (heads + 2) * HD
    extras = len(extra)
    own_rows = cotangent.shape[0]
    cut = balanced(early, crossing(extra, width))

    def kernel(lengths, owners, normed, weights_any, cos_ref, sin_ref, gains, own, *rest):
        pieces, rest = rest[:extras], rest[extras:]
        (proj, out, logs, branch, gathered), rest = rest[:5], rest[5:]
        mixed, rest = rest[:extras], rest[extras:]
        (queries, keys, values, weights, weights_sem), sems = rest[:5], rest[5:]
        fetch = pltpu.make_async_copy(weights_any, weights, weights_sem)
        sequence = pl.program_id(0)
        steps = plan_gather(own, gathered, *sems[:3], cut=cut, rows=early)
        copies = plan_exchanges(pieces, mixed, sems[3:])

        @pl.when(sequence == 0)
        def _():
            fetch.start()
            greet(EVERYONE_NEAR)
            steps[0]()
            for copy in copies:
                copy.start()
            fetch.wait()

        group = lax.axis_index("outer") * TEAM + sequence
        length = sequence_length(lengths, owners, group)
        proj[0] = jnp.dot(
            normed[0], weights[:, :wide], preferred_element_type=jnp.float32
        )
        head_inputs(proj, gains, cos_ref, sin_ref, queries, keys, values, heads)
        lane = lax.broadcasted_iota(jnp.int32, (BLOCK, HD), 1)
        for step in range(rows // BLOCK):
            at = pl.ds(step * BLOCK, BLOCK)
            seen = pl.ds(0, (step + 1) * BLOCK)
            scores = masked_scores(stack_heads(queries, at, heads), keys[seen], step, length)
            top = jnp.max(scores, axis=-1, keepdims=True)
            exponent = jnp.exp(scores - top)
            total = jnp.sum(exponent, axis=-1, keepdims=True)
            probs = (exponent / total).astype(jnp.bfloat16)
            mixed_values = jnp.dot(probs, values[seen], preferred_element_type=jnp.float32)
            log_total = top + jnp.log(total)
            kept = jnp.zeros((BLOCK, HD), jnp.float32)
            for head in range(heads):
                mine = slice(head * BLOCK, (head + 1) * BLOCK)
                out[0, at, columns(head)] = mixed_values[mine].astype(jnp.bfloat16)
                kept = jnp.where(lane == head, log_total[mine], kept)
            logs[0, at] = kept
        across_columns(out[0], weights, wide, heads * HD, branch)

        @pl.when(sequence == 1)
        def _():
            steps[1]()

        @pl.when(sequence == 2)
        def _():
            steps[2]()

        @pl.when(sequence == count - 1)
        def _():
            steps[3]()
            for copy in copies:
                copy.wait()

    outs = pl.pallas_call(
        kernel,
        name="attend",
        grid=(count,),
        out_shape=(
            jax.ShapeDtypeStruct((count, rows, wide), jnp.float32),
            jax.ShapeDtypeStruct((count, rows, heads * HD), jnp.bfloat16),
            jax.ShapeDtypeStruct((count, rows, HD), jnp.float32),
            jax.ShapeDtypeStruct((count, rows, width), jnp.bfloat16),
            layer_rows(own_rows, width),
        )
        + tuple(like(piece) for piece in extra),
        in_specs=[
            pl.BlockSpec(memory_space=pltpu.SMEM),
            pl.BlockSpec(memory_space=pltpu.SMEM),
            per_sequence(rows, width),
            anywhere(),
            whole(rows, HD),
            whole(rows, HD),
            whole(2, HD),
            whole(own_rows, width),
        ]
        + [whole(*piece.shape) for piece in extra],
        out_specs=(
            per_sequence(rows, wide),
            per_sequence(rows, heads * HD),
            per_sequence(rows, HD),
            per_sequence(rows, width),
            anywhere(),
        )
        + (anywhere(),) * extras,
        scratch_shapes=[
            pltpu.VMEM((heads, rows, HD), jnp.bfloat16),
            pltpu.VMEM((rows, HD), jnp.bfloat16),
            pltpu.VMEM((rows, HD), jnp.bfloat16),
            pltpu.VMEM(weights.shape, weights.dtype),
            pltpu.SemaphoreType.DMA,
        ]
        + gather_scratch()
        + exchange_scratch() * extras,
        compiler_params=params(number),
        cost_estimate=cost_of(50),
    )(lengths, owners, normed, weights, cos_full, sin_full, gains, cotangent, *extra)
    return outs


def team_split(width, outer_count):
    split = TEAM if width // outer_count % (TEAM * HD) == 0 else 1
    return split, width // outer_count // split


def local_first(place):
    near, core, _ = spots()
    other_near, other_core = place // 2, place % 2
    return (near + other_near * (1 - 2 * near)) * CORE + core + other_core * (1 - 2 * core)


def ordered(*shape):
    return pl.BlockSpec((1,) + shape, lambda s: (local_first(s),) + (0,) * len(shape))


def attend_back(
    projected,
    normed,
    attended,
    own_grad,
    logs,
    weights,
    part,
    hidden,
    extra,
    outer_count,
    lengths,
    owners,
    cos_full,
    sin_full,
    gains,
    heads,
    number,
):
    count, rows, wide = projected.shape
    own_rows, width = hidden.shape
    extras = len(extra)
    cut = balanced(own_rows, crossing(extra, width))

    every = wide + heads * HD
    split, share = team_split(width, outer_count)

    def kernel(
        lengths, owners, proj, normed, attended, own_grad, logs, weights_any, cos_ref, sin_ref, gains, part, hidden, *rest
    ):
        pieces, rest = rest[:extras], rest[extras:]
        (gathered, gain_grad, back_part, output, grad_weights), rest = rest[:5], rest[5:]
        mixed, rest = rest[:extras], rest[extras:]
        (queries, keys, values, grad_att, grad_q, grad_k, grad_v_sum, summed), rest = rest[:8], rest[8:]
        (total, held, held_sem, out, grad_v, grad_sem), rest = rest[:6], rest[6:]
        (weights, staged, weights_sem, store_sem), rest = rest[:4], rest[4:]
        sums, sems, rest = rest[:SUM_SCRATCH], rest[SUM_SCRATCH : SUM_SCRATCH + 3], rest[SUM_SCRATCH + 3 :]
        place = pl.program_id(0)
        sequence = local_first(place)
        steps, from_tp, from_near = plan_sum_of(part, total, sums, cut)
        gather = plan_gather(own_grad, gathered, *sems, cut=own_rows // 2, parts=True)
        copies = plan_exchanges(pieces, mixed, rest)
        fetch_weights = pltpu.make_async_copy(weights_any, weights, weights_sem)
        store = pltpu.make_async_copy(staged, grad_weights, store_sem)

        def arrival(which):
            member = local_first(which)
            return pltpu.make_async_copy(
                gathered.at[member // CORE, member % CORE],
                grad_v.at[which % 2],
                grad_sem.at[which % 2],
            )

        fetch = pltpu.make_async_copy(hidden, held, held_sem)

        @pl.when(place == 0)
        def _():
            greet(EVERYONE_NEAR)
            gather[0]()
            steps[0]()
            fetch.start()
            fetch_weights.start()
            gain_grad[...] = jnp.zeros_like(gain_grad)
            summed[...] = jnp.zeros_like(summed)
            gather[1]()
            gather[2]()
            gather[3]()
            arrival(0).start()
            fetch_weights.wait()

        @pl.when(place == 2)
        def _():
            arrival(3).start()

        head_inputs(proj, gains, cos_ref, sin_ref, queries, keys, values, heads)
        grad_k[...] = jnp.zeros_like(grad_k)
        grad_v_sum[...] = jnp.zeros_like(grad_v_sum)
        arrival(place).wait()
        grad = grad_v[place % 2].reshape(rows, width)
        group = lax.axis_index("outer") * TEAM + sequence
        length = sequence_length(lengths, owners, group)
        grad_att[...] = jnp.dot(
            grad, weights[:, wide:], preferred_element_type=jnp.float32
        ).astype(jnp.bfloat16)

        for step in range(rows // BLOCK):
            at = pl.ds(step * BLOCK, BLOCK)
            seen = pl.ds(0, (step + 1) * BLOCK)
            stacked = stack_heads(queries, at, heads)
            above = jnp.concatenate([grad_att[at, columns(head)] for head in range(heads)], axis=0)
            log_total = jnp.concatenate(
                [logs[0, at, head : head + 1] for head in range(heads)], axis=0
            )
            probs = jnp.exp(masked_scores(stacked, keys[seen], step, length) - log_total)
            grad_probs = lax.dot_general(
                above, values[seen], (((1,), (1,)), ((), ())), preferred_element_type=jnp.float32
            )
            inner = jnp.sum(probs * grad_probs, axis=-1, keepdims=True)
            grad_scores = (probs * (grad_probs - inner)).astype(jnp.bfloat16)
            by_query = jnp.dot(grad_scores, keys[seen], preferred_element_type=jnp.float32)
            for head in range(heads):
                grad_q[head, at] = by_query[head * BLOCK : (head + 1) * BLOCK] * (HD ** (-0.5))
            grad_k[seen] += lax.dot_general(
                grad_scores, stacked, (((0,), (0,)), ((), ())), preferred_element_type=jnp.float32
            )
            grad_v_sum[seen] += lax.dot_general(
                probs.astype(jnp.bfloat16),
                above,
                (((0,), (0,)), ((), ())),
                preferred_element_type=jnp.float32,
            )

        def settle(column, gain, value):
            back, by_gain = head_back(
                proj[0, :, columns(column)], gains[gain : gain + 1, :], value, cos_ref[...], sin_ref[...]
            )
            out[:, columns(column)] = back.astype(jnp.bfloat16)
            gain_grad[gain] += by_gain.reshape(rows // 8, 8, HD).sum(axis=0)

        for head in range(heads):
            settle(head, 0, grad_q[head])
        settle(heads, 1, grad_k[...] * (HD ** (-0.5)))
        out[:, columns(heads + 1)] = grad_v_sum[...].astype(jnp.bfloat16)

        across_columns(out[...], weights, 0, wide, back_part)

        by_projected, by_attended = out[...].T, attended[0].T
        for start in range(0, width, 512):
            at = pl.ds(start, 512)
            summed[:wide, at] += jnp.dot(
                by_projected, normed[0, :, at], preferred_element_type=jnp.float32
            )
            summed[wide:, at] += jnp.dot(
                by_attended, grad[:, start : start + 512], preferred_element_type=jnp.float32
            )

        @pl.when(place == 0)
        def _():
            gather[5]()
            steps[1]()
            for copy in copies:
                copy.start()
            gather[4]()
            arrival(1).start()

        @pl.when(place == 1)
        def _():
            steps[2]()
            gather[6]()
            arrival(2).start()

        @pl.when(place == count - 1)
        def _():
            for outer in range(outer_count):
                for member in range(split):
                    start = (outer * split + member) * share
                    staged[outer, member] = summed[:, start : start + share].astype(jnp.bfloat16)
            store.start()
            fetch.wait()

            def finish(at):
                value = total[at] + read(from_tp, at) + read(from_near, at)
                output[at] = (held[at] + value).astype(jnp.bfloat16)

            steps[3](finish)
            store.wait()
            for copy in copies:
                copy.wait()

    return pl.pallas_call(
        kernel,
        name="attend_back",
        grid=(count,),
        out_shape=(
            layer_rows(own_rows, width),
            jax.ShapeDtypeStruct((2, 8, HD), jnp.float32),
            jax.ShapeDtypeStruct((count, rows, width), jnp.bfloat16),
            jax.ShapeDtypeStruct((own_rows, width), jnp.bfloat16),
            jax.ShapeDtypeStruct((outer_count, split, every, share), jnp.bfloat16),
        )
        + tuple(like(piece) for piece in extra),
        in_specs=[
            pl.BlockSpec(memory_space=pltpu.SMEM),
            pl.BlockSpec(memory_space=pltpu.SMEM),
            ordered(rows, wide),
            ordered(rows, width),
            ordered(rows, heads * HD),
            whole(own_rows, width),
            ordered(rows, HD),
            anywhere(),
            whole(rows, HD),
            whole(rows, HD),
            whole(2, HD),
            anywhere(),
            anywhere(),
        ]
        + [whole(*piece.shape) for piece in extra],
        out_specs=(
            anywhere(),
            pl.BlockSpec((2, 8, HD), lambda s: (0, 0, 0)),
            ordered(rows, width),
            whole(own_rows, width),
            anywhere(),
        )
        + (anywhere(),) * extras,
        scratch_shapes=[
            pltpu.VMEM((heads, rows, HD), jnp.bfloat16),
            pltpu.VMEM((rows, HD), jnp.bfloat16),
            pltpu.VMEM((rows, HD), jnp.bfloat16),
            pltpu.VMEM((rows, heads * HD), jnp.bfloat16),
            pltpu.VMEM((heads, rows, HD), jnp.float32),
            pltpu.VMEM((rows, HD), jnp.float32),
            pltpu.VMEM((rows, HD), jnp.float32),
            pltpu.VMEM((every, width), jnp.float32),
            pltpu.VMEM((own_rows, width), jnp.float32),
            pltpu.VMEM((own_rows, width), jnp.float32),
            pltpu.SemaphoreType.DMA,
            pltpu.VMEM((rows, wide), jnp.bfloat16),
            pltpu.VMEM((2, 2, own_rows, width), jnp.bfloat16),
            pltpu.SemaphoreType.DMA((2,)),
            pltpu.VMEM(weights.shape, weights.dtype),
            pltpu.VMEM((outer_count, split, every, share), jnp.bfloat16),
            pltpu.SemaphoreType.DMA,
            pltpu.SemaphoreType.DMA,
        ]
        + sum_scratch(own_rows, width, cut)
        + gather_scratch()
        + exchange_scratch() * extras,
        compiler_params=params(number),
        cost_estimate=cost_of(50),
    )(
        lengths,
        owners,
        projected,
        normed,
        attended,
        own_grad,
        logs,
        weights,
        cos_full,
        sin_full,
        gains,
        spread(part, own_rows),
        hidden,
        *extra,
    )


def feed(normed, weights, cotangent, gathered, early, number):
    count, rows, width = normed.shape
    units = weights.shape[1] // 2
    late = cotangent.shape[0] - early

    def kernel(normed, weights_any, own, _, product, active, out, weights, weights_sem, *sems):
        fetch = pltpu.make_async_copy(weights_any, weights, weights_sem)
        steps = plan_gather(
            own, out, *sems, cut=balanced(late, 0), base=early, rows=late
        )
        sequence = pl.program_id(0)

        @pl.when(sequence == 0)
        def _():
            fetch.start()
            greet(NEIGHBOURS)
            steps[0]()
            fetch.wait()

        for start in range(0, units, 256):
            gate_at, up_at = pl.ds(start, 256), pl.ds(units + start, 256)
            gate = jnp.dot(normed[0], weights[:, gate_at], preferred_element_type=jnp.float32)
            up = jnp.dot(normed[0], weights[:, up_at], preferred_element_type=jnp.float32)
            product[0, :, gate_at] = gate
            product[0, :, up_at] = up
            active[0, :, gate_at] = swish_product(gate, up).astype(jnp.bfloat16)

        for place in (1, 2, 3):

            @pl.when(sequence == count - 4 + place)
            def _(place=place):
                steps[place]()

    return pl.pallas_call(
        kernel,
        name="feed",
        grid=(count,),
        out_shape=(
            jax.ShapeDtypeStruct((count, rows, 2 * units), jnp.float32),
            jax.ShapeDtypeStruct((count, rows, units), jnp.bfloat16),
            like(gathered),
        ),
        in_specs=[
            per_sequence(rows, width),
            anywhere(),
            whole(*cotangent.shape),
            anywhere(),
        ],
        out_specs=(per_sequence(rows, 2 * units), per_sequence(rows, units), anywhere()),
        scratch_shapes=[pltpu.VMEM(weights.shape, weights.dtype), pltpu.SemaphoreType.DMA]
        + gather_scratch(),
        input_output_aliases={3: 2},
        compiler_params=params(number),
        cost_estimate=cost_of(28),
    )(normed, weights, cotangent, gathered)


def feed_back(grads, weights, product):
    count, rows, width = grads.shape
    units = weights.shape[1]

    def kernel(grads, weights, product, by_gate, by_up):
        for start in range(0, units, 256):
            gate_at, up_at = pl.ds(start, 256), pl.ds(units + start, 256)
            grad = jnp.dot(grads[0], weights[:, gate_at], preferred_element_type=jnp.float32)
            gate, up = product[0, :, gate_at], product[0, :, up_at]
            share = jax.nn.sigmoid(gate)
            slope = grad * up * share * (1.0 + gate * (1.0 - share))
            by_gate[0, :, gate_at] = slope.astype(jnp.bfloat16)
            by_up[0, :, gate_at] = (grad * gate * share).astype(jnp.bfloat16)

    return pl.pallas_call(
        kernel,
        name="feed_back",
        grid=(count,),
        out_shape=(jax.ShapeDtypeStruct((count, rows, units), jnp.bfloat16),) * 2,
        in_specs=[
            per_sequence(rows, width),
            whole(*weights.shape),
            per_sequence(rows, 2 * units),
        ],
        out_specs=(per_sequence(rows, units),) * 2,
        compiler_params=pltpu.CompilerParams(vmem_limit_bytes=VMEM_LIMIT),
        cost_estimate=cost_of(18),
    )(grads, weights, product)


def spans(widths, base=0):
    for member in range(TEAM):
        first, inside = base, 0
        for width in widths:
            share = width // TEAM
            yield member, pl.ds(first + member * share, share), pl.ds(inside, share)
            first += width
            inside += share


def by_columns(start, height, widths, source):
    def run(pieces, update):
        @pl.loop(0, height // CHUNK)
        def _(row):
            rows = pl.ds(pl.multiple_of(start + row * CHUNK, CHUNK), CHUNK)
            for member, across, inside in spans(widths):
                update(rows, across, pieces[member, rows, inside])

    return source, pl.ds(start, height), pl.ds(0, sum(widths)), run


def by_turned(height, base, widths, source, members=range(TEAM)):
    parts = [part for part in spans(widths, base) if part[0] in members]

    def run(pieces, update):
        for member, across, inside in parts:
            update(pl.ds(0, height), across, pieces[member, inside].T)

    if len(members) == 1:
        columns = parts[0][1]
    else:
        columns = pl.ds(base, sum(widths))
    return source, pl.ds(0, height), columns, run


def by_rows(member, height, width, inside, source):
    at, across = pl.ds(member * height, height), pl.ds(0, width)

    def run(pieces, update):
        if inside is None:
            update(at, across, pieces[member].T)
        else:
            update(at, across, pieces[member, pl.ds(inside, height)])

    return source, at, across, run


def adam_all(sets, pieces, factor, gain_grad, gains, passed):
    jobs = [(place,) + job for place, group in enumerate(sets) for job in group[3]]
    count, total, sources, others = len(jobs), len(sets), len(pieces), len(passed)

    def kernel(*refs):
        inputs, refs = refs[: 3 * total], refs[3 * total :]
        piece_refs, factor, refs = refs[:sources], refs[sources], refs[sources + 1 :]
        (gain_grad, *gains), refs = refs[:4], refs[4:]
        passed, refs = refs[:others], refs[others:]
        outputs, refs = refs[: 4 * total], refs[4 * total :]
        new_gains, refs = refs[:3], refs[3:]
        onward, refs = refs[:others], refs[others:]
        held, refs = refs[: 4 * total], refs[4 * total :]
        held_pieces, refs = refs[:sources], refs[sources:]
        between, (piece_sem, in_sem, out_sem, pass_sem) = refs[:others], refs[others:]
        scale = factor[0:1, 0:1]
        loads = [
            pltpu.make_async_copy(piece_refs[place], held_pieces[place], piece_sem.at[place])
            for place in range(sources)
        ]
        arrivals, stores = [], []
        kept = [
            pltpu.make_async_copy(source, target, pass_sem.at[0, place])
            for place, (source, target) in enumerate(zip(passed, between))
        ]
        kept_on = [
            pltpu.make_async_copy(source, target, pass_sem.at[1, place])
            for place, (source, target) in enumerate(zip(between, onward))
        ]
        for slot, (place, source, at, across, _) in enumerate(jobs):
            arrivals.append(
                [
                    pltpu.make_async_copy(
                        inputs[3 * place + number].at[at, across],
                        held[4 * place + number].at[at, across],
                        in_sem.at[3 * slot + number],
                    )
                    for number in range(3)
                ]
            )
        first_use = {}
        for slot, job in enumerate(jobs):
            first_use.setdefault(job[1], slot)

        def bring(slot):
            if slot < count:
                if first_use[jobs[slot][1]] == slot:
                    loads[jobs[slot][1]].start()
                for copy in arrivals[slot]:
                    copy.start()

        for slot in range(AHEAD):
            bring(slot)
        gain_step = adam_update(
            gains[0][...],
            gain_grad[: gains[0].shape[0]],
            gains[1][...],
            gains[2][...],
            scale,
            0.0,
            gain_rate,
        )
        for target, value in zip(new_gains, gain_step):
            target[...] = value
        for slot, (place, source, at, across, run) in enumerate(jobs):
            weight, moment, square, low = held[4 * place : 4 * place + 4]
            if first_use[source] == slot:
                loads[source].wait()
            for copy in arrivals[slot]:
                copy.wait()
            bring(slot + AHEAD)
            if slot == 0:
                for copy in kept:
                    copy.start()

            def update(rows, columns, gradient):
                where = (rows, columns)
                value, one, two = adam_update(
                    weight[where],
                    gradient.astype(jnp.float32),
                    moment[where],
                    square[where],
                    scale,
                    weight_decay,
                    learn_rate,
                )
                weight[where], moment[where], square[where] = value, one, two
                low[where] = value.astype(jnp.bfloat16)

            run(held_pieces[source], update)
            for number, origin in enumerate((weight, moment, square, low)):
                copy = pltpu.make_async_copy(
                    origin.at[at, across],
                    outputs[4 * place + number].at[at, across],
                    out_sem.at[4 * slot + number],
                )
                copy.start()
                stores.append(copy)
            if slot == 4:
                for arrived, copy in zip(kept, kept_on):
                    arrived.wait()
                    copy.start()
        for copy in stores + kept_on:
            copy.wait()

    args, shapes, scratch = [], [], []
    for weight, moment, square, _ in sets:
        args += [weight, moment, square]
        low = jax.ShapeDtypeStruct(weight.shape, jnp.bfloat16)
        shapes += [like(weight)] * 3 + [low]
        scratch += [pltpu.VMEM(each.shape, each.dtype) for each in (weight, moment, square, low)]
    outs = pl.pallas_call(
        kernel,
        name="adam_all",
        out_shape=tuple(shapes) + (like(gains[0]),) * 3 + tuple(like(each) for each in passed),
        in_specs=[anywhere()] * (3 * total + sources) + [in_vmem()] * 5 + [anywhere()] * others,
        out_specs=(anywhere(),) * (4 * total) + (in_vmem(),) * 3 + (anywhere(),) * others,
        scratch_shapes=scratch
        + [pltpu.VMEM(each.shape, each.dtype) for each in tuple(pieces) + tuple(passed)]
        + [
            pltpu.SemaphoreType.DMA((sources,)),
            pltpu.SemaphoreType.DMA((3 * count,)),
            pltpu.SemaphoreType.DMA((4 * count,)),
            pltpu.SemaphoreType.DMA((2, others)),
        ],
        compiler_params=pltpu.CompilerParams(vmem_limit_bytes=VMEM_LIMIT),
        cost_estimate=cost_of(15),
    )(*args, *pieces, factor, gain_grad, *gains, *passed)
    steps = [outs[4 * place : 4 * place + 4] for place in range(total)]
    return steps + [outs[4 * total : 4 * total + 3], outs[4 * total + 3 :]]


def rotary(count):
    frequency = rope_base ** (-(np.arange(HD // 2) * 2.0 / HD))
    angles = np.arange(count)[:, None] * frequency[None, :]
    cosine, sine = np.cos(angles), np.sin(angles)
    full = [np.concatenate(pair, axis=1) for pair in ((cosine, cosine), (-sine, sine))]
    return [jnp.asarray(table, jnp.float32) for table in full]


def gather_outer(mixed):
    return lax.all_gather(mixed.reshape(-1, mixed.shape[2]), "outer", axis=0, tiled=True)


def team_pieces(summed):
    return summed.reshape(TEAM, -1, summed.shape[-1])


def turned_pieces(summed):
    if summed.shape[1] * TEAM * lax.axis_size("outer") == D:
        return team_pieces(summed)
    return summed.reshape(summed.shape[0], TEAM, -1).transpose(1, 0, 2)


def sum_weight(gradient):
    return lax.psum_scatter(gradient, "outer", scatter_dimension=0, tiled=True)


def after(values, earlier):
    return lax.optimization_barrier((values, earlier))


def adam_update(weight, gradient, moment_one, moment_two, factor, decay_rate, rate_value):
    clipped = gradient * factor
    moment_one = beta_first * moment_one + (1.0 - beta_first) * clipped
    moment_two = beta_second * moment_two + (1.0 - beta_second) * clipped * clipped
    first_fixed = moment_one * (rate_value / (1.0 - beta_first**STEP))
    root_fixed = jnp.sqrt(moment_two) * (1.0 - beta_second**STEP) ** (-0.5)
    kept = weight * (1.0 - rate_value * decay_rate) if decay_rate else weight
    weight = kept - first_fixed / (root_fixed + adam_epsilon)
    return (weight, moment_one, moment_two)


def dot(left, right, contract):
    return lax.dot_general(
        left, right, ((contract[0], contract[1]), ((), ())), preferred_element_type=jnp.float32
    )


def times(left, right):
    return dot(left, right, ((1,), (0,)))


def times_across(left, right):
    return dot(left, right, ((1,), (1,)))


def over_rows(left, right):
    return dot(left, right, ((0,), (0,)))


def local(
    inputs,
    cotangent,
    lengths,
    owners,
    qkv_weight,
    out_weight,
    gate_up_weight,
    down_weight,
    norm_gains,
    qkv_moment,
    out_moment,
    gate_up_moment,
    down_moment,
    gains_moment,
    qkv_square,
    out_square,
    gate_up_square,
    down_square,
    gains_square,
):
    tp_count = lax.axis_size("tp")
    half_rows = inputs.shape[0]
    row_count = half_rows * tp_count
    heads = H // tp_count // TEAM
    hidden_units = FF // tp_count // TEAM
    qkv_widths = (H * HD // tp_count, KV * HD // tp_count, KV * HD // tp_count)
    out_widths = (H * HD // tp_count,)
    part_rows = qkv_weight.shape[0]
    gate_up_widths = (FF // tp_count, FF // tp_count)
    down_widths = (FF // tp_count,)

    cos_full, sin_full = rotary(row_count)
    attn_gain = norm_gains[:D]
    mlp_gain = norm_gains[D : 2 * D]
    head_gains = norm_gains[2 * D :].reshape(2, HD)

    normed_attn, gate_up_mixed, first_full, grad_low, down_pieces = opening(
        qkv_weight,
        out_weight,
        gate_up_weight,
        down_weight,
        inputs,
        attn_gain,
        cotangent,
        lengths,
        owners,
        lax.axis_size("outer"),
        0,
    )
    gate_up_full = gather_outer(gate_up_mixed)
    early = half_rows // 2 // CHUNK * CHUNK
    projected, attended, logs, attn_branch, grad_all, down_mixed = attend(
        normed_attn.reshape(TEAM, row_count, D),
        first_full,
        grad_low,
        (down_pieces,),
        lengths,
        owners,
        cos_full,
        sin_full,
        head_gains,
        heads,
        early,
        1,
    )
    down_full = gather_outer(down_mixed)
    hidden, normed_mlp = branch_and_norm(attn_branch, inputs, mlp_gain, 2, "branch_and_norm")
    gate_up, activated, grad_all = feed(
        normed_mlp.reshape(TEAM, row_count, D), gate_up_full, grad_low, grad_all, early, 8
    )
    grad_down = over_rows(grad_all.reshape(-1, D), activated.reshape(-1, hidden_units))
    grad_all, grad_down = after(grad_all, grad_down.astype(jnp.bfloat16))
    down_sum = sum_weight(grad_down)
    grad_gate, grad_up = feed_back(
        grad_all.reshape(-1, half_rows, D),
        down_full,
        gate_up.reshape(-1, half_rows, 2 * hidden_units),
    )
    grad_gate = grad_gate.reshape(TEAM, row_count, hidden_units)
    grad_up = grad_up.reshape(TEAM, row_count, hidden_units)
    grad_gate_weight = over_rows(normed_mlp, grad_gate.reshape(-1, hidden_units))
    grad_gate, grad_gate_weight = after(grad_gate, grad_gate_weight.astype(jnp.bfloat16))
    gate_sum = sum_weight(grad_gate_weight)
    grad_hidden, grad_mlp_gain, own_grad, mlp_part, grad_up_weight = feed_back_rest(
        grad_gate,
        grad_up,
        gate_up_full,
        activated,
        down_full,
        normed_mlp,
        hidden,
        grad_low,
        mlp_gain,
        lax.axis_size("outer"),
        3,
        "feed_back_rest",
    )
    up_sum = turned_pieces(sum_weight(grad_up_weight.reshape(-1, grad_up_weight.shape[2])))
    _, grad_head_gains, grad_normed_attn, output, grad_first, down_mixed = attend_back(
        projected,
        normed_attn.reshape(TEAM, row_count, D),
        attended,
        own_grad,
        logs,
        first_full,
        mlp_part,
        hidden,
        (team_pieces(down_sum),),
        lax.axis_size("outer"),
        lengths,
        owners,
        cos_full,
        sin_full,
        head_gains,
        heads,
        7,
    )
    grad_first, gate_sum = after(grad_first, gate_sum)
    first_sum = turned_pieces(sum_weight(grad_first.reshape(-1, grad_first.shape[3])))
    input_grad, attn_gain_parts, squares, gate_mixed, up_mixed = norm_back_last(
        grad_normed_attn,
        inputs,
        grad_hidden,
        attn_gain,
        (team_pieces(gate_sum), up_sum),
        (gate_sum, up_sum, down_sum),
        4,
        "norm_back_attn",
    )
    gain_part = jnp.concatenate(
        [jnp.zeros_like(grad_mlp_gain), grad_mlp_gain, grad_head_gains.sum(axis=1).reshape(-1)]
    )
    gain_count = gain_part.shape[0]
    packed = jnp.pad(gain_part, (0, -gain_count % PAD))
    packed, norm_tile, factor_tile, first_mixed = total_everywhere(
        packed.reshape(-1, HD),
        attn_gain_parts,
        squares,
        first_sum,
        lax.axis_size("outer"),
        5,
        "total_everywhere",
    )
    grad_norm = norm_tile[0, 0]
    (
        (new_gate_up, new_gate_up_one, new_gate_up_two, gate_up_copy),
        (new_down, new_down_one, new_down_two, down_copy),
        (new_out, new_out_one, new_out_two, out_copy),
        (new_qkv, new_qkv_one, new_qkv_two, qkv_copy),
        new_gains,
        (output, input_grad),
    ) = adam_all(
        [
            (
                gate_up_weight,
                gate_up_moment,
                gate_up_square,
                [
                    by_columns(start, max(CHUNK, part_rows // 4), gate_up_widths[:1], 0)
                    for start in range(0, part_rows, max(CHUNK, part_rows // 4))
                ]
                + [
                    by_turned(part_rows, gate_up_widths[0], gate_up_widths[1:], 1, (member,))
                    for member in range(TEAM)
                ],
            ),
            (
                down_weight,
                down_moment,
                down_square,
                [by_rows(member, hidden_units, part_rows, None, 2) for member in range(TEAM)],
            ),
            (
                out_weight,
                out_moment,
                out_square,
                [
                    by_rows(member, heads * HD, part_rows, (heads + 2) * HD, 3)
                    for member in range(TEAM)
                ],
            ),
            (
                qkv_weight,
                qkv_moment,
                qkv_square,
                [by_turned(part_rows, 0, qkv_widths, 3)],
            ),
        ],
        (gate_mixed, up_mixed, down_mixed, first_mixed),
        factor_tile,
        packed,
        [each.reshape(-1, HD) for each in (norm_gains, gains_moment, gains_square)],
        (output, input_grad),
    )
    new_gains, new_gains_one, new_gains_two = (each.reshape(-1) for each in new_gains)
    return (
        output,
        input_grad,
        grad_norm,
        new_qkv,
        new_qkv_one,
        new_qkv_two,
        qkv_copy,
        new_out,
        new_out_one,
        new_out_two,
        out_copy,
        new_gate_up,
        new_gate_up_one,
        new_gate_up_two,
        gate_up_copy,
        new_down,
        new_down_one,
        new_down_two,
        down_copy,
        new_gains,
        new_gains_one,
        new_gains_two,
    )


def solution(mesh):
    fsdp_count, tp_count = mesh.shape["fsdp"], mesh.shape["tp"]
    cut = mesh.devices.reshape(fsdp_count // TEAM, NEAR, CORE, tp_count)
    cut_mesh = Mesh(cut, ("outer",) + LAYER)
    fsdp = ("outer", "near", "core")
    rows = P(fsdp + ("tp",), None)
    wide = P(fsdp, "tp")
    tall = P("tp", fsdp)
    weights = (wide, tall, wide, tall, P())
    return jax.shard_map(
        local,
        mesh=cut_mesh,
        in_specs=(rows, rows, P(), P()) + weights * 3,
        out_specs=(rows, rows, P()) + (wide,) * 4 + (tall,) * 4 + (wide,) * 4 + (tall,) * 4 + (P(),) * 3,
        check_vma=False,
    )
```

```python
from functools import partial

import jax
import jax.numpy as jnp
import numpy as np
from jax import lax
from jax.experimental import pallas as pl
from jax.experimental.pallas import tpu as pltpu
from jax.sharding import Mesh, PartitionSpec as P

D = 2048
H = 16
KV = 8
HD = 128
FF = 6144
STEP = 10


norm_epsilon = 1e-06
rope_base = 1000000.0
clip_norm = 1.0
learn_rate = 0.04
gain_rate = 0.8
beta_first = 0.9
beta_second = 0.999
adam_epsilon = 1e-08
weight_decay = 0.1
masked_score = -1e30

NEAR = 2
CORE = 2
TEAM = NEAR * CORE
LAYER = ("near", "core", "tp")
BLOCK = 128
PAD = 8 * 128


def rms_scale(values):
    return lax.rsqrt(jnp.mean(values * values, axis=-1, keepdims=True) + norm_epsilon)


def swish_product(gate_part, up_part):
    return jax.nn.silu(gate_part) * up_part


MESH_ID = pl.DeviceIdType.MESH
VMEM_LIMIT = 60 * 1024 * 1024
CHUNK = 16
GATHER_COPIES = 17
AHEAD = 1000
PART = TEAM // 2
SUM_COPIES = 12
NEIGHBOURS = ((1, 0, 0), (0, 1, 0), (0, 0, 1))
MATES = ((0, 1, 0), (1, 0, 0), (1, 1, 0))
EVERYONE_NEAR = NEIGHBOURS + ((1, 1, 0),)


def spots():
    return tuple(lax.axis_index(name) for name in LAYER)


def flipped(near_flip, core_flip, tp_flip):
    return {
        name: 1 - spot if flip else spot
        for name, spot, flip in zip(LAYER, spots(), (near_flip, core_flip, tp_flip))
    }


def greet(flips):
    barrier = pltpu.get_barrier_semaphore()
    for flip in flips:
        pl.semaphore_signal(barrier, inc=1, device_id=flipped(*flip), device_id_type=MESH_ID)
    pl.semaphore_wait(barrier, len(flips))


def link(source, target, send_sem, recv_sem, flip):
    return pltpu.make_async_remote_copy(
        src_ref=source,
        dst_ref=target,
        send_sem=send_sem,
        recv_sem=recv_sem,
        device_id=flipped(*flip),
        device_id_type=MESH_ID,
    )


TO_NEAR, TO_CORE, TO_TP = NEIGHBOURS


def plan_exchange(pieces, out, send, recv, own_sem):
    near, core, _ = spots()
    own = near * CORE + core
    copies = []
    for number, flip in enumerate(MATES):
        there = (1 - near if flip[0] else near) * CORE + (1 - core if flip[1] else core)
        copies.append(
            link(pieces.at[there], out.at[own], send.at[number], recv.at[number], flip)
        )
    copies.append(pltpu.make_async_copy(pieces.at[own], out.at[own], own_sem))
    return copies


def exchange_scratch():
    return [
        pltpu.SemaphoreType.DMA((len(MATES),)),
        pltpu.SemaphoreType.DMA((len(MATES),)),
        pltpu.SemaphoreType.DMA,
    ]


def crossing(pieces, width):
    return sum(2 * piece.shape[1] * piece.shape[2] for piece in pieces) // width


def plan_exchanges(pieces, mixed, sems):
    copies = []
    for place, (piece, result) in enumerate(zip(pieces, mixed)):
        copies += plan_exchange(piece, result, *sems[3 * place : 3 * place + 3])
    return copies


def plan_gather(own, out, send, recv, own_sem, cut, base=0, rows=None, parts=False, apart=False):
    near, core, tp = spots()
    rows = own.shape[0] if rows is None else rows
    low, high = pl.ds(base, cut), pl.ds(base + cut, rows - cut)
    all_rows = pl.ds(base, rows)

    def make(number, source, target, flip):
        return link(source, target, send.at[number], recv.at[number], flip)

    def give(number, part, flip):
        return make(number, own.at[part], out.at[near, core, tp, part], flip)

    def relay(number, where_near, where_tp, part, flip):
        ref = out.at[where_near, core, where_tp, part]
        return make(number, ref, ref, flip)

    keep = pltpu.make_async_copy(own.at[all_rows], out.at[near, core, tp, all_rows], own_sem)
    twin_own = give(4, all_rows, TO_CORE)
    first_rows = (rows - cut) // 2 // CHUNK * CHUNK
    high_parts = [
        (pl.ds(base + cut, first_rows), 1, 7, 8),
        (pl.ds(base + cut + first_rows, rows - cut - first_rows), 13, 14, 15),
    ]
    near_high = [give(number, part, TO_NEAR) for part, number, _, _ in high_parts]
    tp_high = give(2, high, TO_TP)
    far_high = [relay(number, 1 - near, tp, part, TO_TP) for part, _, number, _ in high_parts]
    twin_beside = [relay(number, 1 - near, tp, part, TO_CORE) for part, _, _, number in high_parts]
    twin_across = relay(9, near, 1 - tp, high, TO_CORE)
    twin_far = [
        relay(number, 1 - near, 1 - tp, part, TO_CORE)
        for (part, *_), number in zip(high_parts, (12, 16))
    ]
    twins = [twin_own, twin_across] + twin_far + twin_beside
    ways = near_high + far_high + [tp_high]
    if cut:
        tp_low = give(0, low, TO_TP)
        near_low = give(3, low, TO_NEAR)
        far_low = relay(5, near, 1 - tp, low, TO_NEAR)
        twin_across_low = relay(6, near, 1 - tp, low, TO_CORE)
        twin_beside_low = relay(10, 1 - near, tp, low, TO_CORE)
        twin_far_low = relay(11, 1 - near, 1 - tp, low, TO_CORE)
        twins += [twin_across_low, twin_beside_low, twin_far_low]
        ways += [tp_low, near_low, far_low]

    def begin_tp():
        if cut:
            tp_low.start()
        tp_high.start()
        twin_own.start()
        keep.start()

    def begin_near():
        for copy in near_high:
            copy.start()
        if cut:
            near_low.start()

    def begin():
        begin_near()
        begin_tp()

    def pass_on(part):
        near_high[part].wait_recv()
        far_high[part].start()
        twin_beside[part].start()

    def middle():
        if cut:
            tp_low.wait_recv()
            far_low.start()
            twin_across_low.start()
        pass_on(0)
        if not apart:
            pass_on(1)

    def later():
        tp_high.wait_recv()
        twin_across.start()
        if cut:
            near_low.wait_recv()
            twin_beside_low.start()

    def own_there():
        keep.wait()

    def twin_there():
        twin_own.wait_recv()
        twin_across.wait_recv()
        if cut:
            twin_across_low.wait_recv()

    def far_there():
        if cut:
            far_low.wait_recv()
            twin_far_low.start()
        for copy, twin in zip(far_high, twin_far):
            copy.wait_recv()
            twin.start()

    def rest_there():
        for copy in twin_beside + twin_far:
            copy.wait_recv()
        if cut:
            twin_beside_low.wait_recv()
            twin_far_low.wait_recv()
        for copy in ways + twins:
            copy.wait_send()

    def finish():
        own_there()
        twin_there()
        far_there()
        rest_there()

    if parts:
        return [begin, middle, later, own_there, twin_there, far_there, rest_there]
    if apart:
        return [begin_tp, begin_near, middle, partial(pass_on, 1), later, finish]
    return [begin, middle, later, finish]


def balanced(rows, beside):
    return max(0, (rows - beside) // 2 // CHUNK * CHUNK)


def gather_scratch():
    return [
        pltpu.SemaphoreType.DMA((GATHER_COPIES,)),
        pltpu.SemaphoreType.DMA((GATHER_COPIES,)),
        pltpu.SemaphoreType.DMA,
    ]


def add_rows(target, start, count, *sources):
    @pl.loop(0, count // CHUNK)
    def _(step):
        at = pl.ds(pl.multiple_of(start + step * CHUNK, CHUNK), CHUNK)
        total = None
        for source, shift in sources:
            where = pl.ds(pl.multiple_of(start - shift + step * CHUNK, CHUNK), CHUNK)
            value = source[where].astype(jnp.float32)
            total = value if total is None else total + value
        target[at] = total.astype(target.dtype)


def halved(start, count):
    half = count // 2 // CHUNK * CHUNK
    return (start, half), (start + half, count - half)


def plan_sum(outgoing, mine, keep, total, scratch, cut):
    theirs, way_near, way_tp, from_tp, from_near, send, recv = scratch
    rows = total.shape[0]
    low, high = pl.ds(0, cut), pl.ds(cut, rows - cut)

    def make(number, source, target, flip):
        return link(source, target, send.at[number], recv.at[number], flip)

    twin = [make(number, outgoing[number], theirs.at[number], TO_CORE) for number in range(4)]
    far, to_tp, to_near, own = mine
    low_parts = halved(0, cut)
    high_parts = halved(cut, rows - cut)
    far_high = make(5, far.at[high], way_tp, TO_TP)
    tp_high = make(6, to_tp.at[high], from_tp.at[high], TO_TP)
    near_high = [
        make(9 + 2 * place, to_near.at[pl.ds(*part)], from_near.at[pl.ds(*part)], TO_NEAR)
        for place, part in enumerate(high_parts)
    ]
    ways = [far_high, tp_high] + near_high
    tp_low = []
    if cut:
        far_low = make(4, far.at[low], way_near, TO_NEAR)
        near_low = make(7, to_near.at[low], from_near.at[low], TO_NEAR)
        tp_low = [
            make(8 + 2 * place, to_tp.at[pl.ds(*part)], from_tp.at[pl.ds(*part)], TO_TP)
            for place, part in enumerate(low_parts)
        ]
        ways += [far_low, near_low] + tp_low

    def ready(number):
        if keep:
            keep[number].wait()
        twin[number].wait_recv()

    def both(number):
        return (mine[number], 0), (theirs.at[number], 0)

    def begin(numbers=range(4)):
        for number in numbers:
            twin[number].start()
            if keep:
                keep[number].start()

    def send_far():
        ready(0)
        if cut:
            add_rows(far, 0, cut, *both(0))
            far_low.start()
        add_rows(far, cut, rows - cut, *both(0))
        far_high.start()

    def send_tp():
        ready(1)
        add_rows(to_tp, cut, rows - cut, *both(1))
        tp_high.start()

    def send_near():
        ready(2)
        if cut:
            add_rows(to_near, 0, cut, *both(2))
            near_low.start()

    def first():
        send_far()
        send_tp()
        send_near()

    def second():
        if cut:
            far_low.wait_recv()
        far_high.wait_recv()
        for place, part in enumerate(high_parts):
            if cut:
                add_rows(to_tp, *low_parts[place], *both(1), (way_near, 0))
                tp_low[place].start()
            add_rows(to_near, *part, *both(2), (way_tp, cut))
            near_high[place].start()
        ready(3)
        add_rows(total, 0, rows, *both(3))

    def finish(body):
        tp_high.wait_recv()
        if cut:
            near_low.wait_recv()
        for place, part in enumerate(high_parts):
            if cut:
                tp_low[place].wait_recv()
                row_loop(*low_parts[place], body)
            near_high[place].wait_recv()
            row_loop(*part, body)
        for copy in twin + ways:
            copy.wait_send()

    return [begin, first, second, finish], (send_far, send_tp, send_near)


def plan_sum_of(part, total, scratch, cut):
    mine, local_sem, *scratch = scratch
    near, core, tp = spots()
    order = [(1 - near, 1 - tp), (near, 1 - tp), (1 - near, tp), (near, tp)]
    outgoing = [part.at[a, 1 - core, b] for a, b in order]
    keep = [
        pltpu.make_async_copy(part.at[a, core, b], mine.at[number], local_sem.at[number])
        for number, (a, b) in enumerate(order)
    ]
    blocks = [mine.at[number] for number in range(4)]
    steps, _ = plan_sum(outgoing, blocks, keep, total, scratch, cut)
    return steps, scratch[3], scratch[4]


def sum_scratch(rows, width, cut, fetched=True):
    low = jnp.bfloat16
    fetch = [pltpu.VMEM((4, rows, width), low), pltpu.SemaphoreType.DMA((4,))]
    return (fetch if fetched else []) + [
        pltpu.VMEM((4, rows, width), low),
        pltpu.VMEM((max(cut, CHUNK), width), low),
        pltpu.VMEM((rows - cut, width), low),
        pltpu.VMEM((rows, width), low),
        pltpu.VMEM((rows, width), low),
        pltpu.SemaphoreType.DMA((SUM_COPIES,)),
        pltpu.SemaphoreType.DMA((SUM_COPIES,)),
    ]


SUM_SCRATCH = 9
COST_SHARE = 1e5


def params(number):
    return pltpu.CompilerParams(
        collective_id=number, has_side_effects=True, vmem_limit_bytes=VMEM_LIMIT
    )


def cost_of(microseconds):
    return pl.CostEstimate(
        flops=0, bytes_accessed=int(microseconds * COST_SHARE), transcendentals=0
    )


def in_vmem():
    return pl.BlockSpec(memory_space=pltpu.VMEM)


def anywhere():
    return pl.BlockSpec(memory_space=pl.ANY)


def like(array):
    return jax.ShapeDtypeStruct(array.shape, array.dtype)


def layer_rows(rows, width):
    return jax.ShapeDtypeStruct((NEAR, CORE, 2, rows, width), jnp.bfloat16)


def row_loop(start, count, body):
    @pl.loop(0, count // CHUNK)
    def _(step):
        body(pl.ds(pl.multiple_of(start + step * CHUNK, CHUNK), CHUNK))


def plan_line(blocks, send, recv, count):
    own = lax.axis_index("outer")

    def handle(side, number, half, there):
        block = blocks.at[there, pl.ds(half * PART, PART)]
        return pltpu.make_async_remote_copy(
            src_ref=block,
            dst_ref=block,
            send_sem=send.at[side, number, half],
            recv_sem=recv.at[side, number, half],
            device_id={"outer": own + 1 if side == 0 else own - 1},
            device_id_type=MESH_ID,
        )

    def message(side, number, half):
        return handle(side, number, half, own - number if side == 0 else own + number)

    def arrival(side, number, half):
        return handle(side, number, half, own - 1 - number if side == 0 else own + 1 + number)

    def sends(side, number):
        if side == 0:
            return (own < count - 1) & (own >= number)
        return (own > 0) & (own + number < count)

    def gets(side, number):
        return own >= number + 1 if side == 0 else own + 1 + number < count

    near = lax.axis_index("near")
    halves = (near, 1 - near)

    def push(number, place):
        for side in range(2):

            @pl.when(sends(side, number))
            def _(side=side):
                message(side, number, halves[place]).start()

    def take(number):
        for half in halves:
            for side in range(2):

                @pl.when(gets(side, number))
                def _(side=side, half=half):
                    arrival(side, number, half).wait_recv()

                if number + 2 < count:

                    @pl.when(sends(side, number + 1))
                    def _(side=side, half=half):
                        message(side, number + 1, half).start()

    def settle():
        for number in range(count - 1):
            for side in range(2):

                @pl.when(sends(side, number))
                def _(side=side, number=number):
                    for half in range(2):
                        message(side, number, half).wait_send()

    return push, take, settle


def greet_all(flips, count, work):
    barrier = pltpu.get_barrier_semaphore()
    own = lax.axis_index("outer")
    for flip in flips:
        pl.semaphore_signal(barrier, inc=1, device_id=flipped(*flip), device_id_type=MESH_ID)
    for there, neighbour in ((own < count - 1, own + 1), (own > 0, own - 1)):

        @pl.when(there)
        def _(neighbour=neighbour):
            pl.semaphore_signal(
                barrier, inc=1, device_id={"outer": neighbour}, device_id_type=MESH_ID
            )

    work()
    beside = jnp.where(own < count - 1, 1, 0) + jnp.where(own > 0, 1, 0)
    pl.semaphore_wait(barrier, len(flips) + beside)


def sequence_length(lengths, owners, group):
    total = jnp.int32(0)
    for place in range(lengths.shape[0]):
        total += jnp.where(owners[place] == group, lengths[place], 0)
    return total


def opening(
    qkv, out_weight, gate_up, down, inputs, gain, cotangent, lengths, owners, outer_count, number
):
    rows, width = inputs.shape
    part_rows, wide = qkv.shape
    tall, units = out_weight.shape[0], down.shape[0]
    widths = (wide // 2, wide // 4, wide // 4)
    first_shape = jax.ShapeDtypeStruct((TEAM, part_rows, (wide + tall) // TEAM), jnp.bfloat16)
    gate_up_shape = jax.ShapeDtypeStruct((TEAM, part_rows, 2 * units // TEAM), jnp.bfloat16)
    down_shape = jax.ShapeDtypeStruct((TEAM, part_rows, units // TEAM), jnp.bfloat16)
    cut = balanced(rows, crossing((first_shape, gate_up_shape), width))

    def kernel(
        lengths, owners, qkv, out_weight, inputs, gain, gate_up, down, cotangent,
        out, mixed, full, low, down_pieces,
        normed, first, pieces, gate_up_v, down_v, cotangent_v, load_sem, line_send, line_recv, *sems
    ):
        near, core, tp = spots()
        outer = lax.axis_index("outer")
        begin_tp, begin_near, middle, middle_rest, later, finish = plan_gather(
            normed, out, *sems[:3], cut=cut, apart=True
        )
        team = plan_exchange(first, full.at[outer], *sems[3:6])
        others = plan_exchange(pieces, mixed, *sems[6:9])
        push, take, settle = plan_line(full, line_send, line_recv, outer_count)
        fetch = [
            pltpu.make_async_copy(source, target, load_sem.at[place])
            for place, (source, target) in enumerate(
                ((cotangent, cotangent_v), (gate_up, gate_up_v), (down, down_v))
            )
        ]
        for copy in fetch:
            copy.start()
        def prepare(at):
            value = inputs[at].astype(jnp.float32)
            normed[at] = (value * rms_scale(value) * gain[...]).astype(jnp.bfloat16)

        def work():
            for member, across, inside in spans(widths):
                first[member, :, inside] = qkv[:, across].astype(jnp.bfloat16)
            for member in range(TEAM):
                at = pl.ds(member * (tall // TEAM), tall // TEAM)
                first[member, :, wide // TEAM :] = out_weight[at].astype(jnp.bfloat16).T
            row_loop(0, rows, prepare)

        greet_all(EVERYONE_NEAR, outer_count, work)
        for copy in team:
            copy.start()
        begin_tp()
        team[0].wait()
        team[3].wait()
        push(0, 0)
        fetch[1].wait()
        for member, across, inside in spans((units, units)):
            pieces[member, :, inside] = gate_up_v[:, across].astype(jnp.bfloat16)
        for copy in team[1:3]:
            copy.wait()
        push(0, 1)
        begin_near()
        take(0)
        length = sequence_length(lengths, owners, outer * TEAM + near * CORE + core)
        fetch[0].wait()

        def mask(at):
            row = lax.broadcasted_iota(jnp.int32, (CHUNK, width), 0) + at.start + tp * rows
            value = jnp.where(row < length, cotangent_v[at].astype(jnp.float32), 0.0)
            low[at] = value.astype(jnp.bfloat16)

        row_loop(0, rows, mask)
        fetch[2].wait()
        for member in range(TEAM):
            at = pl.ds(member * (units // TEAM), units // TEAM)
            down_pieces[member] = down_v[at].astype(jnp.bfloat16).T
        middle()
        if outer_count > 2:
            take(1)
        middle_rest()
        for copy in others:
            copy.start()
        later()
        for step in range(2, outer_count - 1):
            take(step)
        finish()
        settle()
        for copy in others:
            copy.wait()

    scalars = pl.BlockSpec(memory_space=pltpu.SMEM)
    outs = pl.pallas_call(
        kernel,
        name="opening",
        out_shape=(
            layer_rows(rows, width),
            gate_up_shape,
            jax.ShapeDtypeStruct((outer_count,) + first_shape.shape, jnp.bfloat16),
            jax.ShapeDtypeStruct((rows, width), jnp.bfloat16),
            down_shape,
        ),
        in_specs=[scalars] * 2 + [in_vmem()] * 4 + [anywhere()] * 3,
        out_specs=(anywhere(),) * 3 + (in_vmem(),) * 2,
        scratch_shapes=[
            pltpu.VMEM((rows, width), jnp.bfloat16),
            pltpu.VMEM(first_shape.shape, jnp.bfloat16),
            pltpu.VMEM(gate_up_shape.shape, jnp.bfloat16),
            pltpu.VMEM(gate_up.shape, gate_up.dtype),
            pltpu.VMEM(down.shape, down.dtype),
            pltpu.VMEM(cotangent.shape, cotangent.dtype),
            pltpu.SemaphoreType.DMA((3,)),
            pltpu.SemaphoreType.DMA((2, outer_count, 2)),
            pltpu.SemaphoreType.DMA((2, outer_count, 2)),
        ]
        + gather_scratch()
        + exchange_scratch() * 2,
        compiler_params=params(number),
        cost_estimate=cost_of(60),
    )(
        lengths,
        owners,
        qkv,
        out_weight,
        inputs,
        gain.reshape(1, width),
        gate_up,
        down,
        cotangent,
    )
    gathered, mixed, full, low, down_pieces = outs
    return (
        gathered.reshape(-1, width),
        mixed,
        full.reshape(-1, first_shape.shape[2]),
        low,
        down_pieces,
    )


def spread(part, rows):
    return part.reshape(NEAR, CORE, 2, rows, part.shape[-1])


def read(ref, at):
    return ref[at].astype(jnp.float32)


def branch_and_norm(part, residual, gain, number, name):
    rows, width = residual.shape
    cut = rows // 2

    def kernel(part, residual, gain, hidden, out, *scratch):
        normed, sems = scratch[SUM_SCRATCH], scratch[SUM_SCRATCH + 1 :]
        steps, from_tp, from_near = plan_sum_of(part, hidden, scratch[:SUM_SCRATCH], cut)
        onward = plan_gather(normed, out, *sems, cut=cut)
        greet(NEIGHBOURS)
        for step in steps[:3]:
            step()

        def finish(at):
            value = hidden[at] + read(from_tp, at) + read(from_near, at)
            value = read(residual, at) + value
            hidden[at] = value
            normed[at] = (value * rms_scale(value) * gain[...]).astype(jnp.bfloat16)

        steps[3](finish)
        for step in onward:
            step()

    hidden, full = pl.pallas_call(
        kernel,
        name=name,
        out_shape=(jax.ShapeDtypeStruct((rows, width), jnp.float32), layer_rows(rows, width)),
        in_specs=[anywhere(), in_vmem(), in_vmem()],
        out_specs=(in_vmem(), anywhere()),
        scratch_shapes=sum_scratch(rows, width, cut)
        + [pltpu.VMEM((rows, width), jnp.bfloat16)]
        + gather_scratch(),
        compiler_params=params(number),
        cost_estimate=cost_of(95),
    )(spread(part, rows), residual, gain.reshape(1, width))
    return hidden, full.reshape(-1, width)


def norm_back(value, gain, grad):
    scale = rms_scale(value)
    scaled = grad * gain
    inner = jnp.mean(scaled * value, axis=-1, keepdims=True)
    return scale * scaled - value * (scale * scale * scale * inner), grad * value * scale


def sequence_order():
    near, core, _ = spots()
    return [
        (near if place >= 2 else 1 - near) * CORE + (core if place % 2 else 1 - core)
        for place in range(TEAM)
    ]


def times_turned(left, weights, target):
    for start in range(0, weights.shape[0], 512):
        at = pl.ds(start, 512)
        target[:, at] = lax.dot_general(
            left, weights[at, :], (((1,), (1,)), ((), ())), preferred_element_type=jnp.float32
        ).astype(target.dtype)


def feed_back_rest(
    grad_gate, grad_up, weights, active, down, normed, values, upstream, gain, outer_count, number, name
):
    rows, width = values.shape
    count, both_rows, units = grad_gate.shape
    all_rows = count * both_rows
    past = all_rows - width
    cut = rows // 2
    split, share = team_split(width, outer_count)
    turns = width // 512

    def kernel(
        gate, ups, weights, active, down, normed, values, upstream, gain,
        result, gain_grad, low, branch, grad_weight, *scratch
    ):
        (grad_v, weights_v, active_v, down_v, values_v, upstream_v, parts, total), rest = (
            scratch[:8],
            scratch[8:],
        )
        (shares, staged, load_sem, store_sem, chunk_sem, piece_sem), sums = rest[:6], rest[6:]
        from_tp, from_near = sums[3], sums[4]
        near, core, tp = spots()
        members = sequence_order()
        outgoing = [parts.at[place, half] for place, half in ((0, 1 - tp), (2, 1 - tp), (0, tp), (2, tp))]
        mine = [parts.at[place, half] for place, half in ((1, 1 - tp), (3, 1 - tp), (1, tp), (3, tp))]
        steps, (send_far, send_tp, send_near) = plan_sum(outgoing, mine, (), total, sums, cut)
        stores = [
            pltpu.make_async_copy(shares.at[place % 2], branch.at[place], store_sem.at[place])
            for place in range(count)
        ]
        fetch = [
            pltpu.make_async_copy(source, target, load_sem.at[place])
            for place, (source, target) in enumerate(
                (
                    (weights, weights_v),
                    (values, values_v),
                    (upstream, upstream_v),
                    (active, active_v),
                    (down, down_v),
                    (ups, active_v),
                )
            )
        ]
        grads = []
        for place, member in enumerate(members):
            for side, source in enumerate((gate, ups)):
                grads.append(
                    pltpu.make_async_copy(
                        source.at[member],
                        grad_v.at[place % 2, :, :, pl.ds(side * units, units)],
                        load_sem.at[6 + 2 * place + side],
                    )
                )

        def bring(place):
            grads[2 * place].start()
            grads[2 * place + 1].start()

        def brought(place):
            grads[2 * place].wait()
            grads[2 * place + 1].wait()

        def back(place, half):
            times_turned(grad_v[place % 2, half], weights_v, parts.at[place, half])

        def chunk(turn):
            at, slot = pl.ds(turn * 512, 512), turn % 2
            return [
                pltpu.make_async_copy(
                    normed.at[pl.ds(0, width), at],
                    weights_v.at[:, pl.ds(slot * 1024, 512)],
                    chunk_sem.at[slot, 0],
                ),
                pltpu.make_async_copy(
                    normed.at[pl.ds(width, past), at],
                    weights_v.at[pl.ds(slot * past, past), pl.ds(512, 512)],
                    chunk_sem.at[slot, 1],
                ),
            ]

        def pieces(turn):
            slot = turn % 2
            return [
                pltpu.make_async_copy(
                    staged.at[slot, :, pl.ds(place * share, share)],
                    grad_weight.at[turn * (512 // share) + place],
                    piece_sem.at[slot, place],
                )
                for place in range(512 // share)
            ]

        fetch[0].start()
        bring(0)
        bring(1)
        greet(NEIGHBOURS)
        fetch[0].wait()
        brought(0)
        back(0, 1 - tp)
        steps[0]((0,))
        brought(1)
        back(1, 1 - tp)
        send_far()
        back(0, tp)
        steps[0]((2,))
        bring(2)
        for place in (3, 4, 1, 2):
            fetch[place].start()
        back(1, tp)
        send_near()
        bring(3)
        brought(2)
        back(2, 1 - tp)
        steps[0]((1,))
        brought(3)
        back(3, 1 - tp)
        send_tp()
        back(2, tp)
        steps[0]((3,))
        back(3, tp)
        for turn in (0, 1):
            for copy in chunk(turn):
                copy.start()
        fetch[3].wait()
        fetch[4].wait()
        for place in range(count):
            if place >= 2:
                stores[place - 2].wait()
            for half in range(2):
                times_turned(active_v[place, half], down_v, shares.at[place % 2, half])
            stores[place].start()
        fetch[5].start()
        steps[2]()
        fetch[5].wait()
        for turn in range(turns):
            slot = turn % 2
            for copy in chunk(turn):
                copy.wait()
            left = active_v[...].reshape(all_rows, units)
            product = lax.dot_general(
                left[:width],
                weights_v[:, slot * 1024 : slot * 1024 + 512],
                (((0,), (0,)), ((), ())),
                preferred_element_type=jnp.float32,
            ) + lax.dot_general(
                left[width:],
                weights_v[slot * past : (slot + 1) * past, 512:1024],
                (((0,), (0,)), ((), ())),
                preferred_element_type=jnp.float32,
            )
            if turn >= 2:
                for copy in pieces(turn - 2):
                    copy.wait()
            staged[slot] = product.astype(staged.dtype)
            for copy in pieces(turn):
                copy.start()
            if turn + 2 < turns:
                for copy in chunk(turn + 2):
                    copy.start()
        fetch[1].wait()
        fetch[2].wait()
        gain_grad[...] = jnp.zeros_like(gain_grad)

        def finish(at):
            grad = total[at] + read(from_tp, at) + read(from_near, at)
            turned, by_gain = norm_back(values_v[at], gain[...], grad)
            gain_grad[...] += by_gain.reshape(CHUNK // 8, 8, width).sum(axis=0)
            value = read(upstream_v, at) + turned
            total[at] = value
            low[at] = value.astype(jnp.bfloat16)

        steps[3](finish)
        store = pltpu.make_async_copy(total, result, store_sem.at[count])
        store.start()
        for turn in range(max(0, turns - 2), turns):
            for copy in pieces(turn):
                copy.wait()
        for copy in [store] + stores[2:]:
            copy.wait()

    low_type = jnp.bfloat16
    halves = (count, 2, rows, units)
    result, gain_grad, rounded, branch, grad_weight = pl.pallas_call(
        kernel,
        name=name,
        out_shape=(
            jax.ShapeDtypeStruct((rows, width), jnp.float32),
            jax.ShapeDtypeStruct((8, width), jnp.float32),
            jax.ShapeDtypeStruct((rows, width), low_type),
            jax.ShapeDtypeStruct((count, 2, rows, width), low_type),
            jax.ShapeDtypeStruct((outer_count * split, units, share), low_type),
        ),
        in_specs=[anywhere()] * 8 + [in_vmem()],
        out_specs=(anywhere(), in_vmem(), in_vmem(), anywhere(), anywhere()),
        scratch_shapes=[
            pltpu.VMEM((2, 2, rows, 2 * units), low_type),
            pltpu.VMEM(weights.shape, low_type),
            pltpu.VMEM(halves, low_type),
            pltpu.VMEM(down.shape, low_type),
            pltpu.VMEM((rows, width), values.dtype),
            pltpu.VMEM((rows, width), upstream.dtype),
            pltpu.VMEM((count, 2, rows, width), low_type),
            pltpu.VMEM((rows, width), jnp.float32),
            pltpu.VMEM((2, 2, rows, width), low_type),
            pltpu.VMEM((2, units, 512), low_type),
            pltpu.SemaphoreType.DMA((6 + 2 * count,)),
            pltpu.SemaphoreType.DMA((count + 1,)),
            pltpu.SemaphoreType.DMA((2, 2)),
            pltpu.SemaphoreType.DMA((2, 512 // share)),
        ]
        + sum_scratch(rows, width, cut, fetched=False),
        compiler_params=params(number),
        cost_estimate=cost_of(60),
    )(
        grad_gate.reshape(halves),
        grad_up.reshape(halves),
        weights,
        active.reshape(halves),
        down,
        normed,
        values,
        upstream,
        gain.reshape(1, width),
    )
    return result, gain_grad.sum(axis=0), rounded, branch.reshape(-1, width), grad_weight


def square_sum(values):
    values = values.reshape(-1, values.shape[-1]).astype(jnp.float32)
    return jnp.sum(values * values, keepdims=True)


def corner(value):
    row = lax.broadcasted_iota(jnp.int32, (8, HD), 0)
    column = lax.broadcasted_iota(jnp.int32, (8, HD), 1)
    return jnp.where((row == 0) & (column == 0), value, 0.0)


def norm_back_last(part, values, upstream, gain, extra, squared, number, name):
    rows, width = values.shape
    extras, count = len(extra), len(squared)
    cut = balanced(rows, crossing(extra, width))

    def kernel(part, values, upstream, gain, *rest):
        pieces, rest = rest[:extras], rest[extras:]
        squared, (result, gain_grad, squares), rest = (
            rest[:count],
            rest[count : count + 3],
            rest[count + 3 :],
        )
        mixed, rest = rest[:extras], rest[extras:]
        sums, rest = rest[:SUM_SCRATCH], rest[SUM_SCRATCH:]
        (total, values_v, upstream_v, load_sem), rest = rest[:4], rest[4:]
        squared_v, sems = rest[:count], rest[count:]
        steps, from_tp, from_near = plan_sum_of(part, total, sums, cut)
        copies = plan_exchanges(pieces, mixed, sems)
        fetch = [
            pltpu.make_async_copy(source, target, load_sem.at[place])
            for place, (source, target) in enumerate(
                zip((values, upstream) + tuple(squared), (values_v, upstream_v) + tuple(squared_v))
            )
        ]
        greet(EVERYONE_NEAR)
        steps[0]()
        for copy in copies:
            copy.start()
        for copy in fetch:
            copy.start()
        steps[1]()
        for copy in fetch:
            copy.wait()
        squares[...] = corner(sum(square_sum(ref[...]) for ref in squared_v))
        steps[2]()
        gain_grad[...] = jnp.zeros_like(gain_grad)

        def finish(at):
            grad = total[at] + read(from_tp, at) + read(from_near, at)
            back, by_gain = norm_back(read(values_v, at), gain[...], grad)
            gain_grad[...] += by_gain.reshape(CHUNK // 8, 8, width).sum(axis=0)
            result[at] = (upstream_v[at] + back).astype(jnp.bfloat16)

        steps[3](finish)
        for copy in copies:
            copy.wait()

    return pl.pallas_call(
        kernel,
        name=name,
        out_shape=(
            jax.ShapeDtypeStruct((rows, width), jnp.bfloat16),
            jax.ShapeDtypeStruct((8, width), jnp.float32),
            jax.ShapeDtypeStruct((8, HD), jnp.float32),
        )
        + tuple(like(piece) for piece in extra),
        in_specs=[anywhere()] * 3 + [in_vmem()] * (1 + extras) + [anywhere()] * count,
        out_specs=(in_vmem(), in_vmem(), in_vmem()) + (anywhere(),) * extras,
        scratch_shapes=sum_scratch(rows, width, cut)
        + [
            pltpu.VMEM((rows, width), jnp.float32),
            pltpu.VMEM((rows, width), values.dtype),
            pltpu.VMEM((rows, width), upstream.dtype),
            pltpu.SemaphoreType.DMA((2 + count,)),
        ]
        + [pltpu.VMEM(each.shape, each.dtype) for each in squared]
        + exchange_scratch() * extras,
        compiler_params=params(number),
        cost_estimate=cost_of(65),
    )(spread(part, rows), values, upstream, gain.reshape(1, width), *extra, *squared)


def total_everywhere(values, first, squares, pieces, outer_count, number, name):
    gains = values.shape[0]
    shape = (gains + 8, HD)
    width = first.shape[1]

    def kernel(values, first, squares, pieces, out, norm, factor, mixed, layer, outers, send, recv, *sems):
        near, core, tp = spots()
        outer = lax.axis_index("outer")
        partners = [
            flipped(a, b, c)
            for a in range(NEAR)
            for b in range(CORE)
            for c in range(2)
            if a + b + c
        ]
        partners += [{"outer": (outer + step) % outer_count} for step in range(1, outer_count)]
        barrier = pltpu.get_barrier_semaphore()
        for partner in partners:
            pl.semaphore_signal(barrier, inc=1, device_id=partner, device_id_type=MESH_ID)
        pl.semaphore_wait(barrier, len(partners))

        def share(slots, mine, first, count):
            copies = []
            for number in range(first, first + count):
                copy = pltpu.make_async_remote_copy(
                    src_ref=slots.at[mine],
                    dst_ref=slots.at[mine],
                    send_sem=send.at[number],
                    recv_sem=recv.at[number],
                    device_id=partners[number],
                    device_id_type=MESH_ID,
                )
                copy.start()
                copies.append(copy)
            return copies

        mine = near * (CORE * 2) + core * 2 + tp
        others = plan_exchange(pieces, mixed, *sems)
        layer[mine, :gains] = values[...]
        layer[mine, gains:] = squares[...] + corner(square_sum(pieces[...]))
        sums = jnp.sum(first[...], axis=0, keepdims=True)
        for place in range(width // HD):
            layer[mine, place : place + 1] = sums[:, place * HD : (place + 1) * HD]
        copies = share(layer, mine, 0, 7)
        for copy in others:
            copy.start()
        for copy in copies:
            copy.wait()
        total = layer[0]
        for slot in range(1, 8):
            total = total + layer[slot]
        outers[outer] = total
        for copy in share(outers, outer, 7, outer_count - 1):
            copy.wait()
        total = outers[0]
        for slot in range(1, outer_count):
            total = total + outers[slot]
        out[...] = total
        gain_part = total[:gains]
        root = jnp.sqrt(
            jnp.sum(gain_part * gain_part, keepdims=True) + jnp.sum(total[gains:], keepdims=True)
        )
        norm[...] = jnp.broadcast_to(root, norm.shape)
        factor[...] = jnp.broadcast_to(
            jnp.minimum(1.0, clip_norm / (root + 1e-06)), factor.shape
        )
        for copy in others:
            copy.wait()

    tile = jax.ShapeDtypeStruct((8, HD), jnp.float32)
    return pl.pallas_call(
        kernel,
        name=name,
        out_shape=(jax.ShapeDtypeStruct(shape, jnp.float32), tile, tile, like(pieces)),
        in_specs=[in_vmem()] * 4,
        out_specs=(in_vmem(), in_vmem(), in_vmem(), anywhere()),
        scratch_shapes=[
            pltpu.VMEM((8,) + shape, jnp.float32),
            pltpu.VMEM((outer_count,) + shape, jnp.float32),
            pltpu.SemaphoreType.DMA((6 + outer_count,)),
            pltpu.SemaphoreType.DMA((6 + outer_count,)),
        ]
        + exchange_scratch(),
        compiler_params=params(number),
        cost_estimate=cost_of(16),
    )(values, first, squares, pieces)


def head_scale(raw, gain, cos_full, sin_full):
    normed = raw * rms_scale(raw) * gain
    return (normed * cos_full + pltpu.roll(normed, HD // 2, 1) * sin_full).astype(jnp.bfloat16)


def head_back(raw, gain, grad, cos_full, sin_full):
    grad = grad * cos_full - pltpu.roll(grad, HD // 2, 1) * sin_full
    return norm_back(raw, gain, grad)


def columns(index):
    return pl.ds(index * HD, HD)


def head_inputs(proj, gains, cos_ref, sin_ref, queries, keys, values, heads):
    for head in range(heads):
        queries[head] = head_scale(
            proj[0, :, columns(head)], gains[0:1, :], cos_ref[...], sin_ref[...]
        )
    keys[...] = head_scale(
        proj[0, :, columns(heads)], gains[1:2, :], cos_ref[...], sin_ref[...]
    )
    values[...] = proj[0, :, columns(heads + 1)].astype(jnp.bfloat16)


def masked_scores(stacked, keys, step, length):
    scores = lax.dot_general(
        stacked, keys, (((1,), (1,)), ((), ())), preferred_element_type=jnp.float32
    ) * (HD ** (-0.5))
    row = lax.broadcasted_iota(jnp.int32, scores.shape, 0) % BLOCK + step * BLOCK
    column = lax.broadcasted_iota(jnp.int32, scores.shape, 1)
    return jnp.where((column <= row) & (column < length), scores, masked_score)


def stack_heads(ref, at, heads):
    return jnp.concatenate([ref[head, at] for head in range(heads)], axis=0)


def per_sequence(*shape):
    return pl.BlockSpec((1,) + shape, lambda s: (s,) + (0,) * len(shape))


def whole(*shape):
    return pl.BlockSpec(shape, lambda s: (0,) * len(shape), pipeline_mode=pl.Buffered(1))


def across_columns(left, weights, first, width, out):
    total = weights.shape[0]
    for start in range(0, total, 512):
        at = pl.ds(start, 512)
        out[0, :, at] = lax.dot_general(
            left,
            weights[at, first : first + width],
            (((1,), (1,)), ((), ())),
            preferred_element_type=jnp.float32,
        ).astype(out.dtype)


def attend(normed, weights, cotangent, extra, lengths, owners, cos_full, sin_full, gains, heads, early, number):
    count, rows, width = normed.shape
    wide = (heads + 2) * HD
    extras = len(extra)
    own_rows = cotangent.shape[0]
    cut = balanced(early, crossing(extra, width))

    def kernel(lengths, owners, normed, weights_any, cos_ref, sin_ref, gains, own, *rest):
        pieces, rest = rest[:extras], rest[extras:]
        (proj, out, logs, branch, gathered), rest = rest[:5], rest[5:]
        mixed, rest = rest[:extras], rest[extras:]
        (queries, keys, values, weights, weights_sem), sems = rest[:5], rest[5:]
        fetch = pltpu.make_async_copy(weights_any, weights, weights_sem)
        sequence = pl.program_id(0)
        steps = plan_gather(own, gathered, *sems[:3], cut=cut, rows=early)
        copies = plan_exchanges(pieces, mixed, sems[3:])

        @pl.when(sequence == 0)
        def _():
            fetch.start()
            greet(EVERYONE_NEAR)
            steps[0]()
            fetch.wait()

        group = lax.axis_index("outer") * TEAM + sequence
        length = sequence_length(lengths, owners, group)
        proj[0] = jnp.dot(
            normed[0], weights[:, :wide], preferred_element_type=jnp.float32
        )
        head_inputs(proj, gains, cos_ref, sin_ref, queries, keys, values, heads)
        lane = lax.broadcasted_iota(jnp.int32, (BLOCK, HD), 1)
        for step in range(rows // BLOCK):
            at = pl.ds(step * BLOCK, BLOCK)
            seen = pl.ds(0, (step + 1) * BLOCK)
            scores = masked_scores(stack_heads(queries, at, heads), keys[seen], step, length)
            top = jnp.max(scores, axis=-1, keepdims=True)
            exponent = jnp.exp(scores - top)
            total = jnp.sum(exponent, axis=-1, keepdims=True)
            probs = (exponent / total).astype(jnp.bfloat16)
            mixed_values = jnp.dot(probs, values[seen], preferred_element_type=jnp.float32)
            log_total = top + jnp.log(total)
            kept = jnp.zeros((BLOCK, HD), jnp.float32)
            for head in range(heads):
                mine = slice(head * BLOCK, (head + 1) * BLOCK)
                out[0, at, columns(head)] = mixed_values[mine].astype(jnp.bfloat16)
                kept = jnp.where(lane == head, log_total[mine], kept)
            logs[0, at] = kept
        across_columns(out[0], weights, wide, heads * HD, branch)

        @pl.when(sequence == 1)
        def _():
            steps[1]()
            for copy in copies:
                copy.start()

        @pl.when(sequence == 2)
        def _():
            steps[2]()

        @pl.when(sequence == count - 1)
        def _():
            steps[3]()
            for copy in copies:
                copy.wait()

    outs = pl.pallas_call(
        kernel,
        name="attend",
        grid=(count,),
        out_shape=(
            jax.ShapeDtypeStruct((count, rows, wide), jnp.float32),
            jax.ShapeDtypeStruct((count, rows, heads * HD), jnp.bfloat16),
            jax.ShapeDtypeStruct((count, rows, HD), jnp.float32),
            jax.ShapeDtypeStruct((count, rows, width), jnp.bfloat16),
            layer_rows(own_rows, width),
        )
        + tuple(like(piece) for piece in extra),
        in_specs=[
            pl.BlockSpec(memory_space=pltpu.SMEM),
            pl.BlockSpec(memory_space=pltpu.SMEM),
            per_sequence(rows, width),
            anywhere(),
            whole(rows, HD),
            whole(rows, HD),
            whole(2, HD),
            whole(own_rows, width),
        ]
        + [whole(*piece.shape) for piece in extra],
        out_specs=(
            per_sequence(rows, wide),
            per_sequence(rows, heads * HD),
            per_sequence(rows, HD),
            per_sequence(rows, width),
            anywhere(),
        )
        + (anywhere(),) * extras,
        scratch_shapes=[
            pltpu.VMEM((heads, rows, HD), jnp.bfloat16),
            pltpu.VMEM((rows, HD), jnp.bfloat16),
            pltpu.VMEM((rows, HD), jnp.bfloat16),
            pltpu.VMEM(weights.shape, weights.dtype),
            pltpu.SemaphoreType.DMA,
        ]
        + gather_scratch()
        + exchange_scratch() * extras,
        compiler_params=params(number),
        cost_estimate=cost_of(50),
    )(lengths, owners, normed, weights, cos_full, sin_full, gains, cotangent, *extra)
    return outs


def team_split(width, outer_count):
    split = TEAM if width // outer_count % (TEAM * HD) == 0 else 1
    return split, width // outer_count // split


def local_first(place):
    near, core, _ = spots()
    other_near, other_core = place // 2, place % 2
    return (near + other_near * (1 - 2 * near)) * CORE + core + other_core * (1 - 2 * core)


def ordered(*shape):
    return pl.BlockSpec((1,) + shape, lambda s: (local_first(s),) + (0,) * len(shape))


def attend_back(
    projected,
    normed,
    attended,
    own_grad,
    logs,
    weights,
    part,
    hidden,
    extra,
    outer_count,
    lengths,
    owners,
    cos_full,
    sin_full,
    gains,
    heads,
    number,
):
    count, rows, wide = projected.shape
    own_rows, width = hidden.shape
    extras = len(extra)
    cut = balanced(own_rows, crossing(extra, width))

    every = wide + heads * HD
    split, share = team_split(width, outer_count)

    def kernel(
        lengths, owners, proj, normed, attended, own_grad, logs, weights_any, cos_ref, sin_ref, gains, part, hidden, *rest
    ):
        pieces, rest = rest[:extras], rest[extras:]
        (gathered, gain_grad, back_part, output, grad_weights), rest = rest[:5], rest[5:]
        mixed, rest = rest[:extras], rest[extras:]
        (queries, keys, values, grad_att, grad_q, grad_k, grad_v_sum, summed), rest = rest[:8], rest[8:]
        (total, held, held_sem, out, grad_v, grad_sem), rest = rest[:6], rest[6:]
        (weights, staged, weights_sem, store_sem), rest = rest[:4], rest[4:]
        sums, sems, rest = rest[:SUM_SCRATCH], rest[SUM_SCRATCH : SUM_SCRATCH + 3], rest[SUM_SCRATCH + 3 :]
        place = pl.program_id(0)
        sequence = local_first(place)
        steps, from_tp, from_near = plan_sum_of(part, total, sums, cut)
        gather = plan_gather(own_grad, gathered, *sems, cut=own_rows // 2, parts=True)
        copies = plan_exchanges(pieces, mixed, rest)
        fetch_weights = pltpu.make_async_copy(weights_any, weights, weights_sem)
        store = pltpu.make_async_copy(staged, grad_weights, store_sem)

        def arrival(which):
            member = local_first(which)
            return pltpu.make_async_copy(
                gathered.at[member // CORE, member % CORE],
                grad_v.at[which % 2],
                grad_sem.at[which % 2],
            )

        fetch = pltpu.make_async_copy(hidden, held, held_sem)

        @pl.when(place == 0)
        def _():
            greet(EVERYONE_NEAR)
            gather[0]()
            steps[0]()
            fetch.start()
            fetch_weights.start()
            gain_grad[...] = jnp.zeros_like(gain_grad)
            summed[...] = jnp.zeros_like(summed)
            gather[1]()
            gather[2]()
            gather[3]()
            arrival(0).start()
            fetch_weights.wait()

        @pl.when(place == 2)
        def _():
            arrival(3).start()

        head_inputs(proj, gains, cos_ref, sin_ref, queries, keys, values, heads)
        grad_k[...] = jnp.zeros_like(grad_k)
        grad_v_sum[...] = jnp.zeros_like(grad_v_sum)
        arrival(place).wait()
        grad = grad_v[place % 2].reshape(rows, width)
        group = lax.axis_index("outer") * TEAM + sequence
        length = sequence_length(lengths, owners, group)
        grad_att[...] = jnp.dot(
            grad, weights[:, wide:], preferred_element_type=jnp.float32
        ).astype(jnp.bfloat16)

        for step in range(rows // BLOCK):
            at = pl.ds(step * BLOCK, BLOCK)
            seen = pl.ds(0, (step + 1) * BLOCK)
            stacked = stack_heads(queries, at, heads)
            above = jnp.concatenate([grad_att[at, columns(head)] for head in range(heads)], axis=0)
            log_total = jnp.concatenate(
                [logs[0, at, head : head + 1] for head in range(heads)], axis=0
            )
            probs = jnp.exp(masked_scores(stacked, keys[seen], step, length) - log_total)
            grad_probs = lax.dot_general(
                above, values[seen], (((1,), (1,)), ((), ())), preferred_element_type=jnp.float32
            )
            inner = jnp.sum(probs * grad_probs, axis=-1, keepdims=True)
            grad_scores = (probs * (grad_probs - inner)).astype(jnp.bfloat16)
            by_query = jnp.dot(grad_scores, keys[seen], preferred_element_type=jnp.float32)
            for head in range(heads):
                grad_q[head, at] = by_query[head * BLOCK : (head + 1) * BLOCK] * (HD ** (-0.5))
            grad_k[seen] += lax.dot_general(
                grad_scores, stacked, (((0,), (0,)), ((), ())), preferred_element_type=jnp.float32
            )
            grad_v_sum[seen] += lax.dot_general(
                probs.astype(jnp.bfloat16),
                above,
                (((0,), (0,)), ((), ())),
                preferred_element_type=jnp.float32,
            )

        def settle(column, gain, value):
            back, by_gain = head_back(
                proj[0, :, columns(column)], gains[gain : gain + 1, :], value, cos_ref[...], sin_ref[...]
            )
            out[:, columns(column)] = back.astype(jnp.bfloat16)
            gain_grad[gain] += by_gain.reshape(rows // 8, 8, HD).sum(axis=0)

        for head in range(heads):
            settle(head, 0, grad_q[head])
        settle(heads, 1, grad_k[...] * (HD ** (-0.5)))
        out[:, columns(heads + 1)] = grad_v_sum[...].astype(jnp.bfloat16)

        across_columns(out[...], weights, 0, wide, back_part)

        by_projected, by_attended = out[...].T, attended[0].T
        for start in range(0, width, 512):
            at = pl.ds(start, 512)
            summed[:wide, at] += jnp.dot(
                by_projected, normed[0, :, at], preferred_element_type=jnp.float32
            )
            summed[wide:, at] += jnp.dot(
                by_attended, grad[:, start : start + 512], preferred_element_type=jnp.float32
            )

        @pl.when(place == 0)
        def _():
            gather[5]()
            steps[1]()
            gather[4]()
            arrival(1).start()

        @pl.when(place == 1)
        def _():
            steps[2]()
            for copy in copies:
                copy.start()
            gather[6]()
            arrival(2).start()

        @pl.when(place == count - 1)
        def _():
            for outer in range(outer_count):
                for member in range(split):
                    start = (outer * split + member) * share
                    staged[outer, member] = summed[:, start : start + share].astype(jnp.bfloat16)
            store.start()
            fetch.wait()

            def finish(at):
                value = total[at] + read(from_tp, at) + read(from_near, at)
                output[at] = (held[at] + value).astype(jnp.bfloat16)

            steps[3](finish)
            store.wait()
            for copy in copies:
                copy.wait()

    return pl.pallas_call(
        kernel,
        name="attend_back",
        grid=(count,),
        out_shape=(
            layer_rows(own_rows, width),
            jax.ShapeDtypeStruct((2, 8, HD), jnp.float32),
            jax.ShapeDtypeStruct((count, rows, width), jnp.bfloat16),
            jax.ShapeDtypeStruct((own_rows, width), jnp.bfloat16),
            jax.ShapeDtypeStruct((outer_count, split, every, share), jnp.bfloat16),
        )
        + tuple(like(piece) for piece in extra),
        in_specs=[
            pl.BlockSpec(memory_space=pltpu.SMEM),
            pl.BlockSpec(memory_space=pltpu.SMEM),
            ordered(rows, wide),
            ordered(rows, width),
            ordered(rows, heads * HD),
            whole(own_rows, width),
            ordered(rows, HD),
            anywhere(),
            whole(rows, HD),
            whole(rows, HD),
            whole(2, HD),
            anywhere(),
            anywhere(),
        ]
        + [whole(*piece.shape) for piece in extra],
        out_specs=(
            anywhere(),
            pl.BlockSpec((2, 8, HD), lambda s: (0, 0, 0)),
            ordered(rows, width),
            whole(own_rows, width),
            anywhere(),
        )
        + (anywhere(),) * extras,
        scratch_shapes=[
            pltpu.VMEM((heads, rows, HD), jnp.bfloat16),
            pltpu.VMEM((rows, HD), jnp.bfloat16),
            pltpu.VMEM((rows, HD), jnp.bfloat16),
            pltpu.VMEM((rows, heads * HD), jnp.bfloat16),
            pltpu.VMEM((heads, rows, HD), jnp.float32),
            pltpu.VMEM((rows, HD), jnp.float32),
            pltpu.VMEM((rows, HD), jnp.float32),
            pltpu.VMEM((every, width), jnp.float32),
            pltpu.VMEM((own_rows, width), jnp.float32),
            pltpu.VMEM((own_rows, width), jnp.float32),
            pltpu.SemaphoreType.DMA,
            pltpu.VMEM((rows, wide), jnp.bfloat16),
            pltpu.VMEM((2, 2, own_rows, width), jnp.bfloat16),
            pltpu.SemaphoreType.DMA((2,)),
            pltpu.VMEM(weights.shape, weights.dtype),
            pltpu.VMEM((outer_count, split, every, share), jnp.bfloat16),
            pltpu.SemaphoreType.DMA,
            pltpu.SemaphoreType.DMA,
        ]
        + sum_scratch(own_rows, width, cut)
        + gather_scratch()
        + exchange_scratch() * extras,
        compiler_params=params(number),
        cost_estimate=cost_of(50),
    )(
        lengths,
        owners,
        projected,
        normed,
        attended,
        own_grad,
        logs,
        weights,
        cos_full,
        sin_full,
        gains,
        spread(part, own_rows),
        hidden,
        *extra,
    )


def feed(normed, weights, cotangent, gathered, early, number):
    count, rows, width = normed.shape
    units = weights.shape[1] // 2
    late = cotangent.shape[0] - early

    def kernel(normed, weights_any, own, _, product, active, out, weights, weights_sem, *sems):
        fetch = pltpu.make_async_copy(weights_any, weights, weights_sem)
        steps = plan_gather(
            own, out, *sems, cut=balanced(late, 0), base=early, rows=late
        )
        sequence = pl.program_id(0)

        @pl.when(sequence == 0)
        def _():
            fetch.start()
            greet(NEIGHBOURS)
            steps[0]()
            fetch.wait()

        for start in range(0, units, 256):
            gate_at, up_at = pl.ds(start, 256), pl.ds(units + start, 256)
            gate = jnp.dot(normed[0], weights[:, gate_at], preferred_element_type=jnp.float32)
            up = jnp.dot(normed[0], weights[:, up_at], preferred_element_type=jnp.float32)
            product[0, :, gate_at] = gate
            product[0, :, up_at] = up
            active[0, :, gate_at] = swish_product(gate, up).astype(jnp.bfloat16)

        for place in (1, 2, 3):

            @pl.when(sequence == count - 4 + place)
            def _(place=place):
                steps[place]()

    return pl.pallas_call(
        kernel,
        name="feed",
        grid=(count,),
        out_shape=(
            jax.ShapeDtypeStruct((count, rows, 2 * units), jnp.float32),
            jax.ShapeDtypeStruct((count, rows, units), jnp.bfloat16),
            like(gathered),
        ),
        in_specs=[
            per_sequence(rows, width),
            anywhere(),
            whole(*cotangent.shape),
            anywhere(),
        ],
        out_specs=(per_sequence(rows, 2 * units), per_sequence(rows, units), anywhere()),
        scratch_shapes=[pltpu.VMEM(weights.shape, weights.dtype), pltpu.SemaphoreType.DMA]
        + gather_scratch(),
        input_output_aliases={3: 2},
        compiler_params=params(number),
        cost_estimate=cost_of(28),
    )(normed, weights, cotangent, gathered)


def feed_back(grads, weights, product, normed, outer_count):
    count, rows, width = grads.shape
    units = weights.shape[1]
    split, share = team_split(width, outer_count)
    turns = width // 512

    def kernel(grads, weights, product, normed, by_gate, by_up, grad_weight, kept):
        step = pl.program_id(0)

        @pl.when(step < count)
        def _():
            for start in range(0, units, 256):
                gate_at, up_at = pl.ds(start, 256), pl.ds(units + start, 256)
                grad = jnp.dot(grads[0], weights[:, gate_at], preferred_element_type=jnp.float32)
                gate, up = product[0, :, gate_at], product[0, :, up_at]
                part = jax.nn.sigmoid(gate)
                slope = grad * up * part * (1.0 + gate * (1.0 - part))
                by_gate[0, :, gate_at] = slope.astype(jnp.bfloat16)
                by_up[0, :, gate_at] = (grad * gate * part).astype(jnp.bfloat16)
            kept[step] = by_gate[0]

        @pl.when(step >= count)
        def _():
            turned = lax.dot_general(
                kept[...].reshape(count * rows, units),
                normed[...],
                (((0,), (0,)), ((), ())),
                preferred_element_type=jnp.float32,
            ).astype(jnp.bfloat16)
            for place in range(512 // share):
                grad_weight[place] = turned[:, place * share : (place + 1) * share]

    def early(*shape):
        return pl.BlockSpec((1,) + shape, lambda s: (jnp.minimum(s, count - 1), 0, 0))

    def late(s):
        return jnp.maximum(s - count, 0)

    return pl.pallas_call(
        kernel,
        name="feed_back",
        grid=(count + turns,),
        out_shape=(jax.ShapeDtypeStruct((count, rows, units), jnp.bfloat16),) * 2
        + (jax.ShapeDtypeStruct((width // share, units, share), jnp.bfloat16),),
        in_specs=[
            early(rows, width),
            whole(*weights.shape),
            early(rows, 2 * units),
            pl.BlockSpec((count * rows, 512), lambda s: (0, late(s))),
        ],
        out_specs=(
            early(rows, units),
            early(rows, units),
            pl.BlockSpec((512 // share, units, share), lambda s: (late(s), 0, 0)),
        ),
        scratch_shapes=[pltpu.VMEM((count, rows, units), jnp.bfloat16)],
        compiler_params=pltpu.CompilerParams(vmem_limit_bytes=VMEM_LIMIT),
        cost_estimate=cost_of(28),
    )(grads, weights, product, normed)


def spans(widths, base=0):
    for member in range(TEAM):
        first, inside = base, 0
        for width in widths:
            share = width // TEAM
            yield member, pl.ds(first + member * share, share), pl.ds(inside, share)
            first += width
            inside += share


def by_turned(height, base, widths, source, members=range(TEAM)):
    parts = [part for part in spans(widths, base) if part[0] in members]

    def run(pieces, update):
        for member, across, inside in parts:
            update(pl.ds(0, height), across, pieces[member, inside].T)

    if len(members) == 1:
        columns = parts[0][1]
    else:
        columns = pl.ds(base, sum(widths))
    return source, pl.ds(0, height), columns, run


def by_rows(member, height, width, inside, source):
    at, across = pl.ds(member * height, height), pl.ds(0, width)

    def run(pieces, update):
        if inside is None:
            update(at, across, pieces[member].T)
        else:
            update(at, across, pieces[member, pl.ds(inside, height)])

    return source, at, across, run


def adam_all(sets, pieces, factor, gain_grad, gains, passed):
    jobs = [(place,) + job for place, group in enumerate(sets) for job in group[3]]
    count, total, sources, others = len(jobs), len(sets), len(pieces), len(passed)

    def kernel(*refs):
        inputs, refs = refs[: 3 * total], refs[3 * total :]
        piece_refs, factor, refs = refs[:sources], refs[sources], refs[sources + 1 :]
        (gain_grad, *gains), refs = refs[:4], refs[4:]
        passed, refs = refs[:others], refs[others:]
        outputs, refs = refs[: 4 * total], refs[4 * total :]
        new_gains, refs = refs[:3], refs[3:]
        onward, refs = refs[:others], refs[others:]
        held, refs = refs[: 4 * total], refs[4 * total :]
        held_pieces, refs = refs[:sources], refs[sources:]
        between, (piece_sem, in_sem, out_sem, pass_sem) = refs[:others], refs[others:]
        scale = factor[0:1, 0:1]
        loads = [
            pltpu.make_async_copy(piece_refs[place], held_pieces[place], piece_sem.at[place])
            for place in range(sources)
        ]
        arrivals, stores = [], []
        kept = [
            pltpu.make_async_copy(source, target, pass_sem.at[0, place])
            for place, (source, target) in enumerate(zip(passed, between))
        ]
        kept_on = [
            pltpu.make_async_copy(source, target, pass_sem.at[1, place])
            for place, (source, target) in enumerate(zip(between, onward))
        ]
        for slot, (place, source, at, across, _) in enumerate(jobs):
            arrivals.append(
                [
                    pltpu.make_async_copy(
                        inputs[3 * place + number].at[at, across],
                        held[4 * place + number].at[at, across],
                        in_sem.at[3 * slot + number],
                    )
                    for number in range(3)
                ]
            )
        first_use = {}
        for slot, job in enumerate(jobs):
            first_use.setdefault(job[1], slot)

        def bring(slot):
            if slot < count:
                if first_use[jobs[slot][1]] == slot:
                    loads[jobs[slot][1]].start()
                for copy in arrivals[slot]:
                    copy.start()

        for slot in range(AHEAD):
            bring(slot)
        gain_step = adam_update(
            gains[0][...],
            gain_grad[: gains[0].shape[0]],
            gains[1][...],
            gains[2][...],
            scale,
            0.0,
            gain_rate,
        )
        for target, value in zip(new_gains, gain_step):
            target[...] = value
        for slot, (place, source, at, across, run) in enumerate(jobs):
            weight, moment, square, low = held[4 * place : 4 * place + 4]
            if first_use[source] == slot:
                loads[source].wait()
            for copy in arrivals[slot]:
                copy.wait()
            bring(slot + AHEAD)
            if slot == 0:
                for copy in kept:
                    copy.start()

            def update(rows, columns, gradient):
                where = (rows, columns)
                value, one, two = adam_update(
                    weight[where],
                    gradient.astype(jnp.float32),
                    moment[where],
                    square[where],
                    scale,
                    weight_decay,
                    learn_rate,
                )
                weight[where], moment[where], square[where] = value, one, two
                low[where] = value.astype(jnp.bfloat16)

            run(held_pieces[source], update)
            for number, origin in enumerate((weight, moment, square, low)):
                copy = pltpu.make_async_copy(
                    origin.at[at, across],
                    outputs[4 * place + number].at[at, across],
                    out_sem.at[4 * slot + number],
                )
                copy.start()
                stores.append(copy)
            if slot == 4:
                for arrived, copy in zip(kept, kept_on):
                    arrived.wait()
                    copy.start()
        for copy in stores + kept_on:
            copy.wait()

    args, shapes, scratch = [], [], []
    for weight, moment, square, _ in sets:
        args += [weight, moment, square]
        low = jax.ShapeDtypeStruct(weight.shape, jnp.bfloat16)
        shapes += [like(weight)] * 3 + [low]
        scratch += [pltpu.VMEM(each.shape, each.dtype) for each in (weight, moment, square, low)]
    outs = pl.pallas_call(
        kernel,
        name="adam_all",
        out_shape=tuple(shapes) + (like(gains[0]),) * 3 + tuple(like(each) for each in passed),
        in_specs=[anywhere()] * (3 * total + sources) + [in_vmem()] * 5 + [anywhere()] * others,
        out_specs=(anywhere(),) * (4 * total) + (in_vmem(),) * 3 + (anywhere(),) * others,
        scratch_shapes=scratch
        + [pltpu.VMEM(each.shape, each.dtype) for each in tuple(pieces) + tuple(passed)]
        + [
            pltpu.SemaphoreType.DMA((sources,)),
            pltpu.SemaphoreType.DMA((3 * count,)),
            pltpu.SemaphoreType.DMA((4 * count,)),
            pltpu.SemaphoreType.DMA((2, others)),
        ],
        compiler_params=pltpu.CompilerParams(vmem_limit_bytes=VMEM_LIMIT),
        cost_estimate=cost_of(15),
    )(*args, *pieces, factor, gain_grad, *gains, *passed)
    steps = [outs[4 * place : 4 * place + 4] for place in range(total)]
    return steps + [outs[4 * total : 4 * total + 3], outs[4 * total + 3 :]]


def rotary(count):
    frequency = rope_base ** (-(np.arange(HD // 2) * 2.0 / HD))
    angles = np.arange(count)[:, None] * frequency[None, :]
    cosine, sine = np.cos(angles), np.sin(angles)
    full = [np.concatenate(pair, axis=1) for pair in ((cosine, cosine), (-sine, sine))]
    return [jnp.asarray(table, jnp.float32) for table in full]


def gather_outer(mixed):
    return lax.all_gather(mixed.reshape(-1, mixed.shape[2]), "outer", axis=0, tiled=True)


def team_pieces(summed):
    return summed.reshape(TEAM, -1, summed.shape[-1])


def turned_pieces(summed):
    if summed.shape[1] * TEAM * lax.axis_size("outer") == D:
        return team_pieces(summed)
    return summed.reshape(summed.shape[0], TEAM, -1).transpose(1, 0, 2)


def sum_weight(gradient):
    return lax.psum_scatter(gradient, "outer", scatter_dimension=0, tiled=True)


def after(values, earlier):
    return lax.optimization_barrier((values, earlier))


def adam_update(weight, gradient, moment_one, moment_two, factor, decay_rate, rate_value):
    clipped = gradient * factor
    moment_one = beta_first * moment_one + (1.0 - beta_first) * clipped
    moment_two = beta_second * moment_two + (1.0 - beta_second) * clipped * clipped
    first_fixed = moment_one * (rate_value / (1.0 - beta_first**STEP))
    root_fixed = jnp.sqrt(moment_two) * (1.0 - beta_second**STEP) ** (-0.5)
    kept = weight * (1.0 - rate_value * decay_rate) if decay_rate else weight
    weight = kept - first_fixed / (root_fixed + adam_epsilon)
    return (weight, moment_one, moment_two)


def dot(left, right, contract):
    return lax.dot_general(
        left, right, ((contract[0], contract[1]), ((), ())), preferred_element_type=jnp.float32
    )


def times(left, right):
    return dot(left, right, ((1,), (0,)))


def times_across(left, right):
    return dot(left, right, ((1,), (1,)))


def over_rows(left, right):
    return dot(left, right, ((0,), (0,)))


def local(
    inputs,
    cotangent,
    lengths,
    owners,
    qkv_weight,
    out_weight,
    gate_up_weight,
    down_weight,
    norm_gains,
    qkv_moment,
    out_moment,
    gate_up_moment,
    down_moment,
    gains_moment,
    qkv_square,
    out_square,
    gate_up_square,
    down_square,
    gains_square,
):
    tp_count = lax.axis_size("tp")
    half_rows = inputs.shape[0]
    row_count = half_rows * tp_count
    heads = H // tp_count // TEAM
    hidden_units = FF // tp_count // TEAM
    qkv_widths = (H * HD // tp_count, KV * HD // tp_count, KV * HD // tp_count)
    out_widths = (H * HD // tp_count,)
    part_rows = qkv_weight.shape[0]
    gate_up_widths = (FF // tp_count, FF // tp_count)
    down_widths = (FF // tp_count,)

    cos_full, sin_full = rotary(row_count)
    attn_gain = norm_gains[:D]
    mlp_gain = norm_gains[D : 2 * D]
    head_gains = norm_gains[2 * D :].reshape(2, HD)

    normed_attn, gate_up_mixed, first_full, grad_low, down_pieces = opening(
        qkv_weight,
        out_weight,
        gate_up_weight,
        down_weight,
        inputs,
        attn_gain,
        cotangent,
        lengths,
        owners,
        lax.axis_size("outer"),
        0,
    )
    gate_up_full = gather_outer(gate_up_mixed)
    early = half_rows // 2 // CHUNK * CHUNK
    projected, attended, logs, attn_branch, grad_all, down_mixed = attend(
        normed_attn.reshape(TEAM, row_count, D),
        first_full,
        grad_low,
        (down_pieces,),
        lengths,
        owners,
        cos_full,
        sin_full,
        head_gains,
        heads,
        early,
        1,
    )
    down_full = gather_outer(down_mixed)
    hidden, normed_mlp = branch_and_norm(attn_branch, inputs, mlp_gain, 2, "branch_and_norm")
    gate_up, activated, grad_all = feed(
        normed_mlp.reshape(TEAM, row_count, D), gate_up_full, grad_low, grad_all, early, 8
    )
    grad_down = over_rows(grad_all.reshape(-1, D), activated.reshape(-1, hidden_units))
    grad_all, grad_down = after(grad_all, grad_down.astype(jnp.bfloat16))
    down_sum = sum_weight(grad_down)
    grad_gate, grad_up, grad_gate_weight = feed_back(
        grad_all.reshape(TEAM, row_count, D),
        down_full,
        gate_up,
        normed_mlp,
        lax.axis_size("outer"),
    )
    gate_sum = turned_pieces(
        sum_weight(grad_gate_weight.reshape(-1, grad_gate_weight.shape[2]))
    )
    grad_hidden, grad_mlp_gain, own_grad, mlp_part, grad_up_weight = feed_back_rest(
        grad_gate,
        grad_up,
        gate_up_full,
        activated,
        down_full,
        normed_mlp,
        hidden,
        grad_low,
        mlp_gain,
        lax.axis_size("outer"),
        3,
        "feed_back_rest",
    )
    up_sum = turned_pieces(sum_weight(grad_up_weight.reshape(-1, grad_up_weight.shape[2])))
    _, grad_head_gains, grad_normed_attn, output, grad_first, down_mixed = attend_back(
        projected,
        normed_attn.reshape(TEAM, row_count, D),
        attended,
        own_grad,
        logs,
        first_full,
        mlp_part,
        hidden,
        (team_pieces(down_sum),),
        lax.axis_size("outer"),
        lengths,
        owners,
        cos_full,
        sin_full,
        head_gains,
        heads,
        7,
    )
    grad_first, gate_sum = after(grad_first, gate_sum)
    first_sum = turned_pieces(sum_weight(grad_first.reshape(-1, grad_first.shape[3])))
    input_grad, attn_gain_parts, squares, gate_mixed, up_mixed = norm_back_last(
        grad_normed_attn,
        inputs,
        grad_hidden,
        attn_gain,
        (gate_sum, up_sum),
        (gate_sum, up_sum, down_sum),
        4,
        "norm_back_attn",
    )
    gain_part = jnp.concatenate(
        [jnp.zeros_like(grad_mlp_gain), grad_mlp_gain, grad_head_gains.sum(axis=1).reshape(-1)]
    )
    gain_count = gain_part.shape[0]
    packed = jnp.pad(gain_part, (0, -gain_count % PAD))
    packed, norm_tile, factor_tile, first_mixed = total_everywhere(
        packed.reshape(-1, HD),
        attn_gain_parts,
        squares,
        first_sum,
        lax.axis_size("outer"),
        5,
        "total_everywhere",
    )
    grad_norm = norm_tile[0, 0]
    (
        (new_gate_up, new_gate_up_one, new_gate_up_two, gate_up_copy),
        (new_down, new_down_one, new_down_two, down_copy),
        (new_out, new_out_one, new_out_two, out_copy),
        (new_qkv, new_qkv_one, new_qkv_two, qkv_copy),
        new_gains,
        (output, input_grad),
    ) = adam_all(
        [
            (
                gate_up_weight,
                gate_up_moment,
                gate_up_square,
                [
                    by_turned(part_rows, base, gate_up_widths[:1], source, (member,))
                    for source, base in enumerate((0, gate_up_widths[0]))
                    for member in range(TEAM)
                ],
            ),
            (
                down_weight,
                down_moment,
                down_square,
                [by_rows(member, hidden_units, part_rows, None, 2) for member in range(TEAM)],
            ),
            (
                out_weight,
                out_moment,
                out_square,
                [
                    by_rows(member, heads * HD, part_rows, (heads + 2) * HD, 3)
                    for member in range(TEAM)
                ],
            ),
            (
                qkv_weight,
                qkv_moment,
                qkv_square,
                [by_turned(part_rows, 0, qkv_widths, 3)],
            ),
        ],
        (gate_mixed, up_mixed, down_mixed, first_mixed),
        factor_tile,
        packed,
        [each.reshape(-1, HD) for each in (norm_gains, gains_moment, gains_square)],
        (output, input_grad),
    )
    new_gains, new_gains_one, new_gains_two = (each.reshape(-1) for each in new_gains)
    return (
        output,
        input_grad,
        grad_norm,
        new_qkv,
        new_qkv_one,
        new_qkv_two,
        qkv_copy,
        new_out,
        new_out_one,
        new_out_two,
        out_copy,
        new_gate_up,
        new_gate_up_one,
        new_gate_up_two,
        gate_up_copy,
        new_down,
        new_down_one,
        new_down_two,
        down_copy,
        new_gains,
        new_gains_one,
        new_gains_two,
    )


def solution(mesh):
    fsdp_count, tp_count = mesh.shape["fsdp"], mesh.shape["tp"]
    cut = mesh.devices.reshape(fsdp_count // TEAM, NEAR, CORE, tp_count)
    cut_mesh = Mesh(cut, ("outer",) + LAYER)
    fsdp = ("outer", "near", "core")
    rows = P(fsdp + ("tp",), None)
    wide = P(fsdp, "tp")
    tall = P("tp", fsdp)
    weights = (wide, tall, wide, tall, P())
    return jax.shard_map(
        local,
        mesh=cut_mesh,
        in_specs=(rows, rows, P(), P()) + weights * 3,
        out_specs=(rows, rows, P()) + (wide,) * 4 + (tall,) * 4 + (wide,) * 4 + (tall,) * 4 + (P(),) * 3,
        check_vma=False,
    )
```

```python
from functools import partial

import jax
import jax.numpy as jnp
import numpy as np
from jax import lax
from jax.experimental import pallas as pl
from jax.experimental.pallas import tpu as pltpu
from jax.sharding import Mesh, PartitionSpec as P

D = 2048
H = 16
KV = 8
HD = 128
FF = 6144
STEP = 10


norm_epsilon = 1e-06
rope_base = 1000000.0
clip_norm = 1.0
learn_rate = 0.04
gain_rate = 0.8
beta_first = 0.9
beta_second = 0.999
adam_epsilon = 1e-08
weight_decay = 0.1
masked_score = -1e30

NEAR = 2
CORE = 2
TEAM = NEAR * CORE
LAYER = ("near", "core", "tp")
BLOCK = 128
PAD = 8 * 128


def rms_scale(values):
    return lax.rsqrt(jnp.mean(values * values, axis=-1, keepdims=True) + norm_epsilon)


def swish_product(gate_part, up_part):
    return jax.nn.silu(gate_part) * up_part


MESH_ID = pl.DeviceIdType.MESH
VMEM_LIMIT = 60 * 1024 * 1024
CHUNK = 16
GATHER_COPIES = 17
AHEAD = 1000
PART = TEAM // 2
HEAD_GAINS = 2 * D // HD
SUM_COPIES = 12
NEIGHBOURS = ((1, 0, 0), (0, 1, 0), (0, 0, 1))
MATES = ((0, 1, 0), (1, 0, 0), (1, 1, 0))
EVERYONE_NEAR = NEIGHBOURS + ((1, 1, 0),)


def spots():
    return tuple(lax.axis_index(name) for name in LAYER)


def flipped(near_flip, core_flip, tp_flip):
    return {
        name: 1 - spot if flip else spot
        for name, spot, flip in zip(LAYER, spots(), (near_flip, core_flip, tp_flip))
    }


def greet(flips):
    barrier = pltpu.get_barrier_semaphore()
    for flip in flips:
        pl.semaphore_signal(barrier, inc=1, device_id=flipped(*flip), device_id_type=MESH_ID)
    pl.semaphore_wait(barrier, len(flips))


def link(source, target, send_sem, recv_sem, flip):
    return pltpu.make_async_remote_copy(
        src_ref=source,
        dst_ref=target,
        send_sem=send_sem,
        recv_sem=recv_sem,
        device_id=flipped(*flip),
        device_id_type=MESH_ID,
    )


TO_NEAR, TO_CORE, TO_TP = NEIGHBOURS


def plan_exchange(pieces, out, send, recv, own_sem):
    near, core, _ = spots()
    own = near * CORE + core
    copies = []
    for number, flip in enumerate(MATES):
        there = (1 - near if flip[0] else near) * CORE + (1 - core if flip[1] else core)
        copies.append(
            link(pieces.at[there], out.at[own], send.at[number], recv.at[number], flip)
        )
    copies.append(pltpu.make_async_copy(pieces.at[own], out.at[own], own_sem))
    return copies


def exchange_scratch():
    return [
        pltpu.SemaphoreType.DMA((len(MATES),)),
        pltpu.SemaphoreType.DMA((len(MATES),)),
        pltpu.SemaphoreType.DMA,
    ]


def crossing(pieces, width):
    return sum(2 * piece.shape[1] * piece.shape[2] for piece in pieces) // width


def plan_exchanges(pieces, mixed, sems):
    copies = []
    for place, (piece, result) in enumerate(zip(pieces, mixed)):
        copies += plan_exchange(piece, result, *sems[3 * place : 3 * place + 3])
    return copies


def plan_gather(own, out, send, recv, own_sem, cut, base=0, rows=None, parts=False, apart=False):
    near, core, tp = spots()
    rows = own.shape[0] if rows is None else rows
    low, high = pl.ds(base, cut), pl.ds(base + cut, rows - cut)
    all_rows = pl.ds(base, rows)

    def make(number, source, target, flip):
        return link(source, target, send.at[number], recv.at[number], flip)

    def give(number, part, flip):
        return make(number, own.at[part], out.at[near, core, tp, part], flip)

    def relay(number, where_near, where_tp, part, flip):
        ref = out.at[where_near, core, where_tp, part]
        return make(number, ref, ref, flip)

    keep = pltpu.make_async_copy(own.at[all_rows], out.at[near, core, tp, all_rows], own_sem)
    twin_own = give(4, all_rows, TO_CORE)
    first_rows = (rows - cut) // 2 // CHUNK * CHUNK
    high_parts = [
        (pl.ds(base + cut, first_rows), 1, 7, 8),
        (pl.ds(base + cut + first_rows, rows - cut - first_rows), 13, 14, 15),
    ]
    near_high = [give(number, part, TO_NEAR) for part, number, _, _ in high_parts]
    tp_high = give(2, high, TO_TP)
    far_high = [relay(number, 1 - near, tp, part, TO_TP) for part, _, number, _ in high_parts]
    twin_beside = [relay(number, 1 - near, tp, part, TO_CORE) for part, _, _, number in high_parts]
    twin_across = relay(9, near, 1 - tp, high, TO_CORE)
    twin_far = [
        relay(number, 1 - near, 1 - tp, part, TO_CORE)
        for (part, *_), number in zip(high_parts, (12, 16))
    ]
    twins = [twin_own, twin_across] + twin_far + twin_beside
    ways = near_high + far_high + [tp_high]
    if cut:
        tp_low = give(0, low, TO_TP)
        near_low = give(3, low, TO_NEAR)
        far_low = relay(5, near, 1 - tp, low, TO_NEAR)
        twin_across_low = relay(6, near, 1 - tp, low, TO_CORE)
        twin_beside_low = relay(10, 1 - near, tp, low, TO_CORE)
        twin_far_low = relay(11, 1 - near, 1 - tp, low, TO_CORE)
        twins += [twin_across_low, twin_beside_low, twin_far_low]
        ways += [tp_low, near_low, far_low]

    def begin_tp():
        if cut:
            tp_low.start()
        tp_high.start()
        twin_own.start()
        keep.start()

    def begin_near():
        for copy in near_high:
            copy.start()
        if cut:
            near_low.start()

    def begin():
        begin_near()
        begin_tp()

    def pass_on(part):
        near_high[part].wait_recv()
        far_high[part].start()
        twin_beside[part].start()

    def middle():
        if cut:
            tp_low.wait_recv()
            far_low.start()
            twin_across_low.start()
        pass_on(0)
        if not apart:
            pass_on(1)

    def later():
        tp_high.wait_recv()
        twin_across.start()
        if cut:
            near_low.wait_recv()
            twin_beside_low.start()

    def own_there():
        keep.wait()

    def twin_there():
        twin_own.wait_recv()
        twin_across.wait_recv()
        if cut:
            twin_across_low.wait_recv()

    def far_there():
        if cut:
            far_low.wait_recv()
            twin_far_low.start()
        for copy, twin in zip(far_high, twin_far):
            copy.wait_recv()
            twin.start()

    def rest_there():
        for copy in twin_beside + twin_far:
            copy.wait_recv()
        if cut:
            twin_beside_low.wait_recv()
            twin_far_low.wait_recv()
        for copy in ways + twins:
            copy.wait_send()

    def finish():
        own_there()
        twin_there()
        far_there()
        rest_there()

    if parts:
        return [begin, middle, later, own_there, twin_there, far_there, rest_there]
    if apart:
        return [begin_tp, begin_near, middle, partial(pass_on, 1), later, finish]
    return [begin, middle, later, finish]


def balanced(rows, beside):
    return max(0, (rows - beside) // 2 // CHUNK * CHUNK)


def gather_scratch():
    return [
        pltpu.SemaphoreType.DMA((GATHER_COPIES,)),
        pltpu.SemaphoreType.DMA((GATHER_COPIES,)),
        pltpu.SemaphoreType.DMA,
    ]


def add_rows(target, start, count, *sources):
    @pl.loop(0, count // CHUNK)
    def _(step):
        at = pl.ds(pl.multiple_of(start + step * CHUNK, CHUNK), CHUNK)
        total = None
        for source, shift in sources:
            where = pl.ds(pl.multiple_of(start - shift + step * CHUNK, CHUNK), CHUNK)
            value = source[where].astype(jnp.float32)
            total = value if total is None else total + value
        target[at] = total.astype(target.dtype)


def halved(start, count):
    half = count // 2 // CHUNK * CHUNK
    return (start, half), (start + half, count - half)


def plan_sum(outgoing, mine, keep, total, scratch, cut):
    theirs, way_near, way_tp, from_tp, from_near, send, recv = scratch
    rows = total.shape[0]
    low, high = pl.ds(0, cut), pl.ds(cut, rows - cut)

    def make(number, source, target, flip):
        return link(source, target, send.at[number], recv.at[number], flip)

    twin = [make(number, outgoing[number], theirs.at[number], TO_CORE) for number in range(4)]
    far, to_tp, to_near, own = mine
    low_parts = halved(0, cut)
    high_parts = halved(cut, rows - cut)
    far_high = make(5, far.at[high], way_tp, TO_TP)
    tp_high = make(6, to_tp.at[high], from_tp.at[high], TO_TP)
    near_high = [
        make(9 + 2 * place, to_near.at[pl.ds(*part)], from_near.at[pl.ds(*part)], TO_NEAR)
        for place, part in enumerate(high_parts)
    ]
    ways = [far_high, tp_high] + near_high
    tp_low = []
    if cut:
        far_low = make(4, far.at[low], way_near, TO_NEAR)
        near_low = make(7, to_near.at[low], from_near.at[low], TO_NEAR)
        tp_low = [
            make(8 + 2 * place, to_tp.at[pl.ds(*part)], from_tp.at[pl.ds(*part)], TO_TP)
            for place, part in enumerate(low_parts)
        ]
        ways += [far_low, near_low] + tp_low

    def ready(number):
        if keep:
            keep[number].wait()
        twin[number].wait_recv()

    def both(number):
        return (mine[number], 0), (theirs.at[number], 0)

    def begin(numbers=range(4)):
        for number in numbers:
            twin[number].start()
            if keep:
                keep[number].start()

    def send_far():
        ready(0)
        if cut:
            add_rows(far, 0, cut, *both(0))
            far_low.start()
        add_rows(far, cut, rows - cut, *both(0))
        far_high.start()

    def send_tp():
        ready(1)
        add_rows(to_tp, cut, rows - cut, *both(1))
        tp_high.start()

    def send_near():
        ready(2)
        if cut:
            add_rows(to_near, 0, cut, *both(2))
            near_low.start()

    def first():
        send_far()
        send_tp()
        send_near()

    def second():
        if cut:
            far_low.wait_recv()
        far_high.wait_recv()
        for place, part in enumerate(high_parts):
            if cut:
                add_rows(to_tp, *low_parts[place], *both(1), (way_near, 0))
                tp_low[place].start()
            add_rows(to_near, *part, *both(2), (way_tp, cut))
            near_high[place].start()
        ready(3)
        add_rows(total, 0, rows, *both(3))

    def finish(body):
        tp_high.wait_recv()
        if cut:
            near_low.wait_recv()
        for place, part in enumerate(high_parts):
            if cut:
                tp_low[place].wait_recv()
                row_loop(*low_parts[place], body)
            near_high[place].wait_recv()
            row_loop(*part, body)
        for copy in twin + ways:
            copy.wait_send()

    return [begin, first, second, finish], (send_far, send_tp, send_near)


def plan_sum_of(part, total, scratch, cut):
    mine, local_sem, *scratch = scratch
    near, core, tp = spots()
    order = [(1 - near, 1 - tp), (near, 1 - tp), (1 - near, tp), (near, tp)]
    outgoing = [part.at[a, 1 - core, b] for a, b in order]
    keep = [
        pltpu.make_async_copy(part.at[a, core, b], mine.at[number], local_sem.at[number])
        for number, (a, b) in enumerate(order)
    ]
    blocks = [mine.at[number] for number in range(4)]
    steps, _ = plan_sum(outgoing, blocks, keep, total, scratch, cut)
    return steps, scratch[3], scratch[4]


def sum_scratch(rows, width, cut, fetched=True):
    low = jnp.bfloat16
    fetch = [pltpu.VMEM((4, rows, width), low), pltpu.SemaphoreType.DMA((4,))]
    return (fetch if fetched else []) + [
        pltpu.VMEM((4, rows, width), low),
        pltpu.VMEM((max(cut, CHUNK), width), low),
        pltpu.VMEM((rows - cut, width), low),
        pltpu.VMEM((rows, width), low),
        pltpu.VMEM((rows, width), low),
        pltpu.SemaphoreType.DMA((SUM_COPIES,)),
        pltpu.SemaphoreType.DMA((SUM_COPIES,)),
    ]


SUM_SCRATCH = 9
COST_SHARE = 1e5


def params(number):
    return pltpu.CompilerParams(
        collective_id=number, has_side_effects=True, vmem_limit_bytes=VMEM_LIMIT
    )


def cost_of(microseconds):
    return pl.CostEstimate(
        flops=0, bytes_accessed=int(microseconds * COST_SHARE), transcendentals=0
    )


def in_vmem():
    return pl.BlockSpec(memory_space=pltpu.VMEM)


def anywhere():
    return pl.BlockSpec(memory_space=pl.ANY)


def like(array):
    return jax.ShapeDtypeStruct(array.shape, array.dtype)


def layer_rows(rows, width):
    return jax.ShapeDtypeStruct((NEAR, CORE, 2, rows, width), jnp.bfloat16)


def wide_gain(gains, place, width):
    first = place * (width // HD)
    return jnp.concatenate(
        [gains[first + part : first + part + 1] for part in range(width // HD)], axis=1
    )


def row_loop(start, count, body):
    @pl.loop(0, count // CHUNK)
    def _(step):
        body(pl.ds(pl.multiple_of(start + step * CHUNK, CHUNK), CHUNK))


def plan_line(blocks, send, recv, count):
    own = lax.axis_index("outer")

    def handle(side, number, half, there):
        block = blocks.at[there, pl.ds(half * PART, PART)]
        return pltpu.make_async_remote_copy(
            src_ref=block,
            dst_ref=block,
            send_sem=send.at[side, number, half],
            recv_sem=recv.at[side, number, half],
            device_id={"outer": own + 1 if side == 0 else own - 1},
            device_id_type=MESH_ID,
        )

    def message(side, number, half):
        return handle(side, number, half, own - number if side == 0 else own + number)

    def arrival(side, number, half):
        return handle(side, number, half, own - 1 - number if side == 0 else own + 1 + number)

    def sends(side, number):
        if side == 0:
            return (own < count - 1) & (own >= number)
        return (own > 0) & (own + number < count)

    def gets(side, number):
        return own >= number + 1 if side == 0 else own + 1 + number < count

    near = lax.axis_index("near")
    halves = (near, 1 - near)

    def push(number, place):
        for side in range(2):

            @pl.when(sends(side, number))
            def _(side=side):
                message(side, number, halves[place]).start()

    def take(number):
        for half in halves:
            for side in range(2):

                @pl.when(gets(side, number))
                def _(side=side, half=half):
                    arrival(side, number, half).wait_recv()

                if number + 2 < count:

                    @pl.when(sends(side, number + 1))
                    def _(side=side, half=half):
                        message(side, number + 1, half).start()

    def settle():
        for number in range(count - 1):
            for side in range(2):

                @pl.when(sends(side, number))
                def _(side=side, number=number):
                    for half in range(2):
                        message(side, number, half).wait_send()

    return push, take, settle


def greet_all(flips, count, work):
    barrier = pltpu.get_barrier_semaphore()
    own = lax.axis_index("outer")
    for flip in flips:
        pl.semaphore_signal(barrier, inc=1, device_id=flipped(*flip), device_id_type=MESH_ID)
    for there, neighbour in ((own < count - 1, own + 1), (own > 0, own - 1)):

        @pl.when(there)
        def _(neighbour=neighbour):
            pl.semaphore_signal(
                barrier, inc=1, device_id={"outer": neighbour}, device_id_type=MESH_ID
            )

    work()
    beside = jnp.where(own < count - 1, 1, 0) + jnp.where(own > 0, 1, 0)
    pl.semaphore_wait(barrier, len(flips) + beside)


def sequence_length(lengths, owners, group):
    total = jnp.int32(0)
    for place in range(lengths.shape[0]):
        total += jnp.where(owners[place] == group, lengths[place], 0)
    return total


def opening(
    qkv, out_weight, gate_up, down, inputs, gains, cotangent, lengths, owners, outer_count, number
):
    rows, width = inputs.shape
    part_rows, wide = qkv.shape
    tall, units = out_weight.shape[0], down.shape[0]
    widths = (wide // 2, wide // 4, wide // 4)
    first_shape = jax.ShapeDtypeStruct((TEAM, part_rows, (wide + tall) // TEAM), jnp.bfloat16)
    gate_up_shape = jax.ShapeDtypeStruct((TEAM, part_rows, 2 * units // TEAM), jnp.bfloat16)
    down_shape = jax.ShapeDtypeStruct((TEAM, part_rows, units // TEAM), jnp.bfloat16)
    cut = balanced(rows, crossing((first_shape, gate_up_shape), width))

    def kernel(
        lengths, owners, qkv, out_weight, inputs, gains, gate_up, down, cotangent,
        out, mixed, full, low, down_pieces,
        normed, first, pieces, gate_up_v, down_v, cotangent_v, load_sem, line_send, line_recv, *sems
    ):
        near, core, tp = spots()
        outer = lax.axis_index("outer")
        begin_tp, begin_near, middle, middle_rest, later, finish = plan_gather(
            normed, out, *sems[:3], cut=cut, apart=True
        )
        team = plan_exchange(first, full.at[outer], *sems[3:6])
        others = plan_exchange(pieces, mixed, *sems[6:9])
        push, take, settle = plan_line(full, line_send, line_recv, outer_count)
        fetch = [
            pltpu.make_async_copy(source, target, load_sem.at[place])
            for place, (source, target) in enumerate(
                ((cotangent, cotangent_v), (gate_up, gate_up_v), (down, down_v))
            )
        ]
        for copy in fetch:
            copy.start()
        gain = wide_gain(gains, 0, width)

        def prepare(at):
            value = inputs[at].astype(jnp.float32)
            normed[at] = (value * rms_scale(value) * gain).astype(jnp.bfloat16)

        def work():
            for member, across, inside in spans(widths):
                first[member, :, inside] = qkv[:, across].astype(jnp.bfloat16)
            for member in range(TEAM):
                at = pl.ds(member * (tall // TEAM), tall // TEAM)
                first[member, :, wide // TEAM :] = out_weight[at].astype(jnp.bfloat16).T
            row_loop(0, rows, prepare)

        greet_all(EVERYONE_NEAR, outer_count, work)
        for copy in team:
            copy.start()
        begin_tp()
        team[0].wait()
        team[3].wait()
        push(0, 0)
        fetch[1].wait()
        for member, across, inside in spans((units, units)):
            pieces[member, :, inside] = gate_up_v[:, across].astype(jnp.bfloat16)
        for copy in team[1:3]:
            copy.wait()
        push(0, 1)
        begin_near()
        take(0)
        length = sequence_length(lengths, owners, outer * TEAM + near * CORE + core)
        fetch[0].wait()

        def mask(at):
            row = lax.broadcasted_iota(jnp.int32, (CHUNK, width), 0) + at.start + tp * rows
            value = jnp.where(row < length, cotangent_v[at].astype(jnp.float32), 0.0)
            low[at] = value.astype(jnp.bfloat16)

        row_loop(0, rows, mask)
        fetch[2].wait()
        for member in range(TEAM):
            at = pl.ds(member * (units // TEAM), units // TEAM)
            down_pieces[member] = down_v[at].astype(jnp.bfloat16).T
        middle()
        if outer_count > 2:
            take(1)
        middle_rest()
        for copy in others:
            copy.start()
        later()
        for step in range(2, outer_count - 1):
            take(step)
        finish()
        settle()
        for copy in others:
            copy.wait()

    scalars = pl.BlockSpec(memory_space=pltpu.SMEM)
    outs = pl.pallas_call(
        kernel,
        name="opening",
        out_shape=(
            layer_rows(rows, width),
            gate_up_shape,
            jax.ShapeDtypeStruct((outer_count,) + first_shape.shape, jnp.bfloat16),
            jax.ShapeDtypeStruct((rows, width), jnp.bfloat16),
            down_shape,
        ),
        in_specs=[scalars] * 2 + [in_vmem()] * 4 + [anywhere()] * 3,
        out_specs=(anywhere(),) * 3 + (in_vmem(),) * 2,
        scratch_shapes=[
            pltpu.VMEM((rows, width), jnp.bfloat16),
            pltpu.VMEM(first_shape.shape, jnp.bfloat16),
            pltpu.VMEM(gate_up_shape.shape, jnp.bfloat16),
            pltpu.VMEM(gate_up.shape, gate_up.dtype),
            pltpu.VMEM(down.shape, down.dtype),
            pltpu.VMEM(cotangent.shape, cotangent.dtype),
            pltpu.SemaphoreType.DMA((3,)),
            pltpu.SemaphoreType.DMA((2, outer_count, 2)),
            pltpu.SemaphoreType.DMA((2, outer_count, 2)),
        ]
        + gather_scratch()
        + exchange_scratch() * 2,
        compiler_params=params(number),
        cost_estimate=cost_of(60),
    )(
        lengths,
        owners,
        qkv,
        out_weight,
        inputs,
        gains,
        gate_up,
        down,
        cotangent,
    )
    gathered, mixed, full, low, down_pieces = outs
    return (
        gathered.reshape(-1, width),
        mixed,
        full.reshape(-1, first_shape.shape[2]),
        low,
        down_pieces,
    )


def spread(part, rows):
    return part.reshape(NEAR, CORE, 2, rows, part.shape[-1])


def read(ref, at):
    return ref[at].astype(jnp.float32)


def branch_and_norm(part, residual, gains, number, name):
    rows, width = residual.shape
    cut = rows // 2

    def kernel(part, residual, gains, hidden, out, *scratch):
        gain = wide_gain(gains, 1, width)
        normed, sems = scratch[SUM_SCRATCH], scratch[SUM_SCRATCH + 1 :]
        steps, from_tp, from_near = plan_sum_of(part, hidden, scratch[:SUM_SCRATCH], cut)
        onward = plan_gather(normed, out, *sems, cut=cut)
        greet(NEIGHBOURS)
        for step in steps[:3]:
            step()

        def finish(at):
            value = hidden[at] + read(from_tp, at) + read(from_near, at)
            value = read(residual, at) + value
            hidden[at] = value
            normed[at] = (value * rms_scale(value) * gain).astype(jnp.bfloat16)

        steps[3](finish)
        for step in onward:
            step()

    hidden, full = pl.pallas_call(
        kernel,
        name=name,
        out_shape=(jax.ShapeDtypeStruct((rows, width), jnp.float32), layer_rows(rows, width)),
        in_specs=[anywhere(), in_vmem(), in_vmem()],
        out_specs=(in_vmem(), anywhere()),
        scratch_shapes=sum_scratch(rows, width, cut)
        + [pltpu.VMEM((rows, width), jnp.bfloat16)]
        + gather_scratch(),
        compiler_params=params(number),
        cost_estimate=cost_of(95),
    )(spread(part, rows), residual, gains)
    return hidden, full.reshape(-1, width)


def norm_back(value, gain, grad):
    scale = rms_scale(value)
    scaled = grad * gain
    inner = jnp.mean(scaled * value, axis=-1, keepdims=True)
    return scale * scaled - value * (scale * scale * scale * inner), grad * value * scale


def sequence_order():
    near, core, _ = spots()
    return [
        (near if place >= 2 else 1 - near) * CORE + (core if place % 2 else 1 - core)
        for place in range(TEAM)
    ]


def times_turned(left, weights, target):
    for start in range(0, weights.shape[0], 512):
        at = pl.ds(start, 512)
        target[:, at] = lax.dot_general(
            left, weights[at, :], (((1,), (1,)), ((), ())), preferred_element_type=jnp.float32
        ).astype(target.dtype)


def feed_back_rest(
    grad_gate, grad_up, weights, active, down, normed, values, upstream, gains, outer_count, number, name
):
    rows, width = values.shape
    count, both_rows, units = grad_gate.shape
    all_rows = count * both_rows
    past = all_rows - width
    cut = rows // 2
    split, share = team_split(width, outer_count)
    turns = width // 512

    def kernel(
        gate, ups, weights, active, down, normed, values, upstream, gains,
        result, gain_grad, low, branch, grad_weight, *scratch
    ):
        (grad_v, weights_v, active_v, down_v, values_v, upstream_v, parts, total), rest = (
            scratch[:8],
            scratch[8:],
        )
        (shares, staged, load_sem, store_sem, chunk_sem, piece_sem), sums = rest[:6], rest[6:]
        from_tp, from_near = sums[3], sums[4]
        gain = wide_gain(gains, 1, width)
        near, core, tp = spots()
        members = sequence_order()
        outgoing = [parts.at[place, half] for place, half in ((0, 1 - tp), (2, 1 - tp), (0, tp), (2, tp))]
        mine = [parts.at[place, half] for place, half in ((1, 1 - tp), (3, 1 - tp), (1, tp), (3, tp))]
        steps, (send_far, send_tp, send_near) = plan_sum(outgoing, mine, (), total, sums, cut)
        stores = [
            pltpu.make_async_copy(shares.at[place % 2], branch.at[place], store_sem.at[place])
            for place in range(count)
        ]
        fetch = [
            pltpu.make_async_copy(source, target, load_sem.at[place])
            for place, (source, target) in enumerate(
                (
                    (weights, weights_v),
                    (values, values_v),
                    (upstream, upstream_v),
                    (active, active_v),
                    (down, down_v),
                    (ups, active_v),
                )
            )
        ]
        grads = []
        for place, member in enumerate(members):
            for side, source in enumerate((gate, ups)):
                grads.append(
                    pltpu.make_async_copy(
                        source.at[member],
                        grad_v.at[place % 2, :, :, pl.ds(side * units, units)],
                        load_sem.at[6 + 2 * place + side],
                    )
                )

        def bring(place):
            grads[2 * place].start()
            grads[2 * place + 1].start()

        def brought(place):
            grads[2 * place].wait()
            grads[2 * place + 1].wait()

        def back(place, half):
            times_turned(grad_v[place % 2, half], weights_v, parts.at[place, half])

        def chunk(turn):
            at, slot = pl.ds(turn * 512, 512), turn % 2
            return [
                pltpu.make_async_copy(
                    normed.at[pl.ds(0, width), at],
                    weights_v.at[:, pl.ds(slot * 1024, 512)],
                    chunk_sem.at[slot, 0],
                ),
                pltpu.make_async_copy(
                    normed.at[pl.ds(width, past), at],
                    weights_v.at[pl.ds(slot * past, past), pl.ds(512, 512)],
                    chunk_sem.at[slot, 1],
                ),
            ]

        def pieces(turn):
            slot = turn % 2
            return [
                pltpu.make_async_copy(
                    staged.at[slot, :, pl.ds(place * share, share)],
                    grad_weight.at[turn * (512 // share) + place],
                    piece_sem.at[slot, place],
                )
                for place in range(512 // share)
            ]

        fetch[0].start()
        bring(0)
        bring(1)
        greet(NEIGHBOURS)
        fetch[0].wait()
        brought(0)
        back(0, 1 - tp)
        steps[0]((0,))
        brought(1)
        back(1, 1 - tp)
        send_far()
        back(0, tp)
        steps[0]((2,))
        bring(2)
        for place in (3, 4, 1, 2):
            fetch[place].start()
        back(1, tp)
        send_near()
        bring(3)
        brought(2)
        back(2, 1 - tp)
        steps[0]((1,))
        brought(3)
        back(3, 1 - tp)
        send_tp()
        back(2, tp)
        steps[0]((3,))
        back(3, tp)
        for turn in (0, 1):
            for copy in chunk(turn):
                copy.start()
        fetch[3].wait()
        fetch[4].wait()
        for place in range(count):
            if place >= 2:
                stores[place - 2].wait()
            for half in range(2):
                times_turned(active_v[place, half], down_v, shares.at[place % 2, half])
            stores[place].start()
        fetch[5].start()
        steps[2]()
        fetch[5].wait()
        for turn in range(turns):
            slot = turn % 2
            for copy in chunk(turn):
                copy.wait()
            left = active_v[...].reshape(all_rows, units)
            product = lax.dot_general(
                left[:width],
                weights_v[:, slot * 1024 : slot * 1024 + 512],
                (((0,), (0,)), ((), ())),
                preferred_element_type=jnp.float32,
            ) + lax.dot_general(
                left[width:],
                weights_v[slot * past : (slot + 1) * past, 512:1024],
                (((0,), (0,)), ((), ())),
                preferred_element_type=jnp.float32,
            )
            if turn >= 2:
                for copy in pieces(turn - 2):
                    copy.wait()
            staged[slot] = product.astype(staged.dtype)
            for copy in pieces(turn):
                copy.start()
            if turn + 2 < turns:
                for copy in chunk(turn + 2):
                    copy.start()
        fetch[1].wait()
        fetch[2].wait()
        gain_grad[...] = jnp.zeros_like(gain_grad)

        def finish(at):
            grad = total[at] + read(from_tp, at) + read(from_near, at)
            turned, by_gain = norm_back(values_v[at], gain, grad)
            gain_grad[...] += by_gain.reshape(CHUNK // 8, 8, width).sum(axis=0)
            value = read(upstream_v, at) + turned
            total[at] = value
            low[at] = value.astype(jnp.bfloat16)

        steps[3](finish)
        store = pltpu.make_async_copy(total, result, store_sem.at[count])
        store.start()
        for turn in range(max(0, turns - 2), turns):
            for copy in pieces(turn):
                copy.wait()
        for copy in [store] + stores[2:]:
            copy.wait()

    low_type = jnp.bfloat16
    halves = (count, 2, rows, units)
    result, gain_grad, rounded, branch, grad_weight = pl.pallas_call(
        kernel,
        name=name,
        out_shape=(
            jax.ShapeDtypeStruct((rows, width), jnp.float32),
            jax.ShapeDtypeStruct((8, width), jnp.float32),
            jax.ShapeDtypeStruct((rows, width), low_type),
            jax.ShapeDtypeStruct((count, 2, rows, width), low_type),
            jax.ShapeDtypeStruct((outer_count * split, units, share), low_type),
        ),
        in_specs=[anywhere()] * 8 + [in_vmem()],
        out_specs=(anywhere(), in_vmem(), in_vmem(), anywhere(), anywhere()),
        scratch_shapes=[
            pltpu.VMEM((2, 2, rows, 2 * units), low_type),
            pltpu.VMEM(weights.shape, low_type),
            pltpu.VMEM(halves, low_type),
            pltpu.VMEM(down.shape, low_type),
            pltpu.VMEM((rows, width), values.dtype),
            pltpu.VMEM((rows, width), upstream.dtype),
            pltpu.VMEM((count, 2, rows, width), low_type),
            pltpu.VMEM((rows, width), jnp.float32),
            pltpu.VMEM((2, 2, rows, width), low_type),
            pltpu.VMEM((2, units, 512), low_type),
            pltpu.SemaphoreType.DMA((6 + 2 * count,)),
            pltpu.SemaphoreType.DMA((count + 1,)),
            pltpu.SemaphoreType.DMA((2, 2)),
            pltpu.SemaphoreType.DMA((2, 512 // share)),
        ]
        + sum_scratch(rows, width, cut, fetched=False),
        compiler_params=params(number),
        cost_estimate=cost_of(60),
    )(
        grad_gate.reshape(halves),
        grad_up.reshape(halves),
        weights,
        active.reshape(halves),
        down,
        normed,
        values,
        upstream,
        gains,
    )
    return result, gain_grad, rounded, branch.reshape(-1, width), grad_weight


def square_sum(values):
    values = values.reshape(-1, values.shape[-1]).astype(jnp.float32)
    return jnp.sum(values * values, keepdims=True)


def corner(value):
    row = lax.broadcasted_iota(jnp.int32, (8, HD), 0)
    column = lax.broadcasted_iota(jnp.int32, (8, HD), 1)
    return jnp.where((row == 0) & (column == 0), value, 0.0)


def norm_back_last(part, values, upstream, gains, extra, squared, number, name):
    rows, width = values.shape
    extras, count = len(extra), len(squared)
    cut = balanced(rows, crossing(extra, width))

    def kernel(part, values, upstream, gains, *rest):
        gain = wide_gain(gains, 0, width)
        pieces, rest = rest[:extras], rest[extras:]
        squared, (result, gain_grad, squares), rest = (
            rest[:count],
            rest[count : count + 3],
            rest[count + 3 :],
        )
        mixed, rest = rest[:extras], rest[extras:]
        sums, rest = rest[:SUM_SCRATCH], rest[SUM_SCRATCH:]
        (total, values_v, upstream_v, load_sem), rest = rest[:4], rest[4:]
        squared_v, sems = rest[:count], rest[count:]
        steps, from_tp, from_near = plan_sum_of(part, total, sums, cut)
        copies = plan_exchanges(pieces, mixed, sems)
        fetch = [
            pltpu.make_async_copy(source, target, load_sem.at[place])
            for place, (source, target) in enumerate(
                zip((values, upstream) + tuple(squared), (values_v, upstream_v) + tuple(squared_v))
            )
        ]
        greet(EVERYONE_NEAR)
        steps[0]()
        for copy in copies:
            copy.start()
        for copy in fetch:
            copy.start()
        steps[1]()
        for copy in fetch:
            copy.wait()
        squares[...] = corner(sum(square_sum(ref[...]) for ref in squared_v))
        steps[2]()
        gain_grad[...] = jnp.zeros_like(gain_grad)

        def finish(at):
            grad = total[at] + read(from_tp, at) + read(from_near, at)
            back, by_gain = norm_back(read(values_v, at), gain, grad)
            gain_grad[...] += by_gain.reshape(CHUNK // 8, 8, width).sum(axis=0)
            result[at] = (upstream_v[at] + back).astype(jnp.bfloat16)

        steps[3](finish)
        for copy in copies:
            copy.wait()

    return pl.pallas_call(
        kernel,
        name=name,
        out_shape=(
            jax.ShapeDtypeStruct((rows, width), jnp.bfloat16),
            jax.ShapeDtypeStruct((8, width), jnp.float32),
            jax.ShapeDtypeStruct((8, HD), jnp.float32),
        )
        + tuple(like(piece) for piece in extra),
        in_specs=[anywhere()] * 3 + [in_vmem()] * (1 + extras) + [anywhere()] * count,
        out_specs=(in_vmem(), in_vmem(), in_vmem()) + (anywhere(),) * extras,
        scratch_shapes=sum_scratch(rows, width, cut)
        + [
            pltpu.VMEM((rows, width), jnp.float32),
            pltpu.VMEM((rows, width), values.dtype),
            pltpu.VMEM((rows, width), upstream.dtype),
            pltpu.SemaphoreType.DMA((2 + count,)),
        ]
        + [pltpu.VMEM(each.shape, each.dtype) for each in squared]
        + exchange_scratch() * extras,
        compiler_params=params(number),
        cost_estimate=cost_of(65),
    )(spread(part, rows), values, upstream, gains, *extra, *squared)


def total_everywhere(first, second, heads, squares, pieces, outer_count, number, name):
    used = 2 * first.shape[1] // HD + heads.shape[0]
    gains = used + -used % 8
    shape = (gains + 8, HD)
    width = first.shape[1]

    def kernel(first, second, heads, squares, pieces, out, norm, factor, mixed, layer, outers, send, recv, *sems):
        near, core, tp = spots()
        outer = lax.axis_index("outer")
        partners = [
            flipped(a, b, c)
            for a in range(NEAR)
            for b in range(CORE)
            for c in range(2)
            if a + b + c
        ]
        partners += [{"outer": (outer + step) % outer_count} for step in range(1, outer_count)]
        barrier = pltpu.get_barrier_semaphore()
        for partner in partners:
            pl.semaphore_signal(barrier, inc=1, device_id=partner, device_id_type=MESH_ID)
        mine = near * (CORE * 2) + core * 2 + tp
        layer[mine, gains - 8 : gains] = jnp.zeros((8, HD), jnp.float32)
        layer[mine, gains:] = squares[...] + corner(square_sum(pieces[...]))
        place = 0
        for source in (first, second):
            sums = jnp.sum(source[...], axis=0, keepdims=True)
            for start in range(0, width, HD):
                layer[mine, place : place + 1] = sums[:, start : start + HD]
                place += 1
        for head in range(heads.shape[0]):
            layer[mine, place : place + 1] = jnp.sum(heads[head], axis=0, keepdims=True)
            place += 1
        pl.semaphore_wait(barrier, len(partners))

        def share(slots, mine, first, count):
            copies = []
            for number in range(first, first + count):
                copy = pltpu.make_async_remote_copy(
                    src_ref=slots.at[mine],
                    dst_ref=slots.at[mine],
                    send_sem=send.at[number],
                    recv_sem=recv.at[number],
                    device_id=partners[number],
                    device_id_type=MESH_ID,
                )
                copy.start()
                copies.append(copy)
            return copies

        others = plan_exchange(pieces, mixed, *sems)
        copies = share(layer, mine, 0, 7)
        for copy in others:
            copy.start()
        for copy in copies:
            copy.wait()
        total = layer[0]
        for slot in range(1, 8):
            total = total + layer[slot]
        outers[outer] = total
        for copy in share(outers, outer, 7, outer_count - 1):
            copy.wait()
        total = outers[0]
        for slot in range(1, outer_count):
            total = total + outers[slot]
        out[...] = total
        gain_part = total[:gains]
        root = jnp.sqrt(
            jnp.sum(gain_part * gain_part, keepdims=True) + jnp.sum(total[gains:], keepdims=True)
        )
        norm[...] = root
        factor[...] = jnp.broadcast_to(
            jnp.minimum(1.0, clip_norm / (root + 1e-06)), factor.shape
        )
        for copy in others:
            copy.wait()

    tile = jax.ShapeDtypeStruct((8, HD), jnp.float32)
    return pl.pallas_call(
        kernel,
        name=name,
        out_shape=(
            jax.ShapeDtypeStruct(shape, jnp.float32),
            jax.ShapeDtypeStruct((1, 1), jnp.float32),
            tile,
            like(pieces),
        ),
        in_specs=[in_vmem()] * 5,
        out_specs=(in_vmem(), in_vmem(), in_vmem(), anywhere()),
        scratch_shapes=[
            pltpu.VMEM((8,) + shape, jnp.float32),
            pltpu.VMEM((outer_count,) + shape, jnp.float32),
            pltpu.SemaphoreType.DMA((6 + outer_count,)),
            pltpu.SemaphoreType.DMA((6 + outer_count,)),
        ]
        + exchange_scratch(),
        compiler_params=params(number),
        cost_estimate=cost_of(16),
    )(first, second, heads, squares, pieces)


def head_scale(raw, gain, cos_full, sin_full):
    normed = raw * rms_scale(raw) * gain
    return (normed * cos_full + pltpu.roll(normed, HD // 2, 1) * sin_full).astype(jnp.bfloat16)


def head_back(raw, gain, grad, cos_full, sin_full):
    grad = grad * cos_full - pltpu.roll(grad, HD // 2, 1) * sin_full
    return norm_back(raw, gain, grad)


def columns(index):
    return pl.ds(index * HD, HD)


def head_inputs(proj, gains, cos_ref, sin_ref, queries, keys, values, heads):
    for head in range(heads):
        queries[head] = head_scale(
            proj[0, :, columns(head)], gains[HEAD_GAINS : HEAD_GAINS + 1, :], cos_ref[...], sin_ref[...]
        )
    keys[...] = head_scale(
        proj[0, :, columns(heads)], gains[HEAD_GAINS + 1 : HEAD_GAINS + 2, :], cos_ref[...], sin_ref[...]
    )
    values[...] = proj[0, :, columns(heads + 1)].astype(jnp.bfloat16)


def masked_scores(stacked, keys, step, length):
    scores = lax.dot_general(
        stacked, keys, (((1,), (1,)), ((), ())), preferred_element_type=jnp.float32
    ) * (HD ** (-0.5))
    row = lax.broadcasted_iota(jnp.int32, scores.shape, 0) % BLOCK + step * BLOCK
    column = lax.broadcasted_iota(jnp.int32, scores.shape, 1)
    return jnp.where((column <= row) & (column < length), scores, masked_score)


def stack_heads(ref, at, heads):
    return jnp.concatenate([ref[head, at] for head in range(heads)], axis=0)


def per_sequence(*shape):
    return pl.BlockSpec((1,) + shape, lambda s: (s,) + (0,) * len(shape))


def whole(*shape):
    return pl.BlockSpec(shape, lambda s: (0,) * len(shape), pipeline_mode=pl.Buffered(1))


def across_columns(left, weights, first, width, out):
    total = weights.shape[0]
    for start in range(0, total, 512):
        at = pl.ds(start, 512)
        out[0, :, at] = lax.dot_general(
            left,
            weights[at, first : first + width],
            (((1,), (1,)), ((), ())),
            preferred_element_type=jnp.float32,
        ).astype(out.dtype)


def attend(normed, weights, cotangent, extra, lengths, owners, cos_full, sin_full, gains, heads, early, number):
    count, rows, width = normed.shape
    wide = (heads + 2) * HD
    extras = len(extra)
    own_rows = cotangent.shape[0]
    cut = balanced(early, crossing(extra, width))

    def kernel(lengths, owners, normed, weights_any, cos_ref, sin_ref, gains, own, *rest):
        pieces, rest = rest[:extras], rest[extras:]
        (proj, out, logs, branch, gathered), rest = rest[:5], rest[5:]
        mixed, rest = rest[:extras], rest[extras:]
        (queries, keys, values, weights, weights_sem), sems = rest[:5], rest[5:]
        fetch = pltpu.make_async_copy(weights_any, weights, weights_sem)
        sequence = pl.program_id(0)
        steps = plan_gather(own, gathered, *sems[:3], cut=cut, rows=early)
        copies = plan_exchanges(pieces, mixed, sems[3:])

        @pl.when(sequence == 0)
        def _():
            fetch.start()
            greet(EVERYONE_NEAR)
            steps[0]()
            fetch.wait()

        group = lax.axis_index("outer") * TEAM + sequence
        length = sequence_length(lengths, owners, group)
        proj[0] = jnp.dot(
            normed[0], weights[:, :wide], preferred_element_type=jnp.float32
        )
        head_inputs(proj, gains, cos_ref, sin_ref, queries, keys, values, heads)
        lane = lax.broadcasted_iota(jnp.int32, (BLOCK, HD), 1)
        for step in range(rows // BLOCK):
            at = pl.ds(step * BLOCK, BLOCK)
            seen = pl.ds(0, (step + 1) * BLOCK)
            scores = masked_scores(stack_heads(queries, at, heads), keys[seen], step, length)
            top = jnp.max(scores, axis=-1, keepdims=True)
            exponent = jnp.exp(scores - top)
            total = jnp.sum(exponent, axis=-1, keepdims=True)
            probs = (exponent / total).astype(jnp.bfloat16)
            mixed_values = jnp.dot(probs, values[seen], preferred_element_type=jnp.float32)
            log_total = top + jnp.log(total)
            kept = jnp.zeros((BLOCK, HD), jnp.float32)
            for head in range(heads):
                mine = slice(head * BLOCK, (head + 1) * BLOCK)
                out[0, at, columns(head)] = mixed_values[mine].astype(jnp.bfloat16)
                kept = jnp.where(lane == head, log_total[mine], kept)
            logs[0, at] = kept
        across_columns(out[0], weights, wide, heads * HD, branch)

        @pl.when(sequence == 1)
        def _():
            steps[1]()
            for copy in copies:
                copy.start()

        @pl.when(sequence == 2)
        def _():
            steps[2]()

        @pl.when(sequence == count - 1)
        def _():
            steps[3]()
            for copy in copies:
                copy.wait()

    outs = pl.pallas_call(
        kernel,
        name="attend",
        grid=(count,),
        out_shape=(
            jax.ShapeDtypeStruct((count, rows, wide), jnp.float32),
            jax.ShapeDtypeStruct((count, rows, heads * HD), jnp.bfloat16),
            jax.ShapeDtypeStruct((count, rows, HD), jnp.float32),
            jax.ShapeDtypeStruct((count, rows, width), jnp.bfloat16),
            layer_rows(own_rows, width),
        )
        + tuple(like(piece) for piece in extra),
        in_specs=[
            pl.BlockSpec(memory_space=pltpu.SMEM),
            pl.BlockSpec(memory_space=pltpu.SMEM),
            per_sequence(rows, width),
            anywhere(),
            whole(rows, HD),
            whole(rows, HD),
            whole(*gains.shape),
            whole(own_rows, width),
        ]
        + [whole(*piece.shape) for piece in extra],
        out_specs=(
            per_sequence(rows, wide),
            per_sequence(rows, heads * HD),
            per_sequence(rows, HD),
            per_sequence(rows, width),
            anywhere(),
        )
        + (anywhere(),) * extras,
        scratch_shapes=[
            pltpu.VMEM((heads, rows, HD), jnp.bfloat16),
            pltpu.VMEM((rows, HD), jnp.bfloat16),
            pltpu.VMEM((rows, HD), jnp.bfloat16),
            pltpu.VMEM(weights.shape, weights.dtype),
            pltpu.SemaphoreType.DMA,
        ]
        + gather_scratch()
        + exchange_scratch() * extras,
        compiler_params=params(number),
        cost_estimate=cost_of(50),
    )(lengths, owners, normed, weights, cos_full, sin_full, gains, cotangent, *extra)
    return outs


def team_split(width, outer_count):
    split = TEAM if width // outer_count % (TEAM * HD) == 0 else 1
    return split, width // outer_count // split


def local_first(place):
    near, core, _ = spots()
    other_near, other_core = place // 2, place % 2
    return (near + other_near * (1 - 2 * near)) * CORE + core + other_core * (1 - 2 * core)


def ordered(*shape):
    return pl.BlockSpec((1,) + shape, lambda s: (local_first(s),) + (0,) * len(shape))


def attend_back(
    projected,
    normed,
    attended,
    own_grad,
    logs,
    weights,
    part,
    hidden,
    extra,
    outer_count,
    lengths,
    owners,
    cos_full,
    sin_full,
    gains,
    heads,
    number,
):
    count, rows, wide = projected.shape
    own_rows, width = hidden.shape
    extras = len(extra)
    cut = balanced(own_rows, crossing(extra, width))

    every = wide + heads * HD
    split, share = team_split(width, outer_count)

    def kernel(
        lengths, owners, proj, normed, attended, own_grad, logs, weights_any, cos_ref, sin_ref, gains, part, hidden, *rest
    ):
        pieces, rest = rest[:extras], rest[extras:]
        (gathered, gain_grad, back_part, output, grad_weights), rest = rest[:5], rest[5:]
        mixed, rest = rest[:extras], rest[extras:]
        (queries, keys, values, grad_att, grad_q, grad_k, grad_v_sum, summed), rest = rest[:8], rest[8:]
        (total, held, held_sem, out, grad_v, grad_sem), rest = rest[:6], rest[6:]
        (weights, staged, weights_sem, store_sem), rest = rest[:4], rest[4:]
        sums, sems, rest = rest[:SUM_SCRATCH], rest[SUM_SCRATCH : SUM_SCRATCH + 3], rest[SUM_SCRATCH + 3 :]
        place = pl.program_id(0)
        sequence = local_first(place)
        steps, from_tp, from_near = plan_sum_of(part, total, sums, cut)
        gather = plan_gather(own_grad, gathered, *sems, cut=own_rows // 2, parts=True)
        copies = plan_exchanges(pieces, mixed, rest)
        fetch_weights = pltpu.make_async_copy(weights_any, weights, weights_sem)
        store = pltpu.make_async_copy(staged, grad_weights, store_sem)

        def arrival(which):
            member = local_first(which)
            return pltpu.make_async_copy(
                gathered.at[member // CORE, member % CORE],
                grad_v.at[which % 2],
                grad_sem.at[which % 2],
            )

        fetch = pltpu.make_async_copy(hidden, held, held_sem)

        @pl.when(place == 0)
        def _():
            greet(EVERYONE_NEAR)
            gather[0]()
            steps[0]()
            fetch.start()
            fetch_weights.start()
            gain_grad[...] = jnp.zeros_like(gain_grad)
            summed[...] = jnp.zeros_like(summed)
            gather[1]()
            gather[2]()
            gather[3]()
            arrival(0).start()
            fetch_weights.wait()

        @pl.when(place == 2)
        def _():
            arrival(3).start()

        head_inputs(proj, gains, cos_ref, sin_ref, queries, keys, values, heads)
        grad_k[...] = jnp.zeros_like(grad_k)
        grad_v_sum[...] = jnp.zeros_like(grad_v_sum)
        arrival(place).wait()
        grad = grad_v[place % 2].reshape(rows, width)
        group = lax.axis_index("outer") * TEAM + sequence
        length = sequence_length(lengths, owners, group)
        grad_att[...] = jnp.dot(
            grad, weights[:, wide:], preferred_element_type=jnp.float32
        ).astype(jnp.bfloat16)

        for step in range(rows // BLOCK):
            at = pl.ds(step * BLOCK, BLOCK)
            seen = pl.ds(0, (step + 1) * BLOCK)
            stacked = stack_heads(queries, at, heads)
            above = jnp.concatenate([grad_att[at, columns(head)] for head in range(heads)], axis=0)
            log_total = jnp.concatenate(
                [logs[0, at, head : head + 1] for head in range(heads)], axis=0
            )
            probs = jnp.exp(masked_scores(stacked, keys[seen], step, length) - log_total)
            grad_probs = lax.dot_general(
                above, values[seen], (((1,), (1,)), ((), ())), preferred_element_type=jnp.float32
            )
            inner = jnp.sum(probs * grad_probs, axis=-1, keepdims=True)
            grad_scores = (probs * (grad_probs - inner)).astype(jnp.bfloat16)
            by_query = jnp.dot(grad_scores, keys[seen], preferred_element_type=jnp.float32)
            for head in range(heads):
                grad_q[head, at] = by_query[head * BLOCK : (head + 1) * BLOCK] * (HD ** (-0.5))
            grad_k[seen] += lax.dot_general(
                grad_scores, stacked, (((0,), (0,)), ((), ())), preferred_element_type=jnp.float32
            )
            grad_v_sum[seen] += lax.dot_general(
                probs.astype(jnp.bfloat16),
                above,
                (((0,), (0,)), ((), ())),
                preferred_element_type=jnp.float32,
            )

        def settle(column, gain, value):
            back, by_gain = head_back(
                proj[0, :, columns(column)], gains[HEAD_GAINS + gain : HEAD_GAINS + gain + 1, :], value, cos_ref[...], sin_ref[...]
            )
            out[:, columns(column)] = back.astype(jnp.bfloat16)
            gain_grad[gain] += by_gain.reshape(rows // 8, 8, HD).sum(axis=0)

        for head in range(heads):
            settle(head, 0, grad_q[head])
        settle(heads, 1, grad_k[...] * (HD ** (-0.5)))
        out[:, columns(heads + 1)] = grad_v_sum[...].astype(jnp.bfloat16)

        across_columns(out[...], weights, 0, wide, back_part)

        by_projected, by_attended = out[...].T, attended[0].T
        for start in range(0, width, 512):
            at = pl.ds(start, 512)
            summed[:wide, at] += jnp.dot(
                by_projected, normed[0, :, at], preferred_element_type=jnp.float32
            )
            summed[wide:, at] += jnp.dot(
                by_attended, grad[:, start : start + 512], preferred_element_type=jnp.float32
            )

        @pl.when(place == 0)
        def _():
            gather[5]()
            steps[1]()
            gather[4]()
            arrival(1).start()

        @pl.when(place == 1)
        def _():
            steps[2]()
            for copy in copies:
                copy.start()
            gather[6]()
            arrival(2).start()

        @pl.when(place == count - 1)
        def _():
            for outer in range(outer_count):
                for member in range(split):
                    start = (outer * split + member) * share
                    staged[outer, member] = summed[:, start : start + share].astype(jnp.bfloat16)
            store.start()
            fetch.wait()

            def finish(at):
                value = total[at] + read(from_tp, at) + read(from_near, at)
                output[at] = (held[at] + value).astype(jnp.bfloat16)

            steps[3](finish)
            store.wait()
            for copy in copies:
                copy.wait()

    return pl.pallas_call(
        kernel,
        name="attend_back",
        grid=(count,),
        out_shape=(
            layer_rows(own_rows, width),
            jax.ShapeDtypeStruct((2, 8, HD), jnp.float32),
            jax.ShapeDtypeStruct((count, rows, width), jnp.bfloat16),
            jax.ShapeDtypeStruct((own_rows, width), jnp.bfloat16),
            jax.ShapeDtypeStruct((outer_count, split, every, share), jnp.bfloat16),
        )
        + tuple(like(piece) for piece in extra),
        in_specs=[
            pl.BlockSpec(memory_space=pltpu.SMEM),
            pl.BlockSpec(memory_space=pltpu.SMEM),
            ordered(rows, wide),
            ordered(rows, width),
            ordered(rows, heads * HD),
            whole(own_rows, width),
            ordered(rows, HD),
            anywhere(),
            whole(rows, HD),
            whole(rows, HD),
            whole(*gains.shape),
            anywhere(),
            anywhere(),
        ]
        + [whole(*piece.shape) for piece in extra],
        out_specs=(
            anywhere(),
            pl.BlockSpec((2, 8, HD), lambda s: (0, 0, 0)),
            ordered(rows, width),
            whole(own_rows, width),
            anywhere(),
        )
        + (anywhere(),) * extras,
        scratch_shapes=[
            pltpu.VMEM((heads, rows, HD), jnp.bfloat16),
            pltpu.VMEM((rows, HD), jnp.bfloat16),
            pltpu.VMEM((rows, HD), jnp.bfloat16),
            pltpu.VMEM((rows, heads * HD), jnp.bfloat16),
            pltpu.VMEM((heads, rows, HD), jnp.float32),
            pltpu.VMEM((rows, HD), jnp.float32),
            pltpu.VMEM((rows, HD), jnp.float32),
            pltpu.VMEM((every, width), jnp.float32),
            pltpu.VMEM((own_rows, width), jnp.float32),
            pltpu.VMEM((own_rows, width), jnp.float32),
            pltpu.SemaphoreType.DMA,
            pltpu.VMEM((rows, wide), jnp.bfloat16),
            pltpu.VMEM((2, 2, own_rows, width), jnp.bfloat16),
            pltpu.SemaphoreType.DMA((2,)),
            pltpu.VMEM(weights.shape, weights.dtype),
            pltpu.VMEM((outer_count, split, every, share), jnp.bfloat16),
            pltpu.SemaphoreType.DMA,
            pltpu.SemaphoreType.DMA,
        ]
        + sum_scratch(own_rows, width, cut)
        + gather_scratch()
        + exchange_scratch() * extras,
        compiler_params=params(number),
        cost_estimate=cost_of(50),
    )(
        lengths,
        owners,
        projected,
        normed,
        attended,
        own_grad,
        logs,
        weights,
        cos_full,
        sin_full,
        gains,
        spread(part, own_rows),
        hidden,
        *extra,
    )


def feed(normed, weights, cotangent, gathered, early, number):
    count, rows, width = normed.shape
    units = weights.shape[1] // 2
    late = cotangent.shape[0] - early

    def kernel(normed, weights_any, own, _, product, active, out, weights, weights_sem, *sems):
        fetch = pltpu.make_async_copy(weights_any, weights, weights_sem)
        steps = plan_gather(
            own, out, *sems, cut=balanced(late, 0), base=early, rows=late
        )
        sequence = pl.program_id(0)

        @pl.when(sequence == 0)
        def _():
            fetch.start()
            greet(NEIGHBOURS)
            steps[0]()
            fetch.wait()

        for start in range(0, units, 256):
            gate_at, up_at = pl.ds(start, 256), pl.ds(units + start, 256)
            gate = jnp.dot(normed[0], weights[:, gate_at], preferred_element_type=jnp.float32)
            up = jnp.dot(normed[0], weights[:, up_at], preferred_element_type=jnp.float32)
            product[0, :, gate_at] = gate
            product[0, :, up_at] = up
            active[0, :, gate_at] = swish_product(gate, up).astype(jnp.bfloat16)

        for place in (1, 2, 3):

            @pl.when(sequence == count - 4 + place)
            def _(place=place):
                steps[place]()

    return pl.pallas_call(
        kernel,
        name="feed",
        grid=(count,),
        out_shape=(
            jax.ShapeDtypeStruct((count, rows, 2 * units), jnp.float32),
            jax.ShapeDtypeStruct((count, rows, units), jnp.bfloat16),
            like(gathered),
        ),
        in_specs=[
            per_sequence(rows, width),
            anywhere(),
            whole(*cotangent.shape),
            anywhere(),
        ],
        out_specs=(per_sequence(rows, 2 * units), per_sequence(rows, units), anywhere()),
        scratch_shapes=[pltpu.VMEM(weights.shape, weights.dtype), pltpu.SemaphoreType.DMA]
        + gather_scratch(),
        input_output_aliases={3: 2},
        compiler_params=params(number),
        cost_estimate=cost_of(28),
    )(normed, weights, cotangent, gathered)


def feed_back(grads, weights, product, normed, outer_count):
    count, rows, width = grads.shape
    units = weights.shape[1]
    split, share = team_split(width, outer_count)
    turns = width // 512

    def kernel(grads, weights, product, normed, by_gate, by_up, grad_weight, kept):
        step = pl.program_id(0)

        @pl.when(step < count)
        def _():
            for start in range(0, units, 256):
                gate_at, up_at = pl.ds(start, 256), pl.ds(units + start, 256)
                grad = jnp.dot(grads[0], weights[:, gate_at], preferred_element_type=jnp.float32)
                gate, up = product[0, :, gate_at], product[0, :, up_at]
                part = jax.nn.sigmoid(gate)
                slope = grad * up * part * (1.0 + gate * (1.0 - part))
                by_gate[0, :, gate_at] = slope.astype(jnp.bfloat16)
                by_up[0, :, gate_at] = (grad * gate * part).astype(jnp.bfloat16)
            kept[step] = by_gate[0]

        @pl.when(step >= count)
        def _():
            turned = lax.dot_general(
                kept[...].reshape(count * rows, units),
                normed[...],
                (((0,), (0,)), ((), ())),
                preferred_element_type=jnp.float32,
            ).astype(jnp.bfloat16)
            for place in range(512 // share):
                grad_weight[place] = turned[:, place * share : (place + 1) * share]

    def early(*shape):
        return pl.BlockSpec((1,) + shape, lambda s: (jnp.minimum(s, count - 1), 0, 0))

    def late(s):
        return jnp.maximum(s - count, 0)

    return pl.pallas_call(
        kernel,
        name="feed_back",
        grid=(count + turns,),
        out_shape=(jax.ShapeDtypeStruct((count, rows, units), jnp.bfloat16),) * 2
        + (jax.ShapeDtypeStruct((width // share, units, share), jnp.bfloat16),),
        in_specs=[
            early(rows, width),
            whole(*weights.shape),
            early(rows, 2 * units),
            pl.BlockSpec((count * rows, 512), lambda s: (0, late(s))),
        ],
        out_specs=(
            early(rows, units),
            early(rows, units),
            pl.BlockSpec((512 // share, units, share), lambda s: (late(s), 0, 0)),
        ),
        scratch_shapes=[pltpu.VMEM((count, rows, units), jnp.bfloat16)],
        compiler_params=pltpu.CompilerParams(vmem_limit_bytes=VMEM_LIMIT),
        cost_estimate=cost_of(28),
    )(grads, weights, product, normed)


def spans(widths, base=0):
    for member in range(TEAM):
        first, inside = base, 0
        for width in widths:
            share = width // TEAM
            yield member, pl.ds(first + member * share, share), pl.ds(inside, share)
            first += width
            inside += share


def by_turned(height, base, widths, source, members=range(TEAM)):
    parts = [part for part in spans(widths, base) if part[0] in members]

    def run(pieces, update):
        for member, across, inside in parts:
            update(pl.ds(0, height), across, pieces[member, inside].T)

    if len(members) == 1:
        columns = parts[0][1]
    else:
        columns = pl.ds(base, sum(widths))
    return source, pl.ds(0, height), columns, run


def by_rows(member, height, width, inside, source):
    at, across = pl.ds(member * height, height), pl.ds(0, width)

    def run(pieces, update):
        if inside is None:
            update(at, across, pieces[member].T)
        else:
            update(at, across, pieces[member, pl.ds(inside, height)])

    return source, at, across, run


def adam_all(sets, pieces, factor, gain_grad, gains, passed):
    jobs = [(place,) + job for place, group in enumerate(sets) for job in group[3]]
    count, total, sources, others = len(jobs), len(sets), len(pieces), len(passed)

    def kernel(*refs):
        inputs, refs = refs[: 3 * total], refs[3 * total :]
        piece_refs, factor, refs = refs[:sources], refs[sources], refs[sources + 1 :]
        (gain_grad, *gains), refs = refs[:4], refs[4:]
        passed, refs = refs[:others], refs[others:]
        outputs, refs = refs[: 4 * total], refs[4 * total :]
        new_gains, refs = refs[:3], refs[3:]
        onward, refs = refs[:others], refs[others:]
        held, refs = refs[: 4 * total], refs[4 * total :]
        held_pieces, refs = refs[:sources], refs[sources:]
        between, (piece_sem, in_sem, out_sem, pass_sem) = refs[:others], refs[others:]
        scale = factor[0:1, 0:1]
        loads = [
            pltpu.make_async_copy(piece_refs[place], held_pieces[place], piece_sem.at[place])
            for place in range(sources)
        ]
        arrivals, stores = [], []
        kept = [
            pltpu.make_async_copy(source, target, pass_sem.at[0, place])
            for place, (source, target) in enumerate(zip(passed, between))
        ]
        kept_on = [
            pltpu.make_async_copy(source, target, pass_sem.at[1, place])
            for place, (source, target) in enumerate(zip(between, onward))
        ]
        for slot, (place, source, at, across, _) in enumerate(jobs):
            arrivals.append(
                [
                    pltpu.make_async_copy(
                        inputs[3 * place + number].at[at, across],
                        held[4 * place + number].at[at, across],
                        in_sem.at[3 * slot + number],
                    )
                    for number in range(3)
                ]
            )
        first_use = {}
        for slot, job in enumerate(jobs):
            first_use.setdefault(job[1], slot)

        def bring(slot):
            if slot < count:
                if first_use[jobs[slot][1]] == slot:
                    loads[jobs[slot][1]].start()
                for copy in arrivals[slot]:
                    copy.start()

        for slot in range(AHEAD):
            bring(slot)
        gain_step = adam_update(
            gains[0][...],
            gain_grad[: gains[0].shape[0]],
            gains[1][...],
            gains[2][...],
            scale,
            0.0,
            gain_rate,
        )
        for target, value in zip(new_gains, gain_step):
            target[...] = value
        for slot, (place, source, at, across, run) in enumerate(jobs):
            weight, moment, square, low = held[4 * place : 4 * place + 4]
            if first_use[source] == slot:
                loads[source].wait()
            for copy in arrivals[slot]:
                copy.wait()
            bring(slot + AHEAD)
            if slot == 0:
                for copy in kept:
                    copy.start()

            def update(rows, columns, gradient):
                where = (rows, columns)
                value, one, two = adam_update(
                    weight[where],
                    gradient.astype(jnp.float32),
                    moment[where],
                    square[where],
                    scale,
                    weight_decay,
                    learn_rate,
                )
                weight[where], moment[where], square[where] = value, one, two
                low[where] = value.astype(jnp.bfloat16)

            run(held_pieces[source], update)
            for number, origin in enumerate((weight, moment, square, low)):
                copy = pltpu.make_async_copy(
                    origin.at[at, across],
                    outputs[4 * place + number].at[at, across],
                    out_sem.at[4 * slot + number],
                )
                copy.start()
                stores.append(copy)
            if slot == 4:
                for arrived, copy in zip(kept, kept_on):
                    arrived.wait()
                    copy.start()
        for copy in stores + kept_on:
            copy.wait()

    args, shapes, scratch = [], [], []
    for weight, moment, square, _ in sets:
        args += [weight, moment, square]
        low = jax.ShapeDtypeStruct(weight.shape, jnp.bfloat16)
        shapes += [like(weight)] * 3 + [low]
        scratch += [pltpu.VMEM(each.shape, each.dtype) for each in (weight, moment, square, low)]
    outs = pl.pallas_call(
        kernel,
        name="adam_all",
        out_shape=tuple(shapes) + (like(gains[0]),) * 3 + tuple(like(each) for each in passed),
        in_specs=[anywhere()] * (3 * total + sources) + [in_vmem()] * 5 + [anywhere()] * others,
        out_specs=(anywhere(),) * (4 * total) + (in_vmem(),) * 3 + (anywhere(),) * others,
        scratch_shapes=scratch
        + [pltpu.VMEM(each.shape, each.dtype) for each in tuple(pieces) + tuple(passed)]
        + [
            pltpu.SemaphoreType.DMA((sources,)),
            pltpu.SemaphoreType.DMA((3 * count,)),
            pltpu.SemaphoreType.DMA((4 * count,)),
            pltpu.SemaphoreType.DMA((2, others)),
        ],
        compiler_params=pltpu.CompilerParams(vmem_limit_bytes=VMEM_LIMIT),
        cost_estimate=cost_of(15),
    )(*args, *pieces, factor, gain_grad, *gains, *passed)
    steps = [outs[4 * place : 4 * place + 4] for place in range(total)]
    return steps + [outs[4 * total : 4 * total + 3], outs[4 * total + 3 :]]


def rotary(count):
    frequency = rope_base ** (-(np.arange(HD // 2) * 2.0 / HD))
    angles = np.arange(count)[:, None] * frequency[None, :]
    cosine, sine = np.cos(angles), np.sin(angles)
    full = [np.concatenate(pair, axis=1) for pair in ((cosine, cosine), (-sine, sine))]
    return [jnp.asarray(table, jnp.float32) for table in full]


def gather_outer(mixed):
    return lax.all_gather(mixed.reshape(-1, mixed.shape[2]), "outer", axis=0, tiled=True)


def team_pieces(summed):
    return summed.reshape(TEAM, -1, summed.shape[-1])


def turned_pieces(summed):
    if summed.shape[1] * TEAM * lax.axis_size("outer") == D:
        return team_pieces(summed)
    return summed.reshape(summed.shape[0], TEAM, -1).transpose(1, 0, 2)


def sum_weight(gradient):
    return lax.psum_scatter(gradient, "outer", scatter_dimension=0, tiled=True)


def after(values, earlier):
    return lax.optimization_barrier((values, earlier))


def adam_update(weight, gradient, moment_one, moment_two, factor, decay_rate, rate_value):
    clipped = gradient * factor
    moment_one = beta_first * moment_one + (1.0 - beta_first) * clipped
    moment_two = beta_second * moment_two + (1.0 - beta_second) * clipped * clipped
    first_fixed = moment_one * (rate_value / (1.0 - beta_first**STEP))
    root_fixed = jnp.sqrt(moment_two) * (1.0 - beta_second**STEP) ** (-0.5)
    kept = weight * (1.0 - rate_value * decay_rate) if decay_rate else weight
    weight = kept - first_fixed / (root_fixed + adam_epsilon)
    return (weight, moment_one, moment_two)


def dot(left, right, contract):
    return lax.dot_general(
        left, right, ((contract[0], contract[1]), ((), ())), preferred_element_type=jnp.float32
    )


def times(left, right):
    return dot(left, right, ((1,), (0,)))


def times_across(left, right):
    return dot(left, right, ((1,), (1,)))


def over_rows(left, right):
    return dot(left, right, ((0,), (0,)))


def local(
    inputs,
    cotangent,
    lengths,
    owners,
    qkv_weight,
    out_weight,
    gate_up_weight,
    down_weight,
    norm_gains,
    qkv_moment,
    out_moment,
    gate_up_moment,
    down_moment,
    gains_moment,
    qkv_square,
    out_square,
    gate_up_square,
    down_square,
    gains_square,
):
    tp_count = lax.axis_size("tp")
    half_rows = inputs.shape[0]
    row_count = half_rows * tp_count
    heads = H // tp_count // TEAM
    hidden_units = FF // tp_count // TEAM
    qkv_widths = (H * HD // tp_count, KV * HD // tp_count, KV * HD // tp_count)
    out_widths = (H * HD // tp_count,)
    part_rows = qkv_weight.shape[0]
    gate_up_widths = (FF // tp_count, FF // tp_count)
    down_widths = (FF // tp_count,)

    cos_full, sin_full = rotary(row_count)
    gains = norm_gains.reshape(-1, HD)

    normed_attn, gate_up_mixed, first_full, grad_low, down_pieces = opening(
        qkv_weight,
        out_weight,
        gate_up_weight,
        down_weight,
        inputs,
        gains,
        cotangent,
        lengths,
        owners,
        lax.axis_size("outer"),
        0,
    )
    gate_up_full = gather_outer(gate_up_mixed)
    early = half_rows // 2 // CHUNK * CHUNK
    projected, attended, logs, attn_branch, grad_all, down_mixed = attend(
        normed_attn.reshape(TEAM, row_count, D),
        first_full,
        grad_low,
        (down_pieces,),
        lengths,
        owners,
        cos_full,
        sin_full,
        gains,
        heads,
        early,
        1,
    )
    down_full = gather_outer(down_mixed)
    hidden, normed_mlp = branch_and_norm(attn_branch, inputs, gains, 2, "branch_and_norm")
    gate_up, activated, grad_all = feed(
        normed_mlp.reshape(TEAM, row_count, D), gate_up_full, grad_low, grad_all, early, 8
    )
    grad_down = over_rows(grad_all.reshape(-1, D), activated.reshape(-1, hidden_units))
    grad_all, grad_down = after(grad_all, grad_down.astype(jnp.bfloat16))
    down_sum = sum_weight(grad_down)
    grad_gate, grad_up, grad_gate_weight = feed_back(
        grad_all.reshape(TEAM, row_count, D),
        down_full,
        gate_up,
        normed_mlp,
        lax.axis_size("outer"),
    )
    gate_sum = turned_pieces(
        sum_weight(grad_gate_weight.reshape(-1, grad_gate_weight.shape[2]))
    )
    grad_hidden, grad_mlp_gain, own_grad, mlp_part, grad_up_weight = feed_back_rest(
        grad_gate,
        grad_up,
        gate_up_full,
        activated,
        down_full,
        normed_mlp,
        hidden,
        grad_low,
        gains,
        lax.axis_size("outer"),
        3,
        "feed_back_rest",
    )
    up_sum = turned_pieces(sum_weight(grad_up_weight.reshape(-1, grad_up_weight.shape[2])))
    _, grad_head_gains, grad_normed_attn, output, grad_first, down_mixed = attend_back(
        projected,
        normed_attn.reshape(TEAM, row_count, D),
        attended,
        own_grad,
        logs,
        first_full,
        mlp_part,
        hidden,
        (team_pieces(down_sum),),
        lax.axis_size("outer"),
        lengths,
        owners,
        cos_full,
        sin_full,
        gains,
        heads,
        7,
    )
    grad_first, gate_sum = after(grad_first, gate_sum)
    first_sum = turned_pieces(sum_weight(grad_first.reshape(-1, grad_first.shape[3])))
    input_grad, attn_gain_parts, squares, gate_mixed, up_mixed = norm_back_last(
        grad_normed_attn,
        inputs,
        grad_hidden,
        gains,
        (gate_sum, up_sum),
        (gate_sum, up_sum, down_sum),
        4,
        "norm_back_attn",
    )
    packed, norm_value, factor_tile, first_mixed = total_everywhere(
        attn_gain_parts,
        grad_mlp_gain,
        grad_head_gains,
        squares,
        first_sum,
        lax.axis_size("outer"),
        5,
        "total_everywhere",
    )
    grad_norm = norm_value.reshape(())
    (
        (new_gate_up, new_gate_up_one, new_gate_up_two, gate_up_copy),
        (new_down, new_down_one, new_down_two, down_copy),
        (new_out, new_out_one, new_out_two, out_copy),
        (new_qkv, new_qkv_one, new_qkv_two, qkv_copy),
        new_gains,
        (output, input_grad),
    ) = adam_all(
        [
            (
                gate_up_weight,
                gate_up_moment,
                gate_up_square,
                [
                    by_turned(part_rows, base, gate_up_widths[:1], source, (member,))
                    for source, base in enumerate((0, gate_up_widths[0]))
                    for member in range(TEAM)
                ],
            ),
            (
                down_weight,
                down_moment,
                down_square,
                [by_rows(member, hidden_units, part_rows, None, 2) for member in range(TEAM)],
            ),
            (
                out_weight,
                out_moment,
                out_square,
                [
                    by_rows(member, heads * HD, part_rows, (heads + 2) * HD, 3)
                    for member in range(TEAM)
                ],
            ),
            (
                qkv_weight,
                qkv_moment,
                qkv_square,
                [by_turned(part_rows, 0, qkv_widths, 3)],
            ),
        ],
        (gate_mixed, up_mixed, down_mixed, first_mixed),
        factor_tile,
        packed,
        [gains] + [each.reshape(-1, HD) for each in (gains_moment, gains_square)],
        (output, input_grad),
    )
    new_gains, new_gains_one, new_gains_two = (each.reshape(-1) for each in new_gains)
    return (
        output,
        input_grad,
        grad_norm,
        new_qkv,
        new_qkv_one,
        new_qkv_two,
        qkv_copy,
        new_out,
        new_out_one,
        new_out_two,
        out_copy,
        new_gate_up,
        new_gate_up_one,
        new_gate_up_two,
        gate_up_copy,
        new_down,
        new_down_one,
        new_down_two,
        down_copy,
        new_gains,
        new_gains_one,
        new_gains_two,
    )


def solution(mesh):
    fsdp_count, tp_count = mesh.shape["fsdp"], mesh.shape["tp"]
    cut = mesh.devices.reshape(fsdp_count // TEAM, NEAR, CORE, tp_count)
    cut_mesh = Mesh(cut, ("outer",) + LAYER)
    fsdp = ("outer", "near", "core")
    rows = P(fsdp + ("tp",), None)
    wide = P(fsdp, "tp")
    tall = P("tp", fsdp)
    weights = (wide, tall, wide, tall, P())
    return jax.shard_map(
        local,
        mesh=cut_mesh,
        in_specs=(rows, rows, P(), P()) + weights * 3,
        out_specs=(rows, rows, P()) + (wide,) * 4 + (tall,) * 4 + (wide,) * 4 + (tall,) * 4 + (P(),) * 3,
        check_vma=False,
    )
```

```python
from functools import partial

import jax
import jax.numpy as jnp
import numpy as np
from jax import lax
from jax.experimental import pallas as pl
from jax.experimental.pallas import tpu as pltpu
from jax.sharding import Mesh, PartitionSpec as P

D = 2048
H = 16
KV = 8
HD = 128
FF = 6144
STEP = 10


norm_epsilon = 1e-06
rope_base = 1000000.0
clip_norm = 1.0
learn_rate = 0.04
gain_rate = 0.8
beta_first = 0.9
beta_second = 0.999
adam_epsilon = 1e-08
weight_decay = 0.1
masked_score = -1e30

NEAR = 2
CORE = 2
TEAM = NEAR * CORE
LAYER = ("near", "core", "tp")
BLOCK = 128
PAD = 8 * 128


def rms_scale(values):
    return lax.rsqrt(jnp.mean(values * values, axis=-1, keepdims=True) + norm_epsilon)


def swish_product(gate_part, up_part):
    return jax.nn.silu(gate_part) * up_part


MESH_ID = pl.DeviceIdType.MESH
VMEM_LIMIT = 60 * 1024 * 1024
CHUNK = 16
GATHER_COPIES = 17
AHEAD = 1000
PART = TEAM // 2
HEAD_GAINS = 2 * D // HD
SUM_COPIES = 12
NEIGHBOURS = ((1, 0, 0), (0, 1, 0), (0, 0, 1))
MATES = ((0, 1, 0), (1, 0, 0), (1, 1, 0))
EVERYONE_NEAR = NEIGHBOURS + ((1, 1, 0),)


def spots():
    return tuple(lax.axis_index(name) for name in LAYER)


def flipped(near_flip, core_flip, tp_flip):
    return {
        name: 1 - spot if flip else spot
        for name, spot, flip in zip(LAYER, spots(), (near_flip, core_flip, tp_flip))
    }


def greet(flips):
    barrier = pltpu.get_barrier_semaphore()
    for flip in flips:
        pl.semaphore_signal(barrier, inc=1, device_id=flipped(*flip), device_id_type=MESH_ID)
    pl.semaphore_wait(barrier, len(flips))


def link(source, target, send_sem, recv_sem, flip):
    return pltpu.make_async_remote_copy(
        src_ref=source,
        dst_ref=target,
        send_sem=send_sem,
        recv_sem=recv_sem,
        device_id=flipped(*flip),
        device_id_type=MESH_ID,
    )


TO_NEAR, TO_CORE, TO_TP = NEIGHBOURS


def plan_exchange(pieces, out, send, recv, own_sem):
    near, core, _ = spots()
    own = near * CORE + core
    copies = []
    for number, flip in enumerate(MATES):
        there = (1 - near if flip[0] else near) * CORE + (1 - core if flip[1] else core)
        copies.append(
            link(pieces.at[there], out.at[own], send.at[number], recv.at[number], flip)
        )
    copies.append(pltpu.make_async_copy(pieces.at[own], out.at[own], own_sem))
    return copies


def exchange_scratch():
    return [
        pltpu.SemaphoreType.DMA((len(MATES),)),
        pltpu.SemaphoreType.DMA((len(MATES),)),
        pltpu.SemaphoreType.DMA,
    ]


def crossing(pieces, width):
    return sum(2 * piece.shape[1] * piece.shape[2] for piece in pieces) // width


def plan_exchanges(pieces, mixed, sems):
    copies = []
    for place, (piece, result) in enumerate(zip(pieces, mixed)):
        copies += plan_exchange(piece, result, *sems[3 * place : 3 * place + 3])
    return copies


def plan_gather(own, out, send, recv, own_sem, cut, base=0, rows=None, parts=False, apart=False):
    near, core, tp = spots()
    rows = own.shape[0] if rows is None else rows
    low, high = pl.ds(base, cut), pl.ds(base + cut, rows - cut)
    all_rows = pl.ds(base, rows)

    def make(number, source, target, flip):
        return link(source, target, send.at[number], recv.at[number], flip)

    def give(number, part, flip):
        return make(number, own.at[part], out.at[near, core, tp, part], flip)

    def relay(number, where_near, where_tp, part, flip):
        ref = out.at[where_near, core, where_tp, part]
        return make(number, ref, ref, flip)

    keep = pltpu.make_async_copy(own.at[all_rows], out.at[near, core, tp, all_rows], own_sem)
    twin_own = give(4, all_rows, TO_CORE)
    first_rows = (rows - cut) // 2 // CHUNK * CHUNK
    high_parts = [
        (pl.ds(base + cut, first_rows), 1, 7, 8),
        (pl.ds(base + cut + first_rows, rows - cut - first_rows), 13, 14, 15),
    ]
    near_high = [give(number, part, TO_NEAR) for part, number, _, _ in high_parts]
    tp_high = give(2, high, TO_TP)
    far_high = [relay(number, 1 - near, tp, part, TO_TP) for part, _, number, _ in high_parts]
    twin_beside = [relay(number, 1 - near, tp, part, TO_CORE) for part, _, _, number in high_parts]
    twin_across = relay(9, near, 1 - tp, high, TO_CORE)
    twin_far = [
        relay(number, 1 - near, 1 - tp, part, TO_CORE)
        for (part, *_), number in zip(high_parts, (12, 16))
    ]
    twins = [twin_own, twin_across] + twin_far + twin_beside
    ways = near_high + far_high + [tp_high]
    if cut:
        tp_low = give(0, low, TO_TP)
        near_low = give(3, low, TO_NEAR)
        far_low = relay(5, near, 1 - tp, low, TO_NEAR)
        twin_across_low = relay(6, near, 1 - tp, low, TO_CORE)
        twin_beside_low = relay(10, 1 - near, tp, low, TO_CORE)
        twin_far_low = relay(11, 1 - near, 1 - tp, low, TO_CORE)
        twins += [twin_across_low, twin_beside_low, twin_far_low]
        ways += [tp_low, near_low, far_low]

    def begin_tp():
        if cut:
            tp_low.start()
        tp_high.start()
        twin_own.start()
        keep.start()

    def begin_near():
        for copy in near_high:
            copy.start()
        if cut:
            near_low.start()

    def begin():
        begin_near()
        begin_tp()

    def pass_on(part):
        near_high[part].wait_recv()
        far_high[part].start()
        twin_beside[part].start()

    def middle():
        if cut:
            tp_low.wait_recv()
            far_low.start()
            twin_across_low.start()
        pass_on(0)
        if not apart:
            pass_on(1)

    def later():
        tp_high.wait_recv()
        twin_across.start()
        if cut:
            near_low.wait_recv()
            twin_beside_low.start()

    def own_there():
        keep.wait()

    def twin_there():
        twin_own.wait_recv()
        twin_across.wait_recv()
        if cut:
            twin_across_low.wait_recv()

    def far_there():
        if cut:
            far_low.wait_recv()
            twin_far_low.start()
        for copy, twin in zip(far_high, twin_far):
            copy.wait_recv()
            twin.start()

    def rest_there():
        for copy in twin_beside + twin_far:
            copy.wait_recv()
        if cut:
            twin_beside_low.wait_recv()
            twin_far_low.wait_recv()
        for copy in ways + twins:
            copy.wait_send()

    def finish():
        own_there()
        twin_there()
        far_there()
        rest_there()

    if parts:
        return [begin, middle, later, own_there, twin_there, far_there, rest_there]
    if apart:
        return [begin_tp, begin_near, middle, partial(pass_on, 1), later, finish]
    return [begin, middle, later, finish]


def balanced(rows, beside):
    return max(0, (rows - beside) // 2 // CHUNK * CHUNK)


def gather_scratch():
    return [
        pltpu.SemaphoreType.DMA((GATHER_COPIES,)),
        pltpu.SemaphoreType.DMA((GATHER_COPIES,)),
        pltpu.SemaphoreType.DMA,
    ]


def add_rows(target, start, count, *sources):
    @pl.loop(0, count // CHUNK)
    def _(step):
        at = pl.ds(pl.multiple_of(start + step * CHUNK, CHUNK), CHUNK)
        total = None
        for source, shift in sources:
            where = pl.ds(pl.multiple_of(start - shift + step * CHUNK, CHUNK), CHUNK)
            value = source[where].astype(jnp.float32)
            total = value if total is None else total + value
        target[at] = total.astype(target.dtype)


def halved(start, count):
    half = count // 2 // CHUNK * CHUNK
    return (start, half), (start + half, count - half)


def plan_sum(outgoing, mine, keep, total, scratch, cut):
    theirs, way_near, way_tp, from_tp, from_near, send, recv = scratch
    rows = total.shape[0]
    low, high = pl.ds(0, cut), pl.ds(cut, rows - cut)

    def make(number, source, target, flip):
        return link(source, target, send.at[number], recv.at[number], flip)

    twin = [make(number, outgoing[number], theirs.at[number], TO_CORE) for number in range(4)]
    far, to_tp, to_near, own = mine
    low_parts = halved(0, cut)
    high_parts = halved(cut, rows - cut)
    far_high = make(5, far.at[high], way_tp, TO_TP)
    tp_high = make(6, to_tp.at[high], from_tp.at[high], TO_TP)
    near_high = [
        make(9 + 2 * place, to_near.at[pl.ds(*part)], from_near.at[pl.ds(*part)], TO_NEAR)
        for place, part in enumerate(high_parts)
    ]
    ways = [far_high, tp_high] + near_high
    tp_low = []
    if cut:
        far_low = make(4, far.at[low], way_near, TO_NEAR)
        near_low = make(7, to_near.at[low], from_near.at[low], TO_NEAR)
        tp_low = [
            make(8 + 2 * place, to_tp.at[pl.ds(*part)], from_tp.at[pl.ds(*part)], TO_TP)
            for place, part in enumerate(low_parts)
        ]
        ways += [far_low, near_low] + tp_low

    def ready(number):
        if keep:
            keep[number].wait()
        twin[number].wait_recv()

    def both(number):
        return (mine[number], 0), (theirs.at[number], 0)

    def begin(numbers=range(4)):
        for number in numbers:
            twin[number].start()
            if keep:
                keep[number].start()

    def send_far():
        ready(0)
        if cut:
            add_rows(far, 0, cut, *both(0))
            far_low.start()
        add_rows(far, cut, rows - cut, *both(0))
        far_high.start()

    def send_tp():
        ready(1)
        add_rows(to_tp, cut, rows - cut, *both(1))
        tp_high.start()

    def send_near():
        ready(2)
        if cut:
            add_rows(to_near, 0, cut, *both(2))
            near_low.start()

    def first():
        send_far()
        send_tp()
        send_near()

    def second():
        if cut:
            far_low.wait_recv()
        far_high.wait_recv()
        for place, part in enumerate(high_parts):
            if cut:
                add_rows(to_tp, *low_parts[place], *both(1), (way_near, 0))
                tp_low[place].start()
            add_rows(to_near, *part, *both(2), (way_tp, cut))
            near_high[place].start()
        ready(3)
        add_rows(total, 0, rows, *both(3))

    def finish(body):
        tp_high.wait_recv()
        if cut:
            near_low.wait_recv()
        for place, part in enumerate(high_parts):
            if cut:
                tp_low[place].wait_recv()
                row_loop(*low_parts[place], body)
            near_high[place].wait_recv()
            row_loop(*part, body)
        for copy in twin + ways:
            copy.wait_send()

    return [begin, first, second, finish], (send_far, send_tp, send_near)


def plan_sum_of(part, total, scratch, cut):
    mine, local_sem, *scratch = scratch
    near, core, tp = spots()
    order = [(1 - near, 1 - tp), (near, 1 - tp), (1 - near, tp), (near, tp)]
    outgoing = [part.at[a, 1 - core, b] for a, b in order]
    keep = [
        pltpu.make_async_copy(part.at[a, core, b], mine.at[number], local_sem.at[number])
        for number, (a, b) in enumerate(order)
    ]
    blocks = [mine.at[number] for number in range(4)]
    steps, _ = plan_sum(outgoing, blocks, keep, total, scratch, cut)
    return steps, scratch[3], scratch[4]


def sum_scratch(rows, width, cut, fetched=True):
    low = jnp.bfloat16
    fetch = [pltpu.VMEM((4, rows, width), low), pltpu.SemaphoreType.DMA((4,))]
    return (fetch if fetched else []) + [
        pltpu.VMEM((4, rows, width), low),
        pltpu.VMEM((max(cut, CHUNK), width), low),
        pltpu.VMEM((rows - cut, width), low),
        pltpu.VMEM((rows, width), low),
        pltpu.VMEM((rows, width), low),
        pltpu.SemaphoreType.DMA((SUM_COPIES,)),
        pltpu.SemaphoreType.DMA((SUM_COPIES,)),
    ]


SUM_SCRATCH = 9
COST_SHARE = 1e5


def params(number):
    return pltpu.CompilerParams(
        collective_id=number, has_side_effects=True, vmem_limit_bytes=VMEM_LIMIT
    )


def cost_of(microseconds):
    return pl.CostEstimate(
        flops=0, bytes_accessed=int(microseconds * COST_SHARE), transcendentals=0
    )


def in_vmem():
    return pl.BlockSpec(memory_space=pltpu.VMEM)


def anywhere():
    return pl.BlockSpec(memory_space=pl.ANY)


def like(array):
    return jax.ShapeDtypeStruct(array.shape, array.dtype)


def layer_rows(rows, width):
    return jax.ShapeDtypeStruct((NEAR, CORE, 2, rows, width), jnp.bfloat16)


def wide_gain(gains, place, width):
    first = place * (width // HD)
    return jnp.concatenate(
        [gains[first + part : first + part + 1] for part in range(width // HD)], axis=1
    )


def row_loop(start, count, body):
    @pl.loop(0, count // CHUNK)
    def _(step):
        body(pl.ds(pl.multiple_of(start + step * CHUNK, CHUNK), CHUNK))


def plan_line(blocks, send, recv, count):
    own = lax.axis_index("outer")

    def handle(side, number, half, there):
        block = blocks.at[there, pl.ds(half * PART, PART)]
        return pltpu.make_async_remote_copy(
            src_ref=block,
            dst_ref=block,
            send_sem=send.at[side, number, half],
            recv_sem=recv.at[side, number, half],
            device_id={"outer": own + 1 if side == 0 else own - 1},
            device_id_type=MESH_ID,
        )

    def message(side, number, half):
        return handle(side, number, half, own - number if side == 0 else own + number)

    def arrival(side, number, half):
        return handle(side, number, half, own - 1 - number if side == 0 else own + 1 + number)

    def sends(side, number):
        if side == 0:
            return (own < count - 1) & (own >= number)
        return (own > 0) & (own + number < count)

    def gets(side, number):
        return own >= number + 1 if side == 0 else own + 1 + number < count

    near = lax.axis_index("near")
    halves = (near, 1 - near)

    def push(number, place):
        for side in range(2):

            @pl.when(sends(side, number))
            def _(side=side):
                message(side, number, halves[place]).start()

    def take(number):
        for half in halves:
            for side in range(2):

                @pl.when(gets(side, number))
                def _(side=side, half=half):
                    arrival(side, number, half).wait_recv()

                if number + 2 < count:

                    @pl.when(sends(side, number + 1))
                    def _(side=side, half=half):
                        message(side, number + 1, half).start()

    def settle():
        for number in range(count - 1):
            for side in range(2):

                @pl.when(sends(side, number))
                def _(side=side, number=number):
                    for half in range(2):
                        message(side, number, half).wait_send()

    return push, take, settle


def greet_all(flips, count, work):
    barrier = pltpu.get_barrier_semaphore()
    own = lax.axis_index("outer")
    for flip in flips:
        pl.semaphore_signal(barrier, inc=1, device_id=flipped(*flip), device_id_type=MESH_ID)
    for there, neighbour in ((own < count - 1, own + 1), (own > 0, own - 1)):

        @pl.when(there)
        def _(neighbour=neighbour):
            pl.semaphore_signal(
                barrier, inc=1, device_id={"outer": neighbour}, device_id_type=MESH_ID
            )

    work()
    beside = jnp.where(own < count - 1, 1, 0) + jnp.where(own > 0, 1, 0)
    pl.semaphore_wait(barrier, len(flips) + beside)


def sequence_length(lengths, owners, group):
    total = jnp.int32(0)
    for place in range(lengths.shape[0]):
        total += jnp.where(owners[place] == group, lengths[place], 0)
    return total


def opening(
    qkv, out_weight, gate_up, down, inputs, gains, cotangent, lengths, owners, outer_count, number
):
    rows, width = inputs.shape
    part_rows, wide = qkv.shape
    tall, units = out_weight.shape[0], down.shape[0]
    widths = (wide // 2, wide // 4, wide // 4)
    first_shape = jax.ShapeDtypeStruct((TEAM, part_rows, (wide + tall) // TEAM), jnp.bfloat16)
    gate_up_shape = jax.ShapeDtypeStruct((TEAM, part_rows, 2 * units // TEAM), jnp.bfloat16)
    down_shape = jax.ShapeDtypeStruct((TEAM, part_rows, units // TEAM), jnp.bfloat16)
    cut = balanced(rows, crossing((first_shape, gate_up_shape), width))

    def kernel(
        lengths, owners, qkv, out_weight, inputs, gains, gate_up, down, cotangent,
        out, mixed, full, low, down_pieces,
        normed, first, pieces, gate_up_v, down_v, cotangent_v, load_sem, line_send, line_recv, *sems
    ):
        near, core, tp = spots()
        outer = lax.axis_index("outer")
        begin_tp, begin_near, middle, middle_rest, later, finish = plan_gather(
            normed, out, *sems[:3], cut=cut, apart=True
        )
        team = plan_exchange(first, full.at[outer], *sems[3:6])
        others = plan_exchange(pieces, mixed, *sems[6:9])
        push, take, settle = plan_line(full, line_send, line_recv, outer_count)
        fetch = [
            pltpu.make_async_copy(source, target, load_sem.at[place])
            for place, (source, target) in enumerate(
                ((cotangent, cotangent_v), (gate_up, gate_up_v), (down, down_v))
            )
        ]
        for copy in fetch:
            copy.start()
        gain = wide_gain(gains, 0, width)

        def prepare(at):
            value = inputs[at].astype(jnp.float32)
            normed[at] = (value * rms_scale(value) * gain).astype(jnp.bfloat16)

        def work():
            for member, across, inside in spans(widths):
                first[member, :, inside] = qkv[:, across].astype(jnp.bfloat16)
            for member in range(TEAM):
                at = pl.ds(member * (tall // TEAM), tall // TEAM)
                first[member, :, wide // TEAM :] = out_weight[at].astype(jnp.bfloat16).T
            row_loop(0, rows, prepare)

        greet_all(EVERYONE_NEAR, outer_count, work)
        for copy in team:
            copy.start()
        begin_tp()
        team[0].wait()
        team[3].wait()
        push(0, 0)
        fetch[1].wait()
        for member, across, inside in spans((units, units)):
            pieces[member, :, inside] = gate_up_v[:, across].astype(jnp.bfloat16)
        for copy in team[1:3]:
            copy.wait()
        push(0, 1)
        begin_near()
        take(0)
        length = sequence_length(lengths, owners, outer * TEAM + near * CORE + core)
        fetch[0].wait()

        def mask(at):
            row = lax.broadcasted_iota(jnp.int32, (CHUNK, width), 0) + at.start + tp * rows
            value = jnp.where(row < length, cotangent_v[at].astype(jnp.float32), 0.0)
            low[at] = value.astype(jnp.bfloat16)

        row_loop(0, rows, mask)
        fetch[2].wait()
        for member in range(TEAM):
            at = pl.ds(member * (units // TEAM), units // TEAM)
            down_pieces[member] = down_v[at].astype(jnp.bfloat16).T
        middle()
        if outer_count > 2:
            take(1)
        middle_rest()
        for copy in others:
            copy.start()
        later()
        for step in range(2, outer_count - 1):
            take(step)
        finish()
        settle()
        for copy in others:
            copy.wait()

    scalars = pl.BlockSpec(memory_space=pltpu.SMEM)
    outs = pl.pallas_call(
        kernel,
        name="opening",
        out_shape=(
            layer_rows(rows, width),
            gate_up_shape,
            jax.ShapeDtypeStruct((outer_count,) + first_shape.shape, jnp.bfloat16),
            jax.ShapeDtypeStruct((rows, width), jnp.bfloat16),
            down_shape,
        ),
        in_specs=[scalars] * 2 + [in_vmem()] * 4 + [anywhere()] * 3,
        out_specs=(anywhere(),) * 3 + (in_vmem(),) * 2,
        scratch_shapes=[
            pltpu.VMEM((rows, width), jnp.bfloat16),
            pltpu.VMEM(first_shape.shape, jnp.bfloat16),
            pltpu.VMEM(gate_up_shape.shape, jnp.bfloat16),
            pltpu.VMEM(gate_up.shape, gate_up.dtype),
            pltpu.VMEM(down.shape, down.dtype),
            pltpu.VMEM(cotangent.shape, cotangent.dtype),
            pltpu.SemaphoreType.DMA((3,)),
            pltpu.SemaphoreType.DMA((2, outer_count, 2)),
            pltpu.SemaphoreType.DMA((2, outer_count, 2)),
        ]
        + gather_scratch()
        + exchange_scratch() * 2,
        compiler_params=params(number),
        cost_estimate=cost_of(60),
    )(
        lengths,
        owners,
        qkv,
        out_weight,
        inputs,
        gains,
        gate_up,
        down,
        cotangent,
    )
    gathered, mixed, full, low, down_pieces = outs
    return (
        gathered.reshape(-1, width),
        mixed,
        full.reshape(-1, first_shape.shape[2]),
        low,
        down_pieces,
    )


def spread(part, rows):
    return part.reshape(NEAR, CORE, 2, rows, part.shape[-1])


def read(ref, at):
    return ref[at].astype(jnp.float32)


def branch_and_norm(part, residual, gains, number, name):
    rows, width = residual.shape
    cut = rows // 2

    def kernel(part, residual, gains, hidden, out, *scratch):
        gain = wide_gain(gains, 1, width)
        normed, sems = scratch[SUM_SCRATCH], scratch[SUM_SCRATCH + 1 :]
        steps, from_tp, from_near = plan_sum_of(part, hidden, scratch[:SUM_SCRATCH], cut)
        onward = plan_gather(normed, out, *sems, cut=cut)
        greet(NEIGHBOURS)
        for step in steps[:3]:
            step()

        def finish(at):
            value = hidden[at] + read(from_tp, at) + read(from_near, at)
            value = read(residual, at) + value
            hidden[at] = value
            normed[at] = (value * rms_scale(value) * gain).astype(jnp.bfloat16)

        steps[3](finish)
        for step in onward:
            step()

    hidden, full = pl.pallas_call(
        kernel,
        name=name,
        out_shape=(jax.ShapeDtypeStruct((rows, width), jnp.float32), layer_rows(rows, width)),
        in_specs=[anywhere(), in_vmem(), in_vmem()],
        out_specs=(in_vmem(), anywhere()),
        scratch_shapes=sum_scratch(rows, width, cut)
        + [pltpu.VMEM((rows, width), jnp.bfloat16)]
        + gather_scratch(),
        compiler_params=params(number),
        cost_estimate=cost_of(95),
    )(spread(part, rows), residual, gains)
    return hidden, full.reshape(-1, width)


def norm_back(value, gain, grad):
    scale = rms_scale(value)
    scaled = grad * gain
    inner = jnp.mean(scaled * value, axis=-1, keepdims=True)
    return scale * scaled - value * (scale * scale * scale * inner), grad * value * scale


def sequence_order():
    near, core, _ = spots()
    return [
        (near if place >= 2 else 1 - near) * CORE + (core if place % 2 else 1 - core)
        for place in range(TEAM)
    ]


def times_turned(left, weights, target):
    for start in range(0, weights.shape[0], 512):
        at = pl.ds(start, 512)
        target[:, at] = lax.dot_general(
            left, weights[at, :], (((1,), (1,)), ((), ())), preferred_element_type=jnp.float32
        ).astype(target.dtype)


def feed_back_rest(
    grad_gate, grad_up, weights, active, down, normed, values, upstream, gains, outer_count, number, name
):
    rows, width = values.shape
    count, both_rows, units = grad_gate.shape
    all_rows = count * both_rows
    past = all_rows - width
    cut = rows // 2
    split, share = team_split(width, outer_count)
    turns = width // 512

    def kernel(
        gate, ups, weights, active, down, normed, values, upstream, gains,
        result, gain_grad, low, branch, grad_weight, *scratch
    ):
        (grad_v, weights_v, active_v, down_v, values_v, upstream_v, parts, total), rest = (
            scratch[:8],
            scratch[8:],
        )
        (shares, staged, load_sem, store_sem, chunk_sem, piece_sem), sums = rest[:6], rest[6:]
        from_tp, from_near = sums[3], sums[4]
        gain = wide_gain(gains, 1, width)
        near, core, tp = spots()
        members = sequence_order()
        outgoing = [parts.at[place, half] for place, half in ((0, 1 - tp), (2, 1 - tp), (0, tp), (2, tp))]
        mine = [parts.at[place, half] for place, half in ((1, 1 - tp), (3, 1 - tp), (1, tp), (3, tp))]
        steps, (send_far, send_tp, send_near) = plan_sum(outgoing, mine, (), total, sums, cut)
        stores = [
            pltpu.make_async_copy(shares.at[place % 2], branch.at[place], store_sem.at[place])
            for place in range(count)
        ]
        fetch = [
            pltpu.make_async_copy(source, target, load_sem.at[place])
            for place, (source, target) in enumerate(
                (
                    (weights, weights_v),
                    (values, values_v),
                    (upstream, upstream_v),
                    (active, active_v),
                    (down, down_v),
                    (ups, active_v),
                )
            )
        ]
        grads = []
        for place, member in enumerate(members):
            for side, source in enumerate((gate, ups)):
                grads.append(
                    pltpu.make_async_copy(
                        source.at[member],
                        grad_v.at[place % 2, :, :, pl.ds(side * units, units)],
                        load_sem.at[6 + 2 * place + side],
                    )
                )

        def bring(place):
            grads[2 * place].start()
            grads[2 * place + 1].start()

        def brought(place):
            grads[2 * place].wait()
            grads[2 * place + 1].wait()

        def back(place, half):
            times_turned(grad_v[place % 2, half], weights_v, parts.at[place, half])

        def chunk(turn):
            at, slot = pl.ds(turn * 512, 512), turn % 2
            return [
                pltpu.make_async_copy(
                    normed.at[pl.ds(0, width), at],
                    weights_v.at[:, pl.ds(slot * 1024, 512)],
                    chunk_sem.at[slot, 0],
                ),
                pltpu.make_async_copy(
                    normed.at[pl.ds(width, past), at],
                    weights_v.at[pl.ds(slot * past, past), pl.ds(512, 512)],
                    chunk_sem.at[slot, 1],
                ),
            ]

        def pieces(turn):
            slot = turn % 2
            return [
                pltpu.make_async_copy(
                    staged.at[slot, :, pl.ds(place * share, share)],
                    grad_weight.at[turn * (512 // share) + place],
                    piece_sem.at[slot, place],
                )
                for place in range(512 // share)
            ]

        fetch[0].start()
        bring(0)
        bring(1)
        greet(NEIGHBOURS)
        fetch[0].wait()
        brought(0)
        back(0, 1 - tp)
        steps[0]((0,))
        brought(1)
        back(1, 1 - tp)
        send_far()
        back(0, tp)
        steps[0]((2,))
        bring(2)
        for place in (3, 4, 1, 2):
            fetch[place].start()
        back(1, tp)
        send_near()
        bring(3)
        brought(2)
        back(2, 1 - tp)
        steps[0]((1,))
        brought(3)
        back(3, 1 - tp)
        send_tp()
        back(2, tp)
        steps[0]((3,))
        back(3, tp)
        for turn in (0, 1):
            for copy in chunk(turn):
                copy.start()
        fetch[3].wait()
        fetch[4].wait()
        for place in range(count):
            if place >= 2:
                stores[place - 2].wait()
            for half in range(2):
                times_turned(active_v[place, half], down_v, shares.at[place % 2, half])
            stores[place].start()
        fetch[5].start()
        steps[2]()
        fetch[5].wait()
        for turn in range(turns):
            slot = turn % 2
            for copy in chunk(turn):
                copy.wait()
            left = active_v[...].reshape(all_rows, units)
            product = lax.dot_general(
                left[:width],
                weights_v[:, slot * 1024 : slot * 1024 + 512],
                (((0,), (0,)), ((), ())),
                preferred_element_type=jnp.float32,
            ) + lax.dot_general(
                left[width:],
                weights_v[slot * past : (slot + 1) * past, 512:1024],
                (((0,), (0,)), ((), ())),
                preferred_element_type=jnp.float32,
            )
            if turn >= 2:
                for copy in pieces(turn - 2):
                    copy.wait()
            staged[slot] = product.astype(staged.dtype)
            for copy in pieces(turn):
                copy.start()
            if turn + 2 < turns:
                for copy in chunk(turn + 2):
                    copy.start()
        fetch[1].wait()
        fetch[2].wait()
        gain_grad[...] = jnp.zeros_like(gain_grad)

        def finish(at):
            grad = total[at] + read(from_tp, at) + read(from_near, at)
            turned, by_gain = norm_back(values_v[at], gain, grad)
            gain_grad[...] += by_gain.reshape(CHUNK // 8, 8, width).sum(axis=0)
            value = read(upstream_v, at) + turned
            total[at] = value
            low[at] = value.astype(jnp.bfloat16)

        steps[3](finish)
        store = pltpu.make_async_copy(total, result, store_sem.at[count])
        store.start()
        for turn in range(max(0, turns - 2), turns):
            for copy in pieces(turn):
                copy.wait()
        for copy in [store] + stores[2:]:
            copy.wait()

    low_type = jnp.bfloat16
    halves = (count, 2, rows, units)
    result, gain_grad, rounded, branch, grad_weight = pl.pallas_call(
        kernel,
        name=name,
        out_shape=(
            jax.ShapeDtypeStruct((rows, width), jnp.float32),
            jax.ShapeDtypeStruct((8, width), jnp.float32),
            jax.ShapeDtypeStruct((rows, width), low_type),
            jax.ShapeDtypeStruct((count, 2, rows, width), low_type),
            jax.ShapeDtypeStruct((outer_count * split, units, share), low_type),
        ),
        in_specs=[anywhere()] * 8 + [in_vmem()],
        out_specs=(anywhere(), in_vmem(), in_vmem(), anywhere(), anywhere()),
        scratch_shapes=[
            pltpu.VMEM((2, 2, rows, 2 * units), low_type),
            pltpu.VMEM(weights.shape, low_type),
            pltpu.VMEM(halves, low_type),
            pltpu.VMEM(down.shape, low_type),
            pltpu.VMEM((rows, width), values.dtype),
            pltpu.VMEM((rows, width), upstream.dtype),
            pltpu.VMEM((count, 2, rows, width), low_type),
            pltpu.VMEM((rows, width), jnp.float32),
            pltpu.VMEM((2, 2, rows, width), low_type),
            pltpu.VMEM((2, units, 512), low_type),
            pltpu.SemaphoreType.DMA((6 + 2 * count,)),
            pltpu.SemaphoreType.DMA((count + 1,)),
            pltpu.SemaphoreType.DMA((2, 2)),
            pltpu.SemaphoreType.DMA((2, 512 // share)),
        ]
        + sum_scratch(rows, width, cut, fetched=False),
        compiler_params=params(number),
        cost_estimate=cost_of(60),
    )(
        grad_gate.reshape(halves),
        grad_up.reshape(halves),
        weights,
        active.reshape(halves),
        down,
        normed,
        values,
        upstream,
        gains,
    )
    return result, gain_grad, rounded, branch.reshape(-1, width), grad_weight


def square_sum(values):
    values = values.reshape(-1, values.shape[-1]).astype(jnp.float32)
    return jnp.sum(values * values, keepdims=True)


def corner(value):
    row = lax.broadcasted_iota(jnp.int32, (8, HD), 0)
    column = lax.broadcasted_iota(jnp.int32, (8, HD), 1)
    return jnp.where((row == 0) & (column == 0), value, 0.0)


def norm_back_last(part, values, upstream, gains, extra, squared, number, name):
    rows, width = values.shape
    extras, count = len(extra), len(squared)
    cut = balanced(rows, crossing(extra, width))

    def kernel(part, values, upstream, gains, *rest):
        gain = wide_gain(gains, 0, width)
        pieces, rest = rest[:extras], rest[extras:]
        squared, (result, gain_grad, squares), rest = (
            rest[:count],
            rest[count : count + 3],
            rest[count + 3 :],
        )
        mixed, rest = rest[:extras], rest[extras:]
        sums, rest = rest[:SUM_SCRATCH], rest[SUM_SCRATCH:]
        (total, values_v, upstream_v, load_sem), rest = rest[:4], rest[4:]
        squared_v, sems = rest[:count], rest[count:]
        steps, from_tp, from_near = plan_sum_of(part, total, sums, cut)
        copies = plan_exchanges(pieces, mixed, sems)
        fetch = [
            pltpu.make_async_copy(source, target, load_sem.at[place])
            for place, (source, target) in enumerate(
                zip((values, upstream) + tuple(squared), (values_v, upstream_v) + tuple(squared_v))
            )
        ]
        greet(EVERYONE_NEAR)
        steps[0]()
        for copy in copies:
            copy.start()
        for copy in fetch:
            copy.start()
        steps[1]()
        for copy in fetch:
            copy.wait()
        squares[...] = corner(sum(square_sum(ref[...]) for ref in squared_v))
        steps[2]()
        gain_grad[...] = jnp.zeros_like(gain_grad)

        def finish(at):
            grad = total[at] + read(from_tp, at) + read(from_near, at)
            back, by_gain = norm_back(read(values_v, at), gain, grad)
            gain_grad[...] += by_gain.reshape(CHUNK // 8, 8, width).sum(axis=0)
            result[at] = (upstream_v[at] + back).astype(jnp.bfloat16)

        steps[3](finish)
        for copy in copies:
            copy.wait()

    return pl.pallas_call(
        kernel,
        name=name,
        out_shape=(
            jax.ShapeDtypeStruct((rows, width), jnp.bfloat16),
            jax.ShapeDtypeStruct((8, width), jnp.float32),
            jax.ShapeDtypeStruct((8, HD), jnp.float32),
        )
        + tuple(like(piece) for piece in extra),
        in_specs=[anywhere()] * 3 + [in_vmem()] * (1 + extras) + [anywhere()] * count,
        out_specs=(in_vmem(), in_vmem(), in_vmem()) + (anywhere(),) * extras,
        scratch_shapes=sum_scratch(rows, width, cut)
        + [
            pltpu.VMEM((rows, width), jnp.float32),
            pltpu.VMEM((rows, width), values.dtype),
            pltpu.VMEM((rows, width), upstream.dtype),
            pltpu.SemaphoreType.DMA((2 + count,)),
        ]
        + [pltpu.VMEM(each.shape, each.dtype) for each in squared]
        + exchange_scratch() * extras,
        compiler_params=params(number),
        cost_estimate=cost_of(65),
    )(spread(part, rows), values, upstream, gains, *extra, *squared)


def total_everywhere(first, second, heads, squares, pieces, outer_count, number, name):
    used = 2 * first.shape[1] // HD + heads.shape[0]
    gains = used + -used % 8
    shape = (gains + 8, HD)
    width = first.shape[1]

    def kernel(first, second, heads, squares, pieces, out, norm, factor, mixed, layer, outers, send, recv, *sems):
        near, core, tp = spots()
        outer = lax.axis_index("outer")
        partners = [
            flipped(a, b, c)
            for a in range(NEAR)
            for b in range(CORE)
            for c in range(2)
            if a + b + c
        ]
        partners += [{"outer": (outer + step) % outer_count} for step in range(1, outer_count)]
        barrier = pltpu.get_barrier_semaphore()
        for partner in partners:
            pl.semaphore_signal(barrier, inc=1, device_id=partner, device_id_type=MESH_ID)
        mine = near * (CORE * 2) + core * 2 + tp
        layer[mine, gains - 8 : gains] = jnp.zeros((8, HD), jnp.float32)
        layer[mine, gains:] = squares[...] + corner(square_sum(pieces[...]))
        place = 0
        for source in (first, second):
            sums = jnp.sum(source[...], axis=0, keepdims=True)
            for start in range(0, width, HD):
                layer[mine, place : place + 1] = sums[:, start : start + HD]
                place += 1
        for head in range(heads.shape[0]):
            layer[mine, place : place + 1] = jnp.sum(heads[head], axis=0, keepdims=True)
            place += 1
        pl.semaphore_wait(barrier, len(partners))

        def share(slots, mine, first, count):
            copies = []
            for number in range(first, first + count):
                copy = pltpu.make_async_remote_copy(
                    src_ref=slots.at[mine],
                    dst_ref=slots.at[mine],
                    send_sem=send.at[number],
                    recv_sem=recv.at[number],
                    device_id=partners[number],
                    device_id_type=MESH_ID,
                )
                copy.start()
                copies.append(copy)
            return copies

        others = plan_exchange(pieces, mixed, *sems)
        copies = share(layer, mine, 0, 7)
        for copy in others:
            copy.start()
        for copy in copies:
            copy.wait()
        total = layer[0]
        for slot in range(1, 8):
            total = total + layer[slot]
        outers[outer] = total
        for copy in share(outers, outer, 7, outer_count - 1):
            copy.wait()
        total = outers[0]
        for slot in range(1, outer_count):
            total = total + outers[slot]
        out[...] = total
        gain_part = total[:gains]
        root = jnp.sqrt(
            jnp.sum(gain_part * gain_part, keepdims=True) + jnp.sum(total[gains:], keepdims=True)
        )
        norm[...] = root
        factor[...] = jnp.broadcast_to(
            jnp.minimum(1.0, clip_norm / (root + 1e-06)), factor.shape
        )
        for copy in others:
            copy.wait()

    tile = jax.ShapeDtypeStruct((8, HD), jnp.float32)
    return pl.pallas_call(
        kernel,
        name=name,
        out_shape=(
            jax.ShapeDtypeStruct(shape, jnp.float32),
            jax.ShapeDtypeStruct((1, 1), jnp.float32),
            tile,
            like(pieces),
        ),
        in_specs=[in_vmem()] * 5,
        out_specs=(in_vmem(), in_vmem(), in_vmem(), anywhere()),
        scratch_shapes=[
            pltpu.VMEM((8,) + shape, jnp.float32),
            pltpu.VMEM((outer_count,) + shape, jnp.float32),
            pltpu.SemaphoreType.DMA((6 + outer_count,)),
            pltpu.SemaphoreType.DMA((6 + outer_count,)),
        ]
        + exchange_scratch(),
        compiler_params=params(number),
        cost_estimate=cost_of(16),
    )(first, second, heads, squares, pieces)


def head_scale(raw, gain, cos_full, sin_full):
    normed = raw * rms_scale(raw) * gain
    return (normed * cos_full + pltpu.roll(normed, HD // 2, 1) * sin_full).astype(jnp.bfloat16)


def head_back(raw, gain, grad, cos_full, sin_full):
    grad = grad * cos_full - pltpu.roll(grad, HD // 2, 1) * sin_full
    return norm_back(raw, gain, grad)


def columns(index):
    return pl.ds(index * HD, HD)


def head_inputs(proj, gains, cos_ref, sin_ref, queries, keys, values, heads):
    for head in range(heads):
        queries[head] = head_scale(
            proj[0, :, columns(head)], gains[HEAD_GAINS : HEAD_GAINS + 1, :], cos_ref[...], sin_ref[...]
        )
    keys[...] = head_scale(
        proj[0, :, columns(heads)], gains[HEAD_GAINS + 1 : HEAD_GAINS + 2, :], cos_ref[...], sin_ref[...]
    )
    values[...] = proj[0, :, columns(heads + 1)].astype(jnp.bfloat16)


def masked_scores(stacked, keys, step, length):
    scores = lax.dot_general(
        stacked, keys, (((1,), (1,)), ((), ())), preferred_element_type=jnp.float32
    ) * (HD ** (-0.5))
    row = lax.broadcasted_iota(jnp.int32, scores.shape, 0) % BLOCK + step * BLOCK
    column = lax.broadcasted_iota(jnp.int32, scores.shape, 1)
    return jnp.where((column <= row) & (column < length), scores, masked_score)


def stack_heads(ref, at, heads):
    return jnp.concatenate([ref[head, at] for head in range(heads)], axis=0)


def per_sequence(*shape):
    return pl.BlockSpec((1,) + shape, lambda s: (s,) + (0,) * len(shape))


def whole(*shape):
    return pl.BlockSpec(shape, lambda s: (0,) * len(shape), pipeline_mode=pl.Buffered(1))


def across_columns(left, weights, first, width, out):
    total = weights.shape[0]
    for start in range(0, total, 512):
        at = pl.ds(start, 512)
        out[0, :, at] = lax.dot_general(
            left,
            weights[at, first : first + width],
            (((1,), (1,)), ((), ())),
            preferred_element_type=jnp.float32,
        ).astype(out.dtype)


def attend(normed, weights, cotangent, extra, lengths, owners, cos_full, sin_full, gains, heads, early, number):
    count, rows, width = normed.shape
    wide = (heads + 2) * HD
    extras = len(extra)
    own_rows = cotangent.shape[0]
    cut = balanced(early, crossing(extra, width))

    def kernel(lengths, owners, normed, weights_any, cos_ref, sin_ref, gains, own, *rest):
        pieces, rest = rest[:extras], rest[extras:]
        (proj, out, logs, branch, gathered), rest = rest[:5], rest[5:]
        mixed, rest = rest[:extras], rest[extras:]
        (queries, keys, values, weights, weights_sem), sems = rest[:5], rest[5:]
        fetch = pltpu.make_async_copy(weights_any, weights, weights_sem)
        sequence = pl.program_id(0)
        steps = plan_gather(own, gathered, *sems[:3], cut=cut, rows=early)
        copies = plan_exchanges(pieces, mixed, sems[3:])

        @pl.when(sequence == 0)
        def _():
            fetch.start()
            greet(EVERYONE_NEAR)
            steps[0]()
            fetch.wait()

        group = lax.axis_index("outer") * TEAM + sequence
        length = sequence_length(lengths, owners, group)
        proj[0] = jnp.dot(
            normed[0], weights[:, :wide], preferred_element_type=jnp.float32
        )
        head_inputs(proj, gains, cos_ref, sin_ref, queries, keys, values, heads)
        lane = lax.broadcasted_iota(jnp.int32, (BLOCK, HD), 1)
        for step in range(rows // BLOCK):
            at = pl.ds(step * BLOCK, BLOCK)
            seen = pl.ds(0, (step + 1) * BLOCK)
            scores = masked_scores(stack_heads(queries, at, heads), keys[seen], step, length)
            top = jnp.max(scores, axis=-1, keepdims=True)
            exponent = jnp.exp(scores - top)
            total = jnp.sum(exponent, axis=-1, keepdims=True)
            probs = (exponent / total).astype(jnp.bfloat16)
            mixed_values = jnp.dot(probs, values[seen], preferred_element_type=jnp.float32)
            log_total = top + jnp.log(total)
            kept = jnp.zeros((BLOCK, HD), jnp.float32)
            for head in range(heads):
                mine = slice(head * BLOCK, (head + 1) * BLOCK)
                out[0, at, columns(head)] = mixed_values[mine].astype(jnp.bfloat16)
                kept = jnp.where(lane == head, log_total[mine], kept)
            logs[0, at] = kept
        across_columns(out[0], weights, wide, heads * HD, branch)

        @pl.when(sequence == 1)
        def _():
            steps[1]()
            for copy in copies:
                copy.start()

        @pl.when(sequence == 2)
        def _():
            steps[2]()

        @pl.when(sequence == count - 1)
        def _():
            steps[3]()
            for copy in copies:
                copy.wait()

    outs = pl.pallas_call(
        kernel,
        name="attend",
        grid=(count,),
        out_shape=(
            jax.ShapeDtypeStruct((count, rows, wide), jnp.float32),
            jax.ShapeDtypeStruct((count, rows, heads * HD), jnp.bfloat16),
            jax.ShapeDtypeStruct((count, rows, HD), jnp.float32),
            jax.ShapeDtypeStruct((count, rows, width), jnp.bfloat16),
            layer_rows(own_rows, width),
        )
        + tuple(like(piece) for piece in extra),
        in_specs=[
            pl.BlockSpec(memory_space=pltpu.SMEM),
            pl.BlockSpec(memory_space=pltpu.SMEM),
            per_sequence(rows, width),
            anywhere(),
            whole(rows, HD),
            whole(rows, HD),
            whole(*gains.shape),
            whole(own_rows, width),
        ]
        + [whole(*piece.shape) for piece in extra],
        out_specs=(
            per_sequence(rows, wide),
            per_sequence(rows, heads * HD),
            per_sequence(rows, HD),
            per_sequence(rows, width),
            anywhere(),
        )
        + (anywhere(),) * extras,
        scratch_shapes=[
            pltpu.VMEM((heads, rows, HD), jnp.bfloat16),
            pltpu.VMEM((rows, HD), jnp.bfloat16),
            pltpu.VMEM((rows, HD), jnp.bfloat16),
            pltpu.VMEM(weights.shape, weights.dtype),
            pltpu.SemaphoreType.DMA,
        ]
        + gather_scratch()
        + exchange_scratch() * extras,
        compiler_params=params(number),
        cost_estimate=cost_of(50),
    )(lengths, owners, normed, weights, cos_full, sin_full, gains, cotangent, *extra)
    return outs


def team_split(width, outer_count):
    split = TEAM if width // outer_count % (TEAM * HD) == 0 else 1
    return split, width // outer_count // split


def local_first(place):
    near, core, _ = spots()
    other_near, other_core = place // 2, place % 2
    return (near + other_near * (1 - 2 * near)) * CORE + core + other_core * (1 - 2 * core)


def ordered(*shape):
    return pl.BlockSpec((1,) + shape, lambda s: (local_first(s),) + (0,) * len(shape))


def attend_back(
    projected,
    normed,
    attended,
    own_grad,
    logs,
    weights,
    part,
    hidden,
    extra,
    outer_count,
    lengths,
    owners,
    cos_full,
    sin_full,
    gains,
    heads,
    number,
):
    count, rows, wide = projected.shape
    own_rows, width = hidden.shape
    extras = len(extra)
    cut = balanced(own_rows, crossing(extra, width))

    every = wide + heads * HD
    split, share = team_split(width, outer_count)

    def kernel(
        lengths, owners, proj, normed, attended, own_grad, logs, weights_any, cos_ref, sin_ref, gains, part, hidden, *rest
    ):
        pieces, rest = rest[:extras], rest[extras:]
        (gathered, gain_grad, back_part, output, grad_weights), rest = rest[:5], rest[5:]
        mixed, rest = rest[:extras], rest[extras:]
        (queries, keys, values, grad_att, grad_q, grad_k, grad_v_sum, summed), rest = rest[:8], rest[8:]
        (total, held, held_sem, out, grad_v, grad_sem), rest = rest[:6], rest[6:]
        (weights, staged, weights_sem, store_sem), rest = rest[:4], rest[4:]
        sums, sems, rest = rest[:SUM_SCRATCH], rest[SUM_SCRATCH : SUM_SCRATCH + 3], rest[SUM_SCRATCH + 3 :]
        place = pl.program_id(0)
        sequence = local_first(place)
        steps, from_tp, from_near = plan_sum_of(part, total, sums, cut)
        gather = plan_gather(own_grad, gathered, *sems, cut=own_rows // 2, parts=True)
        copies = plan_exchanges(pieces, mixed, rest)
        fetch_weights = pltpu.make_async_copy(weights_any, weights, weights_sem)
        store = pltpu.make_async_copy(staged, grad_weights, store_sem)

        def arrival(which):
            member = local_first(which)
            return pltpu.make_async_copy(
                gathered.at[member // CORE, member % CORE],
                grad_v.at[which % 2],
                grad_sem.at[which % 2],
            )

        fetch = pltpu.make_async_copy(hidden, held, held_sem)

        @pl.when(place == 0)
        def _():
            greet(EVERYONE_NEAR)
            gather[0]()
            steps[0]()
            fetch.start()
            fetch_weights.start()
            gain_grad[...] = jnp.zeros_like(gain_grad)
            summed[...] = jnp.zeros_like(summed)
            gather[1]()
            gather[2]()
            gather[3]()
            arrival(0).start()
            fetch_weights.wait()

        @pl.when(place == 2)
        def _():
            arrival(3).start()

        head_inputs(proj, gains, cos_ref, sin_ref, queries, keys, values, heads)
        grad_k[...] = jnp.zeros_like(grad_k)
        grad_v_sum[...] = jnp.zeros_like(grad_v_sum)
        arrival(place).wait()
        grad = grad_v[place % 2].reshape(rows, width)
        group = lax.axis_index("outer") * TEAM + sequence
        length = sequence_length(lengths, owners, group)
        grad_att[...] = jnp.dot(
            grad, weights[:, wide:], preferred_element_type=jnp.float32
        ).astype(jnp.bfloat16)

        for step in range(rows // BLOCK):
            at = pl.ds(step * BLOCK, BLOCK)
            seen = pl.ds(0, (step + 1) * BLOCK)
            stacked = stack_heads(queries, at, heads)
            above = jnp.concatenate([grad_att[at, columns(head)] for head in range(heads)], axis=0)
            log_total = jnp.concatenate(
                [logs[0, at, head : head + 1] for head in range(heads)], axis=0
            )
            probs = jnp.exp(masked_scores(stacked, keys[seen], step, length) - log_total)
            grad_probs = lax.dot_general(
                above, values[seen], (((1,), (1,)), ((), ())), preferred_element_type=jnp.float32
            )
            inner = jnp.sum(probs * grad_probs, axis=-1, keepdims=True)
            grad_scores = (probs * (grad_probs - inner)).astype(jnp.bfloat16)
            by_query = jnp.dot(grad_scores, keys[seen], preferred_element_type=jnp.float32)
            for head in range(heads):
                grad_q[head, at] = by_query[head * BLOCK : (head + 1) * BLOCK] * (HD ** (-0.5))
            grad_k[seen] += lax.dot_general(
                grad_scores, stacked, (((0,), (0,)), ((), ())), preferred_element_type=jnp.float32
            )
            grad_v_sum[seen] += lax.dot_general(
                probs.astype(jnp.bfloat16),
                above,
                (((0,), (0,)), ((), ())),
                preferred_element_type=jnp.float32,
            )

        def settle(column, gain, value):
            back, by_gain = head_back(
                proj[0, :, columns(column)], gains[HEAD_GAINS + gain : HEAD_GAINS + gain + 1, :], value, cos_ref[...], sin_ref[...]
            )
            out[:, columns(column)] = back.astype(jnp.bfloat16)
            gain_grad[gain] += by_gain.reshape(rows // 8, 8, HD).sum(axis=0)

        for head in range(heads):
            settle(head, 0, grad_q[head])
        settle(heads, 1, grad_k[...] * (HD ** (-0.5)))
        out[:, columns(heads + 1)] = grad_v_sum[...].astype(jnp.bfloat16)

        across_columns(out[...], weights, 0, wide, back_part)

        by_projected, by_attended = out[...].T, attended[0].T
        for start in range(0, width, 512):
            at = pl.ds(start, 512)
            summed[:wide, at] += jnp.dot(
                by_projected, normed[0, :, at], preferred_element_type=jnp.float32
            )
            summed[wide:, at] += jnp.dot(
                by_attended, grad[:, start : start + 512], preferred_element_type=jnp.float32
            )

        @pl.when(place == 0)
        def _():
            gather[5]()
            steps[1]()
            gather[4]()
            arrival(1).start()

        @pl.when(place == 1)
        def _():
            steps[2]()
            for copy in copies:
                copy.start()
            gather[6]()
            arrival(2).start()

        @pl.when(place == count - 1)
        def _():
            for outer in range(outer_count):
                for member in range(split):
                    start = (outer * split + member) * share
                    staged[outer, member] = summed[:, start : start + share].astype(jnp.bfloat16)
            store.start()
            fetch.wait()

            def finish(at):
                value = total[at] + read(from_tp, at) + read(from_near, at)
                output[at] = (held[at] + value).astype(jnp.bfloat16)

            steps[3](finish)
            store.wait()
            for copy in copies:
                copy.wait()

    return pl.pallas_call(
        kernel,
        name="attend_back",
        grid=(count,),
        out_shape=(
            layer_rows(own_rows, width),
            jax.ShapeDtypeStruct((2, 8, HD), jnp.float32),
            jax.ShapeDtypeStruct((count, rows, width), jnp.bfloat16),
            jax.ShapeDtypeStruct((own_rows, width), jnp.bfloat16),
            jax.ShapeDtypeStruct((outer_count, split, every, share), jnp.bfloat16),
        )
        + tuple(like(piece) for piece in extra),
        in_specs=[
            pl.BlockSpec(memory_space=pltpu.SMEM),
            pl.BlockSpec(memory_space=pltpu.SMEM),
            ordered(rows, wide),
            ordered(rows, width),
            ordered(rows, heads * HD),
            whole(own_rows, width),
            ordered(rows, HD),
            anywhere(),
            whole(rows, HD),
            whole(rows, HD),
            whole(*gains.shape),
            anywhere(),
            anywhere(),
        ]
        + [whole(*piece.shape) for piece in extra],
        out_specs=(
            anywhere(),
            pl.BlockSpec((2, 8, HD), lambda s: (0, 0, 0)),
            ordered(rows, width),
            whole(own_rows, width),
            anywhere(),
        )
        + (anywhere(),) * extras,
        scratch_shapes=[
            pltpu.VMEM((heads, rows, HD), jnp.bfloat16),
            pltpu.VMEM((rows, HD), jnp.bfloat16),
            pltpu.VMEM((rows, HD), jnp.bfloat16),
            pltpu.VMEM((rows, heads * HD), jnp.bfloat16),
            pltpu.VMEM((heads, rows, HD), jnp.float32),
            pltpu.VMEM((rows, HD), jnp.float32),
            pltpu.VMEM((rows, HD), jnp.float32),
            pltpu.VMEM((every, width), jnp.float32),
            pltpu.VMEM((own_rows, width), jnp.float32),
            pltpu.VMEM((own_rows, width), jnp.float32),
            pltpu.SemaphoreType.DMA,
            pltpu.VMEM((rows, wide), jnp.bfloat16),
            pltpu.VMEM((2, 2, own_rows, width), jnp.bfloat16),
            pltpu.SemaphoreType.DMA((2,)),
            pltpu.VMEM(weights.shape, weights.dtype),
            pltpu.VMEM((outer_count, split, every, share), jnp.bfloat16),
            pltpu.SemaphoreType.DMA,
            pltpu.SemaphoreType.DMA,
        ]
        + sum_scratch(own_rows, width, cut)
        + gather_scratch()
        + exchange_scratch() * extras,
        compiler_params=params(number),
        cost_estimate=cost_of(50),
    )(
        lengths,
        owners,
        projected,
        normed,
        attended,
        own_grad,
        logs,
        weights,
        cos_full,
        sin_full,
        gains,
        spread(part, own_rows),
        hidden,
        *extra,
    )


def feed(normed, weights, cotangent, gathered, early, outer_count, number):
    count, rows, width = normed.shape
    units = weights.shape[1] // 2
    late = cotangent.shape[0] - early
    split, share = team_split(width, outer_count)
    turns = width // 512

    def kernel(
        normed, weights_any, own, _, product, active, out, grad_weight,
        weights, kept, columns_v, staged, weights_sem, column_sem, piece_sem, *sems
    ):
        fetch = pltpu.make_async_copy(weights_any, weights, weights_sem)
        steps = plan_gather(
            own, out, *sems, cut=balanced(late, 0), base=early, rows=late
        )
        sequence = pl.program_id(0)

        @pl.when(sequence == 0)
        def _():
            fetch.start()
            greet(NEIGHBOURS)
            steps[0]()
            fetch.wait()

        for start in range(0, units, 256):
            gate_at, up_at = pl.ds(start, 256), pl.ds(units + start, 256)
            gate = jnp.dot(normed[0], weights[:, gate_at], preferred_element_type=jnp.float32)
            up = jnp.dot(normed[0], weights[:, up_at], preferred_element_type=jnp.float32)
            product[0, :, gate_at] = gate
            product[0, :, up_at] = up
            active[0, :, gate_at] = swish_product(gate, up).astype(jnp.bfloat16)
        kept[sequence] = active[0]

        for place in (1, 2, 3):

            @pl.when(sequence == count - 4 + place)
            def _(place=place):
                steps[place]()

        @pl.when(sequence == count - 1)
        def _():
            def bring(turn):
                return pltpu.make_async_copy(
                    out.at[:, :, :, :, pl.ds(turn * 512, 512)],
                    columns_v.at[turn % 2],
                    column_sem.at[turn % 2],
                )

            def pieces(turn):
                slot = turn % 2
                return [
                    pltpu.make_async_copy(
                        staged.at[slot, :, pl.ds(place * share, share)],
                        grad_weight.at[turn * (512 // share) + place],
                        piece_sem.at[slot, place],
                    )
                    for place in range(512 // share)
                ]

            for turn in range(min(2, turns)):
                bring(turn).start()
            for turn in range(turns):
                bring(turn).wait()
                turned = lax.dot_general(
                    kept[...].reshape(count * rows, units),
                    columns_v[turn % 2].reshape(count * rows, 512),
                    (((0,), (0,)), ((), ())),
                    preferred_element_type=jnp.float32,
                )
                if turn >= 2:
                    for copy in pieces(turn - 2):
                        copy.wait()
                staged[turn % 2] = turned.astype(jnp.bfloat16)
                for copy in pieces(turn):
                    copy.start()
                if turn + 2 < turns:
                    bring(turn + 2).start()
            for turn in range(max(0, turns - 2), turns):
                for copy in pieces(turn):
                    copy.wait()

    return pl.pallas_call(
        kernel,
        name="feed",
        grid=(count,),
        out_shape=(
            jax.ShapeDtypeStruct((count, rows, 2 * units), jnp.float32),
            jax.ShapeDtypeStruct((count, rows, units), jnp.bfloat16),
            like(gathered),
            jax.ShapeDtypeStruct((outer_count * split, units, share), jnp.bfloat16),
        ),
        in_specs=[
            per_sequence(rows, width),
            anywhere(),
            whole(*cotangent.shape),
            anywhere(),
        ],
        out_specs=(
            per_sequence(rows, 2 * units),
            per_sequence(rows, units),
            anywhere(),
            anywhere(),
        ),
        scratch_shapes=[
            pltpu.VMEM(weights.shape, weights.dtype),
            pltpu.VMEM((count, rows, units), jnp.bfloat16),
            pltpu.VMEM((2,) + gathered.shape[:4] + (512,), jnp.bfloat16),
            pltpu.VMEM((2, units, 512), jnp.bfloat16),
            pltpu.SemaphoreType.DMA,
            pltpu.SemaphoreType.DMA((2,)),
            pltpu.SemaphoreType.DMA((2, 512 // share)),
        ]
        + gather_scratch(),
        input_output_aliases={3: 2},
        compiler_params=params(number),
        cost_estimate=cost_of(28),
    )(normed, weights, cotangent, gathered)


def feed_back(grads, weights, product, normed, outer_count):
    count, rows, width = grads.shape
    units = weights.shape[1]
    split, share = team_split(width, outer_count)
    turns = width // 512

    def kernel(grads, weights, product, normed, by_gate, by_up, grad_weight, kept):
        step = pl.program_id(0)

        @pl.when(step < count)
        def _():
            for start in range(0, units, 256):
                gate_at, up_at = pl.ds(start, 256), pl.ds(units + start, 256)
                grad = jnp.dot(grads[0], weights[:, gate_at], preferred_element_type=jnp.float32)
                gate, up = product[0, :, gate_at], product[0, :, up_at]
                part = jax.nn.sigmoid(gate)
                slope = grad * up * part * (1.0 + gate * (1.0 - part))
                by_gate[0, :, gate_at] = slope.astype(jnp.bfloat16)
                by_up[0, :, gate_at] = (grad * gate * part).astype(jnp.bfloat16)
            kept[step] = by_gate[0]

        @pl.when(step >= count)
        def _():
            turned = lax.dot_general(
                kept[...].reshape(count * rows, units),
                normed[...],
                (((0,), (0,)), ((), ())),
                preferred_element_type=jnp.float32,
            ).astype(jnp.bfloat16)
            for place in range(512 // share):
                grad_weight[place] = turned[:, place * share : (place + 1) * share]

    def early(*shape):
        return pl.BlockSpec((1,) + shape, lambda s: (jnp.minimum(s, count - 1), 0, 0))

    def late(s):
        return jnp.maximum(s - count, 0)

    return pl.pallas_call(
        kernel,
        name="feed_back",
        grid=(count + turns,),
        out_shape=(jax.ShapeDtypeStruct((count, rows, units), jnp.bfloat16),) * 2
        + (jax.ShapeDtypeStruct((width // share, units, share), jnp.bfloat16),),
        in_specs=[
            early(rows, width),
            whole(*weights.shape),
            early(rows, 2 * units),
            pl.BlockSpec((count * rows, 512), lambda s: (0, late(s))),
        ],
        out_specs=(
            early(rows, units),
            early(rows, units),
            pl.BlockSpec((512 // share, units, share), lambda s: (late(s), 0, 0)),
        ),
        scratch_shapes=[pltpu.VMEM((count, rows, units), jnp.bfloat16)],
        compiler_params=pltpu.CompilerParams(vmem_limit_bytes=VMEM_LIMIT),
        cost_estimate=cost_of(28),
    )(grads, weights, product, normed)


def spans(widths, base=0):
    for member in range(TEAM):
        first, inside = base, 0
        for width in widths:
            share = width // TEAM
            yield member, pl.ds(first + member * share, share), pl.ds(inside, share)
            first += width
            inside += share


def by_turned(height, base, widths, source, members=range(TEAM)):
    parts = [part for part in spans(widths, base) if part[0] in members]

    def run(pieces, update):
        for member, across, inside in parts:
            update(pl.ds(0, height), across, pieces[member, inside].T)

    if len(members) == 1:
        columns = parts[0][1]
    else:
        columns = pl.ds(base, sum(widths))
    return source, pl.ds(0, height), columns, run


def by_rows(member, height, width, inside, source):
    at, across = pl.ds(member * height, height), pl.ds(0, width)

    def run(pieces, update):
        if inside is None:
            update(at, across, pieces[member].T)
        else:
            update(at, across, pieces[member, pl.ds(inside, height)])

    return source, at, across, run


def adam_all(sets, pieces, factor, gain_grad, gains, passed):
    jobs = [(place,) + job for place, group in enumerate(sets) for job in group[3]]
    count, total, sources, others = len(jobs), len(sets), len(pieces), len(passed)

    def kernel(*refs):
        inputs, refs = refs[: 3 * total], refs[3 * total :]
        piece_refs, factor, refs = refs[:sources], refs[sources], refs[sources + 1 :]
        (gain_grad, *gains), refs = refs[:4], refs[4:]
        passed, refs = refs[:others], refs[others:]
        outputs, refs = refs[: 4 * total], refs[4 * total :]
        new_gains, refs = refs[:3], refs[3:]
        onward, refs = refs[:others], refs[others:]
        held, refs = refs[: 4 * total], refs[4 * total :]
        held_pieces, refs = refs[:sources], refs[sources:]
        between, (piece_sem, in_sem, out_sem, pass_sem) = refs[:others], refs[others:]
        scale = factor[0:1, 0:1]
        loads = [
            pltpu.make_async_copy(piece_refs[place], held_pieces[place], piece_sem.at[place])
            for place in range(sources)
        ]
        arrivals, stores = [], []
        kept = [
            pltpu.make_async_copy(source, target, pass_sem.at[0, place])
            for place, (source, target) in enumerate(zip(passed, between))
        ]
        kept_on = [
            pltpu.make_async_copy(source, target, pass_sem.at[1, place])
            for place, (source, target) in enumerate(zip(between, onward))
        ]
        for slot, (place, source, at, across, _) in enumerate(jobs):
            arrivals.append(
                [
                    pltpu.make_async_copy(
                        inputs[3 * place + number].at[at, across],
                        held[4 * place + number].at[at, across],
                        in_sem.at[3 * slot + number],
                    )
                    for number in range(3)
                ]
            )
        first_use = {}
        for slot, job in enumerate(jobs):
            first_use.setdefault(job[1], slot)

        def bring(slot):
            if slot < count:
                if first_use[jobs[slot][1]] == slot:
                    loads[jobs[slot][1]].start()
                for copy in arrivals[slot]:
                    copy.start()

        for slot in range(AHEAD):
            bring(slot)
        gain_step = adam_update(
            gains[0][...],
            gain_grad[: gains[0].shape[0]],
            gains[1][...],
            gains[2][...],
            scale,
            0.0,
            gain_rate,
        )
        for target, value in zip(new_gains, gain_step):
            target[...] = value
        for slot, (place, source, at, across, run) in enumerate(jobs):
            weight, moment, square, low = held[4 * place : 4 * place + 4]
            if first_use[source] == slot:
                loads[source].wait()
            for copy in arrivals[slot]:
                copy.wait()
            bring(slot + AHEAD)
            if slot == 0:
                for copy in kept:
                    copy.start()

            def update(rows, columns, gradient):
                where = (rows, columns)
                value, one, two = adam_update(
                    weight[where],
                    gradient.astype(jnp.float32),
                    moment[where],
                    square[where],
                    scale,
                    weight_decay,
                    learn_rate,
                )
                weight[where], moment[where], square[where] = value, one, two
                low[where] = value.astype(jnp.bfloat16)

            run(held_pieces[source], update)
            for number, origin in enumerate((weight, moment, square, low)):
                copy = pltpu.make_async_copy(
                    origin.at[at, across],
                    outputs[4 * place + number].at[at, across],
                    out_sem.at[4 * slot + number],
                )
                copy.start()
                stores.append(copy)
            if slot == 4:
                for arrived, copy in zip(kept, kept_on):
                    arrived.wait()
                    copy.start()
        for copy in stores + kept_on:
            copy.wait()

    args, shapes, scratch = [], [], []
    for weight, moment, square, _ in sets:
        args += [weight, moment, square]
        low = jax.ShapeDtypeStruct(weight.shape, jnp.bfloat16)
        shapes += [like(weight)] * 3 + [low]
        scratch += [pltpu.VMEM(each.shape, each.dtype) for each in (weight, moment, square, low)]
    outs = pl.pallas_call(
        kernel,
        name="adam_all",
        out_shape=tuple(shapes) + (like(gains[0]),) * 3 + tuple(like(each) for each in passed),
        in_specs=[anywhere()] * (3 * total + sources) + [in_vmem()] * 5 + [anywhere()] * others,
        out_specs=(anywhere(),) * (4 * total) + (in_vmem(),) * 3 + (anywhere(),) * others,
        scratch_shapes=scratch
        + [pltpu.VMEM(each.shape, each.dtype) for each in tuple(pieces) + tuple(passed)]
        + [
            pltpu.SemaphoreType.DMA((sources,)),
            pltpu.SemaphoreType.DMA((3 * count,)),
            pltpu.SemaphoreType.DMA((4 * count,)),
            pltpu.SemaphoreType.DMA((2, others)),
        ],
        compiler_params=pltpu.CompilerParams(vmem_limit_bytes=VMEM_LIMIT),
        cost_estimate=cost_of(15),
    )(*args, *pieces, factor, gain_grad, *gains, *passed)
    steps = [outs[4 * place : 4 * place + 4] for place in range(total)]
    return steps + [outs[4 * total : 4 * total + 3], outs[4 * total + 3 :]]


def rotary(count):
    frequency = rope_base ** (-(np.arange(HD // 2) * 2.0 / HD))
    angles = np.arange(count)[:, None] * frequency[None, :]
    cosine, sine = np.cos(angles), np.sin(angles)
    full = [np.concatenate(pair, axis=1) for pair in ((cosine, cosine), (-sine, sine))]
    return [jnp.asarray(table, jnp.float32) for table in full]


def gather_outer(mixed):
    return lax.all_gather(mixed.reshape(-1, mixed.shape[2]), "outer", axis=0, tiled=True)


def team_pieces(summed):
    return summed.reshape(TEAM, -1, summed.shape[-1])


def turned_pieces(summed):
    if summed.shape[1] * TEAM * lax.axis_size("outer") == D:
        return team_pieces(summed)
    return summed.reshape(summed.shape[0], TEAM, -1).transpose(1, 0, 2)


def sum_weight(gradient):
    return lax.psum_scatter(gradient, "outer", scatter_dimension=0, tiled=True)


def after(values, earlier):
    return lax.optimization_barrier((values, earlier))


def adam_update(weight, gradient, moment_one, moment_two, factor, decay_rate, rate_value):
    clipped = gradient * factor
    moment_one = beta_first * moment_one + (1.0 - beta_first) * clipped
    moment_two = beta_second * moment_two + (1.0 - beta_second) * clipped * clipped
    first_fixed = moment_one * (rate_value / (1.0 - beta_first**STEP))
    root_fixed = jnp.sqrt(moment_two) * (1.0 - beta_second**STEP) ** (-0.5)
    kept = weight * (1.0 - rate_value * decay_rate) if decay_rate else weight
    weight = kept - first_fixed / (root_fixed + adam_epsilon)
    return (weight, moment_one, moment_two)


def dot(left, right, contract):
    return lax.dot_general(
        left, right, ((contract[0], contract[1]), ((), ())), preferred_element_type=jnp.float32
    )


def times(left, right):
    return dot(left, right, ((1,), (0,)))


def times_across(left, right):
    return dot(left, right, ((1,), (1,)))


def over_rows(left, right):
    return dot(left, right, ((0,), (0,)))


def local(
    inputs,
    cotangent,
    lengths,
    owners,
    qkv_weight,
    out_weight,
    gate_up_weight,
    down_weight,
    norm_gains,
    qkv_moment,
    out_moment,
    gate_up_moment,
    down_moment,
    gains_moment,
    qkv_square,
    out_square,
    gate_up_square,
    down_square,
    gains_square,
):
    tp_count = lax.axis_size("tp")
    half_rows = inputs.shape[0]
    row_count = half_rows * tp_count
    heads = H // tp_count // TEAM
    hidden_units = FF // tp_count // TEAM
    qkv_widths = (H * HD // tp_count, KV * HD // tp_count, KV * HD // tp_count)
    out_widths = (H * HD // tp_count,)
    part_rows = qkv_weight.shape[0]
    gate_up_widths = (FF // tp_count, FF // tp_count)
    down_widths = (FF // tp_count,)

    cos_full, sin_full = rotary(row_count)
    gains = norm_gains.reshape(-1, HD)

    normed_attn, gate_up_mixed, first_full, grad_low, down_pieces = opening(
        qkv_weight,
        out_weight,
        gate_up_weight,
        down_weight,
        inputs,
        gains,
        cotangent,
        lengths,
        owners,
        lax.axis_size("outer"),
        0,
    )
    gate_up_full = gather_outer(gate_up_mixed)
    early = half_rows // 2 // CHUNK * CHUNK
    projected, attended, logs, attn_branch, grad_all, down_mixed = attend(
        normed_attn.reshape(TEAM, row_count, D),
        first_full,
        grad_low,
        (down_pieces,),
        lengths,
        owners,
        cos_full,
        sin_full,
        gains,
        heads,
        early,
        1,
    )
    down_full = gather_outer(down_mixed)
    hidden, normed_mlp = branch_and_norm(attn_branch, inputs, gains, 2, "branch_and_norm")
    gate_up, activated, grad_all, grad_down = feed(
        normed_mlp.reshape(TEAM, row_count, D),
        gate_up_full,
        grad_low,
        grad_all,
        early,
        lax.axis_size("outer"),
        8,
    )
    down_sum = turned_pieces(sum_weight(grad_down.reshape(-1, grad_down.shape[2])))
    grad_gate, grad_up, grad_gate_weight = feed_back(
        grad_all.reshape(TEAM, row_count, D),
        down_full,
        gate_up,
        normed_mlp,
        lax.axis_size("outer"),
    )
    gate_sum = turned_pieces(
        sum_weight(grad_gate_weight.reshape(-1, grad_gate_weight.shape[2]))
    )
    grad_hidden, grad_mlp_gain, own_grad, mlp_part, grad_up_weight = feed_back_rest(
        grad_gate,
        grad_up,
        gate_up_full,
        activated,
        down_full,
        normed_mlp,
        hidden,
        grad_low,
        gains,
        lax.axis_size("outer"),
        3,
        "feed_back_rest",
    )
    up_sum = turned_pieces(sum_weight(grad_up_weight.reshape(-1, grad_up_weight.shape[2])))
    _, grad_head_gains, grad_normed_attn, output, grad_first, down_mixed = attend_back(
        projected,
        normed_attn.reshape(TEAM, row_count, D),
        attended,
        own_grad,
        logs,
        first_full,
        mlp_part,
        hidden,
        (down_sum,),
        lax.axis_size("outer"),
        lengths,
        owners,
        cos_full,
        sin_full,
        gains,
        heads,
        7,
    )
    grad_first, gate_sum = after(grad_first, gate_sum)
    first_sum = turned_pieces(sum_weight(grad_first.reshape(-1, grad_first.shape[3])))
    input_grad, attn_gain_parts, squares, gate_mixed, up_mixed = norm_back_last(
        grad_normed_attn,
        inputs,
        grad_hidden,
        gains,
        (gate_sum, up_sum),
        (gate_sum, up_sum, down_sum),
        4,
        "norm_back_attn",
    )
    packed, norm_value, factor_tile, first_mixed = total_everywhere(
        attn_gain_parts,
        grad_mlp_gain,
        grad_head_gains,
        squares,
        first_sum,
        lax.axis_size("outer"),
        5,
        "total_everywhere",
    )
    grad_norm = norm_value.reshape(())
    (
        (new_gate_up, new_gate_up_one, new_gate_up_two, gate_up_copy),
        (new_down, new_down_one, new_down_two, down_copy),
        (new_out, new_out_one, new_out_two, out_copy),
        (new_qkv, new_qkv_one, new_qkv_two, qkv_copy),
        new_gains,
        (output, input_grad),
    ) = adam_all(
        [
            (
                gate_up_weight,
                gate_up_moment,
                gate_up_square,
                [
                    by_turned(part_rows, base, gate_up_widths[:1], source, (member,))
                    for source, base in enumerate((0, gate_up_widths[0]))
                    for member in range(TEAM)
                ],
            ),
            (
                down_weight,
                down_moment,
                down_square,
                [by_rows(member, hidden_units, part_rows, 0, 2) for member in range(TEAM)],
            ),
            (
                out_weight,
                out_moment,
                out_square,
                [
                    by_rows(member, heads * HD, part_rows, (heads + 2) * HD, 3)
                    for member in range(TEAM)
                ],
            ),
            (
                qkv_weight,
                qkv_moment,
                qkv_square,
                [by_turned(part_rows, 0, qkv_widths, 3)],
            ),
        ],
        (gate_mixed, up_mixed, down_mixed, first_mixed),
        factor_tile,
        packed,
        [gains] + [each.reshape(-1, HD) for each in (gains_moment, gains_square)],
        (output, input_grad),
    )
    new_gains, new_gains_one, new_gains_two = (each.reshape(-1) for each in new_gains)
    return (
        output,
        input_grad,
        grad_norm,
        new_qkv,
        new_qkv_one,
        new_qkv_two,
        qkv_copy,
        new_out,
        new_out_one,
        new_out_two,
        out_copy,
        new_gate_up,
        new_gate_up_one,
        new_gate_up_two,
        gate_up_copy,
        new_down,
        new_down_one,
        new_down_two,
        down_copy,
        new_gains,
        new_gains_one,
        new_gains_two,
    )


def solution(mesh):
    fsdp_count, tp_count = mesh.shape["fsdp"], mesh.shape["tp"]
    cut = mesh.devices.reshape(fsdp_count // TEAM, NEAR, CORE, tp_count)
    cut_mesh = Mesh(cut, ("outer",) + LAYER)
    fsdp = ("outer", "near", "core")
    rows = P(fsdp + ("tp",), None)
    wide = P(fsdp, "tp")
    tall = P("tp", fsdp)
    weights = (wide, tall, wide, tall, P())
    return jax.shard_map(
        local,
        mesh=cut_mesh,
        in_specs=(rows, rows, P(), P()) + weights * 3,
        out_specs=(rows, rows, P()) + (wide,) * 4 + (tall,) * 4 + (wide,) * 4 + (tall,) * 4 + (P(),) * 3,
        check_vma=False,
    )
```

```python
from functools import partial

import jax
import jax.numpy as jnp
import numpy as np
from jax import lax
from jax.experimental import pallas as pl
from jax.experimental.pallas import tpu as pltpu
from jax.sharding import Mesh, PartitionSpec as P

D = 2048
H = 16
KV = 8
HD = 128
FF = 6144
STEP = 10


norm_epsilon = 1e-06
rope_base = 1000000.0
clip_norm = 1.0
learn_rate = 0.04
gain_rate = 0.8
beta_first = 0.9
beta_second = 0.999
adam_epsilon = 1e-08
weight_decay = 0.1
masked_score = -1e30

NEAR = 2
CORE = 2
TEAM = NEAR * CORE
LAYER = ("near", "core", "tp")
BLOCK = 128
PAD = 8 * 128


def rms_scale(values):
    return lax.rsqrt(jnp.mean(values * values, axis=-1, keepdims=True) + norm_epsilon)


def swish_product(gate_part, up_part):
    return jax.nn.silu(gate_part) * up_part


MESH_ID = pl.DeviceIdType.MESH
VMEM_LIMIT = 60 * 1024 * 1024
CHUNK = 16
GATHER_COPIES = 17
AHEAD = 1000
PART = TEAM // 2
HEAD_GAINS = 2 * D // HD
SUM_COPIES = 12
NEIGHBOURS = ((1, 0, 0), (0, 1, 0), (0, 0, 1))
MATES = ((0, 1, 0), (1, 0, 0), (1, 1, 0))
EVERYONE_NEAR = NEIGHBOURS + ((1, 1, 0),)


def spots():
    return tuple(lax.axis_index(name) for name in LAYER)


def flipped(near_flip, core_flip, tp_flip):
    return {
        name: 1 - spot if flip else spot
        for name, spot, flip in zip(LAYER, spots(), (near_flip, core_flip, tp_flip))
    }


def greet(flips):
    barrier = pltpu.get_barrier_semaphore()
    for flip in flips:
        pl.semaphore_signal(barrier, inc=1, device_id=flipped(*flip), device_id_type=MESH_ID)
    pl.semaphore_wait(barrier, len(flips))


def link(source, target, send_sem, recv_sem, flip):
    return pltpu.make_async_remote_copy(
        src_ref=source,
        dst_ref=target,
        send_sem=send_sem,
        recv_sem=recv_sem,
        device_id=flipped(*flip),
        device_id_type=MESH_ID,
    )


TO_NEAR, TO_CORE, TO_TP = NEIGHBOURS


def plan_exchange(pieces, out, send, recv, own_sem):
    near, core, _ = spots()
    own = near * CORE + core
    copies = []
    for number, flip in enumerate(MATES):
        there = (1 - near if flip[0] else near) * CORE + (1 - core if flip[1] else core)
        copies.append(
            link(pieces.at[there], out.at[own], send.at[number], recv.at[number], flip)
        )
    copies.append(pltpu.make_async_copy(pieces.at[own], out.at[own], own_sem))
    return copies


def exchange_scratch():
    return [
        pltpu.SemaphoreType.DMA((len(MATES),)),
        pltpu.SemaphoreType.DMA((len(MATES),)),
        pltpu.SemaphoreType.DMA,
    ]


def crossing(pieces, width):
    return sum(2 * piece.shape[1] * piece.shape[2] for piece in pieces) // width


def plan_exchanges(pieces, mixed, sems):
    copies = []
    for place, (piece, result) in enumerate(zip(pieces, mixed)):
        copies += plan_exchange(piece, result, *sems[3 * place : 3 * place + 3])
    return copies


def plan_gather(own, out, send, recv, own_sem, cut, base=0, rows=None, parts=False, apart=False):
    near, core, tp = spots()
    rows = own.shape[0] if rows is None else rows
    low, high = pl.ds(base, cut), pl.ds(base + cut, rows - cut)
    all_rows = pl.ds(base, rows)

    def make(number, source, target, flip):
        return link(source, target, send.at[number], recv.at[number], flip)

    def give(number, part, flip):
        return make(number, own.at[part], out.at[near, core, tp, part], flip)

    def relay(number, where_near, where_tp, part, flip):
        ref = out.at[where_near, core, where_tp, part]
        return make(number, ref, ref, flip)

    keep = pltpu.make_async_copy(own.at[all_rows], out.at[near, core, tp, all_rows], own_sem)
    twin_own = give(4, all_rows, TO_CORE)
    first_rows = (rows - cut) // 2 // CHUNK * CHUNK
    high_parts = [
        (pl.ds(base + cut, first_rows), 1, 7, 8),
        (pl.ds(base + cut + first_rows, rows - cut - first_rows), 13, 14, 15),
    ]
    near_high = [give(number, part, TO_NEAR) for part, number, _, _ in high_parts]
    tp_high = give(2, high, TO_TP)
    far_high = [relay(number, 1 - near, tp, part, TO_TP) for part, _, number, _ in high_parts]
    twin_beside = [relay(number, 1 - near, tp, part, TO_CORE) for part, _, _, number in high_parts]
    twin_across = relay(9, near, 1 - tp, high, TO_CORE)
    twin_far = [
        relay(number, 1 - near, 1 - tp, part, TO_CORE)
        for (part, *_), number in zip(high_parts, (12, 16))
    ]
    twins = [twin_own, twin_across] + twin_far + twin_beside
    ways = near_high + far_high + [tp_high]
    if cut:
        tp_low = give(0, low, TO_TP)
        near_low = give(3, low, TO_NEAR)
        far_low = relay(5, near, 1 - tp, low, TO_NEAR)
        twin_across_low = relay(6, near, 1 - tp, low, TO_CORE)
        twin_beside_low = relay(10, 1 - near, tp, low, TO_CORE)
        twin_far_low = relay(11, 1 - near, 1 - tp, low, TO_CORE)
        twins += [twin_across_low, twin_beside_low, twin_far_low]
        ways += [tp_low, near_low, far_low]

    def begin_tp():
        if cut:
            tp_low.start()
        tp_high.start()
        twin_own.start()
        keep.start()

    def begin_near():
        for copy in near_high:
            copy.start()
        if cut:
            near_low.start()

    def begin():
        begin_near()
        begin_tp()

    def pass_on(part):
        near_high[part].wait_recv()
        far_high[part].start()
        twin_beside[part].start()

    def middle():
        if cut:
            tp_low.wait_recv()
            far_low.start()
            twin_across_low.start()
        pass_on(0)
        if not apart:
            pass_on(1)

    def later():
        tp_high.wait_recv()
        twin_across.start()
        if cut:
            near_low.wait_recv()
            twin_beside_low.start()

    def own_there():
        keep.wait()

    def twin_there():
        twin_own.wait_recv()
        twin_across.wait_recv()
        if cut:
            twin_across_low.wait_recv()

    def far_there():
        if cut:
            far_low.wait_recv()
            twin_far_low.start()
        for copy, twin in zip(far_high, twin_far):
            copy.wait_recv()
            twin.start()

    def rest_there():
        for copy in twin_beside + twin_far:
            copy.wait_recv()
        if cut:
            twin_beside_low.wait_recv()
            twin_far_low.wait_recv()
        for copy in ways + twins:
            copy.wait_send()

    def finish():
        own_there()
        twin_there()
        far_there()
        rest_there()

    if parts:
        return [begin, middle, later, own_there, twin_there, far_there, rest_there]
    if apart:
        return [begin_tp, begin_near, middle, partial(pass_on, 1), later, finish]
    return [begin, middle, later, finish]


def balanced(rows, beside):
    return max(0, (rows - beside) // 2 // CHUNK * CHUNK)


def gather_scratch():
    return [
        pltpu.SemaphoreType.DMA((GATHER_COPIES,)),
        pltpu.SemaphoreType.DMA((GATHER_COPIES,)),
        pltpu.SemaphoreType.DMA,
    ]


def add_rows(target, start, count, *sources):
    @pl.loop(0, count // CHUNK)
    def _(step):
        at = pl.ds(pl.multiple_of(start + step * CHUNK, CHUNK), CHUNK)
        total = None
        for source, shift in sources:
            where = pl.ds(pl.multiple_of(start - shift + step * CHUNK, CHUNK), CHUNK)
            value = source[where].astype(jnp.float32)
            total = value if total is None else total + value
        target[at] = total.astype(target.dtype)


def halved(start, count):
    half = count // 2 // CHUNK * CHUNK
    return (start, half), (start + half, count - half)


def plan_sum(outgoing, mine, keep, total, scratch, cut):
    theirs, way_near, way_tp, from_tp, from_near, send, recv = scratch
    rows = total.shape[0]
    low, high = pl.ds(0, cut), pl.ds(cut, rows - cut)

    def make(number, source, target, flip):
        return link(source, target, send.at[number], recv.at[number], flip)

    twin = [make(number, outgoing[number], theirs.at[number], TO_CORE) for number in range(4)]
    far, to_tp, to_near, own = mine
    low_parts = halved(0, cut)
    high_parts = halved(cut, rows - cut)
    far_high = make(5, far.at[high], way_tp, TO_TP)
    tp_high = make(6, to_tp.at[high], from_tp.at[high], TO_TP)
    near_high = [
        make(9 + 2 * place, to_near.at[pl.ds(*part)], from_near.at[pl.ds(*part)], TO_NEAR)
        for place, part in enumerate(high_parts)
    ]
    ways = [far_high, tp_high] + near_high
    tp_low = []
    if cut:
        far_low = make(4, far.at[low], way_near, TO_NEAR)
        near_low = make(7, to_near.at[low], from_near.at[low], TO_NEAR)
        tp_low = [
            make(8 + 2 * place, to_tp.at[pl.ds(*part)], from_tp.at[pl.ds(*part)], TO_TP)
            for place, part in enumerate(low_parts)
        ]
        ways += [far_low, near_low] + tp_low

    def ready(number):
        if keep:
            keep[number].wait()
        twin[number].wait_recv()

    def both(number):
        return (mine[number], 0), (theirs.at[number], 0)

    def begin(numbers=range(4)):
        for number in numbers:
            twin[number].start()
            if keep:
                keep[number].start()

    def send_far():
        ready(0)
        if cut:
            add_rows(far, 0, cut, *both(0))
            far_low.start()
        add_rows(far, cut, rows - cut, *both(0))
        far_high.start()

    def send_tp():
        ready(1)
        add_rows(to_tp, cut, rows - cut, *both(1))
        tp_high.start()

    def send_near():
        ready(2)
        if cut:
            add_rows(to_near, 0, cut, *both(2))
            near_low.start()

    def first():
        send_far()
        send_tp()
        send_near()

    def second():
        if cut:
            far_low.wait_recv()
        far_high.wait_recv()
        for place, part in enumerate(high_parts):
            if cut:
                add_rows(to_tp, *low_parts[place], *both(1), (way_near, 0))
                tp_low[place].start()
            add_rows(to_near, *part, *both(2), (way_tp, cut))
            near_high[place].start()
        ready(3)
        add_rows(total, 0, rows, *both(3))

    def finish(body):
        tp_high.wait_recv()
        if cut:
            near_low.wait_recv()
        for place, part in enumerate(high_parts):
            if cut:
                tp_low[place].wait_recv()
                row_loop(*low_parts[place], body)
            near_high[place].wait_recv()
            row_loop(*part, body)
        for copy in twin + ways:
            copy.wait_send()

    return [begin, first, second, finish], (send_far, send_tp, send_near)


def plan_sum_of(part, total, scratch, cut):
    mine, local_sem, *scratch = scratch
    near, core, tp = spots()
    order = [(1 - near, 1 - tp), (near, 1 - tp), (1 - near, tp), (near, tp)]
    outgoing = [part.at[a, 1 - core, b] for a, b in order]
    keep = [
        pltpu.make_async_copy(part.at[a, core, b], mine.at[number], local_sem.at[number])
        for number, (a, b) in enumerate(order)
    ]
    blocks = [mine.at[number] for number in range(4)]
    steps, _ = plan_sum(outgoing, blocks, keep, total, scratch, cut)
    return steps, scratch[3], scratch[4]


def sum_scratch(rows, width, cut, fetched=True):
    low = jnp.bfloat16
    fetch = [pltpu.VMEM((4, rows, width), low), pltpu.SemaphoreType.DMA((4,))]
    return (fetch if fetched else []) + [
        pltpu.VMEM((4, rows, width), low),
        pltpu.VMEM((max(cut, CHUNK), width), low),
        pltpu.VMEM((rows - cut, width), low),
        pltpu.VMEM((rows, width), low),
        pltpu.VMEM((rows, width), low),
        pltpu.SemaphoreType.DMA((SUM_COPIES,)),
        pltpu.SemaphoreType.DMA((SUM_COPIES,)),
    ]


SUM_SCRATCH = 9
COST_SHARE = 1e5


def params(number):
    return pltpu.CompilerParams(
        collective_id=number, has_side_effects=True, vmem_limit_bytes=VMEM_LIMIT
    )


def cost_of(microseconds):
    return pl.CostEstimate(
        flops=0, bytes_accessed=int(microseconds * COST_SHARE), transcendentals=0
    )


def in_vmem():
    return pl.BlockSpec(memory_space=pltpu.VMEM)


def anywhere():
    return pl.BlockSpec(memory_space=pl.ANY)


def like(array):
    return jax.ShapeDtypeStruct(array.shape, array.dtype)


def layer_rows(rows, width):
    return jax.ShapeDtypeStruct((NEAR, CORE, 2, rows, width), jnp.bfloat16)


def wide_gain(gains, place, width):
    first = place * (width // HD)
    return jnp.concatenate(
        [gains[first + part : first + part + 1] for part in range(width // HD)], axis=1
    )


def row_loop(start, count, body):
    @pl.loop(0, count // CHUNK)
    def _(step):
        body(pl.ds(pl.multiple_of(start + step * CHUNK, CHUNK), CHUNK))


def plan_line(blocks, send, recv, count):
    own = lax.axis_index("outer")

    def handle(side, number, half, there):
        block = blocks.at[there, pl.ds(half * PART, PART)]
        return pltpu.make_async_remote_copy(
            src_ref=block,
            dst_ref=block,
            send_sem=send.at[side, number, half],
            recv_sem=recv.at[side, number, half],
            device_id={"outer": own + 1 if side == 0 else own - 1},
            device_id_type=MESH_ID,
        )

    def message(side, number, half):
        return handle(side, number, half, own - number if side == 0 else own + number)

    def arrival(side, number, half):
        return handle(side, number, half, own - 1 - number if side == 0 else own + 1 + number)

    def sends(side, number):
        if side == 0:
            return (own < count - 1) & (own >= number)
        return (own > 0) & (own + number < count)

    def gets(side, number):
        return own >= number + 1 if side == 0 else own + 1 + number < count

    near = lax.axis_index("near")
    halves = (near, 1 - near)

    def push(number, place):
        for side in range(2):

            @pl.when(sends(side, number))
            def _(side=side):
                message(side, number, halves[place]).start()

    def take(number):
        for half in halves:
            for side in range(2):

                @pl.when(gets(side, number))
                def _(side=side, half=half):
                    arrival(side, number, half).wait_recv()

                if number + 2 < count:

                    @pl.when(sends(side, number + 1))
                    def _(side=side, half=half):
                        message(side, number + 1, half).start()

    def settle():
        for number in range(count - 1):
            for side in range(2):

                @pl.when(sends(side, number))
                def _(side=side, number=number):
                    for half in range(2):
                        message(side, number, half).wait_send()

    return push, take, settle


def greet_all(flips, count, work):
    barrier = pltpu.get_barrier_semaphore()
    own = lax.axis_index("outer")
    for flip in flips:
        pl.semaphore_signal(barrier, inc=1, device_id=flipped(*flip), device_id_type=MESH_ID)
    for there, neighbour in ((own < count - 1, own + 1), (own > 0, own - 1)):

        @pl.when(there)
        def _(neighbour=neighbour):
            pl.semaphore_signal(
                barrier, inc=1, device_id={"outer": neighbour}, device_id_type=MESH_ID
            )

    work()
    beside = jnp.where(own < count - 1, 1, 0) + jnp.where(own > 0, 1, 0)
    pl.semaphore_wait(barrier, len(flips) + beside)


def sequence_length(lengths, owners, group):
    total = jnp.int32(0)
    for place in range(lengths.shape[0]):
        total += jnp.where(owners[place] == group, lengths[place], 0)
    return total


def opening(
    qkv, out_weight, gate_up, down, inputs, gains, cotangent, lengths, owners, outer_count, number
):
    rows, width = inputs.shape
    part_rows, wide = qkv.shape
    tall, units = out_weight.shape[0], down.shape[0]
    widths = (wide // 2, wide // 4, wide // 4)
    first_shape = jax.ShapeDtypeStruct((TEAM, part_rows, (wide + tall) // TEAM), jnp.bfloat16)
    gate_up_shape = jax.ShapeDtypeStruct((TEAM, part_rows, 2 * units // TEAM), jnp.bfloat16)
    down_shape = jax.ShapeDtypeStruct((TEAM, part_rows, units // TEAM), jnp.bfloat16)
    cut = balanced(rows, crossing((first_shape, gate_up_shape), width))

    def kernel(
        lengths, owners, qkv_any, out_any, inputs_any, gains, gate_up, down, cotangent,
        out, mixed, full, low_any, down_any,
        normed, first, pieces, gate_up_v, down_v, cotangent_v,
        qkv, out_weight, inputs, low, down_pieces,
        store_sem, load_sem, line_send, line_recv, *sems
    ):
        near, core, tp = spots()
        outer = lax.axis_index("outer")
        begin_tp, begin_near, middle, middle_rest, later, finish = plan_gather(
            normed, out, *sems[:3], cut=cut, apart=True
        )
        team = plan_exchange(first, full.at[outer], *sems[3:6])
        others = plan_exchange(pieces, mixed, *sems[6:9])
        push, take, settle = plan_line(full, line_send, line_recv, outer_count)
        fetch = [
            pltpu.make_async_copy(source, target, load_sem.at[place])
            for place, (source, target) in enumerate(
                (
                    (cotangent, cotangent_v),
                    (gate_up, gate_up_v),
                    (down, down_v),
                    (qkv_any, qkv),
                    (out_any, out_weight),
                    (inputs_any, inputs),
                )
            )
        ]
        for place in (3, 4, 5, 1, 0, 2):
            fetch[place].start()
        stores = [
            pltpu.make_async_copy(low, low_any, store_sem.at[0]),
            pltpu.make_async_copy(down_pieces, down_any, store_sem.at[1]),
        ]
        gain = wide_gain(gains, 0, width)

        def prepare(at):
            value = inputs[at].astype(jnp.float32)
            normed[at] = (value * rms_scale(value) * gain).astype(jnp.bfloat16)

        def work():
            for copy in fetch[3:]:
                copy.wait()
            for member, across, inside in spans(widths):
                first[member, :, inside] = qkv[:, across].astype(jnp.bfloat16)
            for member in range(TEAM):
                at = pl.ds(member * (tall // TEAM), tall // TEAM)
                first[member, :, wide // TEAM :] = out_weight[at].astype(jnp.bfloat16).T
            row_loop(0, rows, prepare)

        greet_all(EVERYONE_NEAR, outer_count, work)
        for copy in team:
            copy.start()
        begin_tp()
        team[0].wait()
        team[3].wait()
        push(0, 0)
        fetch[1].wait()
        for member, across, inside in spans((units, units)):
            pieces[member, :, inside] = gate_up_v[:, across].astype(jnp.bfloat16)
        for copy in team[1:3]:
            copy.wait()
        push(0, 1)
        begin_near()
        take(0)
        length = sequence_length(lengths, owners, outer * TEAM + near * CORE + core)
        fetch[0].wait()

        def mask(at):
            row = lax.broadcasted_iota(jnp.int32, (CHUNK, width), 0) + at.start + tp * rows
            value = jnp.where(row < length, cotangent_v[at].astype(jnp.float32), 0.0)
            low[at] = value.astype(jnp.bfloat16)

        row_loop(0, rows, mask)
        stores[0].start()
        fetch[2].wait()
        for member in range(TEAM):
            at = pl.ds(member * (units // TEAM), units // TEAM)
            down_pieces[member] = down_v[at].astype(jnp.bfloat16).T
        stores[1].start()
        middle()
        if outer_count > 2:
            take(1)
        middle_rest()
        for copy in others:
            copy.start()
        later()
        for step in range(2, outer_count - 1):
            take(step)
        finish()
        settle()
        for copy in others + stores:
            copy.wait()

    scalars = pl.BlockSpec(memory_space=pltpu.SMEM)
    outs = pl.pallas_call(
        kernel,
        name="opening",
        out_shape=(
            layer_rows(rows, width),
            gate_up_shape,
            jax.ShapeDtypeStruct((outer_count,) + first_shape.shape, jnp.bfloat16),
            jax.ShapeDtypeStruct((rows, width), jnp.bfloat16),
            down_shape,
        ),
        in_specs=[scalars] * 2 + [anywhere()] * 3 + [in_vmem()] + [anywhere()] * 3,
        out_specs=(anywhere(),) * 5,
        scratch_shapes=[
            pltpu.VMEM((rows, width), jnp.bfloat16),
            pltpu.VMEM(first_shape.shape, jnp.bfloat16),
            pltpu.VMEM(gate_up_shape.shape, jnp.bfloat16),
            pltpu.VMEM(gate_up.shape, gate_up.dtype),
            pltpu.VMEM(down.shape, down.dtype),
            pltpu.VMEM(cotangent.shape, cotangent.dtype),
            pltpu.VMEM(qkv.shape, qkv.dtype),
            pltpu.VMEM(out_weight.shape, out_weight.dtype),
            pltpu.VMEM(inputs.shape, inputs.dtype),
            pltpu.VMEM((rows, width), jnp.bfloat16),
            pltpu.VMEM(down_shape.shape, jnp.bfloat16),
            pltpu.SemaphoreType.DMA((2,)),
            pltpu.SemaphoreType.DMA((6,)),
            pltpu.SemaphoreType.DMA((2, outer_count, 2)),
            pltpu.SemaphoreType.DMA((2, outer_count, 2)),
        ]
        + gather_scratch()
        + exchange_scratch() * 2,
        compiler_params=params(number),
        cost_estimate=cost_of(60),
    )(
        lengths,
        owners,
        qkv,
        out_weight,
        inputs,
        gains,
        gate_up,
        down,
        cotangent,
    )
    gathered, mixed, full, low, down_pieces = outs
    return (
        gathered.reshape(-1, width),
        mixed,
        full.reshape(-1, first_shape.shape[2]),
        low,
        down_pieces,
    )


def spread(part, rows):
    return part.reshape(NEAR, CORE, 2, rows, part.shape[-1])


def read(ref, at):
    return ref[at].astype(jnp.float32)


def branch_and_norm(part, residual, gains, number, name):
    rows, width = residual.shape
    cut = rows // 2

    def kernel(part, residual, gains, hidden, out, *scratch):
        gain = wide_gain(gains, 1, width)
        normed, sems = scratch[SUM_SCRATCH], scratch[SUM_SCRATCH + 1 :]
        steps, from_tp, from_near = plan_sum_of(part, hidden, scratch[:SUM_SCRATCH], cut)
        onward = plan_gather(normed, out, *sems, cut=cut)
        greet(NEIGHBOURS)
        for step in steps[:3]:
            step()

        def finish(at):
            value = hidden[at] + read(from_tp, at) + read(from_near, at)
            value = read(residual, at) + value
            hidden[at] = value
            normed[at] = (value * rms_scale(value) * gain).astype(jnp.bfloat16)

        steps[3](finish)
        for step in onward:
            step()

    hidden, full = pl.pallas_call(
        kernel,
        name=name,
        out_shape=(jax.ShapeDtypeStruct((rows, width), jnp.float32), layer_rows(rows, width)),
        in_specs=[anywhere(), in_vmem(), in_vmem()],
        out_specs=(in_vmem(), anywhere()),
        scratch_shapes=sum_scratch(rows, width, cut)
        + [pltpu.VMEM((rows, width), jnp.bfloat16)]
        + gather_scratch(),
        compiler_params=params(number),
        cost_estimate=cost_of(95),
    )(spread(part, rows), residual, gains)
    return hidden, full.reshape(-1, width)


def norm_back(value, gain, grad):
    scale = rms_scale(value)
    scaled = grad * gain
    inner = jnp.mean(scaled * value, axis=-1, keepdims=True)
    return scale * scaled - value * (scale * scale * scale * inner), grad * value * scale


def sequence_order():
    near, core, _ = spots()
    return [
        (near if place >= 2 else 1 - near) * CORE + (core if place % 2 else 1 - core)
        for place in range(TEAM)
    ]


def times_turned(left, weights, target):
    for start in range(0, weights.shape[0], 512):
        at = pl.ds(start, 512)
        target[:, at] = lax.dot_general(
            left, weights[at, :], (((1,), (1,)), ((), ())), preferred_element_type=jnp.float32
        ).astype(target.dtype)


def feed_back_rest(
    grad_gate, grad_up, weights, active, down, normed, values, upstream, gains, outer_count, number, name
):
    rows, width = values.shape
    count, both_rows, units = grad_gate.shape
    all_rows = count * both_rows
    past = all_rows - width
    cut = rows // 2
    split, share = team_split(width, outer_count)
    turns = width // 512

    def kernel(
        gate, ups, weights, active, down, normed, values, upstream, gains,
        result, gain_grad, low, branch, grad_weight, *scratch
    ):
        (grad_v, weights_v, active_v, down_v, values_v, upstream_v, parts, total), rest = (
            scratch[:8],
            scratch[8:],
        )
        (shares, staged, load_sem, store_sem, chunk_sem, piece_sem), sums = rest[:6], rest[6:]
        from_tp, from_near = sums[3], sums[4]
        gain = wide_gain(gains, 1, width)
        near, core, tp = spots()
        members = sequence_order()
        outgoing = [parts.at[place, half] for place, half in ((0, 1 - tp), (2, 1 - tp), (0, tp), (2, tp))]
        mine = [parts.at[place, half] for place, half in ((1, 1 - tp), (3, 1 - tp), (1, tp), (3, tp))]
        steps, (send_far, send_tp, send_near) = plan_sum(outgoing, mine, (), total, sums, cut)
        stores = [
            pltpu.make_async_copy(shares.at[place % 2], branch.at[place], store_sem.at[place])
            for place in range(count)
        ]
        fetch = [
            pltpu.make_async_copy(source, target, load_sem.at[place])
            for place, (source, target) in enumerate(
                (
                    (weights, weights_v),
                    (values, values_v),
                    (upstream, upstream_v),
                    (active, active_v),
                    (down, down_v),
                    (ups, active_v),
                )
            )
        ]
        grads = []
        for place, member in enumerate(members):
            for side, source in enumerate((gate, ups)):
                grads.append(
                    pltpu.make_async_copy(
                        source.at[member],
                        grad_v.at[place % 2, :, :, pl.ds(side * units, units)],
                        load_sem.at[6 + 2 * place + side],
                    )
                )

        def bring(place):
            grads[2 * place].start()
            grads[2 * place + 1].start()

        def brought(place):
            grads[2 * place].wait()
            grads[2 * place + 1].wait()

        def back(place, half):
            times_turned(grad_v[place % 2, half], weights_v, parts.at[place, half])

        def chunk(turn):
            at, slot = pl.ds(turn * 512, 512), turn % 2
            return [
                pltpu.make_async_copy(
                    normed.at[pl.ds(0, width), at],
                    weights_v.at[:, pl.ds(slot * 1024, 512)],
                    chunk_sem.at[slot, 0],
                ),
                pltpu.make_async_copy(
                    normed.at[pl.ds(width, past), at],
                    weights_v.at[pl.ds(slot * past, past), pl.ds(512, 512)],
                    chunk_sem.at[slot, 1],
                ),
            ]

        def pieces(turn):
            slot = turn % 2
            return [
                pltpu.make_async_copy(
                    staged.at[slot, :, pl.ds(place * share, share)],
                    grad_weight.at[turn * (512 // share) + place],
                    piece_sem.at[slot, place],
                )
                for place in range(512 // share)
            ]

        fetch[0].start()
        bring(0)
        bring(1)
        greet(NEIGHBOURS)
        fetch[0].wait()
        brought(0)
        back(0, 1 - tp)
        steps[0]((0,))
        brought(1)
        back(1, 1 - tp)
        send_far()
        back(0, tp)
        steps[0]((2,))
        bring(2)
        for place in (3, 4, 1, 2):
            fetch[place].start()
        back(1, tp)
        send_near()
        bring(3)
        brought(2)
        back(2, 1 - tp)
        steps[0]((1,))
        brought(3)
        back(3, 1 - tp)
        send_tp()
        back(2, tp)
        steps[0]((3,))
        back(3, tp)
        for turn in (0, 1):
            for copy in chunk(turn):
                copy.start()
        fetch[3].wait()
        fetch[4].wait()
        for place in range(count):
            if place >= 2:
                stores[place - 2].wait()
            for half in range(2):
                times_turned(active_v[place, half], down_v, shares.at[place % 2, half])
            stores[place].start()
        fetch[5].start()
        steps[2]()
        fetch[5].wait()
        for turn in range(turns):
            slot = turn % 2
            for copy in chunk(turn):
                copy.wait()
            left = active_v[...].reshape(all_rows, units)
            product = lax.dot_general(
                left[:width],
                weights_v[:, slot * 1024 : slot * 1024 + 512],
                (((0,), (0,)), ((), ())),
                preferred_element_type=jnp.float32,
            ) + lax.dot_general(
                left[width:],
                weights_v[slot * past : (slot + 1) * past, 512:1024],
                (((0,), (0,)), ((), ())),
                preferred_element_type=jnp.float32,
            )
            if turn >= 2:
                for copy in pieces(turn - 2):
                    copy.wait()
            staged[slot] = product.astype(staged.dtype)
            for copy in pieces(turn):
                copy.start()
            if turn + 2 < turns:
                for copy in chunk(turn + 2):
                    copy.start()
        fetch[1].wait()
        fetch[2].wait()
        gain_grad[...] = jnp.zeros_like(gain_grad)

        def finish(at):
            grad = total[at] + read(from_tp, at) + read(from_near, at)
            turned, by_gain = norm_back(values_v[at], gain, grad)
            gain_grad[...] += by_gain.reshape(CHUNK // 8, 8, width).sum(axis=0)
            value = read(upstream_v, at) + turned
            total[at] = value
            low[at] = value.astype(jnp.bfloat16)

        steps[3](finish)
        store = pltpu.make_async_copy(total, result, store_sem.at[count])
        store.start()
        for turn in range(max(0, turns - 2), turns):
            for copy in pieces(turn):
                copy.wait()
        for copy in [store] + stores[2:]:
            copy.wait()

    low_type = jnp.bfloat16
    halves = (count, 2, rows, units)
    result, gain_grad, rounded, branch, grad_weight = pl.pallas_call(
        kernel,
        name=name,
        out_shape=(
            jax.ShapeDtypeStruct((rows, width), jnp.float32),
            jax.ShapeDtypeStruct((8, width), jnp.float32),
            jax.ShapeDtypeStruct((rows, width), low_type),
            jax.ShapeDtypeStruct((count, 2, rows, width), low_type),
            jax.ShapeDtypeStruct((outer_count * split, units, share), low_type),
        ),
        in_specs=[anywhere()] * 8 + [in_vmem()],
        out_specs=(anywhere(), in_vmem(), in_vmem(), anywhere(), anywhere()),
        scratch_shapes=[
            pltpu.VMEM((2, 2, rows, 2 * units), low_type),
            pltpu.VMEM(weights.shape, low_type),
            pltpu.VMEM(halves, low_type),
            pltpu.VMEM(down.shape, low_type),
            pltpu.VMEM((rows, width), values.dtype),
            pltpu.VMEM((rows, width), upstream.dtype),
            pltpu.VMEM((count, 2, rows, width), low_type),
            pltpu.VMEM((rows, width), jnp.float32),
            pltpu.VMEM((2, 2, rows, width), low_type),
            pltpu.VMEM((2, units, 512), low_type),
            pltpu.SemaphoreType.DMA((6 + 2 * count,)),
            pltpu.SemaphoreType.DMA((count + 1,)),
            pltpu.SemaphoreType.DMA((2, 2)),
            pltpu.SemaphoreType.DMA((2, 512 // share)),
        ]
        + sum_scratch(rows, width, cut, fetched=False),
        compiler_params=params(number),
        cost_estimate=cost_of(60),
    )(
        grad_gate.reshape(halves),
        grad_up.reshape(halves),
        weights,
        active.reshape(halves),
        down,
        normed,
        values,
        upstream,
        gains,
    )
    return result, gain_grad, rounded, branch.reshape(-1, width), grad_weight


def square_sum(values):
    values = values.reshape(-1, values.shape[-1]).astype(jnp.float32)
    return jnp.sum(values * values, keepdims=True)


def corner(value):
    row = lax.broadcasted_iota(jnp.int32, (8, HD), 0)
    column = lax.broadcasted_iota(jnp.int32, (8, HD), 1)
    return jnp.where((row == 0) & (column == 0), value, 0.0)


def norm_back_last(part, values, upstream, gains, extra, squared, number, name):
    rows, width = values.shape
    extras, count = len(extra), len(squared)
    cut = balanced(rows, crossing(extra, width))

    def kernel(part, values, upstream, gains, *rest):
        gain = wide_gain(gains, 0, width)
        pieces, rest = rest[:extras], rest[extras:]
        squared, (result, gain_grad, squares), rest = (
            rest[:count],
            rest[count : count + 3],
            rest[count + 3 :],
        )
        mixed, rest = rest[:extras], rest[extras:]
        sums, rest = rest[:SUM_SCRATCH], rest[SUM_SCRATCH:]
        (total, values_v, upstream_v, load_sem), rest = rest[:4], rest[4:]
        squared_v, sems = rest[:count], rest[count:]
        steps, from_tp, from_near = plan_sum_of(part, total, sums, cut)
        copies = plan_exchanges(pieces, mixed, sems)
        fetch = [
            pltpu.make_async_copy(source, target, load_sem.at[place])
            for place, (source, target) in enumerate(
                zip((values, upstream) + tuple(squared), (values_v, upstream_v) + tuple(squared_v))
            )
        ]
        greet(EVERYONE_NEAR)
        steps[0]()
        for copy in copies:
            copy.start()
        for copy in fetch:
            copy.start()
        steps[1]()
        for copy in fetch:
            copy.wait()
        squares[...] = corner(sum(square_sum(ref[...]) for ref in squared_v))
        steps[2]()
        gain_grad[...] = jnp.zeros_like(gain_grad)

        def finish(at):
            grad = total[at] + read(from_tp, at) + read(from_near, at)
            back, by_gain = norm_back(read(values_v, at), gain, grad)
            gain_grad[...] += by_gain.reshape(CHUNK // 8, 8, width).sum(axis=0)
            result[at] = (upstream_v[at] + back).astype(jnp.bfloat16)

        steps[3](finish)
        for copy in copies:
            copy.wait()

    return pl.pallas_call(
        kernel,
        name=name,
        out_shape=(
            jax.ShapeDtypeStruct((rows, width), jnp.bfloat16),
            jax.ShapeDtypeStruct((8, width), jnp.float32),
            jax.ShapeDtypeStruct((8, HD), jnp.float32),
        )
        + tuple(like(piece) for piece in extra),
        in_specs=[anywhere()] * 3 + [in_vmem()] * (1 + extras) + [anywhere()] * count,
        out_specs=(in_vmem(), in_vmem(), in_vmem()) + (anywhere(),) * extras,
        scratch_shapes=sum_scratch(rows, width, cut)
        + [
            pltpu.VMEM((rows, width), jnp.float32),
            pltpu.VMEM((rows, width), values.dtype),
            pltpu.VMEM((rows, width), upstream.dtype),
            pltpu.SemaphoreType.DMA((2 + count,)),
        ]
        + [pltpu.VMEM(each.shape, each.dtype) for each in squared]
        + exchange_scratch() * extras,
        compiler_params=params(number),
        cost_estimate=cost_of(65),
    )(spread(part, rows), values, upstream, gains, *extra, *squared)


def total_everywhere(first, second, heads, squares, pieces, outer_count, number, name):
    used = 2 * first.shape[1] // HD + heads.shape[0]
    gains = used + -used % 8
    shape = (gains + 8, HD)
    width = first.shape[1]

    def kernel(first, second, heads, squares, pieces, out, norm, factor, mixed, layer, outers, send, recv, *sems):
        near, core, tp = spots()
        outer = lax.axis_index("outer")
        partners = [
            flipped(a, b, c)
            for a in range(NEAR)
            for b in range(CORE)
            for c in range(2)
            if a + b + c
        ]
        partners += [{"outer": (outer + step) % outer_count} for step in range(1, outer_count)]
        barrier = pltpu.get_barrier_semaphore()
        for partner in partners:
            pl.semaphore_signal(barrier, inc=1, device_id=partner, device_id_type=MESH_ID)
        mine = near * (CORE * 2) + core * 2 + tp
        layer[mine, gains - 8 : gains] = jnp.zeros((8, HD), jnp.float32)
        layer[mine, gains:] = squares[...] + corner(square_sum(pieces[...]))
        place = 0
        for source in (first, second):
            sums = jnp.sum(source[...], axis=0, keepdims=True)
            for start in range(0, width, HD):
                layer[mine, place : place + 1] = sums[:, start : start + HD]
                place += 1
        for head in range(heads.shape[0]):
            layer[mine, place : place + 1] = jnp.sum(heads[head], axis=0, keepdims=True)
            place += 1
        pl.semaphore_wait(barrier, len(partners))

        def share(slots, mine, first, count):
            copies = []
            for number in range(first, first + count):
                copy = pltpu.make_async_remote_copy(
                    src_ref=slots.at[mine],
                    dst_ref=slots.at[mine],
                    send_sem=send.at[number],
                    recv_sem=recv.at[number],
                    device_id=partners[number],
                    device_id_type=MESH_ID,
                )
                copy.start()
                copies.append(copy)
            return copies

        others = plan_exchange(pieces, mixed, *sems)
        copies = share(layer, mine, 0, 7)
        for copy in others:
            copy.start()
        for copy in copies:
            copy.wait()
        total = layer[0]
        for slot in range(1, 8):
            total = total + layer[slot]
        outers[outer] = total
        for copy in share(outers, outer, 7, outer_count - 1):
            copy.wait()
        total = outers[0]
        for slot in range(1, outer_count):
            total = total + outers[slot]
        out[...] = total
        gain_part = total[:gains]
        root = jnp.sqrt(
            jnp.sum(gain_part * gain_part, keepdims=True) + jnp.sum(total[gains:], keepdims=True)
        )
        norm[...] = root
        factor[...] = jnp.broadcast_to(
            jnp.minimum(1.0, clip_norm / (root + 1e-06)), factor.shape
        )
        for copy in others:
            copy.wait()

    tile = jax.ShapeDtypeStruct((8, HD), jnp.float32)
    return pl.pallas_call(
        kernel,
        name=name,
        out_shape=(
            jax.ShapeDtypeStruct(shape, jnp.float32),
            jax.ShapeDtypeStruct((1, 1), jnp.float32),
            tile,
            like(pieces),
        ),
        in_specs=[in_vmem()] * 5,
        out_specs=(in_vmem(), in_vmem(), in_vmem(), anywhere()),
        scratch_shapes=[
            pltpu.VMEM((8,) + shape, jnp.float32),
            pltpu.VMEM((outer_count,) + shape, jnp.float32),
            pltpu.SemaphoreType.DMA((6 + outer_count,)),
            pltpu.SemaphoreType.DMA((6 + outer_count,)),
        ]
        + exchange_scratch(),
        compiler_params=params(number),
        cost_estimate=cost_of(16),
    )(first, second, heads, squares, pieces)


def head_scale(raw, gain, cos_full, sin_full):
    normed = raw * rms_scale(raw) * gain
    return (normed * cos_full + pltpu.roll(normed, HD // 2, 1) * sin_full).astype(jnp.bfloat16)


def head_back(raw, gain, grad, cos_full, sin_full):
    grad = grad * cos_full - pltpu.roll(grad, HD // 2, 1) * sin_full
    return norm_back(raw, gain, grad)


def columns(index):
    return pl.ds(index * HD, HD)


def head_inputs(proj, gains, cos_ref, sin_ref, queries, keys, values, heads):
    for head in range(heads):
        queries[head] = head_scale(
            proj[0, :, columns(head)], gains[HEAD_GAINS : HEAD_GAINS + 1, :], cos_ref[...], sin_ref[...]
        )
    keys[...] = head_scale(
        proj[0, :, columns(heads)], gains[HEAD_GAINS + 1 : HEAD_GAINS + 2, :], cos_ref[...], sin_ref[...]
    )
    values[...] = proj[0, :, columns(heads + 1)].astype(jnp.bfloat16)


def masked_scores(stacked, keys, step, length):
    scores = lax.dot_general(
        stacked, keys, (((1,), (1,)), ((), ())), preferred_element_type=jnp.float32
    ) * (HD ** (-0.5))
    row = lax.broadcasted_iota(jnp.int32, scores.shape, 0) % BLOCK + step * BLOCK
    column = lax.broadcasted_iota(jnp.int32, scores.shape, 1)
    return jnp.where((column <= row) & (column < length), scores, masked_score)


def stack_heads(ref, at, heads):
    return jnp.concatenate([ref[head, at] for head in range(heads)], axis=0)


def per_sequence(*shape):
    return pl.BlockSpec((1,) + shape, lambda s: (s,) + (0,) * len(shape))


def whole(*shape):
    return pl.BlockSpec(shape, lambda s: (0,) * len(shape), pipeline_mode=pl.Buffered(1))


def across_columns(left, weights, first, width, out):
    total = weights.shape[0]
    for start in range(0, total, 512):
        at = pl.ds(start, 512)
        out[0, :, at] = lax.dot_general(
            left,
            weights[at, first : first + width],
            (((1,), (1,)), ((), ())),
            preferred_element_type=jnp.float32,
        ).astype(out.dtype)


def attend(normed, weights, cotangent, extra, lengths, owners, cos_full, sin_full, gains, heads, early, number):
    count, rows, width = normed.shape
    wide = (heads + 2) * HD
    extras = len(extra)
    own_rows = cotangent.shape[0]
    cut = balanced(early, crossing(extra, width))

    def kernel(lengths, owners, normed, weights_any, cos_ref, sin_ref, gains, own, *rest):
        pieces, rest = rest[:extras], rest[extras:]
        (proj, out, logs, branch, gathered), rest = rest[:5], rest[5:]
        mixed, rest = rest[:extras], rest[extras:]
        (queries, keys, values, weights, weights_sem), sems = rest[:5], rest[5:]
        fetch = pltpu.make_async_copy(weights_any, weights, weights_sem)
        sequence = pl.program_id(0)
        steps = plan_gather(own, gathered, *sems[:3], cut=cut, rows=early)
        copies = plan_exchanges(pieces, mixed, sems[3:])

        @pl.when(sequence == 0)
        def _():
            fetch.start()
            greet(EVERYONE_NEAR)
            steps[0]()
            fetch.wait()

        group = lax.axis_index("outer") * TEAM + sequence
        length = sequence_length(lengths, owners, group)
        proj[0] = jnp.dot(
            normed[0], weights[:, :wide], preferred_element_type=jnp.float32
        )
        head_inputs(proj, gains, cos_ref, sin_ref, queries, keys, values, heads)
        lane = lax.broadcasted_iota(jnp.int32, (BLOCK, HD), 1)
        for step in range(rows // BLOCK):
            at = pl.ds(step * BLOCK, BLOCK)
            seen = pl.ds(0, (step + 1) * BLOCK)
            scores = masked_scores(stack_heads(queries, at, heads), keys[seen], step, length)
            top = jnp.max(scores, axis=-1, keepdims=True)
            exponent = jnp.exp(scores - top)
            total = jnp.sum(exponent, axis=-1, keepdims=True)
            probs = (exponent / total).astype(jnp.bfloat16)
            mixed_values = jnp.dot(probs, values[seen], preferred_element_type=jnp.float32)
            log_total = top + jnp.log(total)
            kept = jnp.zeros((BLOCK, HD), jnp.float32)
            for head in range(heads):
                mine = slice(head * BLOCK, (head + 1) * BLOCK)
                out[0, at, columns(head)] = mixed_values[mine].astype(jnp.bfloat16)
                kept = jnp.where(lane == head, log_total[mine], kept)
            logs[0, at] = kept
        across_columns(out[0], weights, wide, heads * HD, branch)

        @pl.when(sequence == 1)
        def _():
            steps[1]()
            for copy in copies:
                copy.start()

        @pl.when(sequence == 2)
        def _():
            steps[2]()

        @pl.when(sequence == count - 1)
        def _():
            steps[3]()
            for copy in copies:
                copy.wait()

    outs = pl.pallas_call(
        kernel,
        name="attend",
        grid=(count,),
        out_shape=(
            jax.ShapeDtypeStruct((count, rows, wide), jnp.float32),
            jax.ShapeDtypeStruct((count, rows, heads * HD), jnp.bfloat16),
            jax.ShapeDtypeStruct((count, rows, HD), jnp.float32),
            jax.ShapeDtypeStruct((count, rows, width), jnp.bfloat16),
            layer_rows(own_rows, width),
        )
        + tuple(like(piece) for piece in extra),
        in_specs=[
            pl.BlockSpec(memory_space=pltpu.SMEM),
            pl.BlockSpec(memory_space=pltpu.SMEM),
            per_sequence(rows, width),
            anywhere(),
            whole(rows, HD),
            whole(rows, HD),
            whole(*gains.shape),
            whole(own_rows, width),
        ]
        + [whole(*piece.shape) for piece in extra],
        out_specs=(
            per_sequence(rows, wide),
            per_sequence(rows, heads * HD),
            per_sequence(rows, HD),
            per_sequence(rows, width),
            anywhere(),
        )
        + (anywhere(),) * extras,
        scratch_shapes=[
            pltpu.VMEM((heads, rows, HD), jnp.bfloat16),
            pltpu.VMEM((rows, HD), jnp.bfloat16),
            pltpu.VMEM((rows, HD), jnp.bfloat16),
            pltpu.VMEM(weights.shape, weights.dtype),
            pltpu.SemaphoreType.DMA,
        ]
        + gather_scratch()
        + exchange_scratch() * extras,
        compiler_params=params(number),
        cost_estimate=cost_of(50),
    )(lengths, owners, normed, weights, cos_full, sin_full, gains, cotangent, *extra)
    return outs


def team_split(width, outer_count):
    split = TEAM if width // outer_count % (TEAM * HD) == 0 else 1
    return split, width // outer_count // split


def local_first(place):
    near, core, _ = spots()
    other_near, other_core = place // 2, place % 2
    return (near + other_near * (1 - 2 * near)) * CORE + core + other_core * (1 - 2 * core)


def ordered(*shape):
    return pl.BlockSpec((1,) + shape, lambda s: (local_first(s),) + (0,) * len(shape))


def attend_back(
    projected,
    normed,
    attended,
    own_grad,
    logs,
    weights,
    part,
    hidden,
    extra,
    outer_count,
    lengths,
    owners,
    cos_full,
    sin_full,
    gains,
    heads,
    number,
):
    count, rows, wide = projected.shape
    own_rows, width = hidden.shape
    extras = len(extra)
    cut = balanced(own_rows, crossing(extra, width))

    every = wide + heads * HD
    split, share = team_split(width, outer_count)

    def kernel(
        lengths, owners, proj, normed, attended, own_grad, logs, weights_any, cos_ref, sin_ref, gains, part, hidden, *rest
    ):
        pieces, rest = rest[:extras], rest[extras:]
        (gathered, gain_grad, back_part, output, grad_weights), rest = rest[:5], rest[5:]
        mixed, rest = rest[:extras], rest[extras:]
        (queries, keys, values, grad_att, grad_q, grad_k, grad_v_sum, summed), rest = rest[:8], rest[8:]
        (total, held, held_sem, out, grad_v, grad_sem), rest = rest[:6], rest[6:]
        (weights, staged, weights_sem, store_sem), rest = rest[:4], rest[4:]
        sums, sems, rest = rest[:SUM_SCRATCH], rest[SUM_SCRATCH : SUM_SCRATCH + 3], rest[SUM_SCRATCH + 3 :]
        place = pl.program_id(0)
        sequence = local_first(place)
        steps, from_tp, from_near = plan_sum_of(part, total, sums, cut)
        gather = plan_gather(own_grad, gathered, *sems, cut=own_rows // 2, parts=True)
        copies = plan_exchanges(pieces, mixed, rest)
        fetch_weights = pltpu.make_async_copy(weights_any, weights, weights_sem)
        store = pltpu.make_async_copy(staged, grad_weights, store_sem)

        def arrival(which):
            member = local_first(which)
            return pltpu.make_async_copy(
                gathered.at[member // CORE, member % CORE],
                grad_v.at[which % 2],
                grad_sem.at[which % 2],
            )

        fetch = pltpu.make_async_copy(hidden, held, held_sem)

        @pl.when(place == 0)
        def _():
            greet(EVERYONE_NEAR)
            gather[0]()
            steps[0]()
            fetch.start()
            fetch_weights.start()
            gain_grad[...] = jnp.zeros_like(gain_grad)
            summed[...] = jnp.zeros_like(summed)
            gather[1]()
            gather[2]()
            gather[3]()
            arrival(0).start()
            fetch_weights.wait()

        @pl.when(place == 2)
        def _():
            arrival(3).start()

        head_inputs(proj, gains, cos_ref, sin_ref, queries, keys, values, heads)
        grad_k[...] = jnp.zeros_like(grad_k)
        grad_v_sum[...] = jnp.zeros_like(grad_v_sum)
        arrival(place).wait()
        grad = grad_v[place % 2].reshape(rows, width)
        group = lax.axis_index("outer") * TEAM + sequence
        length = sequence_length(lengths, owners, group)
        grad_att[...] = jnp.dot(
            grad, weights[:, wide:], preferred_element_type=jnp.float32
        ).astype(jnp.bfloat16)

        for step in range(rows // BLOCK):
            at = pl.ds(step * BLOCK, BLOCK)
            seen = pl.ds(0, (step + 1) * BLOCK)
            stacked = stack_heads(queries, at, heads)
            above = jnp.concatenate([grad_att[at, columns(head)] for head in range(heads)], axis=0)
            log_total = jnp.concatenate(
                [logs[0, at, head : head + 1] for head in range(heads)], axis=0
            )
            probs = jnp.exp(masked_scores(stacked, keys[seen], step, length) - log_total)
            grad_probs = lax.dot_general(
                above, values[seen], (((1,), (1,)), ((), ())), preferred_element_type=jnp.float32
            )
            inner = jnp.sum(probs * grad_probs, axis=-1, keepdims=True)
            grad_scores = (probs * (grad_probs - inner)).astype(jnp.bfloat16)
            by_query = jnp.dot(grad_scores, keys[seen], preferred_element_type=jnp.float32)
            for head in range(heads):
                grad_q[head, at] = by_query[head * BLOCK : (head + 1) * BLOCK] * (HD ** (-0.5))
            grad_k[seen] += lax.dot_general(
                grad_scores, stacked, (((0,), (0,)), ((), ())), preferred_element_type=jnp.float32
            )
            grad_v_sum[seen] += lax.dot_general(
                probs.astype(jnp.bfloat16),
                above,
                (((0,), (0,)), ((), ())),
                preferred_element_type=jnp.float32,
            )

        def settle(column, gain, value):
            back, by_gain = head_back(
                proj[0, :, columns(column)], gains[HEAD_GAINS + gain : HEAD_GAINS + gain + 1, :], value, cos_ref[...], sin_ref[...]
            )
            out[:, columns(column)] = back.astype(jnp.bfloat16)
            gain_grad[gain] += by_gain.reshape(rows // 8, 8, HD).sum(axis=0)

        for head in range(heads):
            settle(head, 0, grad_q[head])
        settle(heads, 1, grad_k[...] * (HD ** (-0.5)))
        out[:, columns(heads + 1)] = grad_v_sum[...].astype(jnp.bfloat16)

        across_columns(out[...], weights, 0, wide, back_part)

        by_projected, by_attended = out[...].T, attended[0].T
        for start in range(0, width, 512):
            at = pl.ds(start, 512)
            summed[:wide, at] += jnp.dot(
                by_projected, normed[0, :, at], preferred_element_type=jnp.float32
            )
            summed[wide:, at] += jnp.dot(
                by_attended, grad[:, start : start + 512], preferred_element_type=jnp.float32
            )

        @pl.when(place == 0)
        def _():
            gather[5]()
            steps[1]()
            gather[4]()
            arrival(1).start()

        @pl.when(place == 1)
        def _():
            steps[2]()
            for copy in copies:
                copy.start()
            gather[6]()
            arrival(2).start()

        @pl.when(place == count - 1)
        def _():
            for outer in range(outer_count):
                for member in range(split):
                    start = (outer * split + member) * share
                    staged[outer, member] = summed[:, start : start + share].astype(jnp.bfloat16)
            store.start()
            fetch.wait()

            def finish(at):
                value = total[at] + read(from_tp, at) + read(from_near, at)
                output[at] = (held[at] + value).astype(jnp.bfloat16)

            steps[3](finish)
            store.wait()
            for copy in copies:
                copy.wait()

    return pl.pallas_call(
        kernel,
        name="attend_back",
        grid=(count,),
        out_shape=(
            layer_rows(own_rows, width),
            jax.ShapeDtypeStruct((2, 8, HD), jnp.float32),
            jax.ShapeDtypeStruct((count, rows, width), jnp.bfloat16),
            jax.ShapeDtypeStruct((own_rows, width), jnp.bfloat16),
            jax.ShapeDtypeStruct((outer_count, split, every, share), jnp.bfloat16),
        )
        + tuple(like(piece) for piece in extra),
        in_specs=[
            pl.BlockSpec(memory_space=pltpu.SMEM),
            pl.BlockSpec(memory_space=pltpu.SMEM),
            ordered(rows, wide),
            ordered(rows, width),
            ordered(rows, heads * HD),
            whole(own_rows, width),
            ordered(rows, HD),
            anywhere(),
            whole(rows, HD),
            whole(rows, HD),
            whole(*gains.shape),
            anywhere(),
            anywhere(),
        ]
        + [whole(*piece.shape) for piece in extra],
        out_specs=(
            anywhere(),
            pl.BlockSpec((2, 8, HD), lambda s: (0, 0, 0)),
            ordered(rows, width),
            whole(own_rows, width),
            anywhere(),
        )
        + (anywhere(),) * extras,
        scratch_shapes=[
            pltpu.VMEM((heads, rows, HD), jnp.bfloat16),
            pltpu.VMEM((rows, HD), jnp.bfloat16),
            pltpu.VMEM((rows, HD), jnp.bfloat16),
            pltpu.VMEM((rows, heads * HD), jnp.bfloat16),
            pltpu.VMEM((heads, rows, HD), jnp.float32),
            pltpu.VMEM((rows, HD), jnp.float32),
            pltpu.VMEM((rows, HD), jnp.float32),
            pltpu.VMEM((every, width), jnp.float32),
            pltpu.VMEM((own_rows, width), jnp.float32),
            pltpu.VMEM((own_rows, width), jnp.float32),
            pltpu.SemaphoreType.DMA,
            pltpu.VMEM((rows, wide), jnp.bfloat16),
            pltpu.VMEM((2, 2, own_rows, width), jnp.bfloat16),
            pltpu.SemaphoreType.DMA((2,)),
            pltpu.VMEM(weights.shape, weights.dtype),
            pltpu.VMEM((outer_count, split, every, share), jnp.bfloat16),
            pltpu.SemaphoreType.DMA,
            pltpu.SemaphoreType.DMA,
        ]
        + sum_scratch(own_rows, width, cut)
        + gather_scratch()
        + exchange_scratch() * extras,
        compiler_params=params(number),
        cost_estimate=cost_of(50),
    )(
        lengths,
        owners,
        projected,
        normed,
        attended,
        own_grad,
        logs,
        weights,
        cos_full,
        sin_full,
        gains,
        spread(part, own_rows),
        hidden,
        *extra,
    )


def feed(normed, weights, cotangent, gathered, early, outer_count, number):
    count, rows, width = normed.shape
    units = weights.shape[1] // 2
    late = cotangent.shape[0] - early
    split, share = team_split(width, outer_count)
    turns = width // 512

    def kernel(
        normed, weights_any, own, _, product, active, out, grad_weight,
        weights, kept, columns_v, staged, weights_sem, column_sem, piece_sem, *sems
    ):
        fetch = pltpu.make_async_copy(weights_any, weights, weights_sem)
        steps = plan_gather(
            own, out, *sems, cut=balanced(late, 0), base=early, rows=late
        )
        sequence = pl.program_id(0)

        @pl.when(sequence == 0)
        def _():
            fetch.start()
            greet(NEIGHBOURS)
            steps[0]()
            fetch.wait()

        for start in range(0, units, 256):
            gate_at, up_at = pl.ds(start, 256), pl.ds(units + start, 256)
            gate = jnp.dot(normed[0], weights[:, gate_at], preferred_element_type=jnp.float32)
            up = jnp.dot(normed[0], weights[:, up_at], preferred_element_type=jnp.float32)
            product[0, :, gate_at] = gate
            product[0, :, up_at] = up
            active[0, :, gate_at] = swish_product(gate, up).astype(jnp.bfloat16)
        kept[sequence] = active[0]

        for place in (1, 2, 3):

            @pl.when(sequence == count - 4 + place)
            def _(place=place):
                steps[place]()

        @pl.when(sequence == count - 1)
        def _():
            def bring(turn):
                return pltpu.make_async_copy(
                    out.at[:, :, :, :, pl.ds(turn * 512, 512)],
                    columns_v.at[turn % 2],
                    column_sem.at[turn % 2],
                )

            def pieces(turn):
                slot = turn % 2
                return [
                    pltpu.make_async_copy(
                        staged.at[slot, :, pl.ds(place * share, share)],
                        grad_weight.at[turn * (512 // share) + place],
                        piece_sem.at[slot, place],
                    )
                    for place in range(512 // share)
                ]

            for turn in range(min(2, turns)):
                bring(turn).start()
            for turn in range(turns):
                bring(turn).wait()
                turned = lax.dot_general(
                    kept[...].reshape(count * rows, units),
                    columns_v[turn % 2].reshape(count * rows, 512),
                    (((0,), (0,)), ((), ())),
                    preferred_element_type=jnp.float32,
                )
                if turn >= 2:
                    for copy in pieces(turn - 2):
                        copy.wait()
                staged[turn % 2] = turned.astype(jnp.bfloat16)
                for copy in pieces(turn):
                    copy.start()
                if turn + 2 < turns:
                    bring(turn + 2).start()
            for turn in range(max(0, turns - 2), turns):
                for copy in pieces(turn):
                    copy.wait()

    return pl.pallas_call(
        kernel,
        name="feed",
        grid=(count,),
        out_shape=(
            jax.ShapeDtypeStruct((count, rows, 2 * units), jnp.float32),
            jax.ShapeDtypeStruct((count, rows, units), jnp.bfloat16),
            like(gathered),
            jax.ShapeDtypeStruct((outer_count * split, units, share), jnp.bfloat16),
        ),
        in_specs=[
            per_sequence(rows, width),
            anywhere(),
            whole(*cotangent.shape),
            anywhere(),
        ],
        out_specs=(
            per_sequence(rows, 2 * units),
            per_sequence(rows, units),
            anywhere(),
            anywhere(),
        ),
        scratch_shapes=[
            pltpu.VMEM(weights.shape, weights.dtype),
            pltpu.VMEM((count, rows, units), jnp.bfloat16),
            pltpu.VMEM((2,) + gathered.shape[:4] + (512,), jnp.bfloat16),
            pltpu.VMEM((2, units, 512), jnp.bfloat16),
            pltpu.SemaphoreType.DMA,
            pltpu.SemaphoreType.DMA((2,)),
            pltpu.SemaphoreType.DMA((2, 512 // share)),
        ]
        + gather_scratch(),
        input_output_aliases={3: 2},
        compiler_params=params(number),
        cost_estimate=cost_of(28),
    )(normed, weights, cotangent, gathered)


def feed_back(grads, weights, product, normed, outer_count):
    count, rows, width = grads.shape
    units = weights.shape[1]
    split, share = team_split(width, outer_count)
    turns = width // 512

    def kernel(grads, weights, product, normed, by_gate, by_up, grad_weight, kept):
        step = pl.program_id(0)

        @pl.when(step < count)
        def _():
            for start in range(0, units, 256):
                gate_at, up_at = pl.ds(start, 256), pl.ds(units + start, 256)
                grad = jnp.dot(grads[0], weights[:, gate_at], preferred_element_type=jnp.float32)
                gate, up = product[0, :, gate_at], product[0, :, up_at]
                part = jax.nn.sigmoid(gate)
                slope = grad * up * part * (1.0 + gate * (1.0 - part))
                by_gate[0, :, gate_at] = slope.astype(jnp.bfloat16)
                by_up[0, :, gate_at] = (grad * gate * part).astype(jnp.bfloat16)
            kept[step] = by_gate[0]

        @pl.when(step >= count)
        def _():
            turned = lax.dot_general(
                kept[...].reshape(count * rows, units),
                normed[...],
                (((0,), (0,)), ((), ())),
                preferred_element_type=jnp.float32,
            ).astype(jnp.bfloat16)
            for place in range(512 // share):
                grad_weight[place] = turned[:, place * share : (place + 1) * share]

    def early(*shape):
        return pl.BlockSpec((1,) + shape, lambda s: (jnp.minimum(s, count - 1), 0, 0))

    def late(s):
        return jnp.maximum(s - count, 0)

    return pl.pallas_call(
        kernel,
        name="feed_back",
        grid=(count + turns,),
        out_shape=(jax.ShapeDtypeStruct((count, rows, units), jnp.bfloat16),) * 2
        + (jax.ShapeDtypeStruct((width // share, units, share), jnp.bfloat16),),
        in_specs=[
            early(rows, width),
            whole(*weights.shape),
            early(rows, 2 * units),
            pl.BlockSpec((count * rows, 512), lambda s: (0, late(s))),
        ],
        out_specs=(
            early(rows, units),
            early(rows, units),
            pl.BlockSpec((512 // share, units, share), lambda s: (late(s), 0, 0)),
        ),
        scratch_shapes=[pltpu.VMEM((count, rows, units), jnp.bfloat16)],
        compiler_params=pltpu.CompilerParams(vmem_limit_bytes=VMEM_LIMIT),
        cost_estimate=cost_of(28),
    )(grads, weights, product, normed)


def spans(widths, base=0):
    for member in range(TEAM):
        first, inside = base, 0
        for width in widths:
            share = width // TEAM
            yield member, pl.ds(first + member * share, share), pl.ds(inside, share)
            first += width
            inside += share


def by_turned(height, base, widths, source, members=range(TEAM)):
    parts = [part for part in spans(widths, base) if part[0] in members]

    def run(pieces, update):
        for member, across, inside in parts:
            update(pl.ds(0, height), across, pieces[member, inside].T)

    if len(members) == 1:
        columns = parts[0][1]
    else:
        columns = pl.ds(base, sum(widths))
    return source, pl.ds(0, height), columns, run


def by_rows(member, height, width, inside, source):
    at, across = pl.ds(member * height, height), pl.ds(0, width)

    def run(pieces, update):
        if inside is None:
            update(at, across, pieces[member].T)
        else:
            update(at, across, pieces[member, pl.ds(inside, height)])

    return source, at, across, run


def adam_all(sets, pieces, factor, gain_grad, gains, passed):
    jobs = [(place,) + job for place, group in enumerate(sets) for job in group[3]]
    count, total, sources, others = len(jobs), len(sets), len(pieces), len(passed)

    def kernel(*refs):
        inputs, refs = refs[: 3 * total], refs[3 * total :]
        piece_refs, factor, refs = refs[:sources], refs[sources], refs[sources + 1 :]
        (gain_grad, *gains), refs = refs[:4], refs[4:]
        passed, refs = refs[:others], refs[others:]
        outputs, refs = refs[: 4 * total], refs[4 * total :]
        new_gains, refs = refs[:3], refs[3:]
        onward, refs = refs[:others], refs[others:]
        held, refs = refs[: 4 * total], refs[4 * total :]
        held_pieces, refs = refs[:sources], refs[sources:]
        between, (piece_sem, in_sem, out_sem, pass_sem) = refs[:others], refs[others:]
        scale = factor[0:1, 0:1]
        loads = [
            pltpu.make_async_copy(piece_refs[place], held_pieces[place], piece_sem.at[place])
            for place in range(sources)
        ]
        arrivals, stores = [], []
        kept = [
            pltpu.make_async_copy(source, target, pass_sem.at[0, place])
            for place, (source, target) in enumerate(zip(passed, between))
        ]
        kept_on = [
            pltpu.make_async_copy(source, target, pass_sem.at[1, place])
            for place, (source, target) in enumerate(zip(between, onward))
        ]
        for slot, (place, source, at, across, _) in enumerate(jobs):
            arrivals.append(
                [
                    pltpu.make_async_copy(
                        inputs[3 * place + number].at[at, across],
                        held[4 * place + number].at[at, across],
                        in_sem.at[3 * slot + number],
                    )
                    for number in range(3)
                ]
            )
        first_use = {}
        for slot, job in enumerate(jobs):
            first_use.setdefault(job[1], slot)

        def bring(slot):
            if slot < count:
                if first_use[jobs[slot][1]] == slot:
                    loads[jobs[slot][1]].start()
                for copy in arrivals[slot]:
                    copy.start()

        for slot in range(AHEAD):
            bring(slot)
        gain_step = adam_update(
            gains[0][...],
            gain_grad[: gains[0].shape[0]],
            gains[1][...],
            gains[2][...],
            scale,
            0.0,
            gain_rate,
        )
        for target, value in zip(new_gains, gain_step):
            target[...] = value
        for slot, (place, source, at, across, run) in enumerate(jobs):
            weight, moment, square, low = held[4 * place : 4 * place + 4]
            if first_use[source] == slot:
                loads[source].wait()
            for copy in arrivals[slot]:
                copy.wait()
            bring(slot + AHEAD)
            if slot == 0:
                for copy in kept:
                    copy.start()

            def update(rows, columns, gradient):
                where = (rows, columns)
                value, one, two = adam_update(
                    weight[where],
                    gradient.astype(jnp.float32),
                    moment[where],
                    square[where],
                    scale,
                    weight_decay,
                    learn_rate,
                )
                weight[where], moment[where], square[where] = value, one, two
                low[where] = value.astype(jnp.bfloat16)

            run(held_pieces[source], update)
            for number, origin in enumerate((weight, moment, square, low)):
                copy = pltpu.make_async_copy(
                    origin.at[at, across],
                    outputs[4 * place + number].at[at, across],
                    out_sem.at[4 * slot + number],
                )
                copy.start()
                stores.append(copy)
            if slot == 4:
                for arrived, copy in zip(kept, kept_on):
                    arrived.wait()
                    copy.start()
        for copy in stores + kept_on:
            copy.wait()

    args, shapes, scratch = [], [], []
    for weight, moment, square, _ in sets:
        args += [weight, moment, square]
        low = jax.ShapeDtypeStruct(weight.shape, jnp.bfloat16)
        shapes += [like(weight)] * 3 + [low]
        scratch += [pltpu.VMEM(each.shape, each.dtype) for each in (weight, moment, square, low)]
    outs = pl.pallas_call(
        kernel,
        name="adam_all",
        out_shape=tuple(shapes) + (like(gains[0]),) * 3 + tuple(like(each) for each in passed),
        in_specs=[anywhere()] * (3 * total + sources) + [in_vmem()] * 5 + [anywhere()] * others,
        out_specs=(anywhere(),) * (4 * total) + (in_vmem(),) * 3 + (anywhere(),) * others,
        scratch_shapes=scratch
        + [pltpu.VMEM(each.shape, each.dtype) for each in tuple(pieces) + tuple(passed)]
        + [
            pltpu.SemaphoreType.DMA((sources,)),
            pltpu.SemaphoreType.DMA((3 * count,)),
            pltpu.SemaphoreType.DMA((4 * count,)),
            pltpu.SemaphoreType.DMA((2, others)),
        ],
        compiler_params=pltpu.CompilerParams(vmem_limit_bytes=VMEM_LIMIT),
        cost_estimate=cost_of(15),
    )(*args, *pieces, factor, gain_grad, *gains, *passed)
    steps = [outs[4 * place : 4 * place + 4] for place in range(total)]
    return steps + [outs[4 * total : 4 * total + 3], outs[4 * total + 3 :]]


def rotary(count):
    frequency = rope_base ** (-(np.arange(HD // 2) * 2.0 / HD))
    angles = np.arange(count)[:, None] * frequency[None, :]
    cosine, sine = np.cos(angles), np.sin(angles)
    full = [np.concatenate(pair, axis=1) for pair in ((cosine, cosine), (-sine, sine))]
    return [jnp.asarray(table, jnp.float32) for table in full]


def gather_outer(mixed):
    return lax.all_gather(mixed.reshape(-1, mixed.shape[2]), "outer", axis=0, tiled=True)


def team_pieces(summed):
    return summed.reshape(TEAM, -1, summed.shape[-1])


def turned_pieces(summed):
    if summed.shape[1] * TEAM * lax.axis_size("outer") == D:
        return team_pieces(summed)
    return summed.reshape(summed.shape[0], TEAM, -1).transpose(1, 0, 2)


def sum_weight(gradient):
    return lax.psum_scatter(gradient, "outer", scatter_dimension=0, tiled=True)


def after(values, earlier):
    return lax.optimization_barrier((values, earlier))


def adam_update(weight, gradient, moment_one, moment_two, factor, decay_rate, rate_value):
    clipped = gradient * factor
    moment_one = beta_first * moment_one + (1.0 - beta_first) * clipped
    moment_two = beta_second * moment_two + (1.0 - beta_second) * clipped * clipped
    first_fixed = moment_one * (rate_value / (1.0 - beta_first**STEP))
    root_fixed = jnp.sqrt(moment_two) * (1.0 - beta_second**STEP) ** (-0.5)
    kept = weight * (1.0 - rate_value * decay_rate) if decay_rate else weight
    weight = kept - first_fixed / (root_fixed + adam_epsilon)
    return (weight, moment_one, moment_two)


def dot(left, right, contract):
    return lax.dot_general(
        left, right, ((contract[0], contract[1]), ((), ())), preferred_element_type=jnp.float32
    )


def times(left, right):
    return dot(left, right, ((1,), (0,)))


def times_across(left, right):
    return dot(left, right, ((1,), (1,)))


def over_rows(left, right):
    return dot(left, right, ((0,), (0,)))


def local(
    inputs,
    cotangent,
    lengths,
    owners,
    qkv_weight,
    out_weight,
    gate_up_weight,
    down_weight,
    norm_gains,
    qkv_moment,
    out_moment,
    gate_up_moment,
    down_moment,
    gains_moment,
    qkv_square,
    out_square,
    gate_up_square,
    down_square,
    gains_square,
):
    tp_count = lax.axis_size("tp")
    half_rows = inputs.shape[0]
    row_count = half_rows * tp_count
    heads = H // tp_count // TEAM
    hidden_units = FF // tp_count // TEAM
    qkv_widths = (H * HD // tp_count, KV * HD // tp_count, KV * HD // tp_count)
    out_widths = (H * HD // tp_count,)
    part_rows = qkv_weight.shape[0]
    gate_up_widths = (FF // tp_count, FF // tp_count)
    down_widths = (FF // tp_count,)

    cos_full, sin_full = rotary(row_count)
    gains = norm_gains.reshape(-1, HD)

    normed_attn, gate_up_mixed, first_full, grad_low, down_pieces = opening(
        qkv_weight,
        out_weight,
        gate_up_weight,
        down_weight,
        inputs,
        gains,
        cotangent,
        lengths,
        owners,
        lax.axis_size("outer"),
        0,
    )
    gate_up_full = gather_outer(gate_up_mixed)
    early = half_rows // 2 // CHUNK * CHUNK
    projected, attended, logs, attn_branch, grad_all, down_mixed = attend(
        normed_attn.reshape(TEAM, row_count, D),
        first_full,
        grad_low,
        (down_pieces,),
        lengths,
        owners,
        cos_full,
        sin_full,
        gains,
        heads,
        early,
        1,
    )
    down_full = gather_outer(down_mixed)
    hidden, normed_mlp = branch_and_norm(attn_branch, inputs, gains, 2, "branch_and_norm")
    gate_up, activated, grad_all, grad_down = feed(
        normed_mlp.reshape(TEAM, row_count, D),
        gate_up_full,
        grad_low,
        grad_all,
        early,
        lax.axis_size("outer"),
        8,
    )
    down_sum = turned_pieces(sum_weight(grad_down.reshape(-1, grad_down.shape[2])))
    grad_gate, grad_up, grad_gate_weight = feed_back(
        grad_all.reshape(TEAM, row_count, D),
        down_full,
        gate_up,
        normed_mlp,
        lax.axis_size("outer"),
    )
    gate_sum = turned_pieces(
        sum_weight(grad_gate_weight.reshape(-1, grad_gate_weight.shape[2]))
    )
    grad_hidden, grad_mlp_gain, own_grad, mlp_part, grad_up_weight = feed_back_rest(
        grad_gate,
        grad_up,
        gate_up_full,
        activated,
        down_full,
        normed_mlp,
        hidden,
        grad_low,
        gains,
        lax.axis_size("outer"),
        3,
        "feed_back_rest",
    )
    up_sum = turned_pieces(sum_weight(grad_up_weight.reshape(-1, grad_up_weight.shape[2])))
    _, grad_head_gains, grad_normed_attn, output, grad_first, down_mixed = attend_back(
        projected,
        normed_attn.reshape(TEAM, row_count, D),
        attended,
        own_grad,
        logs,
        first_full,
        mlp_part,
        hidden,
        (down_sum,),
        lax.axis_size("outer"),
        lengths,
        owners,
        cos_full,
        sin_full,
        gains,
        heads,
        7,
    )
    grad_first, gate_sum = after(grad_first, gate_sum)
    first_sum = turned_pieces(sum_weight(grad_first.reshape(-1, grad_first.shape[3])))
    input_grad, attn_gain_parts, squares, gate_mixed, up_mixed = norm_back_last(
        grad_normed_attn,
        inputs,
        grad_hidden,
        gains,
        (gate_sum, up_sum),
        (gate_sum, up_sum, down_sum),
        4,
        "norm_back_attn",
    )
    packed, norm_value, factor_tile, first_mixed = total_everywhere(
        attn_gain_parts,
        grad_mlp_gain,
        grad_head_gains,
        squares,
        first_sum,
        lax.axis_size("outer"),
        5,
        "total_everywhere",
    )
    grad_norm = norm_value.reshape(())
    (
        (new_gate_up, new_gate_up_one, new_gate_up_two, gate_up_copy),
        (new_down, new_down_one, new_down_two, down_copy),
        (new_out, new_out_one, new_out_two, out_copy),
        (new_qkv, new_qkv_one, new_qkv_two, qkv_copy),
        new_gains,
        (output, input_grad),
    ) = adam_all(
        [
            (
                gate_up_weight,
                gate_up_moment,
                gate_up_square,
                [
                    by_turned(part_rows, base, gate_up_widths[:1], source, (member,))
                    for source, base in enumerate((0, gate_up_widths[0]))
                    for member in range(TEAM)
                ],
            ),
            (
                down_weight,
                down_moment,
                down_square,
                [by_rows(member, hidden_units, part_rows, 0, 2) for member in range(TEAM)],
            ),
            (
                out_weight,
                out_moment,
                out_square,
                [
                    by_rows(member, heads * HD, part_rows, (heads + 2) * HD, 3)
                    for member in range(TEAM)
                ],
            ),
            (
                qkv_weight,
                qkv_moment,
                qkv_square,
                [by_turned(part_rows, 0, qkv_widths, 3)],
            ),
        ],
        (gate_mixed, up_mixed, down_mixed, first_mixed),
        factor_tile,
        packed,
        [gains] + [each.reshape(-1, HD) for each in (gains_moment, gains_square)],
        (output, input_grad),
    )
    new_gains, new_gains_one, new_gains_two = (each.reshape(-1) for each in new_gains)
    return (
        output,
        input_grad,
        grad_norm,
        new_qkv,
        new_qkv_one,
        new_qkv_two,
        qkv_copy,
        new_out,
        new_out_one,
        new_out_two,
        out_copy,
        new_gate_up,
        new_gate_up_one,
        new_gate_up_two,
        gate_up_copy,
        new_down,
        new_down_one,
        new_down_two,
        down_copy,
        new_gains,
        new_gains_one,
        new_gains_two,
    )


def solution(mesh):
    fsdp_count, tp_count = mesh.shape["fsdp"], mesh.shape["tp"]
    cut = mesh.devices.reshape(fsdp_count // TEAM, NEAR, CORE, tp_count)
    cut_mesh = Mesh(cut, ("outer",) + LAYER)
    fsdp = ("outer", "near", "core")
    rows = P(fsdp + ("tp",), None)
    wide = P(fsdp, "tp")
    tall = P("tp", fsdp)
    weights = (wide, tall, wide, tall, P())
    return jax.shard_map(
        local,
        mesh=cut_mesh,
        in_specs=(rows, rows, P(), P()) + weights * 3,
        out_specs=(rows, rows, P()) + (wide,) * 4 + (tall,) * 4 + (wide,) * 4 + (tall,) * 4 + (P(),) * 3,
        check_vma=False,
    )
```
